32 devices in a mesh: row: 8 (over z, x), col: 4 (over y, core).
Axes of the slice: x: 2, y: 2, z: 4, core: 2. Of those that a mesh axis runs over, the one named last changes fastest.
Arguments:
- features: bfloat16 [192, 52, 2048], P('row', 'col'), may hold values from -6 to 6
- crop_rows: int32 [5], replicated, may hold values from 1 to 49, 192 in all
- crop_cols: int32 [5], replicated, may hold values from 25 to 49
- w_point: bfloat16 [2048, 256], P('row'), may hold values from -0.125 to 0.125
- w_atrous: bfloat16 [2048, 27, 256], P('row'), may hold values from -0.046875 to 0.046875
- w_pool: bfloat16 [2048, 256], P('row'), may hold values from -0.125 to 0.125
- w_proj: bfloat16 [1280, 256], P('row'), may hold values from -0.15625 to 0.15625
- gains: float32 [6, 256], replicated, may hold values from 0.5 to 1.5
- biases: float32 [6, 256], replicated, may hold values from -3 to 3
- cotangent: bfloat16 [192, 52, 256], P('row', 'col'), may hold values from -6 to 6
Outputs:
- result: bfloat16 [192, 52, 256], P('row', 'col')
- d_features: bfloat16 [192, 52, 2048], P('row', 'col')
- d_point: float32 [2048, 256], P('row')
- d_atrous: float32 [2048, 27, 256], P('row')
- d_pool: float32 [2048, 256], P('row')
- d_proj: float32 [1280, 256], P('row')
- d_gains: float32 [6, 256], replicated
- d_biases: float32 [6, 256], replicated
The draws below stay inside these ranges and needn't reach their ends.
Inputs may be any that keep to these rules, and one draw needn't show every extreme that they name: `crop_rows`: crop heights sum to 192; the tallest crop has 49 rows.
All inputs are finite; a program needn't handle non-finite values.
Results may differ from the reference program's by a relative error of at most 0.02.
Values may be sent and summed in bfloat16 or wider, within the bound.
A program may use at most 384 MiB of HBM per device.

```python
import math
import jax
import jax.numpy as jnp
import numpy as np
from jax import lax

CIN = 2048
BR = 256
ROWS_DEV = 24
ROWS = 192
COLS = 52
CROPS = 5


def place_ends(drawn, key, low, largest):
    longest = drawn.shape.index(max(drawn.shape))
    spots = []
    for shift in (0, 1):
        where = [jax.random.randint(jax.random.fold_in(key, axis), (), 0, length) for axis, length in enumerate(drawn.shape)]
        where[longest] = (where[longest] + shift) % drawn.shape[longest]
        spots.append(tuple(where))
    return drawn.at[spots[0]].set(low).at[spots[1]].set(largest)


def level_of(own_key, extent, split, least, largest):
    level, own = 1.0, jax.random.fold_in(own_key, 6)
    for dim, blocks in split:
        heights = jnp.exp(jax.random.uniform(jax.random.fold_in(own, dim), (blocks,), jnp.float32, least / len(split), largest / len(split)))
        level = level * jnp.repeat(heights, extent[dim] // blocks).reshape([-1 if axis == dim else 1 for axis in range(len(extent))])
    return level


def length_profile(number_of, total, reach, slope):
    portions = [(1 << 20) // math.isqrt(standing ** slope) + 1 for standing in range(2, number_of + 1)]
    surplus, holding = total - reach - (number_of - 1), [1] * (number_of - 1)
    while surplus > 0:
        candidates = [i for i in range(number_of - 1) if holding[i] < reach]
        pool, remaining = sum([portions[i] for i in candidates]), surplus
        for i in candidates:
            addition = min(reach - holding[i], max(1, remaining * portions[i] // pool), surplus)
            holding[i] = holding[i] + addition
            surplus = surplus - addition
    return np.array([reach] + holding)


def uneven_parts(key, amount, total, limit, slope):
    if amount == 2:
        one = jax.random.randint(key, (), max(1, total - limit), min(limit, total - 1) + 1)
        return jnp.stack([one, total - one])
    sizes = jnp.asarray(length_profile(amount, total, limit, slope), jnp.int32)
    twos = (amount - 1) // 2
    source_of, taker = sizes[1:1 + 2 * twos:2], sizes[2:2 + 2 * twos:2]
    margin = jnp.minimum(source_of - 1, limit - taker)
    passed = jax.random.randint(jax.random.fold_in(key, 1), (twos,), 0, 1 << 20) % (margin + 1)
    sizes = sizes.at[1:1 + 2 * twos:2].set(source_of - passed).at[2:2 + 2 * twos:2].set(taker + passed)
    return sizes[jax.random.permutation(jax.random.fold_in(key, 2), amount)]


def gaussian(own_key, extent, spread, most, split=(), held_as=jnp.bfloat16):
    array = jax.random.normal(own_key, extent, jnp.float32) * spread
    if len(split) > 0:
        array = level_of(own_key, extent, split, -0.22, 0.18) * array
    return jnp.clip(array, min=-most, max=most).astype(held_as)


def setup_inputs(seed: int = 0) -> dict:
    seeds = jax.random.split(jax.random.key(seed), 11)
    features = gaussian(seeds[0], (ROWS, COLS, CIN), 1.0, 6.0, ((0, 8), (1, 4)))
    crop_rows = uneven_parts(seeds[1], CROPS, ROWS, 49, 2).astype(jnp.int32)
    crop_cols = place_ends(jax.random.randint(seeds[2], (CROPS,), 25, 50), jax.random.fold_in(seeds[2], 1), 25, 49).astype(jnp.int32)
    w_point = gaussian(seeds[3], (CIN, BR), CIN ** -0.5, 0.125, ((0, 8),))
    w_atrous = gaussian(seeds[4], (CIN, 27, BR), (9 * CIN) ** -0.5, 0.046875, ((0, 8),))
    w_pool = gaussian(seeds[5], (CIN, BR), CIN ** -0.5, 0.125, ((0, 8),))
    w_proj = gaussian(seeds[6], (5 * BR, BR), (5 * BR) ** -0.5, 0.15625, ((0, 8),))
    gains = jnp.clip(1.0 + 0.1 * jax.random.normal(seeds[7], (6, BR), jnp.float32), 0.5, 1.5)
    biases = gaussian(seeds[8], (6, BR), 0.5, 3.0, (), jnp.float32)
    cotangent = gaussian(seeds[9], (ROWS, COLS, BR), 1.0, 6.0, ((0, 8), (1, 4)))
    return {"features": features, "crop_rows": crop_rows, "crop_cols": crop_cols, "w_point": w_point, "w_atrous": w_atrous, "w_pool": w_pool, "w_proj": w_proj, "gains": gains, "biases": biases, "cotangent": cotangent}


EPSILON = 1e-05
MARGIN = 18
DILATIONS = (6, 12, 18)
HIGHEST = lax.Precision.HIGHEST

@jax.custom_vjp
def low(v):
    return lax.optimization_barrier(v.astype(jnp.bfloat16)).astype(jnp.float32)

@jax.custom_vjp
def low_back(v):
    return v

def low_keep(v):
    return (low(v), None)

def low_pass(kept, grad):
    return (grad,)

def back_keep(v):
    return (v, None)

def back_low(kept, grad):
    return (low(grad),)
low.defvjp(low_keep, low_pass)
low_back.defvjp(back_keep, back_low)

def masked_norm(preact, pixel_mask, pixels, gain, shift):
    centre = lax.optimization_barrier(jnp.sum(preact * pixel_mask, axis=(0, 1))) / pixels
    square = lax.optimization_barrier(jnp.sum(preact * preact * pixel_mask, axis=(0, 1))) / pixels
    inv_scale = lax.rsqrt(square - centre * centre + EPSILON)
    return jax.nn.silu(gain * (preact - centre) * inv_scale + shift)

def reference(features, crop_rows, crop_cols, w_point, w_atrous, w_pool, w_proj, gains, biases, cotangent):
    crop_ends = jnp.cumsum(crop_rows).astype(jnp.int32)
    row_ids = jnp.arange(ROWS, dtype=jnp.int32)
    crop_of = lax.optimization_barrier(jnp.sum((row_ids[:, None] >= crop_ends[None, :]).astype(jnp.int32), axis=1)).astype(jnp.int32)
    member = (crop_of[:, None] == jnp.arange(CROPS, dtype=jnp.int32)[None, :]).astype(jnp.float32)
    widths = lax.optimization_barrier(jnp.sum(member * crop_cols.astype(jnp.float32)[None, :], axis=1))
    valid_mask = (jnp.arange(COLS, dtype=jnp.int32)[None, :].astype(jnp.float32) < widths[:, None]).astype(jnp.float32)
    pixel_mask = valid_mask[:, :, None]
    counts = (crop_rows * crop_cols).astype(jnp.float32)
    pixels = jnp.sum(counts)
    block_rows = 4 * ROWS_DEV
    blocks = ROWS // block_rows
    row_index = (jnp.arange(blocks, dtype=jnp.int32) * block_rows)[:, None] + jnp.arange(block_rows + 2 * MARGIN, dtype=jnp.int32)[None, :]
    crop_padded = jnp.pad(crop_of, MARGIN, constant_values=-1)
    crop_windows = crop_padded[row_index]

    def forward(feats, wpt, watr, wpl, wpj, gain_all, bias_all):
        masked = feats * pixel_mask
        point = low_back(jnp.einsum('rcf,fo->rco', masked, wpt, precision=HIGHEST))
        row_padded = jnp.pad(masked, ((MARGIN, MARGIN), (0, 0), (0, 0)))
        windows = row_padded[row_index]

        def atrous_block(block_item):
            window, crop_window = block_item
            widened = jnp.pad(window, ((0, 0), (MARGIN, MARGIN), (0, 0)))
            own_crop = crop_window[MARGIN:MARGIN + block_rows]
            outputs = []
            for branch_idx, dilation in enumerate(DILATIONS):
                running = jnp.zeros((block_rows, COLS, BR), window.dtype)
                for i in (-1, 0, 1):
                    same_crop = (crop_window[MARGIN + i * dilation:MARGIN + i * dilation + block_rows] == own_crop).astype(window.dtype)
                    for j in (-1, 0, 1):
                        tap_index = 9 * branch_idx + 3 * (i + 1) + (j + 1)
                        shifted = widened[MARGIN + i * dilation:MARGIN + i * dilation + block_rows, MARGIN + j * dilation:MARGIN + j * dilation + COLS]
                        running = running + same_crop[:, None, None] * jnp.einsum('rcf,fo->rco', shifted, watr[:, tap_index, :], precision=HIGHEST)
                outputs.append(running)
            return jnp.stack(outputs)
        stacked = lax.map(jax.checkpoint(atrous_block), (windows, crop_windows))
        atrous = low_back(jnp.transpose(stacked, (1, 0, 2, 3, 4)).reshape(3, ROWS, COLS, BR))
        crop_sums = jnp.einsum('rk,rcf->kf', member, masked, precision=HIGHEST)
        pooled = low(crop_sums / counts[:, None])
        pool_pre = low_back(jnp.dot(pooled, wpl, precision=HIGHEST))
        pool_centre = lax.optimization_barrier(jnp.mean(pool_pre, axis=0))
        pool_square = lax.optimization_barrier(jnp.mean(pool_pre * pool_pre, axis=0))
        pool_out = jax.nn.silu(gain_all[4] * (pool_pre - pool_centre) * lax.rsqrt(pool_square - pool_centre * pool_centre + EPSILON) + bias_all[4])
        pool_pixels = jnp.dot(member, pool_out, precision=HIGHEST)
        branches = [masked_norm(point, pixel_mask, pixels, gain_all[0], bias_all[0])]
        for branch_idx in range(3):
            branches.append(masked_norm(atrous[branch_idx], pixel_mask, pixels, gain_all[branch_idx + 1], bias_all[branch_idx + 1]))
        branches.append(jnp.broadcast_to(pool_pixels[:, None, :], (ROWS, COLS, BR)))
        joined = low(jnp.concatenate(branches, axis=-1))
        projected = low_back(jnp.einsum('rch,ho->rco', joined, wpj, precision=HIGHEST))
        return masked_norm(projected, pixel_mask, pixels, gain_all[5], bias_all[5]) * pixel_mask
    float_args = (features.astype(jnp.float32), w_point.astype(jnp.float32), w_atrous.astype(jnp.float32), w_pool.astype(jnp.float32), w_proj.astype(jnp.float32), gains.astype(jnp.float32), biases.astype(jnp.float32))
    result, pullback = jax.vjp(forward, *float_args)
    grads = pullback(cotangent.astype(jnp.float32))
    return (result.astype(jnp.bfloat16), grads[0].astype(jnp.bfloat16), grads[1], grads[2], grads[3], grads[4], grads[5], grads[6])
```

```python
import functools

import jax
import jax.numpy as jnp
import numpy as np
from jax import lax
from jax.experimental import pallas as pl
from jax.experimental.pallas import tpu as pltpu
from jax.sharding import PartitionSpec as P

EPSILON = 1e-05
MARGIN = 18
DILATIONS = (6, 12, 18)
MEMBERS = 8
TAPS = 29
MESH = pl.DeviceIdType.MESH
F32 = jnp.float32
BF16 = jnp.bfloat16
GROUPS = ((0, 4), (4, 7), (7, 10), (10, 13), (13, 16), (16, 19), (19, 22), (22, 25), (25, 29))


def up_to(value, multiple):
    return -(-value // multiple) * multiple


class Plan:
    def __init__(self, rows_axis, cols_axis, h, bc, channels, width, crops):
        self.R, self.C = rows_axis, cols_axis
        self.h, self.bc, self.channels, self.width = h, bc, channels, width
        self.G = MEMBERS // self.C
        self.slabs = self.R // self.G
        self.H = self.G * h
        self.cols = bc * self.C
        self.S = up_to(self.cols, 8)
        self.rpb = self.H // MEMBERS
        self.px = self.rpb * self.S
        self.own = MEMBERS * self.px
        self.hb = MARGIN // self.rpb
        self.nb = MEMBERS + 2 * self.hb
        self.ext = self.nb * self.px
        self.bp = up_to(bc, 16)
        self.cs = channels // MEMBERS
        self.part = self.cs // self.C
        self.crops = crops
        self.ncp = up_to(crops, 16)
        self.exchange = self.slabs == self.C and self.R == MEMBERS
        self.steps = tuple(d // self.rpb for d in DILATIONS)


def remote(src, dst, send, recv, device):
    return pltpu.make_async_remote_copy(
        src_ref=src, dst_ref=dst, send_sem=send, recv_sem=recv, device_id=device, device_id_type=MESH
    )


def greet_all(pn, row, col):
    total = pn.R * pn.C
    barrier = pltpu.get_barrier_semaphore()
    me = row * pn.C + col

    def hello(k, carry):
        other = lax.rem(me + k, total)
        pl.semaphore_signal(
            barrier, inc=1, device_id=(other // pn.C, lax.rem(other, pn.C)), device_id_type=MESH
        )
        return carry

    lax.fori_loop(1, total, hello, 0)
    pl.semaphore_wait(barrier, total - 1)


def dot(a, b):
    return jnp.dot(a, b, preferred_element_type=F32)


def dot_nt(a, b):
    return lax.dot_general(a, b, (((1,), (1,)), ((), ())), preferred_element_type=F32)


def dot_tn(a, b):
    return lax.dot_general(a, b, (((0,), (0,)), ((), ())), preferred_element_type=F32)


def split_dot(dot_fn, a, b):
    high = a.astype(BF16)
    low = (a - high.astype(F32)).astype(BF16)
    return dot_fn(high, b) + dot_fn(low, b)


def conv_kernel(pn, feats, w_in, cot, masks, sel, hot_t, inv_counts, p_out, x_out, w_out, m_out, p4_out, cot_out,
                ring, xs, wbuf, acc, pbuf, cbuf, sbuf, rbuf, cx,
                f_s, f_r, h_s, h_up, h_dn, c_s, c_r, w_s, w_r, w_l, r1_s, r1_r, r2_s, r2_r, o_s):
    row, col = lax.axis_index("row"), lax.axis_index("col")
    slab, x = row // pn.G, lax.rem(row, pn.G)
    me = x * pn.C + col
    core, quad = lax.rem(col, 2), me // 2
    h, H, bp, px = pn.h, pn.H, pn.bp, pn.px

    def member(s, k):
        return (s * pn.G + k // pn.C, lax.rem(k, pn.C))

    greet_all(pn, row, col)

    own_cols = pl.ds(pl.multiple_of(col * bp, bp), bp)
    own_rows = pl.ds(MARGIN + h * x, h)
    sent = []
    for kk in range(1, MEMBERS):
        other = lax.rem(me + kk, MEMBERS)
        c = remote(feats.at[other], ring.at[own_rows, own_cols], f_s.at[kk], f_r.at[kk], member(slab, other))
        c.start()
        sent.append(c)
    keep = pltpu.make_async_copy(feats.at[me], ring.at[own_rows, own_cols], f_r.at[0])
    keep.start()
    to_up, to_down = (x == 0) & (slab > 0), (x == pn.G - 1) & (slab < pn.slabs - 1)

    def halo(kk, down):
        if down:
            src, dst, sem, s = feats.at[kk, pl.ds(h - MARGIN, MARGIN)], ring.at[pl.ds(0, MARGIN), own_cols], h_up, slab + 1
        else:
            src, dst, sem, s = feats.at[kk, pl.ds(0, MARGIN)], ring.at[pl.ds(MARGIN + H, MARGIN), own_cols], h_dn, slab - 1
        return remote(src, dst, h_s.at[int(down), kk], sem.at[col], (s * pn.G + kk // pn.C, kk % pn.C))

    @pl.when(to_up)
    def _():
        for kk in range(MEMBERS):
            halo(kk, False).start()

    @pl.when(to_down)
    def _():
        for kk in range(MEMBERS):
            halo(kk, True).start()

    cot_sent = []
    for cc in range(1, pn.C):
        cd = lax.rem(col + cc, pn.C)
        c = remote(cot.at[pl.ds(cd * pn.rpb, pn.rpb)], cx.at[:, own_cols], c_s.at[cc], c_r.at[cc], (row, cd))
        c.start()
        cot_sent.append(c)
    cot_keep = pltpu.make_async_copy(cot.at[pl.ds(col * pn.rpb, pn.rpb)], cx.at[:, own_cols], c_r.at[0])
    cot_keep.start()

    def w_local(g):
        a, b = GROUPS[g]
        return pltpu.make_async_copy(w_in.at[pl.ds(a, b - a)], wbuf.at[pl.ds(a, b - a)], w_l.at[g])

    def w_send(g, zz, src_col):
        a, b = GROUPS[g]
        to = lax.rem(slab + zz, pn.slabs)
        rows = pl.ds(pl.multiple_of(src_col * pn.part, pn.part), pn.part)
        return remote(w_in.at[pl.ds(a, b - a), rows], wbuf.at[pl.ds(a, b - a), rows],
                      w_s.at[zz, g], w_r.at[g, src_col], (to * pn.G + x, slab))

    if pn.exchange:
        for g in range(len(GROUPS)):
            for zz in range(1, pn.slabs):
                w_send(g, zz, col).start()

        @pl.when(slab == col)
        def _():
            for g in range(len(GROUPS)):
                w_local(g).start()
    else:
        for g in range(len(GROUPS)):
            w_local(g).start()

    def w_wait(g):
        if pn.exchange:
            @pl.when(slab == col)
            def _():
                w_local(g).wait()

            @pl.when(slab != col)
            def _():
                for j in range(pn.C):
                    w_send(g, 1, j).wait_recv()
        else:
            w_local(g).wait()

    @pl.when(slab == 0)
    def _():
        ring[pl.ds(0, MARGIN)] = jnp.zeros((MARGIN, pn.C * bp, pn.cs), BF16)

    @pl.when(slab == pn.slabs - 1)
    def _():
        ring[pl.ds(MARGIN + H, MARGIN)] = jnp.zeros((MARGIN, pn.C * bp, pn.cs), BF16)

    for c in sent:
        c.wait()
    keep.wait()

    @pl.when(slab > 0)
    def _():
        for j in range(pn.C):
            remote(feats.at[0, pl.ds(0, MARGIN)], ring.at[pl.ds(0, MARGIN), pl.ds(j * bp, bp)], h_s.at[0, 0], h_up.at[j],
                   member(slab - 1, me)).wait_recv()

    @pl.when(slab < pn.slabs - 1)
    def _():
        for j in range(pn.C):
            remote(feats.at[0, pl.ds(0, MARGIN)], ring.at[pl.ds(MARGIN + H, MARGIN), pl.ds(j * bp, bp)], h_s.at[0, 0],
                   h_dn.at[j], member(slab + 1, me)).wait_recv()

    def assemble(rp, carry):
        pair = ring[pl.ds(2 * rp, 2)].reshape(2 * pn.C * bp, pn.cs)
        moved = dot(sel[...], pair).astype(BF16)
        at = pl.multiple_of(rp * 2 * pn.S, 16)
        for v in range(7):
            xs[v, pl.ds(at, 2 * pn.S)] = moved[v * 2 * pn.S:(v + 1) * 2 * pn.S]
        return carry

    lax.fori_loop(0, pn.nb * pn.rpb // 2, assemble, 0)
    x_save = pltpu.make_async_copy(xs, x_out, o_s.at[0])
    x_save.start()

    for c in cot_sent:
        c.wait()
    cot_keep.wait()
    for rp in range(pn.rpb // 2):
        pair = cx[2 * rp:2 * rp + 2].reshape(2 * pn.C * bp, pn.width)
        cot_out[pl.ds(rp * 2 * pn.S, 2 * pn.S)] = dot(sel[pl.ds(3 * 2 * pn.S, 2 * pn.S)], pair).astype(BF16)

    def first_stage(slot):
        return remote(pbuf.at[slot, :, 1 - core], cbuf.at[slot], r1_s.at[slot], r1_r.at[slot], (row, col + 1 - 2 * core))

    def second_stage(slot, i):
        q = lax.rem(quad + i, MEMBERS // 2)
        return remote(sbuf.at[slot, i - 1], rbuf.at[slot, i - 1], r2_s.at[slot, i - 1], r2_r.at[slot, i - 1],
                      member(slab, 2 * q + core))

    def middle(slot):
        first_stage(slot).wait()
        for i in range(MEMBERS // 2):
            q = lax.rem(quad + i, MEMBERS // 2)
            s = pbuf[slot, q, core].astype(F32) + cbuf[slot, q].astype(F32)
            if i == 0:
                p_out[slot] = s
            else:
                sbuf[slot, i - 1] = s.astype(BF16)
                second_stage(slot, i).start()

    def last(slot):
        total = p_out[slot]
        for i in range(1, MEMBERS // 2):
            second_stage(slot, i).wait()
            total = total + rbuf[slot, i - 1].astype(F32)
        p_out[slot] = total

    for branch in (1, 2, 3):
        step = pn.steps[branch - 1]
        for i in (-1, 0, 1):
            g = 3 * (branch - 1) + i + 1
            tap = 1 + 3 * g
            w_wait(g)
            mask_at = (2 * (branch - 1) + (i + 1) // 2) * H

            if g == 0:
                def point(rb, carry):
                    at = pl.multiple_of(rb * px, 16)
                    y = dot(xs[3, pl.ds(pl.multiple_of(pn.hb * px + at, 16), px)], wbuf[0])
                    pbuf[0, rb // 2, lax.rem(rb, 2)] = y.astype(BF16)
                    return carry

                lax.fori_loop(0, MEMBERS, point, 0)
                first_stage(0).start()

            def block(rb, carry, step=step, i=i, tap=tap, mask_at=mask_at, branch=branch):
                at = pl.multiple_of(rb * px, 16)
                window = pl.ds(pl.multiple_of((rb + pn.hb + i * step) * px, 16), px)
                y = dot(xs[3 - branch, window], wbuf[tap])
                y = y + dot(xs[3, window], wbuf[tap + 1])
                y = y + dot(xs[3 + branch, window], wbuf[tap + 2])
                if i != 0:
                    y = jnp.concatenate(
                        [y[r * pn.S:(r + 1) * pn.S] * masks[mask_at + rb * pn.rpb + r] for r in range(pn.rpb)], axis=0
                    )
                if i > -1:
                    y = y + acc[pl.ds(at, px)]
                if i < 1:
                    acc[pl.ds(at, px)] = y
                else:
                    pbuf[branch, rb // 2, lax.rem(rb, 2)] = y.astype(BF16)
                return carry

            lax.fori_loop(0, MEMBERS, block, 0)
        first_stage(branch).start()
        middle(branch - 1)

    sums = dot(hot_t[...], xs[3, pl.ds(pn.hb * px, pn.own)])
    means = sums * inv_counts[...]
    m_out[...] = means
    p4_out[...] = split_dot(dot, means, wbuf[TAPS - 1])
    w_save = pltpu.make_async_copy(wbuf, w_out, o_s.at[1])
    w_save.start()
    middle(3)
    for slot in range(4):
        last(slot)

    @pl.when(to_up)
    def _():
        for kk in range(MEMBERS):
            halo(kk, False).wait_send()

    @pl.when(to_down)
    def _():
        for kk in range(MEMBERS):
            halo(kk, True).wait_send()

    if pn.exchange:
        for g in range(len(GROUPS)):
            for zz in range(1, pn.slabs):
                w_send(g, zz, col).wait_send()
    x_save.wait()
    w_save.wait()


def conv_forward(pn, feats, w, cot, masks, sel, hot_t, inv_counts):
    half = MEMBERS // 2
    dma = pltpu.SemaphoreType.DMA
    vmem = pl.BlockSpec(memory_space=pltpu.VMEM)
    hbm = pl.BlockSpec(memory_space=pl.ANY)
    shape = jax.ShapeDtypeStruct
    ng = len(GROUPS)
    return pl.pallas_call(
        functools.partial(conv_kernel, pn),
        out_shape=(
            shape((4, pn.px, pn.width), F32),
            shape((7, pn.ext, pn.cs), BF16),
            shape((TAPS, pn.cs, pn.width), BF16),
            shape((pn.ncp, pn.cs), F32),
            shape((pn.ncp, pn.width), F32),
            shape((pn.px, pn.width), BF16),
        ),
        in_specs=[hbm, hbm, hbm, pl.BlockSpec(memory_space=pltpu.SMEM), vmem, vmem, vmem],
        out_specs=(vmem, hbm, hbm, vmem, vmem, vmem),
        scratch_shapes=[
            pltpu.VMEM((pn.nb * pn.rpb, pn.C * pn.bp, pn.cs), BF16),
            pltpu.VMEM((7, pn.ext, pn.cs), BF16),
            pltpu.VMEM((TAPS, pn.cs, pn.width), BF16),
            pltpu.VMEM((pn.own, pn.width), F32),
            pltpu.VMEM((4, half, 2, pn.px, pn.width), BF16),
            pltpu.VMEM((4, half, pn.px, pn.width), BF16),
            pltpu.VMEM((4, half - 1, pn.px, pn.width), BF16),
            pltpu.VMEM((4, half - 1, pn.px, pn.width), BF16),
            pltpu.VMEM((pn.rpb, pn.C * pn.bp, pn.width), BF16),
            dma((MEMBERS,)), dma((MEMBERS,)), dma((2, MEMBERS)), dma((pn.C,)), dma((pn.C,)), dma((pn.C,)), dma((pn.C,)),
            dma((pn.C, ng)), dma((ng, pn.C)), dma((ng,)), dma((4,)), dma((4,)), dma((4, 3)), dma((4, 3)), dma((2,)),
        ],
        compiler_params=pltpu.CompilerParams(collective_id=0, has_side_effects=True, vmem_limit_bytes=60 * 2**20),
        name="conv_forward",
    )(feats, w, cot, masks, sel, hot_t, inv_counts)


def norm_kernel(pn, p, p4_in, gains, biases, valid, pixels, w_proj, cot, hot, hot_t, sel_t,
                q_out, q4_out, dproj_out, res_out, dg_out, db_out,
                norm, slope, hbuf, gact, dh4, rx,
                a1, b1, a2, b2, a3, b3, a4, b4, as_s, as_r, bs_s, bs_r, e_s, e_r):
    row, col = lax.axis_index("row"), lax.axis_index("col")
    slab, x = row // pn.G, lax.rem(row, pn.G)
    me = x * pn.C + col
    crops = float(pn.crops)
    v = valid[...]
    inv_px = pixels[0]
    width, bp = pn.width, pn.bp

    def member(s, k):
        return (s * pn.G + k // pn.C, lax.rem(k, pn.C))

    barrier = pltpu.get_barrier_semaphore()
    for kk in range(1, MEMBERS):
        pl.semaphore_signal(barrier, inc=1, device_id=member(slab, lax.rem(me + kk, MEMBERS)), device_id_type=MESH)

    def hello(k, carry):
        pl.semaphore_signal(barrier, inc=1, device_id=member(lax.rem(slab + k, pn.slabs), me), device_id_type=MESH)
        return carry

    lax.fori_loop(1, pn.slabs, hello, 0)

    def peer_a(n, abuf, kk):
        return remote(abuf.at[me], abuf.at[me], as_s.at[n, kk], as_r.at[n, kk], member(slab, lax.rem(me + kk, MEMBERS)))

    def peer_b(n, bbuf, k):
        return remote(bbuf.at[slab], bbuf.at[slab], bs_s.at[n, k], bs_r.at[n, k], member(lax.rem(slab + k, pn.slabs), me))

    def reduce_start(n, abuf):
        for kk in range(1, MEMBERS):
            peer_a(n, abuf, kk).start()

    def reduce_end(n, abuf, bbuf):
        for kk in range(1, MEMBERS):
            peer_a(n, abuf, kk).wait()
        total = abuf[0]
        for k in range(1, MEMBERS):
            total = total + abuf[k]
        bbuf[slab] = total
        for k in range(1, pn.slabs):
            peer_b(n, bbuf, k).start()
        for k in range(1, pn.slabs):
            peer_b(n, bbuf, k).wait()
        total = bbuf[0]
        for k in range(1, pn.slabs):
            total = total + bbuf[k]
        return total

    def column_sum(value):
        return jnp.sum(value, axis=0, keepdims=True)

    for b in range(4):
        pv = p[b] * v
        a1[me, pl.ds(b, 1)] = column_sum(pv)
        a1[me, pl.ds(4 + b, 1)] = column_sum(pv * p[b])
    a1[me, pl.ds(8, pn.ncp)] = p4_in[...]
    pl.semaphore_wait(barrier, MEMBERS - 1 + pn.slabs - 1)
    reduce_start(0, a1)
    total = reduce_end(0, a1, b1)
    inv = []
    for b in range(4):
        centre = total[b:b + 1] * inv_px
        scale = lax.rsqrt(total[4 + b:5 + b] * inv_px - centre * centre + EPSILON)
        inv.append(scale)
        n = (p[b] - centre) * scale
        u = gains[b:b + 1] * n + biases[b:b + 1]
        s = jax.nn.sigmoid(u)
        norm[b] = n
        slope[b] = s * (1.0 + u * (1.0 - s))
        hbuf[b] = (u * s).astype(BF16)
    p4 = total[8:8 + pn.ncp]
    centre4 = column_sum(p4) * (1.0 / crops)
    inv4 = lax.rsqrt(column_sum(p4 * p4) * (1.0 / crops) - centre4 * centre4 + EPSILON)
    n4 = (p4 - centre4) * inv4
    u4 = gains[4:5] * n4 + biases[4:5]
    s4 = jax.nn.sigmoid(u4)
    slope4 = s4 * (1.0 + u4 * (1.0 - s4))
    hbuf[4] = dot(hot[...], (u4 * s4).astype(BF16)).astype(BF16)

    p5 = dot(hbuf[0], w_proj[pl.ds(0, width)])
    for b in range(1, 5):
        p5 = p5 + dot(hbuf[b], w_proj[pl.ds(b * width, width)])
    pv = p5 * v
    a2[me, pl.ds(0, 1)] = column_sum(pv)
    a2[me, pl.ds(1, 1)] = column_sum(pv * p5)
    a2[me, pl.ds(2, 6)] = jnp.zeros((6, width), F32)
    reduce_start(1, a2)
    total = reduce_end(1, a2, b2)
    centre5 = total[0:1] * inv_px
    inv5 = lax.rsqrt(total[1:2] * inv_px - centre5 * centre5 + EPSILON)
    n5 = (p5 - centre5) * inv5
    u5 = gains[5:6] * n5 + biases[5:6]
    s5 = jax.nn.sigmoid(u5)
    g5 = cot[...].astype(F32) * v * (s5 * (1.0 + u5 * (1.0 - s5)))
    norm[4] = n5
    gact[4] = g5
    a3[me, pl.ds(0, 1)] = column_sum(g5)
    a3[me, pl.ds(1, 1)] = column_sum(g5 * n5)
    a3[me, pl.ds(2, 6)] = jnp.zeros((6, width), F32)
    reduce_start(2, a3)
    hbuf[5] = (v * u5 * s5).astype(BF16)
    for rp in range(pn.rpb // 2):
        pair = hbuf[5, pl.ds(rp * 2 * pn.S, 2 * pn.S)]
        rx[2 * rp:2 * rp + 2] = dot(sel_t[...], pair).astype(BF16).reshape(2, pn.C * bp, width)
    back = []
    for cc in range(1, pn.C):
        cd = lax.rem(col + cc, pn.C)
        c = remote(rx.at[:, pl.ds(pl.multiple_of(cd * bp, bp), bp)], res_out.at[pl.ds(col * pn.rpb, pn.rpb)],
                   e_s.at[cc], e_r.at[cc], (row, cd))
        c.start()
        back.append(c)
    c = pltpu.make_async_copy(rx.at[:, pl.ds(pl.multiple_of(col * bp, bp), bp)], res_out.at[pl.ds(col * pn.rpb, pn.rpb)],
                              e_r.at[0])
    c.start()
    back.append(c)
    total = reduce_end(2, a3, b3)
    db5, dg5 = total[0:1], total[1:2]
    q5 = (gains[5:6] * inv5 * (gact[4] - v * (db5 + norm[4] * dg5) * inv_px)).astype(BF16)
    hbuf[5] = q5

    for b in range(4):
        g = dot_nt(q5, w_proj[pl.ds(b * width, width)]) * slope[b]
        gact[b] = g
        a4[me, pl.ds(b, 1)] = column_sum(g)
        a4[me, pl.ds(4 + b, 1)] = column_sum(g * norm[b])
    dh4[...] = dot_nt(q5, w_proj[pl.ds(4 * width, width)])
    high = dh4[...].astype(BF16)
    low = (dh4[...] - high.astype(F32)).astype(BF16)
    a4[me, pl.ds(8, pn.ncp)] = dot(hot_t[...], high) + dot(hot_t[...], low)
    reduce_start(3, a4)
    for b in range(5):
        dproj_out[pl.ds(b * width, width)] = dot_tn(hbuf[b], hbuf[5]).astype(BF16)
    total = reduce_end(3, a4, b4)
    for b in range(4):
        db, dg = total[b:b + 1], total[4 + b:5 + b]
        db_out[pl.ds(b, 1)] = db
        dg_out[pl.ds(b, 1)] = dg
        q_out[b] = (gains[b:b + 1] * inv[b] * (gact[b] - v * (db + norm[b] * dg) * inv_px)).astype(BF16)
    g4 = total[8:8 + pn.ncp] * slope4
    db4, dg4 = column_sum(g4), column_sum(g4 * n4)
    db_out[pl.ds(4, 1)] = db4
    dg_out[pl.ds(4, 1)] = dg4
    db_out[pl.ds(5, 1)] = db5
    dg_out[pl.ds(5, 1)] = dg5
    q4_out[...] = (gains[4:5] * inv4 * (g4 - (db4 + n4 * dg4) * (1.0 / crops))).astype(BF16)
    for c in back:
        c.wait()


def norms(pn, p, p4, gains, biases, valid, pixels, w_proj, cot, hot, hot_t, sel_t):
    dma = pltpu.SemaphoreType.DMA
    vmem = pl.BlockSpec(memory_space=pltpu.VMEM)
    shape = jax.ShapeDtypeStruct
    big, small = 8 + pn.ncp, 8
    bufs = []
    for n in (big, small, small, big):
        bufs += [pltpu.VMEM((MEMBERS, n, pn.width), F32), pltpu.VMEM((pn.slabs, n, pn.width), F32)]
    return pl.pallas_call(
        functools.partial(norm_kernel, pn),
        out_shape=(
            shape((4, pn.px, pn.width), BF16),
            shape((pn.ncp, pn.width), BF16),
            shape((5 * pn.width, pn.width), BF16),
            shape((pn.h, pn.bp, pn.width), BF16),
            shape((6, pn.width), F32),
            shape((6, pn.width), F32),
        ),
        in_specs=[vmem] * 5 + [pl.BlockSpec(memory_space=pltpu.SMEM)] + [vmem] * 5,
        out_specs=(vmem,) * 6,
        scratch_shapes=[
            pltpu.VMEM((5, pn.px, pn.width), F32),
            pltpu.VMEM((4, pn.px, pn.width), F32),
            pltpu.VMEM((6, pn.px, pn.width), BF16),
            pltpu.VMEM((5, pn.px, pn.width), F32),
            pltpu.VMEM((pn.px, pn.width), F32),
            pltpu.VMEM((pn.rpb, pn.C * pn.bp, pn.width), BF16),
            *bufs,
            dma((4, MEMBERS)), dma((4, MEMBERS)), dma((4, pn.slabs)), dma((4, pn.slabs)), dma((pn.C,)), dma((pn.C,)),
        ],
        compiler_params=pltpu.CompilerParams(collective_id=1, has_side_effects=True, vmem_limit_bytes=48 * 2**20),
        name="norms",
    )(p, p4, gains, biases, valid, pixels, w_proj, cot, hot, hot_t, sel_t)


BACK = tuple((b, i) for b in (1, 2, 3) for i in (-1, 1)) + tuple((b, 0) for b in (1, 2, 3))


def back_kernel(pn, q_in, x_in, w_in, q4, means, hot_px, inv_counts, masks, lane_masks, shifts, sel_t,
                dw_out, dx_out,
                xs, wbuf, qraw, qs, qt, dxe, dwbuf, dwr, dwsum, hsend, hrecv, pack,
                l_s, q_s, q_r, k_s, k_r, f_s, f_r, d_s, d_r, g_s, g_r, h_s, h_r, x_s, x_r):
    row, col = lax.axis_index("row"), lax.axis_index("col")
    slab, x = row // pn.G, lax.rem(row, pn.G)
    me = x * pn.C + col
    core, quad = lax.rem(col, 2), me // 2
    h, H, bp, px, S = pn.h, pn.H, pn.bp, pn.px, pn.S
    half = MEMBERS // 2
    partner = (row, col + 1 - 2 * core)

    def member(s, k):
        return (s * pn.G + k // pn.C, lax.rem(k, pn.C))

    load_x = pltpu.make_async_copy(x_in, xs, l_s.at[0])
    load_w = pltpu.make_async_copy(w_in, wbuf, l_s.at[1])
    load_x.start()
    load_w.start()
    greet_all(pn, row, col)

    def straight(slot, i):
        other = 2 * lax.rem(quad + i, half) + core
        return remote(q_in.at[slot], qraw.at[slot, pl.ds(pl.multiple_of(me * px, 16), px)], q_s.at[slot, i], q_r.at[slot, i],
                      member(slab, other))

    def to_partner(slot):
        return remote(q_in.at[slot], qraw.at[slot, pl.ds(pl.multiple_of(me * px, 16), px)], k_s.at[slot], k_r.at[slot], partner)

    def passed(slot, i):
        origin = 2 * lax.rem(quad - i + half, half) + core
        at = pl.ds(pl.multiple_of(origin * px, 16), px)
        return remote(qraw.at[slot, at], qraw.at[slot, at], f_s.at[slot, i], f_r.at[slot, i], partner)

    slots = (1, 2, 3, 0)
    for slot in slots:
        for i in range(1, half):
            straight(slot, i).start()
        to_partner(slot).start()
    own_q = []
    for slot in slots:
        c = pltpu.make_async_copy(q_in.at[slot], qraw.at[slot, pl.ds(pl.multiple_of(me * px, 16), px)], l_s.at[2 + slot])
        c.start()
        own_q.append(c)

    def clear(rb, carry):
        dxe[pl.ds(pl.multiple_of(rb * px, 16), px)] = jnp.zeros((px, pn.cs), F32)
        return carry

    lax.fori_loop(0, pn.nb, clear, 0)

    def receive(slot):
        for i in range(1, half):
            straight(slot, i).wait()
            passed(slot, i).start()

    def received(slot):
        to_partner(slot).wait()
        own_q[slots.index(slot)].wait()
        for i in range(1, half):
            passed(slot, i).wait()

    def out_piece(n, jj):
        taps = back_taps(n)
        j = lax.rem(col + jj, pn.C)
        src = dwbuf.at[pl.ds(taps[0], len(taps)), pl.ds(pl.multiple_of(j * pn.part, pn.part), pn.part)]
        dst = dwr.at[slab, pl.ds(taps[0], len(taps))]
        return src, dst, (col * pn.G + x, j)

    def send_piece(n):
        if not pn.exchange:
            return
        for jj in range(1, pn.C):
            src, dst, to = out_piece(n, jj)
            remote(src, dst, d_s.at[n, jj], d_r.at[n, slab], to).start()
        src, dst, to = out_piece(n, 0)

        @pl.when(slab == col)
        def _():
            pltpu.make_async_copy(src, dst, d_r.at[n, slab]).start()

        @pl.when(slab != col)
        def _():
            remote(src, dst, d_s.at[n, 0], d_r.at[n, slab], to).start()

    def piece_sent(n):
        for jj in range(1, pn.C):
            src, dst, to = out_piece(n, jj)
            remote(src, dst, d_s.at[n, jj], d_r.at[n, slab], to).wait_send()
        src, dst, to = out_piece(n, 0)

        @pl.when(slab != col)
        def _():
            remote(src, dst, d_s.at[n, 0], d_r.at[n, slab], to).wait_send()

    def back_taps(n):
        if n < len(BACK):
            b, i = BACK[n]
            first = 1 + 9 * (b - 1) + 3 * (i + 1)
            return (first, first + 1, first + 2)
        return (0,) if n == len(BACK) else (TAPS - 1,)

    load_x.wait()
    load_w.wait()
    receive(1)
    for n, (branch, i) in enumerate(BACK):
        step = pn.steps[branch - 1]
        taps = back_taps(n)
        if i == -1:
            received(branch)
            if branch < 3:
                receive(branch + 1)
            else:
                receive(0)

            def turn(rp, carry, branch=branch):
                at = pl.multiple_of(rp * 2 * S, 16)
                moved = dot(shifts[pl.ds((branch - 1) * 4 * S, 4 * S)], qraw[branch, pl.ds(at, 2 * S)]).astype(BF16)
                qs[branch - 1, 0, pl.ds(at, 2 * S)] = moved[:2 * S]
                qs[branch - 1, 1, pl.ds(at, 2 * S)] = moved[2 * S:]
                return carry

            lax.fori_loop(0, H // 2, turn, 0)
            qt[branch] = qraw[branch].T

        q_turned = qt[branch]
        if i != 0:
            q_turned = q_turned * lane_masks[pl.ds(2 * (branch - 1) + (i + 1) // 2, 1)]
        window = pl.ds((pn.hb + i * step) * px, pn.own)
        for j, tap in zip((-1, 0, 1), taps):
            dwbuf[tap] = dot(q_turned, xs[3 + j * branch, window]).T.astype(BF16)
        send_piece(n)
        mask_at = (2 * (branch - 1) + (i + 1) // 2) * H

        def block(rb, carry, branch=branch, i=i, step=step, taps=taps, mask_at=mask_at):
            at = pl.ds(pl.multiple_of(rb * px, 16), px)
            y = dot_nt(qs[branch - 1, 0, at], wbuf[taps[0]])
            y = y + dot_nt(qraw[branch, at], wbuf[taps[1]])
            y = y + dot_nt(qs[branch - 1, 1, at], wbuf[taps[2]])
            if i != 0:
                y = jnp.concatenate([y[r * S:(r + 1) * S] * masks[mask_at + rb * pn.rpb + r] for r in range(pn.rpb)], axis=0)
            to = pl.ds(pl.multiple_of((rb + pn.hb + i * step) * px, 16), px)
            dxe[to] = dxe[to] + y
            return carry

        lax.fori_loop(0, MEMBERS, block, 0)
        if n == 5:
            hsend[0] = dxe[pl.ds(0, pn.hb * px)].astype(BF16)
            hsend[1] = dxe[pl.ds((pn.hb + MEMBERS) * px, pn.hb * px)].astype(BF16)

            @pl.when(slab > 0)
            def _():
                remote(hsend.at[0], hrecv.at[1], h_s.at[0], h_r.at[1], member(slab - 1, me)).start()

            @pl.when(slab < pn.slabs - 1)
            def _():
                remote(hsend.at[1], hrecv.at[0], h_s.at[1], h_r.at[0], member(slab + 1, me)).start()

    received(0)
    n_point, n_pool = len(BACK), len(BACK) + 1
    dwbuf[TAPS - 1] = dot_tn(means[...].astype(BF16), q4[...]).astype(BF16)
    dwbuf[0] = dot(qraw[0].T, xs[3, pl.ds(pn.hb * px, pn.own)]).T.astype(BF16)
    send_piece(n_point)
    send_piece(n_pool)
    pooled = dot_nt(q4[...], wbuf[TAPS - 1]) * inv_counts[...]
    pooled_high = pooled.astype(BF16)
    pooled_low = (pooled - pooled_high.astype(F32)).astype(BF16)

    @pl.when(slab > 0)
    def _():
        remote(hsend.at[0], hrecv.at[1], h_s.at[0], h_r.at[1], member(slab - 1, me)).wait_send()
        remote(hsend.at[1], hrecv.at[0], h_s.at[1], h_r.at[0], member(slab - 1, me)).wait_recv()

    @pl.when(slab < pn.slabs - 1)
    def _():
        remote(hsend.at[1], hrecv.at[0], h_s.at[1], h_r.at[0], member(slab + 1, me)).wait_send()
        remote(hsend.at[0], hrecv.at[1], h_s.at[0], h_r.at[1], member(slab + 1, me)).wait_recv()

    @pl.when(slab == 0)
    def _():
        hrecv[0] = jnp.zeros((pn.hb * px, pn.cs), BF16)

    @pl.when(slab == pn.slabs - 1)
    def _():
        hrecv[1] = jnp.zeros((pn.hb * px, pn.cs), BF16)

    def finish(rb, carry):
        at = pl.ds(pl.multiple_of(rb * px, 16), px)
        y = dxe[pl.ds(pl.multiple_of((rb + pn.hb) * px, 16), px)] + dot_nt(qraw[0, at], wbuf[0])
        hot = hot_px[at]
        y = y + dot(hot, pooled_high) + dot(hot, pooled_low)
        dxe[pl.ds(pl.multiple_of((rb + pn.hb) * px, 16), px)] = y
        return carry

    lax.fori_loop(0, MEMBERS, finish, 0)
    for rb in range(pn.hb):
        low, high = (pn.hb + rb) * px, (MEMBERS + rb) * px
        dxe[pl.ds(low, px)] = dxe[pl.ds(low, px)] + hrecv[0, pl.ds(rb * px, px)].astype(F32)
        dxe[pl.ds(high, px)] = dxe[pl.ds(high, px)] + hrecv[1, pl.ds(rb * px, px)].astype(F32)

    def packing(rp, carry):
        pair = dxe[pl.ds(pl.multiple_of(pn.hb * px + rp * 2 * S, 16), 2 * S)].astype(BF16)
        pack[pl.ds(2 * rp, 2)] = dot(sel_t[...], pair).astype(BF16).reshape(2, pn.C * bp, pn.cs)
        return carry

    lax.fori_loop(0, H // 2, packing, 0)
    home = []
    for kk in range(1, MEMBERS):
        other = lax.rem(me + kk, MEMBERS)
        xo, co = other // pn.C, lax.rem(other, pn.C)
        c = remote(pack.at[pl.ds(xo * h, h), pl.ds(pl.multiple_of(co * bp, bp), bp)], dx_out.at[me], x_s.at[kk], x_r.at[kk],
                   member(slab, other))
        c.start()
        home.append(c)
    c = pltpu.make_async_copy(pack.at[pl.ds(x * h, h), pl.ds(pl.multiple_of(col * bp, bp), bp)], dx_out.at[me], x_r.at[0])
    c.start()
    home.append(c)

    own_part = pl.ds(pl.multiple_of(col * pn.part, pn.part), pn.part)

    def share(n, jj):
        taps = back_taps(n)
        t = pl.ds(taps[0], len(taps))
        return remote(dwsum.at[t], dw_out.at[t, own_part], g_s.at[n, jj], g_r.at[n, jj], (row, lax.rem(col + jj, pn.C)))

    def share_own(n):
        taps = back_taps(n)
        t = pl.ds(taps[0], len(taps))
        return pltpu.make_async_copy(dwsum.at[t], dw_out.at[t, own_part], g_r.at[n, 0])

    pieces = len(BACK) + 2
    if pn.exchange:
        for n in range(pieces):
            taps = back_taps(n)
            t = pl.ds(taps[0], len(taps))
            for z in range(pn.slabs):
                pltpu.make_async_copy(dwr.at[z, t], dwr.at[z, t], d_r.at[n, z]).wait()
            for tap in taps:
                total = dwr[0, tap].astype(F32)
                for z in range(1, pn.slabs):
                    total = total + dwr[z, tap].astype(F32)
                dwsum[tap] = total.astype(BF16)
            for jj in range(1, pn.C):
                share(n, jj).start()
            share_own(n).start()
        for n in range(pieces):
            piece_sent(n)
            for jj in range(1, pn.C):
                share(n, jj).wait()
            share_own(n).wait()
    else:
        c = pltpu.make_async_copy(dwbuf, dw_out, g_r.at[0, 0])
        c.start()
        c.wait()
    for c in home:
        c.wait()


def conv_backward(pn, q, xs, w, q4, means, hot_px, inv_counts, masks, lane_masks, shifts, sel_t):
    dma = pltpu.SemaphoreType.DMA
    vmem = pl.BlockSpec(memory_space=pltpu.VMEM)
    hbm = pl.BlockSpec(memory_space=pl.ANY)
    shape = jax.ShapeDtypeStruct
    half = MEMBERS // 2
    pieces = len(BACK) + 2
    return pl.pallas_call(
        functools.partial(back_kernel, pn),
        out_shape=(
            shape((TAPS, pn.cs, pn.width), BF16),
            shape((MEMBERS, pn.h, pn.bp, pn.cs), BF16),
        ),
        in_specs=[hbm, hbm, hbm, vmem, vmem, vmem, vmem, pl.BlockSpec(memory_space=pltpu.SMEM), vmem, vmem, vmem],
        out_specs=(hbm, hbm),
        scratch_shapes=[
            pltpu.VMEM((7, pn.ext, pn.cs), BF16),
            pltpu.VMEM((TAPS, pn.cs, pn.width), BF16),
            pltpu.VMEM((4, pn.own, pn.width), BF16),
            pltpu.VMEM((3, 2, pn.own, pn.width), BF16),
            pltpu.VMEM((4, pn.width, pn.own), BF16),
            pltpu.VMEM((pn.ext, pn.cs), F32),
            pltpu.VMEM((TAPS, pn.cs, pn.width), BF16),
            pltpu.VMEM((pn.C, TAPS, pn.part, pn.width), BF16),
            pltpu.VMEM((TAPS, pn.part, pn.width), BF16),
            pltpu.VMEM((2, pn.hb * pn.px, pn.cs), BF16),
            pltpu.VMEM((2, pn.hb * pn.px, pn.cs), BF16),
            pltpu.VMEM((pn.H, pn.C * pn.bp, pn.cs), BF16),
            dma((6,)), dma((4, half)), dma((4, half)), dma((4,)), dma((4,)), dma((4, half)), dma((4, half)),
            dma((pieces, pn.C)), dma((pieces, pn.C)), dma((pieces, pn.C)), dma((pieces, pn.C)),
            dma((2,)), dma((2,)), dma((MEMBERS,)), dma((MEMBERS,)),
        ],
        compiler_params=pltpu.CompilerParams(collective_id=2, has_side_effects=True, vmem_limit_bytes=61 * 2**20),
        name="conv_backward",
    )(q, xs, w, q4, means, hot_px, inv_counts, masks, lane_masks, shifts, sel_t)


def column_tables(pn):
    S, bp, bc = pn.S, pn.bp, pn.bc
    sel = np.zeros((7, 2, S, 2, pn.C * bp), np.float32)
    shifts = np.zeros((3, 2, 2, S, 2, S), np.float32)
    for r in range(2):
        for c in range(pn.cols):
            for v in range(-3, 4):
                s = c + v * DILATIONS[0]
                if 0 <= s < pn.cols:
                    sel[v + 3, r, c, r, (s // bc) * bp + s % bc] = 1.0
            for b, d in enumerate(DILATIONS):
                for n, j in enumerate((-1, 1)):
                    s = c - j * d
                    if 0 <= s < pn.cols:
                        shifts[b, n, r, c, r, s] = 1.0
    sel = sel.reshape(7 * 2 * S, 2 * pn.C * bp)
    sel_t = sel[3 * 2 * S:4 * 2 * S].T
    return (jnp.asarray(sel, BF16), jnp.asarray(sel_t, BF16), jnp.asarray(shifts.reshape(12 * S, 2 * S), BF16))


def per_device(
    features, crop_rows, crop_cols, w_point, w_atrous, w_pool, w_proj, gains, biases, cotangent
):
    h, bc, channels = features.shape
    pn = Plan(lax.axis_size("row"), lax.axis_size("col"), h, bc, channels, gains.shape[1], crop_rows.shape[0])
    row, col = lax.axis_index("row"), lax.axis_index("col")
    slab, x = row // pn.G, row % pn.G
    crop_ids = jnp.arange(pn.crops, dtype=jnp.int32)
    ends = jnp.cumsum(crop_rows)
    counts = (crop_rows * crop_cols).astype(F32)
    pixels = jnp.sum(counts)

    def crop_of(rows):
        found = jnp.sum((rows[:, None] >= ends[None, :]).astype(jnp.int32), axis=1)
        return jnp.where(rows < 0, -1, found)

    def widths_of(crop):
        return jnp.sum(jnp.where(crop[:, None] == crop_ids[None, :], crop_cols[None, :], 0), axis=1)

    own_crop = crop_of(row * h + jnp.arange(h, dtype=jnp.int32))
    own_columns = col * bc + jnp.arange(bc, dtype=jnp.int32)
    own_valid = own_columns[None, :] < widths_of(own_crop)[:, None]
    masked = jnp.where(own_valid[:, :, None], features, 0)
    feats = masked.reshape(h, bc, pn.C, pn.G, pn.cs).transpose(3, 2, 0, 1, 4).reshape(MEMBERS, h, bc, pn.cs)
    feats = jnp.pad(feats, ((0, 0), (0, 0), (0, pn.bp - bc), (0, 0)))
    cot = jnp.pad(cotangent, ((0, 0), (0, pn.bp - bc), (0, 0)))

    slab_rows = slab * pn.H - MARGIN + jnp.arange(pn.H + 2 * MARGIN, dtype=jnp.int32)
    crops = crop_of(slab_rows)
    mid = crops[MARGIN:MARGIN + pn.H]
    same = jnp.stack(
        [crops[MARGIN + i * d:MARGIN + i * d + pn.H] == mid for d in DILATIONS for i in (-1, 1)]
    ).astype(F32)
    lane_masks = jnp.pad(jnp.repeat(same, pn.S, axis=1), ((0, 2), (0, 0))).astype(BF16)
    ncp_ids = jnp.arange(pn.ncp, dtype=jnp.int32)
    hot_rows = (mid[:, None] == ncp_ids[None, :]).astype(BF16)
    hot_px = jnp.repeat(hot_rows, pn.S, axis=0)
    hot_t = jnp.repeat(hot_rows.T, pn.S, axis=1)
    inv_counts = jnp.pad(1.0 / counts, (0, pn.ncp - pn.crops))[:, None]

    k = x * pn.C + col
    block_crop = lax.dynamic_slice_in_dim(mid, k * pn.rpb, pn.rpb)
    columns = jnp.arange(pn.S, dtype=jnp.int32)
    valid = (columns[None, :] < widths_of(block_crop)[:, None]).astype(F32).reshape(pn.px, 1)
    block_hot = jnp.repeat((block_crop[:, None] == ncp_ids[None, :]).astype(BF16), pn.S, axis=0)
    block_hot_t = jnp.repeat((ncp_ids[:, None] == block_crop[None, :]).astype(BF16), pn.S, axis=1)

    sel, sel_t, shifts = column_tables(pn)
    w = jnp.concatenate([w_point[None], w_atrous.transpose(1, 0, 2), w_pool[None]], axis=0)
    full_proj = lax.all_gather(w_proj, "row", axis=0, tiled=True)
    if not pn.exchange:
        w = lax.all_gather(w, "row", axis=1, tiled=True)
        w = lax.dynamic_slice_in_dim(w, (col * pn.G + x) * pn.cs, pn.cs, axis=1)
    flat = same.reshape(-1)
    p, xs, w_own, means, p4, own_cot = conv_forward(pn, feats, w, cot, flat, sel, hot_t, inv_counts)
    q, q4, d_proj, res, d_gains, d_biases = norms(
        pn, p, p4, gains, biases, valid, (1.0 / pixels)[None], full_proj, own_cot, block_hot, block_hot_t, sel_t
    )
    dw, dx = conv_backward(pn, q, xs, w_own, q4, means, hot_px, inv_counts, flat, lane_masks, shifts, sel_t)
    if not pn.exchange:
        whole = jnp.zeros((TAPS, channels, pn.width), BF16)
        whole = lax.dynamic_update_slice(whole, dw, (0, (col * pn.G + x) * pn.cs, 0))
        whole = lax.psum(whole, "col")
        dw = lax.psum_scatter(whole, "row", scatter_dimension=1, tiled=True)
    d_proj = lax.psum(d_proj, "col")
    d_proj = lax.psum_scatter(d_proj.astype(F32), "row", scatter_dimension=0, tiled=True)
    result = res[:, :bc]
    dx = dx[:, :, :bc].reshape(pn.G, pn.C, h, bc, pn.cs).transpose(2, 3, 1, 0, 4).reshape(h, bc, channels)
    d_features = jnp.where(own_valid[:, :, None], dx, 0)
    d_point = dw[0].astype(F32)
    d_atrous = dw[1:TAPS - 1].astype(F32).transpose(1, 0, 2)
    d_pool = dw[TAPS - 1].astype(F32)
    return (result, d_features, d_point, d_atrous, d_pool, d_proj, d_gains, d_biases)


def solution(mesh):
    return jax.shard_map(
        per_device,
        mesh=mesh,
        in_specs=(
            P("row", "col", None),
            P(),
            P(),
            P("row", None),
            P("row", None, None),
            P("row", None),
            P("row", None),
            P(),
            P(),
            P("row", "col", None),
        ),
        out_specs=(
            P("row", "col", None),
            P("row", "col", None),
            P("row", None),
            P("row", None, None),
            P("row", None),
            P("row", None),
            P(),
            P(),
        ),
        check_vma=False,
    )
```

```python
import functools

import jax
import jax.numpy as jnp
import numpy as np
from jax import lax
from jax.experimental import pallas as pl
from jax.experimental.pallas import tpu as pltpu
from jax.sharding import PartitionSpec as P

EPSILON = 1e-05
MARGIN = 18
DILATIONS = (6, 12, 18)
MEMBERS = 8
TAPS = 30
POINT, POOL, GROUPS = 27, 28, 10
MESH = pl.DeviceIdType.MESH
F32 = jnp.float32
BF16 = jnp.bfloat16

def up_to(value, multiple):
    return -(-value // multiple) * multiple


class Plan:
    def __init__(self, rows_axis, cols_axis, h, bc, channels, width, crops):
        self.R, self.C = rows_axis, cols_axis
        self.h, self.bc, self.channels, self.width = h, bc, channels, width
        self.G = MEMBERS // self.C
        self.slabs = self.R // self.G
        self.H = self.G * h
        self.cols = bc * self.C
        self.S = up_to(self.cols, 8)
        self.rpb = self.H // MEMBERS
        self.px = self.rpb * self.S
        self.own = MEMBERS * self.px
        self.hb = MARGIN // self.rpb
        self.nb = MEMBERS + 2 * self.hb
        self.ext = self.nb * self.px
        self.bp = up_to(bc, 16)
        self.cs = channels // MEMBERS
        self.part = self.cs // self.C
        self.crops = crops
        self.ncp = up_to(crops, 16)
        self.exchange = self.slabs == self.C and self.R == MEMBERS
        self.steps = tuple(d // self.rpb for d in DILATIONS)
        self.proj = 5 * width // self.R
        self.piece = up_to(self.proj // self.C, 16)


def remote(src, dst, send, recv, device):
    return pltpu.make_async_remote_copy(
        src_ref=src, dst_ref=dst, send_sem=send, recv_sem=recv, device_id=device, device_id_type=MESH
    )


def greet_all(pn, row, col):
    total = pn.R * pn.C
    barrier = pltpu.get_barrier_semaphore()
    me = row * pn.C + col

    def hello(k, carry):
        other = lax.rem(me + k, total)
        pl.semaphore_signal(
            barrier, inc=1, device_id=(other // pn.C, lax.rem(other, pn.C)), device_id_type=MESH
        )
        return carry

    lax.fori_loop(1, total, hello, 0)
    pl.semaphore_wait(barrier, total - 1)


def dot(a, b):
    return jnp.dot(a, b, preferred_element_type=F32)


def dot_nt(a, b):
    return lax.dot_general(a, b, (((1,), (1,)), ((), ())), preferred_element_type=F32)


def dot_tn(a, b):
    return lax.dot_general(a, b, (((0,), (0,)), ((), ())), preferred_element_type=F32)


def split_dot(dot_fn, a, b):
    high = a.astype(BF16)
    low = (a - high.astype(F32)).astype(BF16)
    return dot_fn(high, b) + dot_fn(low, b)


def conv_kernel(pn, feats, w_in, cot, proj, masks, sel, hot_t, inv_counts,
                p_out, x_out, w_out, m_out, p4_out, cot_out, proj_out,
                ring, xs, wbuf, relay, acc, pbuf, cbuf, sbuf, rbuf, cx,
                f_s, f_r, h_s, h_r, c_s, c_r, j_s, j_r, t_s, t_r, w_s, w_r, w_l, d_s, d_r,
                r1_s, r1_r, r2_s, r2_r, o_s):
    row, col = lax.axis_index("row"), lax.axis_index("col")
    slab, x = row // pn.G, lax.rem(row, pn.G)
    me = x * pn.C + col
    core, quad = lax.rem(col, 2), me // 2
    h, H, bp, px, n = pn.h, pn.H, pn.bp, pn.px, pn.slabs
    many = 4

    def member(s, k):
        return (s * pn.G + k // pn.C, lax.rem(k, pn.C))

    greet_all(pn, row, col)

    own_cols = pl.ds(pl.multiple_of(col * bp, bp), bp)
    own_rows = pl.ds(MARGIN + h * x, h)
    sent = []
    for kk in range(1, MEMBERS):
        other = lax.rem(me + kk, MEMBERS)
        c = remote(feats.at[other], ring.at[own_rows, own_cols], f_s.at[kk], f_r.at[kk], member(slab, other))
        c.start()
        sent.append(c)
    keep = pltpu.make_async_copy(feats.at[me], ring.at[own_rows, own_cols], f_r.at[0])
    keep.start()

    quarter = pl.ds(pl.multiple_of(col * pn.part, pn.part), pn.part)

    def taps(g):
        return pl.ds(3 * g, 3)

    def hop(g, d, down):
        origin = slab + d - 1 if down else slab - d + 1
        to = slab - 1 if down else slab + 1
        src = w_in.at[taps(g), quarter] if d == 1 else relay.at[origin, taps(g)]
        return remote(src, relay.at[origin, taps(g)], w_s.at[int(down), d, g], w_r.at[int(down), d, g], (to * pn.G + x, col))

    def arrival(g, d, down):
        other = slab + 1 if down else slab - 1
        origin = slab + d if down else slab - d
        return remote(relay.at[origin, taps(g)], relay.at[origin, taps(g)], w_s.at[int(down), d, g],
                      w_r.at[int(down), d, g], (other * pn.G + x, col))

    def hand_over(g, d, down):
        origin = slab + d if down else slab - d
        return remote(relay.at[origin, taps(g)], wbuf.at[taps(g), quarter], d_s.at[int(down), d, g], d_r.at[g, col],
                      (row, origin))

    def serve(g, d):
        for down in (False, True):
            origin = slab + d if down else slab - d
            there = (origin < n) if down else (origin >= 0)
            further = (slab > 0) if down else (slab < n - 1)

            @pl.when(there)
            def _(down=down, origin=origin, further=further):
                arrival(g, d, down).wait_recv()

                @pl.when(further)
                def _():
                    hop(g, d + 1, down).start()

                @pl.when(origin == col)
                def _():
                    pltpu.make_async_copy(relay.at[origin, taps(g)], wbuf.at[taps(g), quarter], d_r.at[g, col]).start()

                @pl.when(origin != col)
                def _():
                    hand_over(g, d, down).start()

    def settle(g):
        @pl.when(slab < n - 1)
        def _():
            hop(g, 1, False).wait_send()

        @pl.when(slab > 0)
        def _():
            hop(g, 1, True).wait_send()

        for d in range(1, n):
            for down in (False, True):
                origin = slab + d if down else slab - d
                there = (origin < n) if down else (origin >= 0)
                further = (slab > 0) if down else (slab < n - 1)

                @pl.when(there & further)
                def _(d=d, down=down):
                    hop(g, d + 1, down).wait_send()

                @pl.when(there & (origin != col))
                def _(d=d, down=down):
                    hand_over(g, d, down).wait_send()

    def own_copy(g):
        return pltpu.make_async_copy(w_in.at[taps(g)], wbuf.at[taps(g)], w_l.at[g])

    def w_wait(g):
        if pn.exchange:
            @pl.when(slab == col)
            def _():
                own_copy(g).wait()

            @pl.when(slab != col)
            def _():
                for j in range(pn.C):
                    at = wbuf.at[taps(g), pl.ds(j * pn.part, pn.part)]
                    pltpu.make_async_copy(at, at, d_r.at[g, j]).wait()
        else:
            own_copy(g).wait()

    if pn.exchange:
        def begin(g, carry):
            @pl.when(slab < n - 1)
            def _():
                hop(g, 1, False).start()

            @pl.when(slab > 0)
            def _():
                hop(g, 1, True).start()

            @pl.when(slab == col)
            def _():
                own_copy(g).start()

            return carry
    else:
        def begin(g, carry):
            own_copy(g).start()
            return carry

    lax.fori_loop(0, GROUPS, begin, 0)

    cot_sent = []
    for cc in range(1, pn.C):
        cd = lax.rem(col + cc, pn.C)
        c = remote(cot.at[pl.ds(cd * pn.rpb, pn.rpb)], cx.at[:, own_cols], c_s.at[cc], c_r.at[cc], (row, cd))
        c.start()
        cot_sent.append(c)
    cot_keep = pltpu.make_async_copy(cot.at[pl.ds(col * pn.rpb, pn.rpb)], cx.at[:, own_cols], c_r.at[0])
    cot_keep.start()

    def proj_row(k):
        return remote(proj.at[col], proj_out.at[col, row], j_s.at[k], j_r.at[k], (lax.rem(row + k, pn.R), col))

    def proj_col(k):
        return remote(proj_out.at[col], proj_out.at[col], t_s.at[k], t_r.at[k], (row, lax.rem(col + k, pn.C)))

    def proj_begin(k, carry):
        proj_row(k).start()
        return carry

    def proj_wait(k, carry):
        proj_row(k).wait()
        return carry

    lax.fori_loop(1, pn.R, proj_begin, 0)
    proj_keep = pltpu.make_async_copy(proj.at[col], proj_out.at[col, row], j_r.at[0])
    proj_keep.start()

    @pl.when(slab == 0)
    def _():
        ring[pl.ds(0, MARGIN)] = jnp.zeros((MARGIN, pn.C * bp, pn.cs), BF16)

    @pl.when(slab == n - 1)
    def _():
        ring[pl.ds(MARGIN + H, MARGIN)] = jnp.zeros((MARGIN, pn.C * bp, pn.cs), BF16)

    for c in sent:
        c.wait()
    keep.wait()

    def margin_down():
        return remote(ring.at[pl.ds(MARGIN, MARGIN)], ring.at[pl.ds(MARGIN + H, MARGIN)], h_s.at[0], h_r.at[0],
                      member(slab - 1, me))

    def margin_up():
        return remote(ring.at[pl.ds(H, MARGIN)], ring.at[pl.ds(0, MARGIN)], h_s.at[1], h_r.at[1], member(slab + 1, me))

    @pl.when(slab > 0)
    def _():
        margin_down().start()

    @pl.when(slab < n - 1)
    def _():
        margin_up().start()

    if pn.exchange:
        def near(g, carry):
            serve(g, 1)
            return carry

        lax.fori_loop(0, GROUPS, near, 0)

    def assemble(rp, carry):
        pair = ring[pl.ds(2 * rp, 2)].reshape(2 * pn.C * bp, pn.cs)
        moved = dot(sel[...], pair).astype(BF16)
        at = pl.multiple_of(rp * 2 * pn.S, 16)
        for v in range(7):
            xs[v, pl.ds(at, 2 * pn.S)] = moved[v * 2 * pn.S:(v + 1) * 2 * pn.S]
        return carry

    lax.fori_loop(MARGIN // 2, (MARGIN + H) // 2, assemble, 0, unroll=6)
    for c in cot_sent:
        c.wait()
    cot_keep.wait()
    for rp in range(pn.rpb // 2):
        pair = cx[2 * rp:2 * rp + 2].reshape(2 * pn.C * bp, pn.width)
        cot_out[pl.ds(rp * 2 * pn.S, 2 * pn.S)] = dot(sel[pl.ds(3 * 2 * pn.S, 2 * pn.S)], pair).astype(BF16)
    lax.fori_loop(1, pn.R, proj_wait, 0)
    proj_keep.wait()
    for k in range(1, pn.C):
        proj_col(k).start()

    @pl.when(slab > 0)
    def _():
        margin_down().wait_send()
        margin_up().wait_recv()

    @pl.when(slab < n - 1)
    def _():
        margin_up().wait_send()
        margin_down().wait_recv()

    lax.fori_loop(0, MARGIN // 2, assemble, 0, unroll=3)
    lax.fori_loop((MARGIN + H) // 2, pn.nb * pn.rpb // 2, assemble, 0, unroll=3)
    x_save = pltpu.make_async_copy(xs, x_out, o_s.at[0])
    x_save.start()

    def first_stage(slot):
        return remote(pbuf.at[slot, :, 1 - core], cbuf.at[slot], r1_s.at[slot], r1_r.at[slot], (row, col + 1 - 2 * core))

    def second_stage(slot, i):
        q = lax.rem(quad + i, MEMBERS // 2)
        return remote(sbuf.at[slot, i - 1], rbuf.at[slot, i - 1], r2_s.at[slot, i - 1], r2_r.at[slot, i - 1],
                      member(slab, 2 * q + core))

    def middle(slot):
        first_stage(slot).wait()
        for i in (1, 2, 3, 0):
            q = lax.rem(quad + i, MEMBERS // 2)
            s = pbuf[slot, q, core].astype(F32) + cbuf[slot, q].astype(F32)
            if i == 0:
                p_out[slot] = s
            else:
                sbuf[slot, i - 1] = s.astype(BF16)
                second_stage(slot, i).start()

    def last(slot):
        total = p_out[slot]
        for i in range(1, MEMBERS // 2):
            second_stage(slot, i).wait()
            total = total + rbuf[slot, i - 1].astype(F32)
        p_out[slot] = total

    def scatter(slot, rb, y):
        for r in range(many):
            pbuf[slot, (many * rb + r) // 2, r % 2] = y[r * px:(r + 1) * px].astype(BF16)

    def far(g):
        if pn.exchange:
            for d in range(2, n):
                serve(g, d)
        w_wait(g)

    for branch in (1, 2, 3):
        step = pn.steps[branch - 1]
        for i in (-1, 0, 1):
            g = 3 * (branch - 1) + i + 1
            mask_at = (2 * (branch - 1) + (i + 1) // 2) * H
            far(g)

            def block(rb, carry, step=step, i=i, g=g, mask_at=mask_at, branch=branch):
                at = pl.multiple_of(rb * many * px, 16)
                window = pl.ds(pl.multiple_of((rb * many + pn.hb + i * step) * px, 16), many * px)
                y = dot(xs[3 - branch, window], wbuf[3 * g])
                y = y + dot(xs[3, window], wbuf[3 * g + 1])
                y = y + dot(xs[3 + branch, window], wbuf[3 * g + 2])
                if i != 0:
                    y = jnp.concatenate(
                        [y[r * pn.S:(r + 1) * pn.S] * masks[mask_at + rb * many * pn.rpb + r]
                         for r in range(many * pn.rpb)], axis=0
                    )
                if i > -1:
                    y = y + acc[pl.ds(at, many * px)]
                if i < 1:
                    acc[pl.ds(at, many * px)] = y
                else:
                    scatter(branch, rb, y)
                return carry

            lax.fori_loop(0, MEMBERS // many, block, 0)
            if i == 0 and branch > 1:
                middle(branch - 1)
        first_stage(branch).start()

    far(GROUPS - 1)

    def point(rb, carry):
        at = pl.ds(pl.multiple_of((rb * many + pn.hb) * px, 16), many * px)
        scatter(0, rb, dot(xs[3, at], wbuf[POINT]))
        return carry

    lax.fori_loop(0, MEMBERS // many, point, 0)
    first_stage(0).start()
    middle(3)

    sums = dot(hot_t[...], xs[3, pl.ds(pn.hb * px, pn.own)])
    means = sums * inv_counts[...]
    m_out[...] = means
    p4_out[...] = split_dot(dot, means, wbuf[POOL])
    w_save = pltpu.make_async_copy(wbuf, w_out, o_s.at[1])
    w_save.start()
    middle(0)
    for slot in (1, 2, 3):
        last(slot)
    for k in range(1, pn.C):
        proj_col(k).wait()
    if pn.exchange:
        def settled(g, carry):
            settle(g)
            return carry

        lax.fori_loop(0, GROUPS, settled, 0)
    last(0)
    x_save.wait()
    w_save.wait()


def conv_forward(pn, feats, w, cot, proj, masks, sel, hot_t, inv_counts):
    half = MEMBERS // 2
    dma = pltpu.SemaphoreType.DMA
    vmem = pl.BlockSpec(memory_space=pltpu.VMEM)
    hbm = pl.BlockSpec(memory_space=pl.ANY)
    shape = jax.ShapeDtypeStruct
    n = pn.slabs if pn.exchange else 1
    return pl.pallas_call(
        functools.partial(conv_kernel, pn),
        out_shape=(
            shape((4, pn.px, pn.width), F32),
            shape((7, pn.ext, pn.cs), BF16),
            shape((TAPS, pn.cs, pn.width), BF16),
            shape((pn.ncp, pn.cs), F32),
            shape((pn.ncp, pn.width), F32),
            shape((pn.px, pn.width), BF16),
            shape((pn.C, pn.R, pn.piece, pn.width), BF16),
        ),
        in_specs=[hbm, hbm, hbm, hbm, pl.BlockSpec(memory_space=pltpu.SMEM), vmem, vmem, vmem],
        out_specs=(vmem, hbm, hbm, vmem, vmem, vmem, vmem),
        scratch_shapes=[
            pltpu.VMEM((pn.nb * pn.rpb, pn.C * pn.bp, pn.cs), BF16),
            pltpu.VMEM((7, pn.ext, pn.cs), BF16),
            pltpu.VMEM((TAPS, pn.cs, pn.width), BF16),
            pltpu.VMEM((n, TAPS, pn.part, pn.width), BF16),
            pltpu.VMEM((pn.own, pn.width), F32),
            pltpu.VMEM((4, half, 2, pn.px, pn.width), BF16),
            pltpu.VMEM((4, half, pn.px, pn.width), BF16),
            pltpu.VMEM((4, half - 1, pn.px, pn.width), BF16),
            pltpu.VMEM((4, half - 1, pn.px, pn.width), BF16),
            pltpu.VMEM((pn.rpb, pn.C * pn.bp, pn.width), BF16),
            dma((MEMBERS,)), dma((MEMBERS,)), dma((2,)), dma((2,)), dma((pn.C,)), dma((pn.C,)),
            dma((pn.R,)), dma((pn.R,)), dma((pn.C,)), dma((pn.C,)),
            dma((2, n + 1, GROUPS)), dma((2, n + 1, GROUPS)), dma((GROUPS,)), dma((2, n + 1, GROUPS)), dma((GROUPS, pn.C)),
            dma((4,)), dma((4,)), dma((4, 3)), dma((4, 3)), dma((2,)),
        ],
        compiler_params=pltpu.CompilerParams(collective_id=0, has_side_effects=True, vmem_limit_bytes=60 * 2**20),
        name="conv_forward",
    )(feats, w, cot, proj, masks, sel, hot_t, inv_counts)


def norm_kernel(pn, p, p4_in, gains, biases, valid, pixels, w_proj, cot, hot, hot_t, sel_t,
                q_out, q4_out, dproj_out, res_out, dg_out, db_out,
                norm, slope, hbuf, gact, dh4, rx,
                a1, b1, a2, b2, a3, b3, a4, b4, as_s, as_r, bs_s, bs_r, e_s, e_r):
    row, col = lax.axis_index("row"), lax.axis_index("col")
    slab, x = row // pn.G, lax.rem(row, pn.G)
    me = x * pn.C + col
    crops = float(pn.crops)
    v = valid[...]
    inv_px = pixels[0]
    width, bp = pn.width, pn.bp

    def member(s, k):
        return (s * pn.G + k // pn.C, lax.rem(k, pn.C))

    barrier = pltpu.get_barrier_semaphore()
    for kk in range(1, MEMBERS):
        pl.semaphore_signal(barrier, inc=1, device_id=member(slab, lax.rem(me + kk, MEMBERS)), device_id_type=MESH)

    def hello(k, carry):
        pl.semaphore_signal(barrier, inc=1, device_id=member(lax.rem(slab + k, pn.slabs), me), device_id_type=MESH)
        return carry

    lax.fori_loop(1, pn.slabs, hello, 0)

    def peer_a(n, abuf, kk):
        return remote(abuf.at[me], abuf.at[me], as_s.at[n, kk], as_r.at[n, kk], member(slab, lax.rem(me + kk, MEMBERS)))

    def peer_b(n, bbuf, k):
        return remote(bbuf.at[slab], bbuf.at[slab], bs_s.at[n, k], bs_r.at[n, k], member(lax.rem(slab + k, pn.slabs), me))

    def reduce_start(n, abuf):
        for kk in range(1, MEMBERS):
            peer_a(n, abuf, kk).start()

    def reduce_end(n, abuf, bbuf):
        for kk in range(1, MEMBERS):
            peer_a(n, abuf, kk).wait()
        total = abuf[0]
        for k in range(1, MEMBERS):
            total = total + abuf[k]
        bbuf[slab] = total
        for k in range(1, pn.slabs):
            peer_b(n, bbuf, k).start()
        for k in range(1, pn.slabs):
            peer_b(n, bbuf, k).wait()
        total = bbuf[0]
        for k in range(1, pn.slabs):
            total = total + bbuf[k]
        return total

    def column_sum(value):
        return jnp.sum(value, axis=0, keepdims=True)

    for b in range(4):
        pv = p[b] * v
        a1[me, pl.ds(b, 1)] = column_sum(pv)
        a1[me, pl.ds(4 + b, 1)] = column_sum(pv * p[b])
    a1[me, pl.ds(8, pn.ncp)] = p4_in[...]
    pl.semaphore_wait(barrier, MEMBERS - 1 + pn.slabs - 1)
    reduce_start(0, a1)
    total = reduce_end(0, a1, b1)
    inv = []
    for b in range(4):
        centre = total[b:b + 1] * inv_px
        scale = lax.rsqrt(total[4 + b:5 + b] * inv_px - centre * centre + EPSILON)
        inv.append(scale)
        n = (p[b] - centre) * scale
        u = gains[b:b + 1] * n + biases[b:b + 1]
        s = jax.nn.sigmoid(u)
        norm[b] = n
        slope[b] = s * (1.0 + u * (1.0 - s))
        hbuf[b] = (u * s).astype(BF16)
    p4 = total[8:8 + pn.ncp]
    centre4 = column_sum(p4) * (1.0 / crops)
    inv4 = lax.rsqrt(column_sum(p4 * p4) * (1.0 / crops) - centre4 * centre4 + EPSILON)
    n4 = (p4 - centre4) * inv4
    u4 = gains[4:5] * n4 + biases[4:5]
    s4 = jax.nn.sigmoid(u4)
    slope4 = s4 * (1.0 + u4 * (1.0 - s4))
    hbuf[4] = dot(hot[...], (u4 * s4).astype(BF16)).astype(BF16)

    p5 = dot(hbuf[0], w_proj[pl.ds(0, width)])
    for b in range(1, 5):
        p5 = p5 + dot(hbuf[b], w_proj[pl.ds(b * width, width)])
    pv = p5 * v
    a2[me, pl.ds(0, 1)] = column_sum(pv)
    a2[me, pl.ds(1, 1)] = column_sum(pv * p5)
    a2[me, pl.ds(2, 6)] = jnp.zeros((6, width), F32)
    reduce_start(1, a2)
    total = reduce_end(1, a2, b2)
    centre5 = total[0:1] * inv_px
    inv5 = lax.rsqrt(total[1:2] * inv_px - centre5 * centre5 + EPSILON)
    n5 = (p5 - centre5) * inv5
    u5 = gains[5:6] * n5 + biases[5:6]
    s5 = jax.nn.sigmoid(u5)
    g5 = cot[...].astype(F32) * v * (s5 * (1.0 + u5 * (1.0 - s5)))
    norm[4] = n5
    gact[4] = g5
    a3[me, pl.ds(0, 1)] = column_sum(g5)
    a3[me, pl.ds(1, 1)] = column_sum(g5 * n5)
    a3[me, pl.ds(2, 6)] = jnp.zeros((6, width), F32)
    reduce_start(2, a3)
    hbuf[5] = (v * u5 * s5).astype(BF16)
    for rp in range(pn.rpb // 2):
        pair = hbuf[5, pl.ds(rp * 2 * pn.S, 2 * pn.S)]
        rx[2 * rp:2 * rp + 2] = dot(sel_t[...], pair).astype(BF16).reshape(2, pn.C * bp, width)
    back = []
    for cc in range(1, pn.C):
        cd = lax.rem(col + cc, pn.C)
        c = remote(rx.at[:, pl.ds(pl.multiple_of(cd * bp, bp), bp)], res_out.at[pl.ds(col * pn.rpb, pn.rpb)],
                   e_s.at[cc], e_r.at[cc], (row, cd))
        c.start()
        back.append(c)
    c = pltpu.make_async_copy(rx.at[:, pl.ds(pl.multiple_of(col * bp, bp), bp)], res_out.at[pl.ds(col * pn.rpb, pn.rpb)],
                              e_r.at[0])
    c.start()
    back.append(c)
    total = reduce_end(2, a3, b3)
    db5, dg5 = total[0:1], total[1:2]
    q5 = (gains[5:6] * inv5 * (gact[4] - v * (db5 + norm[4] * dg5) * inv_px)).astype(BF16)
    hbuf[5] = q5

    for b in range(4):
        g = dot_nt(q5, w_proj[pl.ds(b * width, width)]) * slope[b]
        gact[b] = g
        a4[me, pl.ds(b, 1)] = column_sum(g)
        a4[me, pl.ds(4 + b, 1)] = column_sum(g * norm[b])
    dh4[...] = dot_nt(q5, w_proj[pl.ds(4 * width, width)])
    high = dh4[...].astype(BF16)
    low = (dh4[...] - high.astype(F32)).astype(BF16)
    a4[me, pl.ds(8, pn.ncp)] = dot(hot_t[...], high) + dot(hot_t[...], low)
    reduce_start(3, a4)
    for b in range(5):
        dproj_out[pl.ds(b * width, width)] = dot_tn(hbuf[b], hbuf[5]).astype(BF16)
    total = reduce_end(3, a4, b4)
    for b in range(4):
        db, dg = total[b:b + 1], total[4 + b:5 + b]
        db_out[pl.ds(b, 1)] = db
        dg_out[pl.ds(b, 1)] = dg
        q_out[b] = (gains[b:b + 1] * inv[b] * (gact[b] - v * (db + norm[b] * dg) * inv_px)).astype(BF16)
    g4 = total[8:8 + pn.ncp] * slope4
    db4, dg4 = column_sum(g4), column_sum(g4 * n4)
    db_out[pl.ds(4, 1)] = db4
    dg_out[pl.ds(4, 1)] = dg4
    db_out[pl.ds(5, 1)] = db5
    dg_out[pl.ds(5, 1)] = dg5
    q4_out[...] = (gains[4:5] * inv4 * (g4 - (db4 + n4 * dg4) * (1.0 / crops))).astype(BF16)
    for c in back:
        c.wait()


def norms(pn, p, p4, gains, biases, valid, pixels, w_proj, cot, hot, hot_t, sel_t):
    dma = pltpu.SemaphoreType.DMA
    vmem = pl.BlockSpec(memory_space=pltpu.VMEM)
    shape = jax.ShapeDtypeStruct
    big, small = 8 + pn.ncp, 8
    bufs = []
    for n in (big, small, small, big):
        bufs += [pltpu.VMEM((MEMBERS, n, pn.width), F32), pltpu.VMEM((pn.slabs, n, pn.width), F32)]
    return pl.pallas_call(
        functools.partial(norm_kernel, pn),
        out_shape=(
            shape((4, pn.px, pn.width), BF16),
            shape((pn.ncp, pn.width), BF16),
            shape((5 * pn.width, pn.width), BF16),
            shape((pn.h, pn.bp, pn.width), BF16),
            shape((6, pn.width), F32),
            shape((6, pn.width), F32),
        ),
        in_specs=[vmem] * 5 + [pl.BlockSpec(memory_space=pltpu.SMEM)] + [vmem] * 5,
        out_specs=(vmem,) * 6,
        scratch_shapes=[
            pltpu.VMEM((5, pn.px, pn.width), F32),
            pltpu.VMEM((4, pn.px, pn.width), F32),
            pltpu.VMEM((6, pn.px, pn.width), BF16),
            pltpu.VMEM((5, pn.px, pn.width), F32),
            pltpu.VMEM((pn.px, pn.width), F32),
            pltpu.VMEM((pn.rpb, pn.C * pn.bp, pn.width), BF16),
            *bufs,
            dma((4, MEMBERS)), dma((4, MEMBERS)), dma((4, pn.slabs)), dma((4, pn.slabs)), dma((pn.C,)), dma((pn.C,)),
        ],
        compiler_params=pltpu.CompilerParams(collective_id=1, has_side_effects=True, vmem_limit_bytes=48 * 2**20),
        name="norms",
    )(p, p4, gains, biases, valid, pixels, w_proj, cot, hot, hot_t, sel_t)


BACK = tuple((b, i) for b in (1, 2, 3) for i in (-1, 1)) + tuple((b, 0) for b in (1, 2, 3))


def group_of(k):
    middle = k // 6
    return (1 - middle) * (3 * (k // 2) + 2 * (k % 2)) + middle * jnp.minimum(1 + 3 * (k - 6), GROUPS - 1)


def back_kernel(pn, q_in, x_in, w_in, dproj_in, q4, means, hot_px, inv_counts, masks, lane_masks, shifts, sel_t,
                dw_out, dx_out, dproj_out,
                xs, wbuf, qraw, qs, qt, dxe, dwbuf, mine, chain, above, hsend, hrecv, pack, dp1, dps, dp2, dpf,
                l_s, q_s, q_r, k_s, k_r, f_s, f_r, d_s, d_r, n_s, n_r, a_s, a_r, g_s, g_r, h_s, h_r, x_s, x_r,
                p1_s, p1_r, p2_s, p2_r, p3_s, p3_r):
    row, col = lax.axis_index("row"), lax.axis_index("col")
    slab, x = row // pn.G, lax.rem(row, pn.G)
    me = x * pn.C + col
    core, quad = lax.rem(col, 2), me // 2
    h, H, bp, px, S, n = pn.h, pn.H, pn.bp, pn.px, pn.S, pn.slabs
    half = MEMBERS // 2
    many = 4
    partner = (row, col + 1 - 2 * core)

    def member(s, k):
        return (s * pn.G + k // pn.C, lax.rem(k, pn.C))

    load_x = pltpu.make_async_copy(x_in, xs, l_s.at[0])
    load_w = pltpu.make_async_copy(w_in, wbuf, l_s.at[1])
    load_x.start()
    load_w.start()
    greet_all(pn, row, col)

    own_px = pl.ds(pl.multiple_of(me * px, 16), px)

    def straight(slot, i):
        other = 2 * lax.rem(quad + i, half) + core
        return remote(q_in.at[slot], qraw.at[slot, own_px], q_s.at[slot, i], q_r.at[slot, i], member(slab, other))

    def to_partner(slot):
        return remote(q_in.at[slot], qraw.at[slot, own_px], k_s.at[slot], k_r.at[slot], partner)

    def passed(slot, i):
        origin = 2 * lax.rem(quad - i + half, half) + core
        at = pl.ds(pl.multiple_of(origin * px, 16), px)
        return remote(qraw.at[slot, at], qraw.at[slot, at], f_s.at[slot, i], f_r.at[slot, i], partner)

    def kept(slot):
        return pltpu.make_async_copy(q_in.at[slot], qraw.at[slot, own_px], l_s.at[2 + slot])

    slots = (1, 2, 3, 0)
    for slot in slots:
        for i in range(1, half):
            straight(slot, i).start()
        to_partner(slot).start()
        kept(slot).start()

    block_rows = 5 * pn.width // MEMBERS
    home_slab = me // pn.G

    def dproj_slab(kk):
        other = lax.rem(me + kk, MEMBERS)
        return remote(dproj_in.at[pl.ds(pl.multiple_of(other * block_rows, 16), block_rows)], dp1.at[me],
                      p1_s.at[kk], p1_r.at[kk], member(slab, other))

    def dproj_own():
        return pltpu.make_async_copy(dproj_in.at[pl.ds(pl.multiple_of(me * block_rows, 16), block_rows)], dp1.at[me],
                                     p1_r.at[0])

    def dproj_home():
        return remote(dps, dp2.at[slab], p2_s.at[0], p2_r.at[slab], member(home_slab, me))

    def dproj_give(c):
        return remote(dpf, dproj_out, p3_s.at[c], p3_r.at[0], (slab * pn.G + lax.rem(me, pn.G), c))

    if pn.exchange:
        for kk in range(1, MEMBERS):
            dproj_slab(kk).start()
        dproj_own().start()

    def clear(rb, carry):
        dxe[pl.ds(pl.multiple_of(rb * px, 16), px)] = jnp.zeros((px, pn.cs), F32)
        return carry

    lax.fori_loop(0, pn.nb, clear, 0)

    def receive(slot):
        for i in range(1, half):
            straight(slot, i).wait()
            passed(slot, i).start()

    def received(slot):
        to_partner(slot).wait()
        kept(slot).wait()
        for i in range(1, half):
            passed(slot, i).wait()

    def taps(g):
        return pl.ds(3 * g, 3)

    def quarter(j):
        return pl.ds(pl.multiple_of(j * pn.part, pn.part), pn.part)

    def deal(g, jj):
        j = lax.rem(col + jj, pn.C)
        return remote(dwbuf.at[taps(g), quarter(j)], mine.at[col, taps(g)], d_s.at[g, jj], d_r.at[g, col], (row, j))

    def deal_own(g):
        return pltpu.make_async_copy(dwbuf.at[taps(g), quarter(col)], mine.at[col, taps(g)], d_r.at[g, col])

    def dealt(g):
        for home in range(pn.C):
            at = mine.at[home, taps(g)]
            pltpu.make_async_copy(at, at, d_r.at[g, home]).wait()

    def link_up(g, home):
        return remote(mine.at[home, taps(g)], chain.at[home, taps(g)], n_s.at[g, home], n_r.at[g, home],
                      ((slab + 1) * pn.G + x, col))

    def link_down(g, home):
        return remote(mine.at[home, taps(g)], chain.at[home, taps(g)], n_s.at[g, home], n_r.at[g, home],
                      ((slab - 1) * pn.G + x, col))

    def link_last(g, home):
        return remote(mine.at[home, taps(g)], above.at[taps(g)], n_s.at[g, home], a_r.at[g], ((slab - 1) * pn.G + x, col))

    def arrived(g, home):
        at = chain.at[home, taps(g)]
        return pltpu.make_async_copy(at, at, n_r.at[g, home])

    def add_on(g, home):
        arrived(g, home).wait()
        mine[home, taps(g)] = (mine[home, taps(g)].astype(F32) + chain[home, taps(g)].astype(F32)).astype(BF16)

    def go_up(g, first):
        def one(k, carry):
            home = n - 1 - k
            if not first:
                add_on(g, home)
            link_up(g, home).start()
            return carry

        lax.fori_loop(0, n - 1 - slab, one, 0)

    def go_down(g, first):
        def one(home, carry):
            if not first:
                add_on(g, home)

            @pl.when(home < slab - 1)
            def _():
                link_down(g, home).start()

            @pl.when(home == slab - 1)
            def _():
                link_last(g, home).start()

            return carry

        lax.fori_loop(0, slab, one, 0)

    def begin(g):
        dealt(g)

        @pl.when(slab == 0)
        def _():
            go_up(g, True)

        @pl.when(slab == n - 1)
        def _():
            go_down(g, True)

    def share(g, jj):
        return remote(mine.at[slab, taps(g)], dw_out.at[taps(g), quarter(col)], g_s.at[g, jj], g_r.at[g, jj],
                      (row, lax.rem(col + jj, pn.C)))

    def share_own(g):
        return pltpu.make_async_copy(mine.at[slab, taps(g)], dw_out.at[taps(g), quarter(col)], g_r.at[g, 0])

    def finish_group(g):
        @pl.when(slab > 0)
        def _():
            add_on(g, slab)

        @pl.when(slab < n - 1)
        def _():
            at = above.at[taps(g)]
            pltpu.make_async_copy(at, at, a_r.at[g]).wait()
            mine[slab, taps(g)] = (mine[slab, taps(g)].astype(F32) + above[taps(g)].astype(F32)).astype(BF16)

        for jj in range(1, pn.C):
            share(g, jj).start()
        share_own(g).start()

    def serve(t, carry):
        for L in range(1, n - 1):
            k = t - L + 1
            g = group_of(jnp.clip(k, 0, GROUPS - 1))
            live = (k >= 0) & (k < GROUPS)

            @pl.when(live & (slab == L))
            def _(g=g):
                go_up(g, False)

            @pl.when(live & (slab == n - 1 - L))
            def _(g=g):
                go_down(g, False)

        k = t - n + 2

        @pl.when((k >= 0) & (k < GROUPS))
        def _():
            finish_group(group_of(jnp.clip(k, 0, GROUPS - 1)))

        return carry

    load_x.wait()
    load_w.wait()
    receive(1)

    def start_group(k):
        if not pn.exchange:
            return
        g = int(group_index(k))
        for jj in range(1, pn.C):
            deal(g, jj).start()
        deal_own(g).start()
        if k > 0:
            begin(int(group_index(k - 1)))

    def group_index(k):
        if k < len(BACK):
            b, i = BACK[k]
            return 3 * (b - 1) + i + 1
        return GROUPS - 1

    for k, (branch, i) in enumerate(BACK):
        step = pn.steps[branch - 1]
        g = group_index(k)
        if i == -1:
            received(branch)
            receive(branch + 1 if branch < 3 else 0)

            def turn(rp, carry, branch=branch):
                at = pl.multiple_of(rp * 2 * S, 16)
                moved = dot(shifts[pl.ds((branch - 1) * 4 * S, 4 * S)], qraw[branch, pl.ds(at, 2 * S)]).astype(BF16)
                qs[branch - 1, 0, pl.ds(at, 2 * S)] = moved[:2 * S]
                qs[branch - 1, 1, pl.ds(at, 2 * S)] = moved[2 * S:]
                return carry

            lax.fori_loop(0, H // 2, turn, 0, unroll=6)
        if i != 1:
            qt[...] = qraw[branch].T
        q_turned = qt[...]
        if i != 0:
            q_turned = q_turned * lane_masks[pl.ds(2 * (branch - 1) + (i + 1) // 2, 1)]
        window = pl.ds((pn.hb + i * step) * px, pn.own)
        for j in (-1, 0, 1):
            dwbuf[3 * g + j + 1] = dot(q_turned, xs[3 + j * branch, window]).T.astype(BF16)
        start_group(k)
        mask_at = (2 * (branch - 1) + (i + 1) // 2) * H

        def block(rb, carry, branch=branch, i=i, step=step, g=g, mask_at=mask_at):
            at = pl.ds(pl.multiple_of(rb * many * px, 16), many * px)
            y = dot_nt(qs[branch - 1, 0, at], wbuf[3 * g])
            y = y + dot_nt(qraw[branch, at], wbuf[3 * g + 1])
            y = y + dot_nt(qs[branch - 1, 1, at], wbuf[3 * g + 2])
            if i != 0:
                y = jnp.concatenate(
                    [y[r * S:(r + 1) * S] * masks[mask_at + rb * many * pn.rpb + r] for r in range(many * pn.rpb)], axis=0
                )
            to = pl.ds(pl.multiple_of((rb * many + pn.hb + i * step) * px, 16), many * px)
            dxe[to] = dxe[to] + y
            return carry

        lax.fori_loop(0, MEMBERS // many, block, 0)
        if k == 5:
            hsend[0] = dxe[pl.ds(0, pn.hb * px)].astype(BF16)
            hsend[1] = dxe[pl.ds((pn.hb + MEMBERS) * px, pn.hb * px)].astype(BF16)

            @pl.when(slab > 0)
            def _():
                remote(hsend.at[0], hrecv.at[1], h_s.at[0], h_r.at[1], member(slab - 1, me)).start()

            @pl.when(slab < n - 1)
            def _():
                remote(hsend.at[1], hrecv.at[0], h_s.at[1], h_r.at[0], member(slab + 1, me)).start()

        if pn.exchange and k == 3:
            for kk in range(1, MEMBERS):
                dproj_slab(kk).wait()
            dproj_own().wait()
            total = dp1[0].astype(F32)
            for m in range(1, MEMBERS):
                total = total + dp1[m].astype(F32)
            dps[...] = total.astype(BF16)

            @pl.when(slab != home_slab)
            def _():
                dproj_home().start()

            @pl.when(slab == home_slab)
            def _():
                pltpu.make_async_copy(dps, dp2.at[slab], p2_r.at[slab]).start()

    received(0)
    dwbuf[POOL] = dot_tn(means[...].astype(BF16), q4[...]).astype(BF16)
    dwbuf[POINT] = dot(qraw[0].T, xs[3, pl.ds(pn.hb * px, pn.own)]).T.astype(BF16)
    dwbuf[TAPS - 1] = jnp.zeros((pn.cs, pn.width), BF16)
    start_group(GROUPS - 1)
    pooled = dot_nt(q4[...], wbuf[POOL]) * inv_counts[...]
    pooled_high = pooled.astype(BF16)
    pooled_low = (pooled - pooled_high.astype(F32)).astype(BF16)

    def finish(rb, carry):
        at = pl.ds(pl.multiple_of(rb * many * px, 16), many * px)
        to = pl.ds(pl.multiple_of((rb * many + pn.hb) * px, 16), many * px)
        hot = hot_px[at]
        y = dot_nt(qraw[0, at], wbuf[POINT]) + dot(hot, pooled_high) + dot(hot, pooled_low)
        dxe[to] = dxe[to] + y
        return carry

    lax.fori_loop(0, MEMBERS // many, finish, 0)
    if pn.exchange:
        begin(GROUPS - 1)
        lax.fori_loop(0, 3, serve, 0)

        @pl.when(slab == home_slab)
        def _():
            for z in range(n):
                pltpu.make_async_copy(dp2.at[z], dp2.at[z], p2_r.at[z]).wait()
            total = dp2[0].astype(F32)
            for z in range(1, n):
                total = total + dp2[z].astype(F32)
            dpf[...] = total
            for c in range(pn.C):
                @pl.when((x == lax.rem(me, pn.G)) & (col == c))
                def _():
                    pltpu.make_async_copy(dpf, dproj_out, p3_r.at[0]).start()

                @pl.when(jnp.logical_not((x == lax.rem(me, pn.G)) & (col == c)))
                def _(c=c):
                    dproj_give(c).start()

    @pl.when(slab > 0)
    def _():
        remote(hsend.at[0], hrecv.at[1], h_s.at[0], h_r.at[1], member(slab - 1, me)).wait_send()
        remote(hsend.at[1], hrecv.at[0], h_s.at[1], h_r.at[0], member(slab - 1, me)).wait_recv()

    @pl.when(slab < n - 1)
    def _():
        remote(hsend.at[1], hrecv.at[0], h_s.at[1], h_r.at[0], member(slab + 1, me)).wait_send()
        remote(hsend.at[0], hrecv.at[1], h_s.at[0], h_r.at[1], member(slab + 1, me)).wait_recv()

    @pl.when(slab == 0)
    def _():
        hrecv[0] = jnp.zeros((pn.hb * px, pn.cs), BF16)

    @pl.when(slab == n - 1)
    def _():
        hrecv[1] = jnp.zeros((pn.hb * px, pn.cs), BF16)

    for rb in range(pn.hb):
        low, high = (pn.hb + rb) * px, (MEMBERS + rb) * px
        dxe[pl.ds(low, px)] = dxe[pl.ds(low, px)] + hrecv[0, pl.ds(rb * px, px)].astype(F32)
        dxe[pl.ds(high, px)] = dxe[pl.ds(high, px)] + hrecv[1, pl.ds(rb * px, px)].astype(F32)

    def packing(rp, carry):
        pair = dxe[pl.ds(pl.multiple_of(pn.hb * px + rp * 2 * S, 16), 2 * S)].astype(BF16)
        pack[pl.ds(2 * rp, 2)] = dot(sel_t[...], pair).astype(BF16).reshape(2, pn.C * bp, pn.cs)
        return carry

    lax.fori_loop(0, H // 2, packing, 0, unroll=6)
    home = []
    for kk in range(1, MEMBERS):
        other = lax.rem(me + kk, MEMBERS)
        xo, co = other // pn.C, lax.rem(other, pn.C)
        c = remote(pack.at[pl.ds(xo * h, h), pl.ds(pl.multiple_of(co * bp, bp), bp)], dx_out.at[me], x_s.at[kk], x_r.at[kk],
                   member(slab, other))
        c.start()
        home.append(c)
    c = pltpu.make_async_copy(pack.at[pl.ds(x * h, h), pl.ds(pl.multiple_of(col * bp, bp), bp)], dx_out.at[me], x_r.at[0])
    c.start()
    home.append(c)

    if pn.exchange:
        lax.fori_loop(3, GROUPS + n - 2, serve, 0)

        def settle(g, carry):
            for jj in range(1, pn.C):
                deal(g, jj).wait_send()
                share(g, jj).wait()
            share_own(g).wait()

            def sent(home, inner):
                @pl.when(home != slab)
                def _():
                    link_last(g, home).wait_send()

                return inner

            lax.fori_loop(0, n, sent, 0)
            return carry

        lax.fori_loop(0, GROUPS, settle, 0)

        @pl.when(slab != home_slab)
        def _():
            dproj_home().wait_send()

        @pl.when(slab == home_slab)
        def _():
            for c in range(pn.C):
                @pl.when(jnp.logical_not((x == lax.rem(me, pn.G)) & (col == c)))
                def _(c=c):
                    dproj_give(c).wait_send()

        pltpu.make_async_copy(dproj_out, dproj_out, p3_r.at[0]).wait()
    else:
        c = pltpu.make_async_copy(dwbuf, dw_out, g_r.at[0, 0])
        c.start()
        c.wait()
        dproj_out[...] = jnp.zeros(dproj_out.shape, F32)
    for c in home:
        c.wait()


def conv_backward(pn, q, xs, w, dproj, q4, means, hot_px, inv_counts, masks, lane_masks, shifts, sel_t):
    dma = pltpu.SemaphoreType.DMA
    vmem = pl.BlockSpec(memory_space=pltpu.VMEM)
    hbm = pl.BlockSpec(memory_space=pl.ANY)
    shape = jax.ShapeDtypeStruct
    half = MEMBERS // 2
    n = pn.slabs if pn.exchange else 1
    sums = TAPS if pn.exchange else 1
    block_rows = 5 * pn.width // MEMBERS
    return pl.pallas_call(
        functools.partial(back_kernel, pn),
        out_shape=(
            shape((TAPS, pn.cs, pn.width), BF16),
            shape((MEMBERS, pn.h, pn.bp, pn.cs), BF16),
            shape((block_rows, pn.width), F32),
        ),
        in_specs=[hbm] * 4 + [vmem] * 4 + [pl.BlockSpec(memory_space=pltpu.SMEM)] + [vmem] * 3,
        out_specs=(hbm, hbm, vmem),
        scratch_shapes=[
            pltpu.VMEM((7, pn.ext, pn.cs), BF16),
            pltpu.VMEM((TAPS, pn.cs, pn.width), BF16),
            pltpu.VMEM((4, pn.own, pn.width), BF16),
            pltpu.VMEM((3, 2, pn.own, pn.width), BF16),
            pltpu.VMEM((pn.width, pn.own), BF16),
            pltpu.VMEM((pn.ext, pn.cs), F32),
            pltpu.VMEM((TAPS, pn.cs, pn.width), BF16),
            pltpu.VMEM((n, sums, pn.part, pn.width), BF16),
            pltpu.VMEM((n, sums, pn.part, pn.width), BF16),
            pltpu.VMEM((sums, pn.part, pn.width), BF16),
            pltpu.VMEM((2, pn.hb * pn.px, pn.cs), BF16),
            pltpu.VMEM((2, pn.hb * pn.px, pn.cs), BF16),
            pltpu.VMEM((pn.H, pn.C * pn.bp, pn.cs), BF16),
            pltpu.VMEM((MEMBERS, block_rows, pn.width), BF16),
            pltpu.VMEM((block_rows, pn.width), BF16),
            pltpu.VMEM((n, block_rows, pn.width), BF16),
            pltpu.VMEM((block_rows, pn.width), F32),
            dma((6,)), dma((4, half)), dma((4, half)), dma((4,)), dma((4,)), dma((4, half)), dma((4, half)),
            dma((GROUPS, pn.C)), dma((GROUPS, pn.C)), dma((GROUPS, n)), dma((GROUPS, n)), dma((1,)), dma((GROUPS,)),
            dma((GROUPS, pn.C)), dma((GROUPS, pn.C)),
            dma((2,)), dma((2,)), dma((MEMBERS,)), dma((MEMBERS,)),
            dma((MEMBERS,)), dma((MEMBERS,)), dma((1,)), dma((n,)), dma((pn.C,)), dma((1,)),
        ],
        compiler_params=pltpu.CompilerParams(collective_id=2, has_side_effects=True, vmem_limit_bytes=61900 * 1024),
        name="conv_backward",
    )(q, xs, w, dproj, q4, means, hot_px, inv_counts, masks, lane_masks, shifts, sel_t)


def column_tables(pn):
    S, bp, bc = pn.S, pn.bp, pn.bc
    sel = np.zeros((7, 2, S, 2, pn.C * bp), np.float32)
    shifts = np.zeros((3, 2, 2, S, 2, S), np.float32)
    for r in range(2):
        for c in range(pn.cols):
            for v in range(-3, 4):
                s = c + v * DILATIONS[0]
                if 0 <= s < pn.cols:
                    sel[v + 3, r, c, r, (s // bc) * bp + s % bc] = 1.0
            for b, d in enumerate(DILATIONS):
                for n, j in enumerate((-1, 1)):
                    s = c - j * d
                    if 0 <= s < pn.cols:
                        shifts[b, n, r, c, r, s] = 1.0
    sel = sel.reshape(7 * 2 * S, 2 * pn.C * bp)
    sel_t = sel[3 * 2 * S:4 * 2 * S].T
    return (jnp.asarray(sel, BF16), jnp.asarray(sel_t, BF16), jnp.asarray(shifts.reshape(12 * S, 2 * S), BF16))


def per_device(
    features, crop_rows, crop_cols, w_point, w_atrous, w_pool, w_proj, gains, biases, cotangent
):
    h, bc, channels = features.shape
    pn = Plan(lax.axis_size("row"), lax.axis_size("col"), h, bc, channels, gains.shape[1], crop_rows.shape[0])
    row, col = lax.axis_index("row"), lax.axis_index("col")
    slab, x = row // pn.G, row % pn.G
    crop_ids = jnp.arange(pn.crops, dtype=jnp.int32)
    ends = jnp.cumsum(crop_rows)
    counts = (crop_rows * crop_cols).astype(F32)
    pixels = jnp.sum(counts)

    def crop_of(rows):
        found = jnp.sum((rows[:, None] >= ends[None, :]).astype(jnp.int32), axis=1)
        return jnp.where(rows < 0, -1, found)

    def widths_of(crop):
        return jnp.sum(jnp.where(crop[:, None] == crop_ids[None, :], crop_cols[None, :], 0), axis=1)

    own_crop = crop_of(row * h + jnp.arange(h, dtype=jnp.int32))
    own_columns = col * bc + jnp.arange(bc, dtype=jnp.int32)
    own_valid = own_columns[None, :] < widths_of(own_crop)[:, None]
    masked = jnp.where(own_valid[:, :, None], features, 0)
    feats = masked.reshape(h, bc, pn.C, pn.G, pn.cs).transpose(3, 2, 0, 1, 4).reshape(MEMBERS, h, bc, pn.cs)
    feats = jnp.pad(feats, ((0, 0), (0, 0), (0, pn.bp - bc), (0, 0)))
    cot = jnp.pad(cotangent, ((0, 0), (0, pn.bp - bc), (0, 0)))

    slab_rows = slab * pn.H - MARGIN + jnp.arange(pn.H + 2 * MARGIN, dtype=jnp.int32)
    crops = crop_of(slab_rows)
    mid = crops[MARGIN:MARGIN + pn.H]
    same = jnp.stack(
        [crops[MARGIN + i * d:MARGIN + i * d + pn.H] == mid for d in DILATIONS for i in (-1, 1)]
    ).astype(F32)
    lane_masks = jnp.pad(jnp.repeat(same, pn.S, axis=1), ((0, 2), (0, 0))).astype(BF16)
    ncp_ids = jnp.arange(pn.ncp, dtype=jnp.int32)
    hot_rows = (mid[:, None] == ncp_ids[None, :]).astype(BF16)
    hot_px = jnp.repeat(hot_rows, pn.S, axis=0)
    hot_t = jnp.repeat(hot_rows.T, pn.S, axis=1)
    inv_counts = jnp.pad(1.0 / counts, (0, pn.ncp - pn.crops))[:, None]

    k = x * pn.C + col
    block_crop = lax.dynamic_slice_in_dim(mid, k * pn.rpb, pn.rpb)
    columns = jnp.arange(pn.S, dtype=jnp.int32)
    valid = (columns[None, :] < widths_of(block_crop)[:, None]).astype(F32).reshape(pn.px, 1)
    block_hot = jnp.repeat((block_crop[:, None] == ncp_ids[None, :]).astype(BF16), pn.S, axis=0)
    block_hot_t = jnp.repeat((ncp_ids[:, None] == block_crop[None, :]).astype(BF16), pn.S, axis=1)

    sel, sel_t, shifts = column_tables(pn)
    none = jnp.zeros((1, *w_point.shape), BF16)
    w = jnp.concatenate([w_atrous.transpose(1, 0, 2), w_point[None], w_pool[None], none], axis=0)
    proj = w_proj.reshape(pn.C, pn.proj // pn.C, pn.width)
    proj = jnp.pad(proj, ((0, 0), (0, pn.piece - pn.proj // pn.C), (0, 0)))
    if not pn.exchange:
        w = lax.all_gather(w, "row", axis=1, tiled=True)
        w = lax.dynamic_slice_in_dim(w, (col * pn.G + x) * pn.cs, pn.cs, axis=1)
    flat = same.reshape(-1)
    p, xs, w_own, means, p4, own_cot, pieces = conv_forward(pn, feats, w, cot, proj, flat, sel, hot_t, inv_counts)
    full_proj = pieces[:, :, :pn.proj // pn.C].transpose(1, 0, 2, 3).reshape(5 * pn.width, pn.width)
    q, q4, d_proj, res, d_gains, d_biases = norms(
        pn, p, p4, gains, biases, valid, (1.0 / pixels)[None], full_proj, own_cot, block_hot, block_hot_t, sel_t
    )
    dw, dx, dproj_sum = conv_backward(
        pn, q, xs, w_own, d_proj, q4, means, hot_px, inv_counts, flat, lane_masks, shifts, sel_t
    )
    if pn.exchange:
        d_proj = dproj_sum
    else:
        whole = jnp.zeros((TAPS, channels, pn.width), BF16)
        whole = lax.dynamic_update_slice(whole, dw, (0, (col * pn.G + x) * pn.cs, 0))
        whole = lax.psum(whole, "col")
        dw = lax.psum_scatter(whole, "row", scatter_dimension=1, tiled=True)
        d_proj = lax.psum(d_proj, "col")
        d_proj = lax.psum_scatter(d_proj.astype(F32), "row", scatter_dimension=0, tiled=True)
    result = res[:, :bc]
    dx = dx[:, :, :bc].reshape(pn.G, pn.C, h, bc, pn.cs).transpose(2, 3, 1, 0, 4).reshape(h, bc, channels)
    d_features = jnp.where(own_valid[:, :, None], dx, 0)
    d_point = dw[POINT].astype(F32)
    d_atrous = dw[:POINT].astype(F32).transpose(1, 0, 2)
    d_pool = dw[POOL].astype(F32)
    return (result, d_features, d_point, d_atrous, d_pool, d_proj, d_gains, d_biases)


def solution(mesh):
    return jax.shard_map(
        per_device,
        mesh=mesh,
        in_specs=(
            P("row", "col", None),
            P(),
            P(),
            P("row", None),
            P("row", None, None),
            P("row", None),
            P("row", None),
            P(),
            P(),
            P("row", "col", None),
        ),
        out_specs=(
            P("row", "col", None),
            P("row", "col", None),
            P("row", None),
            P("row", None, None),
            P("row", None),
            P("row", None),
            P(),
            P(),
        ),
        check_vma=False,
    )
```

```python
import functools

import jax
import jax.numpy as jnp
import numpy as np
from jax import lax
from jax.experimental import pallas as pl
from jax.experimental.pallas import tpu as pltpu
from jax.sharding import PartitionSpec as P

EPSILON = 1e-05
MARGIN = 18
DILATIONS = (6, 12, 18)
MEMBERS = 8
TAPS = 30
POINT, POOL, GROUPS = 27, 28, 10
MESH = pl.DeviceIdType.MESH
F32 = jnp.float32
BF16 = jnp.bfloat16

def up_to(value, multiple):
    return -(-value // multiple) * multiple


class Plan:
    def __init__(self, rows_axis, cols_axis, h, bc, channels, width, crops):
        self.R, self.C = rows_axis, cols_axis
        self.h, self.bc, self.channels, self.width = h, bc, channels, width
        self.G = MEMBERS // self.C
        self.slabs = self.R // self.G
        self.H = self.G * h
        self.cols = bc * self.C
        self.S = up_to(self.cols, 8)
        self.rpb = self.H // MEMBERS
        self.px = self.rpb * self.S
        self.own = MEMBERS * self.px
        self.hb = MARGIN // self.rpb
        self.nb = MEMBERS + 2 * self.hb
        self.ext = self.nb * self.px
        self.bp = up_to(bc, 16)
        self.cs = channels // MEMBERS
        self.crops = crops
        self.ncp = up_to(crops, 16)
        self.exchange = self.slabs == self.C and self.R == MEMBERS
        self.steps = tuple(d // self.rpb for d in DILATIONS)
        self.proj = 5 * width // self.R
        self.piece = up_to(self.proj // self.C, 16)


def home_of(pn, col):
    if pn.C != 4:
        return col
    y, c = col // 2, lax.rem(col, 2)
    return (1 - y) * 3 * c + y * (1 + c)


def slice_of(pn, k):
    return pn.G * home_of(pn, lax.rem(k, pn.C)) + k // pn.C


def remote(src, dst, send, recv, device):
    return pltpu.make_async_remote_copy(
        src_ref=src, dst_ref=dst, send_sem=send, recv_sem=recv, device_id=device, device_id_type=MESH
    )


def greet_all(pn, row, col):
    total = pn.R * pn.C
    barrier = pltpu.get_barrier_semaphore()
    me = row * pn.C + col

    def hello(k, carry):
        other = lax.rem(me + k, total)
        pl.semaphore_signal(
            barrier, inc=1, device_id=(other // pn.C, lax.rem(other, pn.C)), device_id_type=MESH
        )
        return carry

    lax.fori_loop(1, total, hello, 0)
    pl.semaphore_wait(barrier, total - 1)


def dot(a, b):
    return jnp.dot(a, b, preferred_element_type=F32)


def dot_nt(a, b):
    return lax.dot_general(a, b, (((1,), (1,)), ((), ())), preferred_element_type=F32)


def dot_tn(a, b):
    return lax.dot_general(a, b, (((0,), (0,)), ((), ())), preferred_element_type=F32)


def split_dot(dot_fn, a, b):
    high = a.astype(BF16)
    low = (a - high.astype(F32)).astype(BF16)
    return dot_fn(high, b) + dot_fn(low, b)


def conv_kernel(pn, feats, w_in, cot, proj, masks, sel, hot_t, inv_counts,
                p_out, x_out, w_out, m_out, p4_out, cot_out, proj_out,
                ring, xs, wbuf, acc, pbuf, cbuf, sbuf, rbuf, cx,
                f_s, f_r, h_s, h_r, c_s, c_r, j_s, j_r, t_s, t_r, w_s, w_r, w_l, e_s,
                r1_s, r1_r, r2_s, r2_r, o_s):
    row, col = lax.axis_index("row"), lax.axis_index("col")
    slab, x = row // pn.G, lax.rem(row, pn.G)
    me = x * pn.C + col
    core, quad = lax.rem(col, 2), me // 2
    h, H, bp, px, n = pn.h, pn.H, pn.bp, pn.px, pn.slabs
    many = 4

    def member(s, k):
        return (s * pn.G + k // pn.C, lax.rem(k, pn.C))

    greet_all(pn, row, col)

    own_cols = pl.ds(pl.multiple_of(col * bp, bp), bp)
    own_rows = pl.ds(MARGIN + h * x, h)
    sent = []
    for kk in range(1, MEMBERS):
        other = lax.rem(me + kk, MEMBERS)
        c = remote(feats.at[slice_of(pn, other)], ring.at[own_rows, own_cols], f_s.at[kk], f_r.at[kk], member(slab, other))
        c.start()
        sent.append(c)
    keep = pltpu.make_async_copy(feats.at[slice_of(pn, me)], ring.at[own_rows, own_cols], f_r.at[0])
    keep.start()

    home = home_of(pn, col)
    source, rising, falling = slab == home, (slab > home) & (slab < n - 1), (slab < home) & (slab > 0)
    help_up, help_down = (slab == n - 2) & (col == 1), (slab == 1) & (col == 0)
    half_rows = pn.cs // 2

    def taps(g):
        return pl.ds(3 * g, 3)

    def part_of(ref, g, half):
        return ref.at[taps(g), pl.ds(half * half_rows, half_rows)]

    def ship(g, half, up, src):
        to = slab + 1 if up else slab - 1
        return remote(part_of(src, g, half), part_of(wbuf, g, half), w_s.at[int(up), half, g], w_r.at[half, g],
                      (to * pn.G + x, col))

    def assist(g, up):
        to = slab + 1 if up else slab - 1
        return remote(part_of(w_in, g, 1), part_of(wbuf, g, 1), e_s.at[g], w_r.at[1, g], (to * pn.G + x, col + 2))

    def own_copy(g):
        return pltpu.make_async_copy(w_in.at[taps(g)], wbuf.at[taps(g)], w_l.at[g])

    def arrived(g):
        for half in (0, 1):
            at = part_of(wbuf, g, half)
            pltpu.make_async_copy(at, at, w_r.at[half, g]).wait()

    def pass_on(g):
        for role, up in ((rising, True), (falling, False)):
            @pl.when(role)
            def _(up=up):
                arrived(g)
                for half in (0, 1):
                    ship(g, half, up, wbuf).start()

    def w_wait(g):
        if pn.exchange:
            @pl.when(source)
            def _():
                own_copy(g).wait()

            @pl.when(jnp.logical_not(source | rising | falling))
            def _():
                arrived(g)
        else:
            own_copy(g).wait()

    def each_shipment(g, act):
        for half in (0, 1):
            @pl.when(source & ((slab < n - 2) if half else (slab < n - 1)))
            def _(half=half):
                act(ship(g, half, True, w_in))

            @pl.when(source & ((slab > 1) if half else (slab > 0)))
            def _(half=half):
                act(ship(g, half, False, w_in))

        @pl.when(help_up)
        def _():
            act(assist(g, True))

        @pl.when(help_down)
        def _():
            act(assist(g, False))

    if pn.exchange:
        def begin(g, carry):
            each_shipment(g, lambda c: c.start())

            @pl.when(source)
            def _():
                own_copy(g).start()

            return carry
    else:
        def begin(g, carry):
            own_copy(g).start()
            return carry

    lax.fori_loop(0, GROUPS, begin, 0)

    cot_sent = []
    for cc in range(1, pn.C):
        cd = lax.rem(col + cc, pn.C)
        c = remote(cot.at[pl.ds(cd * pn.rpb, pn.rpb)], cx.at[:, own_cols], c_s.at[cc], c_r.at[cc], (row, cd))
        c.start()
        cot_sent.append(c)
    cot_keep = pltpu.make_async_copy(cot.at[pl.ds(col * pn.rpb, pn.rpb)], cx.at[:, own_cols], c_r.at[0])
    cot_keep.start()

    def proj_row(k):
        return remote(proj.at[col], proj_out.at[col, row], j_s.at[k], j_r.at[k], (lax.rem(row + k, pn.R), col))

    def proj_col(k):
        return remote(proj_out.at[col], proj_out.at[col], t_s.at[k], t_r.at[k], (row, lax.rem(col + k, pn.C)))

    def proj_begin(k, carry):
        proj_row(k).start()
        return carry

    def proj_wait(k, carry):
        proj_row(k).wait()
        return carry

    lax.fori_loop(1, pn.R, proj_begin, 0)
    proj_keep = pltpu.make_async_copy(proj.at[col], proj_out.at[col, row], j_r.at[0])
    proj_keep.start()

    @pl.when(slab == 0)
    def _():
        ring[pl.ds(0, MARGIN)] = jnp.zeros((MARGIN, pn.C * bp, pn.cs), BF16)

    @pl.when(slab == n - 1)
    def _():
        ring[pl.ds(MARGIN + H, MARGIN)] = jnp.zeros((MARGIN, pn.C * bp, pn.cs), BF16)

    for c in sent:
        c.wait()
    keep.wait()

    def margin_down():
        return remote(ring.at[pl.ds(MARGIN, MARGIN)], ring.at[pl.ds(MARGIN + H, MARGIN)], h_s.at[0], h_r.at[0],
                      member(slab - 1, me))

    def margin_up():
        return remote(ring.at[pl.ds(H, MARGIN)], ring.at[pl.ds(0, MARGIN)], h_s.at[1], h_r.at[1], member(slab + 1, me))

    @pl.when(slab > 0)
    def _():
        margin_down().start()

    @pl.when(slab < n - 1)
    def _():
        margin_up().start()

    def pass_many(first, end):
        def one(g, carry):
            pass_on(g)
            return carry

        if pn.exchange:
            lax.fori_loop(first, end, one, 0)

    pass_many(0, 3)

    def assemble(rp, carry):
        pair = ring[pl.ds(2 * rp, 2)].reshape(2 * pn.C * bp, pn.cs)
        moved = dot(sel[...], pair).astype(BF16)
        at = pl.multiple_of(rp * 2 * pn.S, 16)
        for v in range(7):
            xs[v, pl.ds(at, 2 * pn.S)] = moved[v * 2 * pn.S:(v + 1) * 2 * pn.S]
        return carry

    lax.fori_loop(MARGIN // 2, (MARGIN + H) // 2, assemble, 0, unroll=6)
    for c in cot_sent:
        c.wait()
    cot_keep.wait()
    for rp in range(pn.rpb // 2):
        pair = cx[2 * rp:2 * rp + 2].reshape(2 * pn.C * bp, pn.width)
        cot_out[pl.ds(rp * 2 * pn.S, 2 * pn.S)] = dot(sel[pl.ds(3 * 2 * pn.S, 2 * pn.S)], pair).astype(BF16)
    lax.fori_loop(1, pn.R, proj_wait, 0)
    proj_keep.wait()
    for k in range(1, pn.C):
        proj_col(k).start()
    pass_many(3, 5)

    @pl.when(slab > 0)
    def _():
        margin_down().wait_send()
        margin_up().wait_recv()

    @pl.when(slab < n - 1)
    def _():
        margin_up().wait_send()
        margin_down().wait_recv()

    lax.fori_loop(0, MARGIN // 2, assemble, 0, unroll=3)
    lax.fori_loop((MARGIN + H) // 2, pn.nb * pn.rpb // 2, assemble, 0, unroll=3)
    x_save = pltpu.make_async_copy(xs, x_out, o_s.at[0])
    x_save.start()

    def first_stage(slot):
        return remote(pbuf.at[slot, :, 1 - core], cbuf.at[slot], r1_s.at[slot], r1_r.at[slot], (row, col + 1 - 2 * core))

    def second_stage(slot, i):
        q = lax.rem(quad + i, MEMBERS // 2)
        return remote(sbuf.at[slot, i - 1], rbuf.at[slot, i - 1], r2_s.at[slot, i - 1], r2_r.at[slot, i - 1],
                      member(slab, 2 * q + core))

    def middle(slot):
        first_stage(slot).wait()
        for i in (1, 2, 3, 0):
            q = lax.rem(quad + i, MEMBERS // 2)
            s = pbuf[slot, q, core].astype(F32) + cbuf[slot, q].astype(F32)
            if i == 0:
                p_out[slot] = s
            else:
                sbuf[slot, i - 1] = s.astype(BF16)
                second_stage(slot, i).start()

    def last(slot):
        total = p_out[slot]
        for i in range(1, MEMBERS // 2):
            second_stage(slot, i).wait()
            total = total + rbuf[slot, i - 1].astype(F32)
        p_out[slot] = total

    def scatter(slot, rb, y):
        for r in range(many):
            pbuf[slot, (many * rb + r) // 2, r % 2] = y[r * px:(r + 1) * px].astype(BF16)

    def far(g):
        if g + 5 < GROUPS:
            pass_many(g + 5, g + 6)
        w_wait(g)

    for branch in (1, 2, 3):
        step = pn.steps[branch - 1]
        for i in (-1, 0, 1):
            g = 3 * (branch - 1) + i + 1
            mask_at = (2 * (branch - 1) + (i + 1) // 2) * H
            far(g)

            def block(rb, carry, step=step, i=i, g=g, mask_at=mask_at, branch=branch):
                at = pl.multiple_of(rb * many * px, 16)
                window = pl.ds(pl.multiple_of((rb * many + pn.hb + i * step) * px, 16), many * px)
                y = dot(xs[3 - branch, window], wbuf[3 * g])
                y = y + dot(xs[3, window], wbuf[3 * g + 1])
                y = y + dot(xs[3 + branch, window], wbuf[3 * g + 2])
                if i != 0:
                    y = jnp.concatenate(
                        [y[r * pn.S:(r + 1) * pn.S] * masks[mask_at + rb * many * pn.rpb + r]
                         for r in range(many * pn.rpb)], axis=0
                    )
                if i > -1:
                    y = y + acc[pl.ds(at, many * px)]
                if i < 1:
                    acc[pl.ds(at, many * px)] = y
                else:
                    scatter(branch, rb, y)
                return carry

            lax.fori_loop(0, MEMBERS // many, block, 0)
            if i == 0 and branch > 1:
                middle(branch - 1)
        first_stage(branch).start()

    far(GROUPS - 1)

    def point(rb, carry):
        at = pl.ds(pl.multiple_of((rb * many + pn.hb) * px, 16), many * px)
        scatter(0, rb, dot(xs[3, at], wbuf[POINT]))
        return carry

    lax.fori_loop(0, MEMBERS // many, point, 0)
    first_stage(0).start()
    middle(3)

    sums = dot(hot_t[...], xs[3, pl.ds(pn.hb * px, pn.own)])
    means = sums * inv_counts[...]
    m_out[...] = means
    p4_out[...] = split_dot(dot, means, wbuf[POOL])
    w_save = pltpu.make_async_copy(wbuf, w_out, o_s.at[1])
    w_save.start()
    middle(0)
    for slot in (1, 2, 3):
        last(slot)
    for k in range(1, pn.C):
        proj_col(k).wait()
    if pn.exchange:
        def settled(g, carry):
            each_shipment(g, lambda c: c.wait_send())
            for role, up in ((rising, True), (falling, False)):
                @pl.when(role)
                def _(up=up):
                    for half in (0, 1):
                        ship(g, half, up, wbuf).wait_send()
            return carry

        lax.fori_loop(0, GROUPS, settled, 0)
    last(0)
    x_save.wait()
    w_save.wait()


def conv_forward(pn, feats, w, cot, proj, masks, sel, hot_t, inv_counts):
    half = MEMBERS // 2
    dma = pltpu.SemaphoreType.DMA
    vmem = pl.BlockSpec(memory_space=pltpu.VMEM)
    hbm = pl.BlockSpec(memory_space=pl.ANY)
    shape = jax.ShapeDtypeStruct
    return pl.pallas_call(
        functools.partial(conv_kernel, pn),
        out_shape=(
            shape((4, pn.px, pn.width), F32),
            shape((7, pn.ext, pn.cs), BF16),
            shape((TAPS, pn.cs, pn.width), BF16),
            shape((pn.ncp, pn.cs), F32),
            shape((pn.ncp, pn.width), F32),
            shape((pn.px, pn.width), BF16),
            shape((pn.C, pn.R, pn.piece, pn.width), BF16),
        ),
        in_specs=[hbm, hbm, hbm, hbm, pl.BlockSpec(memory_space=pltpu.SMEM), vmem, vmem, vmem],
        out_specs=(vmem, hbm, hbm, vmem, vmem, vmem, vmem),
        scratch_shapes=[
            pltpu.VMEM((pn.nb * pn.rpb, pn.C * pn.bp, pn.cs), BF16),
            pltpu.VMEM((7, pn.ext, pn.cs), BF16),
            pltpu.VMEM((TAPS, pn.cs, pn.width), BF16),
            pltpu.VMEM((pn.own, pn.width), F32),
            pltpu.VMEM((4, half, 2, pn.px, pn.width), BF16),
            pltpu.VMEM((4, half, pn.px, pn.width), BF16),
            pltpu.VMEM((4, half - 1, pn.px, pn.width), BF16),
            pltpu.VMEM((4, half - 1, pn.px, pn.width), BF16),
            pltpu.VMEM((pn.rpb, pn.C * pn.bp, pn.width), BF16),
            dma((MEMBERS,)), dma((MEMBERS,)), dma((2,)), dma((2,)), dma((pn.C,)), dma((pn.C,)),
            dma((pn.R,)), dma((pn.R,)), dma((pn.C,)), dma((pn.C,)),
            dma((2, 2, GROUPS)), dma((2, GROUPS)), dma((GROUPS,)), dma((GROUPS,)),
            dma((4,)), dma((4,)), dma((4, 3)), dma((4, 3)), dma((2,)),
        ],
        compiler_params=pltpu.CompilerParams(collective_id=0, has_side_effects=True, vmem_limit_bytes=60 * 2**20),
        name="conv_forward",
    )(feats, w, cot, proj, masks, sel, hot_t, inv_counts)


def norm_kernel(pn, p, p4_in, gains, biases, valid, pixels, w_proj, cot, hot, hot_t, sel_t,
                q_out, q4_out, dproj_out, res_out, dg_out, db_out,
                norm, slope, hbuf, gact, dh4, rx,
                a1, b1, a2, b2, a3, b3, a4, b4, as_s, as_r, bs_s, bs_r, e_s, e_r):
    row, col = lax.axis_index("row"), lax.axis_index("col")
    slab, x = row // pn.G, lax.rem(row, pn.G)
    me = x * pn.C + col
    crops = float(pn.crops)
    v = valid[...]
    inv_px = pixels[0]
    width, bp = pn.width, pn.bp

    def member(s, k):
        return (s * pn.G + k // pn.C, lax.rem(k, pn.C))

    barrier = pltpu.get_barrier_semaphore()
    for kk in range(1, MEMBERS):
        pl.semaphore_signal(barrier, inc=1, device_id=member(slab, lax.rem(me + kk, MEMBERS)), device_id_type=MESH)

    def hello(k, carry):
        pl.semaphore_signal(barrier, inc=1, device_id=member(lax.rem(slab + k, pn.slabs), me), device_id_type=MESH)
        return carry

    lax.fori_loop(1, pn.slabs, hello, 0)

    def peer_a(n, abuf, kk):
        return remote(abuf.at[me], abuf.at[me], as_s.at[n, kk], as_r.at[n, kk], member(slab, lax.rem(me + kk, MEMBERS)))

    def peer_b(n, bbuf, k):
        return remote(bbuf.at[slab], bbuf.at[slab], bs_s.at[n, k], bs_r.at[n, k], member(lax.rem(slab + k, pn.slabs), me))

    def reduce_start(n, abuf):
        for kk in range(1, MEMBERS):
            peer_a(n, abuf, kk).start()

    def reduce_end(n, abuf, bbuf):
        for kk in range(1, MEMBERS):
            peer_a(n, abuf, kk).wait()
        total = abuf[0]
        for k in range(1, MEMBERS):
            total = total + abuf[k]
        bbuf[slab] = total
        for k in range(1, pn.slabs):
            peer_b(n, bbuf, k).start()
        for k in range(1, pn.slabs):
            peer_b(n, bbuf, k).wait()
        total = bbuf[0]
        for k in range(1, pn.slabs):
            total = total + bbuf[k]
        return total

    def column_sum(value):
        return jnp.sum(value, axis=0, keepdims=True)

    for b in range(4):
        pv = p[b] * v
        a1[me, pl.ds(b, 1)] = column_sum(pv)
        a1[me, pl.ds(4 + b, 1)] = column_sum(pv * p[b])
    a1[me, pl.ds(8, pn.ncp)] = p4_in[...]
    pl.semaphore_wait(barrier, MEMBERS - 1 + pn.slabs - 1)
    reduce_start(0, a1)
    total = reduce_end(0, a1, b1)
    inv = []
    for b in range(4):
        centre = total[b:b + 1] * inv_px
        scale = lax.rsqrt(total[4 + b:5 + b] * inv_px - centre * centre + EPSILON)
        inv.append(scale)
        n = (p[b] - centre) * scale
        u = gains[b:b + 1] * n + biases[b:b + 1]
        s = jax.nn.sigmoid(u)
        norm[b] = n
        slope[b] = s * (1.0 + u * (1.0 - s))
        hbuf[b] = (u * s).astype(BF16)
    p4 = total[8:8 + pn.ncp]
    centre4 = column_sum(p4) * (1.0 / crops)
    inv4 = lax.rsqrt(column_sum(p4 * p4) * (1.0 / crops) - centre4 * centre4 + EPSILON)
    n4 = (p4 - centre4) * inv4
    u4 = gains[4:5] * n4 + biases[4:5]
    s4 = jax.nn.sigmoid(u4)
    slope4 = s4 * (1.0 + u4 * (1.0 - s4))
    hbuf[4] = dot(hot[...], (u4 * s4).astype(BF16)).astype(BF16)

    p5 = dot(hbuf[0], w_proj[pl.ds(0, width)])
    for b in range(1, 5):
        p5 = p5 + dot(hbuf[b], w_proj[pl.ds(b * width, width)])
    pv = p5 * v
    a2[me, pl.ds(0, 1)] = column_sum(pv)
    a2[me, pl.ds(1, 1)] = column_sum(pv * p5)
    a2[me, pl.ds(2, 6)] = jnp.zeros((6, width), F32)
    reduce_start(1, a2)
    total = reduce_end(1, a2, b2)
    centre5 = total[0:1] * inv_px
    inv5 = lax.rsqrt(total[1:2] * inv_px - centre5 * centre5 + EPSILON)
    n5 = (p5 - centre5) * inv5
    u5 = gains[5:6] * n5 + biases[5:6]
    s5 = jax.nn.sigmoid(u5)
    g5 = cot[...].astype(F32) * v * (s5 * (1.0 + u5 * (1.0 - s5)))
    norm[4] = n5
    gact[4] = g5
    a3[me, pl.ds(0, 1)] = column_sum(g5)
    a3[me, pl.ds(1, 1)] = column_sum(g5 * n5)
    a3[me, pl.ds(2, 6)] = jnp.zeros((6, width), F32)
    reduce_start(2, a3)
    hbuf[5] = (v * u5 * s5).astype(BF16)
    for rp in range(pn.rpb // 2):
        pair = hbuf[5, pl.ds(rp * 2 * pn.S, 2 * pn.S)]
        rx[2 * rp:2 * rp + 2] = dot(sel_t[...], pair).astype(BF16).reshape(2, pn.C * bp, width)
    back = []
    for cc in range(1, pn.C):
        cd = lax.rem(col + cc, pn.C)
        c = remote(rx.at[:, pl.ds(pl.multiple_of(cd * bp, bp), bp)], res_out.at[pl.ds(col * pn.rpb, pn.rpb)],
                   e_s.at[cc], e_r.at[cc], (row, cd))
        c.start()
        back.append(c)
    c = pltpu.make_async_copy(rx.at[:, pl.ds(pl.multiple_of(col * bp, bp), bp)], res_out.at[pl.ds(col * pn.rpb, pn.rpb)],
                              e_r.at[0])
    c.start()
    back.append(c)
    total = reduce_end(2, a3, b3)
    db5, dg5 = total[0:1], total[1:2]
    q5 = (gains[5:6] * inv5 * (gact[4] - v * (db5 + norm[4] * dg5) * inv_px)).astype(BF16)
    hbuf[5] = q5

    for b in range(4):
        g = dot_nt(q5, w_proj[pl.ds(b * width, width)]) * slope[b]
        gact[b] = g
        a4[me, pl.ds(b, 1)] = column_sum(g)
        a4[me, pl.ds(4 + b, 1)] = column_sum(g * norm[b])
    dh4[...] = dot_nt(q5, w_proj[pl.ds(4 * width, width)])
    high = dh4[...].astype(BF16)
    low = (dh4[...] - high.astype(F32)).astype(BF16)
    a4[me, pl.ds(8, pn.ncp)] = dot(hot_t[...], high) + dot(hot_t[...], low)
    reduce_start(3, a4)
    for b in range(5):
        dproj_out[pl.ds(b * width, width)] = dot_tn(hbuf[b], hbuf[5]).astype(BF16)
    total = reduce_end(3, a4, b4)
    for b in range(4):
        db, dg = total[b:b + 1], total[4 + b:5 + b]
        db_out[pl.ds(b, 1)] = db
        dg_out[pl.ds(b, 1)] = dg
        q_out[b] = (gains[b:b + 1] * inv[b] * (gact[b] - v * (db + norm[b] * dg) * inv_px)).astype(BF16)
    g4 = total[8:8 + pn.ncp] * slope4
    db4, dg4 = column_sum(g4), column_sum(g4 * n4)
    db_out[pl.ds(4, 1)] = db4
    dg_out[pl.ds(4, 1)] = dg4
    db_out[pl.ds(5, 1)] = db5
    dg_out[pl.ds(5, 1)] = dg5
    q4_out[...] = (gains[4:5] * inv4 * (g4 - (db4 + n4 * dg4) * (1.0 / crops))).astype(BF16)
    for c in back:
        c.wait()


def norms(pn, p, p4, gains, biases, valid, pixels, w_proj, cot, hot, hot_t, sel_t):
    dma = pltpu.SemaphoreType.DMA
    vmem = pl.BlockSpec(memory_space=pltpu.VMEM)
    shape = jax.ShapeDtypeStruct
    big, small = 8 + pn.ncp, 8
    bufs = []
    for n in (big, small, small, big):
        bufs += [pltpu.VMEM((MEMBERS, n, pn.width), F32), pltpu.VMEM((pn.slabs, n, pn.width), F32)]
    return pl.pallas_call(
        functools.partial(norm_kernel, pn),
        out_shape=(
            shape((4, pn.px, pn.width), BF16),
            shape((pn.ncp, pn.width), BF16),
            shape((5 * pn.width, pn.width), BF16),
            shape((pn.h, pn.bp, pn.width), BF16),
            shape((6, pn.width), F32),
            shape((6, pn.width), F32),
        ),
        in_specs=[vmem] * 5 + [pl.BlockSpec(memory_space=pltpu.SMEM)] + [vmem] * 5,
        out_specs=(vmem,) * 6,
        scratch_shapes=[
            pltpu.VMEM((5, pn.px, pn.width), F32),
            pltpu.VMEM((4, pn.px, pn.width), F32),
            pltpu.VMEM((6, pn.px, pn.width), BF16),
            pltpu.VMEM((5, pn.px, pn.width), F32),
            pltpu.VMEM((pn.px, pn.width), F32),
            pltpu.VMEM((pn.rpb, pn.C * pn.bp, pn.width), BF16),
            *bufs,
            dma((4, MEMBERS)), dma((4, MEMBERS)), dma((4, pn.slabs)), dma((4, pn.slabs)), dma((pn.C,)), dma((pn.C,)),
        ],
        compiler_params=pltpu.CompilerParams(collective_id=1, has_side_effects=True, vmem_limit_bytes=48 * 2**20),
        name="norms",
    )(p, p4, gains, biases, valid, pixels, w_proj, cot, hot, hot_t, sel_t)


BACK = tuple((b, i) for b in (1, 2, 3) for i in (-1, 1)) + tuple((b, 0) for b in (1, 2, 3))


def group_of(k):
    middle = k // 6
    return (1 - middle) * (3 * (k // 2) + 2 * (k % 2)) + middle * jnp.minimum(1 + 3 * (k - 6), GROUPS - 1)


def back_kernel(pn, q_in, x_in, w_in, dproj_in, q4, means, hot_px, inv_counts, masks, lane_masks, shifts, sel_t,
                dw_out, dx_out, dproj_out,
                xs, wbuf, qraw, qs, qt, dxe, dwbuf, inn, hsend, hrecv, pack, dp1, dps, dp2, dpf,
                l_s, q_s, q_r, k_s, k_r, f_s, f_r, n_s, n_r, e_s, e_r, g_s, g_r, h_s, h_r, x_s, x_r,
                p1_s, p1_r, p2_s, p2_r, p3_s, p3_r):
    row, col = lax.axis_index("row"), lax.axis_index("col")
    slab, x = row // pn.G, lax.rem(row, pn.G)
    me = x * pn.C + col
    core, quad = lax.rem(col, 2), me // 2
    h, H, bp, px, S, n = pn.h, pn.H, pn.bp, pn.px, pn.S, pn.slabs
    half = MEMBERS // 2
    many = 4
    partner = (row, col + 1 - 2 * core)

    def member(s, k):
        return (s * pn.G + k // pn.C, lax.rem(k, pn.C))

    load_x = pltpu.make_async_copy(x_in, xs, l_s.at[0])
    load_w = pltpu.make_async_copy(w_in, wbuf, l_s.at[1])
    load_x.start()
    load_w.start()
    greet_all(pn, row, col)

    own_px = pl.ds(pl.multiple_of(me * px, 16), px)
    along_y, along_x = (row, lax.rem(col + 2, pn.C)), (slab * pn.G + lax.rem(x + 1, pn.G), col)
    from_y = x * pn.C + lax.rem(col + 2, pn.C)
    from_x = lax.rem(me + pn.C, MEMBERS)
    from_xy = lax.rem(from_y + pn.C, MEMBERS)

    def block_of(slot, k):
        return qraw.at[slot, pl.ds(pl.multiple_of(k * px, 16), px)]

    def to_y(slot):
        return remote(q_in.at[slot], qraw.at[slot, own_px], q_s.at[slot, 0], q_r.at[slot, 0], along_y)

    def to_x(slot):
        return remote(q_in.at[slot], qraw.at[slot, own_px], q_s.at[slot, 1], q_r.at[slot, 1], along_x)

    def on_to_x(slot):
        return remote(block_of(slot, from_y), block_of(slot, from_y), q_s.at[slot, 2], q_r.at[slot, 2], along_x)

    def to_partner(slot):
        return remote(q_in.at[slot], qraw.at[slot, own_px], k_s.at[slot], k_r.at[slot], partner)

    def passed(slot, i):
        at = block_of(slot, (from_y, from_x, from_xy)[i])
        return remote(at, at, f_s.at[slot, i], f_r.at[slot, i], partner)

    def kept(slot):
        return pltpu.make_async_copy(q_in.at[slot], qraw.at[slot, own_px], l_s.at[2 + slot])

    slots = (1, 2, 3, 0)
    for slot in slots:
        to_y(slot).start()
        to_x(slot).start()
        to_partner(slot).start()
        kept(slot).start()

    block_rows = 5 * pn.width // MEMBERS
    home_slab = me // pn.G

    def dproj_slab(kk):
        other = lax.rem(me + kk, MEMBERS)
        return remote(dproj_in.at[pl.ds(pl.multiple_of(other * block_rows, 16), block_rows)], dp1.at[me],
                      p1_s.at[kk], p1_r.at[kk], member(slab, other))

    def dproj_own():
        return pltpu.make_async_copy(dproj_in.at[pl.ds(pl.multiple_of(me * block_rows, 16), block_rows)], dp1.at[me],
                                     p1_r.at[0])

    def dproj_home():
        return remote(dps, dp2.at[slab], p2_s.at[0], p2_r.at[slab], member(home_slab, me))

    def dproj_give(c):
        return remote(dpf, dproj_out, p3_s.at[c], p3_r.at[0], (slab * pn.G + lax.rem(me, pn.G), c))

    if pn.exchange:
        for kk in range(1, MEMBERS):
            dproj_slab(kk).start()
        dproj_own().start()

    def clear(rb, carry):
        dxe[pl.ds(pl.multiple_of(rb * px, 16), px)] = jnp.zeros((px, pn.cs), F32)
        return carry

    lax.fori_loop(0, pn.nb, clear, 0)

    def receive_y(slot):
        to_y(slot).wait()
        on_to_x(slot).start()
        passed(slot, 0).start()

    def receive_x(slot):
        to_x(slot).wait()
        passed(slot, 1).start()
        on_to_x(slot).wait()
        passed(slot, 2).start()

    def received(slot):
        to_partner(slot).wait()
        kept(slot).wait()
        for i in range(3):
            passed(slot, i).wait()

    home = home_of(pn, col)
    closing, rising, falling = slab == home, slab < home, slab > home
    first = (slab == 0) | (slab == n - 1)
    half_rows = pn.cs // 2
    detour_up, detour_down = (slab == 0) & (col == 2), (slab == n - 1) & (col == 3)
    relay_up, relay_down = (slab == 0) & (col == 0), (slab == n - 1) & (col == 1)

    def taps(g):
        return pl.ds(3 * g, 3)

    def part_of(ref, g, half):
        return ref.at[taps(g), pl.ds(half * half_rows, half_rows)]

    def link(g, half, up):
        side, to = (0, slab + 1) if up else (1, slab - 1)
        return remote(part_of(dwbuf, g, half), part_of(inn.at[side], g, half), n_s.at[half, g], n_r.at[side, half, g],
                      (to * pn.G + x, col))

    def detour(g, up):
        side = 0 if up else 1
        return remote(part_of(dwbuf, g, 1), part_of(inn.at[side], g, 1), n_s.at[1, g], e_r.at[g], (row, col - 2))

    def relay(g, up):
        side, to = (0, slab + 1) if up else (1, slab - 1)
        return remote(part_of(inn.at[side], g, 1), part_of(inn.at[side], g, 1), e_s.at[g], n_r.at[side, 1, g],
                      (to * pn.G + x, col + 2))

    def each_link(g, act):
        for going, up, around in ((rising, True, detour_up), (falling, False, detour_down)):
            @pl.when(going)
            def _(up=up):
                act(link(g, 0, up))

            @pl.when(going & jnp.logical_not(around))
            def _(up=up):
                act(link(g, 1, up))

            @pl.when(around)
            def _(up=up):
                act(detour(g, up))

    def arrived(g, side):
        for half in (0, 1):
            at = part_of(inn.at[side], g, half)
            pltpu.make_async_copy(at, at, n_r.at[side, half, g]).wait()

    def add(g, side):
        dwbuf[taps(g)] = (dwbuf[taps(g)].astype(F32) + inn[side, taps(g)].astype(F32)).astype(BF16)

    def share_y(g):
        return remote(dwbuf.at[taps(g)], dw_out.at[taps(g)], g_s.at[0, g], g_r.at[g], (row, lax.rem(col + 2, pn.C)))

    def share_core(g):
        return remote(dwbuf.at[taps(g)], dw_out.at[taps(g)], g_s.at[1, g], g_r.at[g], partner)

    def share_on(g):
        return remote(dw_out.at[taps(g)], dw_out.at[taps(g)], g_s.at[0, g], g_r.at[g], partner)

    shared_on = home_of(pn, lax.rem(col + 2, pn.C)) == slab

    def landed(g):
        pltpu.make_async_copy(dw_out.at[taps(g)], dw_out.at[taps(g)], g_r.at[g]).wait()

    def serve(k, carry):
        g = group_of(k)
        for role, up in ((relay_up, True), (relay_down, False)):
            @pl.when(role)
            def _(up=up):
                side = 0 if up else 1
                at = part_of(inn.at[side], g, 1)
                pltpu.make_async_copy(at, at, e_r.at[g]).wait()
                relay(g, up).start()

        @pl.when(rising & jnp.logical_not(first))
        def _():
            arrived(g, 0)
            add(g, 0)
            for half in (0, 1):
                link(g, half, True).start()

        @pl.when(falling & jnp.logical_not(first))
        def _():
            arrived(g, 1)
            add(g, 1)
            for half in (0, 1):
                link(g, half, False).start()

        @pl.when(closing)
        def _():
            @pl.when(slab > 0)
            def _():
                arrived(g, 0)
                add(g, 0)

            @pl.when(slab < n - 1)
            def _():
                arrived(g, 1)
                add(g, 1)

            share_y(g).start()
            share_core(g).start()
            pltpu.make_async_copy(dwbuf.at[taps(g)], dw_out.at[taps(g)], g_r.at[g]).start()

        @pl.when(shared_on & (k > 1))
        def _():
            before = group_of(jnp.maximum(k - 2, 0))
            landed(before)
            share_on(before).start()

        return carry

    receive_y(1)
    receive_y(2)
    load_x.wait()
    load_w.wait()
    receive_x(1)
    receive_y(3)

    def start_group(k):
        if not pn.exchange:
            return
        g = group_index(k)

        @pl.when(first)
        def _():
            each_link(g, lambda c: c.start())

    def group_index(k):
        if k < len(BACK):
            b, i = BACK[k]
            return 3 * (b - 1) + i + 1
        return GROUPS - 1

    for k, (branch, i) in enumerate(BACK):
        step = pn.steps[branch - 1]
        g = group_index(k)
        if i == -1:
            received(branch)
            if branch == 2:
                receive_y(0)
            receive_x(branch + 1 if branch < 3 else 0)

            def turn(rp, carry, branch=branch):
                at = pl.multiple_of(rp * 2 * S, 16)
                moved = dot(shifts[pl.ds((branch - 1) * 4 * S, 4 * S)], qraw[branch, pl.ds(at, 2 * S)]).astype(BF16)
                qs[branch - 1, 0, pl.ds(at, 2 * S)] = moved[:2 * S]
                qs[branch - 1, 1, pl.ds(at, 2 * S)] = moved[2 * S:]
                return carry

            lax.fori_loop(0, H // 2, turn, 0, unroll=6)
        if i != 1:
            qt[...] = qraw[branch].T
        q_turned = qt[...]
        if i != 0:
            q_turned = q_turned * lane_masks[pl.ds(2 * (branch - 1) + (i + 1) // 2, 1)]
        window = pl.ds((pn.hb + i * step) * px, pn.own)
        for j in (-1, 0, 1):
            dwbuf[3 * g + j + 1] = dot(q_turned, xs[3 + j * branch, window]).T.astype(BF16)
        start_group(k)
        mask_at = (2 * (branch - 1) + (i + 1) // 2) * H

        def block(rb, carry, branch=branch, i=i, step=step, g=g, mask_at=mask_at):
            at = pl.ds(pl.multiple_of(rb * many * px, 16), many * px)
            y = dot_nt(qs[branch - 1, 0, at], wbuf[3 * g])
            y = y + dot_nt(qraw[branch, at], wbuf[3 * g + 1])
            y = y + dot_nt(qs[branch - 1, 1, at], wbuf[3 * g + 2])
            if i != 0:
                y = jnp.concatenate(
                    [y[r * S:(r + 1) * S] * masks[mask_at + rb * many * pn.rpb + r] for r in range(many * pn.rpb)], axis=0
                )
            to = pl.ds(pl.multiple_of((rb * many + pn.hb + i * step) * px, 16), many * px)
            dxe[to] = dxe[to] + y
            return carry

        lax.fori_loop(0, MEMBERS // many, block, 0)
        if k == 5:
            hsend[0] = dxe[pl.ds(0, pn.hb * px)].astype(BF16)
            hsend[1] = dxe[pl.ds((pn.hb + MEMBERS) * px, pn.hb * px)].astype(BF16)

            @pl.when(slab > 0)
            def _():
                remote(hsend.at[0], hrecv.at[1], h_s.at[0], h_r.at[1], member(slab - 1, me)).start()

            @pl.when(slab < n - 1)
            def _():
                remote(hsend.at[1], hrecv.at[0], h_s.at[1], h_r.at[0], member(slab + 1, me)).start()

        if pn.exchange and k == 3:
            for kk in range(1, MEMBERS):
                dproj_slab(kk).wait()
            dproj_own().wait()
            total = dp1[0].astype(F32)
            for m in range(1, MEMBERS):
                total = total + dp1[m].astype(F32)
            dps[...] = total.astype(BF16)

            @pl.when(slab != home_slab)
            def _():
                dproj_home().start()

            @pl.when(slab == home_slab)
            def _():
                pltpu.make_async_copy(dps, dp2.at[slab], p2_r.at[slab]).start()

    received(0)
    dwbuf[POOL] = dot_tn(means[...].astype(BF16), q4[...]).astype(BF16)
    dwbuf[POINT] = dot(qraw[0].T, xs[3, pl.ds(pn.hb * px, pn.own)]).T.astype(BF16)
    dwbuf[TAPS - 1] = jnp.zeros((pn.cs, pn.width), BF16)
    start_group(GROUPS - 1)
    pooled = dot_nt(q4[...], wbuf[POOL]) * inv_counts[...]
    pooled_high = pooled.astype(BF16)
    pooled_low = (pooled - pooled_high.astype(F32)).astype(BF16)

    def finish(rb, carry):
        at = pl.ds(pl.multiple_of(rb * many * px, 16), many * px)
        to = pl.ds(pl.multiple_of((rb * many + pn.hb) * px, 16), many * px)
        hot = hot_px[at]
        y = dot_nt(qraw[0, at], wbuf[POINT]) + dot(hot, pooled_high) + dot(hot, pooled_low)
        dxe[to] = dxe[to] + y
        return carry

    lax.fori_loop(0, MEMBERS // many, finish, 0)
    if pn.exchange:
        lax.fori_loop(0, 6, serve, 0)

        @pl.when(slab == home_slab)
        def _():
            for z in range(n):
                pltpu.make_async_copy(dp2.at[z], dp2.at[z], p2_r.at[z]).wait()
            total = dp2[0].astype(F32)
            for z in range(1, n):
                total = total + dp2[z].astype(F32)
            dpf[...] = total
            for c in range(pn.C):
                @pl.when((x == lax.rem(me, pn.G)) & (col == c))
                def _():
                    pltpu.make_async_copy(dpf, dproj_out, p3_r.at[0]).start()

                @pl.when(jnp.logical_not((x == lax.rem(me, pn.G)) & (col == c)))
                def _(c=c):
                    dproj_give(c).start()

    @pl.when(slab > 0)
    def _():
        remote(hsend.at[0], hrecv.at[1], h_s.at[0], h_r.at[1], member(slab - 1, me)).wait_send()
        remote(hsend.at[1], hrecv.at[0], h_s.at[1], h_r.at[0], member(slab - 1, me)).wait_recv()

    @pl.when(slab < n - 1)
    def _():
        remote(hsend.at[1], hrecv.at[0], h_s.at[1], h_r.at[0], member(slab + 1, me)).wait_send()
        remote(hsend.at[0], hrecv.at[1], h_s.at[0], h_r.at[1], member(slab + 1, me)).wait_recv()

    @pl.when(slab == 0)
    def _():
        hrecv[0] = jnp.zeros((pn.hb * px, pn.cs), BF16)

    @pl.when(slab == n - 1)
    def _():
        hrecv[1] = jnp.zeros((pn.hb * px, pn.cs), BF16)

    for rb in range(pn.hb):
        low, high = (pn.hb + rb) * px, (MEMBERS + rb) * px
        dxe[pl.ds(low, px)] = dxe[pl.ds(low, px)] + hrecv[0, pl.ds(rb * px, px)].astype(F32)
        dxe[pl.ds(high, px)] = dxe[pl.ds(high, px)] + hrecv[1, pl.ds(rb * px, px)].astype(F32)

    def packing(rp, carry):
        pair = dxe[pl.ds(pl.multiple_of(pn.hb * px + rp * 2 * S, 16), 2 * S)].astype(BF16)
        pack[pl.ds(2 * rp, 2)] = dot(sel_t[...], pair).astype(BF16).reshape(2, pn.C * bp, pn.cs)
        return carry

    lax.fori_loop(0, H // 2, packing, 0, unroll=6)
    back = []
    for kk in range(1, MEMBERS):
        other = lax.rem(me + kk, MEMBERS)
        xo, co = other // pn.C, lax.rem(other, pn.C)
        c = remote(pack.at[pl.ds(xo * h, h), pl.ds(pl.multiple_of(co * bp, bp), bp)], dx_out.at[slice_of(pn, me)], x_s.at[kk], x_r.at[kk],
                   member(slab, other))
        c.start()
        back.append(c)
    c = pltpu.make_async_copy(pack.at[pl.ds(x * h, h), pl.ds(pl.multiple_of(col * bp, bp), bp)], dx_out.at[slice_of(pn, me)], x_r.at[0])
    c.start()
    back.append(c)

    if pn.exchange:
        lax.fori_loop(6, GROUPS, serve, 0)

        @pl.when(shared_on)
        def _():
            for k in (GROUPS - 2, GROUPS - 1):
                landed(group_index(k))
                share_on(group_index(k)).start()

        def settle(g, carry):
            each_link(g, lambda c: c.wait_send())
            for role, up in ((relay_up, True), (relay_down, False)):
                @pl.when(role)
                def _(up=up):
                    relay(g, up).wait_send()

            @pl.when(closing)
            def _():
                share_y(g).wait_send()
                share_core(g).wait_send()

            @pl.when(shared_on)
            def _():
                share_on(g).wait_send()

            @pl.when(jnp.logical_not(shared_on))
            def _():
                landed(g)

            return carry

        lax.fori_loop(0, GROUPS, settle, 0)

        @pl.when(slab != home_slab)
        def _():
            dproj_home().wait_send()

        @pl.when(slab == home_slab)
        def _():
            for c in range(pn.C):
                @pl.when(jnp.logical_not((x == lax.rem(me, pn.G)) & (col == c)))
                def _(c=c):
                    dproj_give(c).wait_send()

        pltpu.make_async_copy(dproj_out, dproj_out, p3_r.at[0]).wait()
    else:
        c = pltpu.make_async_copy(dwbuf, dw_out, g_r.at[0])
        c.start()
        c.wait()
        dproj_out[...] = jnp.zeros(dproj_out.shape, F32)
    for c in back:
        c.wait()


def conv_backward(pn, q, xs, w, dproj, q4, means, hot_px, inv_counts, masks, lane_masks, shifts, sel_t):
    dma = pltpu.SemaphoreType.DMA
    vmem = pl.BlockSpec(memory_space=pltpu.VMEM)
    hbm = pl.BlockSpec(memory_space=pl.ANY)
    shape = jax.ShapeDtypeStruct
    n = pn.slabs if pn.exchange else 1
    sums = TAPS if pn.exchange else 1
    block_rows = 5 * pn.width // MEMBERS
    return pl.pallas_call(
        functools.partial(back_kernel, pn),
        out_shape=(
            shape((TAPS, pn.cs, pn.width), BF16),
            shape((MEMBERS, pn.h, pn.bp, pn.cs), BF16),
            shape((block_rows, pn.width), F32),
        ),
        in_specs=[hbm] * 4 + [vmem] * 4 + [pl.BlockSpec(memory_space=pltpu.SMEM)] + [vmem] * 3,
        out_specs=(hbm, hbm, vmem),
        scratch_shapes=[
            pltpu.VMEM((7, pn.ext, pn.cs), BF16),
            pltpu.VMEM((TAPS, pn.cs, pn.width), BF16),
            pltpu.VMEM((4, pn.own, pn.width), BF16),
            pltpu.VMEM((3, 2, pn.own, pn.width), BF16),
            pltpu.VMEM((pn.width, pn.own), BF16),
            pltpu.VMEM((pn.ext, pn.cs), F32),
            pltpu.VMEM((TAPS, pn.cs, pn.width), BF16),
            pltpu.VMEM((2, sums, pn.cs, pn.width), BF16),
            pltpu.VMEM((2, pn.hb * pn.px, pn.cs), BF16),
            pltpu.VMEM((2, pn.hb * pn.px, pn.cs), BF16),
            pltpu.VMEM((pn.H, pn.C * pn.bp, pn.cs), BF16),
            pltpu.VMEM((MEMBERS, block_rows, pn.width), BF16),
            pltpu.VMEM((block_rows, pn.width), BF16),
            pltpu.VMEM((n, block_rows, pn.width), BF16),
            pltpu.VMEM((block_rows, pn.width), F32),
            dma((6,)), dma((4, 3)), dma((4, 3)), dma((4,)), dma((4,)), dma((4, 3)), dma((4, 3)),
            dma((2, GROUPS)), dma((2, 2, GROUPS)), dma((GROUPS,)), dma((GROUPS,)), dma((2, GROUPS)), dma((GROUPS,)),
            dma((2,)), dma((2,)), dma((MEMBERS,)), dma((MEMBERS,)),
            dma((MEMBERS,)), dma((MEMBERS,)), dma((1,)), dma((n,)), dma((pn.C,)), dma((1,)),
        ],
        compiler_params=pltpu.CompilerParams(collective_id=2, has_side_effects=True, vmem_limit_bytes=61900 * 1024),
        name="conv_backward",
    )(q, xs, w, dproj, q4, means, hot_px, inv_counts, masks, lane_masks, shifts, sel_t)


def column_tables(pn):
    S, bp, bc = pn.S, pn.bp, pn.bc
    sel = np.zeros((7, 2, S, 2, pn.C * bp), np.float32)
    shifts = np.zeros((3, 2, 2, S, 2, S), np.float32)
    for r in range(2):
        for c in range(pn.cols):
            for v in range(-3, 4):
                s = c + v * DILATIONS[0]
                if 0 <= s < pn.cols:
                    sel[v + 3, r, c, r, (s // bc) * bp + s % bc] = 1.0
            for b, d in enumerate(DILATIONS):
                for n, j in enumerate((-1, 1)):
                    s = c - j * d
                    if 0 <= s < pn.cols:
                        shifts[b, n, r, c, r, s] = 1.0
    sel = sel.reshape(7 * 2 * S, 2 * pn.C * bp)
    sel_t = sel[3 * 2 * S:4 * 2 * S].T
    return (jnp.asarray(sel, BF16), jnp.asarray(sel_t, BF16), jnp.asarray(shifts.reshape(12 * S, 2 * S), BF16))


def per_device(
    features, crop_rows, crop_cols, w_point, w_atrous, w_pool, w_proj, gains, biases, cotangent
):
    h, bc, channels = features.shape
    pn = Plan(lax.axis_size("row"), lax.axis_size("col"), h, bc, channels, gains.shape[1], crop_rows.shape[0])
    row, col = lax.axis_index("row"), lax.axis_index("col")
    slab, x = row // pn.G, row % pn.G
    crop_ids = jnp.arange(pn.crops, dtype=jnp.int32)
    ends = jnp.cumsum(crop_rows)
    counts = (crop_rows * crop_cols).astype(F32)
    pixels = jnp.sum(counts)

    def crop_of(rows):
        found = jnp.sum((rows[:, None] >= ends[None, :]).astype(jnp.int32), axis=1)
        return jnp.where(rows < 0, -1, found)

    def widths_of(crop):
        return jnp.sum(jnp.where(crop[:, None] == crop_ids[None, :], crop_cols[None, :], 0), axis=1)

    own_crop = crop_of(row * h + jnp.arange(h, dtype=jnp.int32))
    own_columns = col * bc + jnp.arange(bc, dtype=jnp.int32)
    own_valid = own_columns[None, :] < widths_of(own_crop)[:, None]
    masked = jnp.where(own_valid[:, :, None], features, 0)
    feats = masked.reshape(h, bc, MEMBERS, pn.cs).transpose(2, 0, 1, 3)
    feats = jnp.pad(feats, ((0, 0), (0, 0), (0, pn.bp - bc), (0, 0)))
    cot = jnp.pad(cotangent, ((0, 0), (0, pn.bp - bc), (0, 0)))

    slab_rows = slab * pn.H - MARGIN + jnp.arange(pn.H + 2 * MARGIN, dtype=jnp.int32)
    crops = crop_of(slab_rows)
    mid = crops[MARGIN:MARGIN + pn.H]
    same = jnp.stack(
        [crops[MARGIN + i * d:MARGIN + i * d + pn.H] == mid for d in DILATIONS for i in (-1, 1)]
    ).astype(F32)
    lane_masks = jnp.pad(jnp.repeat(same, pn.S, axis=1), ((0, 2), (0, 0))).astype(BF16)
    ncp_ids = jnp.arange(pn.ncp, dtype=jnp.int32)
    hot_rows = (mid[:, None] == ncp_ids[None, :]).astype(BF16)
    hot_px = jnp.repeat(hot_rows, pn.S, axis=0)
    hot_t = jnp.repeat(hot_rows.T, pn.S, axis=1)
    inv_counts = jnp.pad(1.0 / counts, (0, pn.ncp - pn.crops))[:, None]

    k = x * pn.C + col
    block_crop = lax.dynamic_slice_in_dim(mid, k * pn.rpb, pn.rpb)
    columns = jnp.arange(pn.S, dtype=jnp.int32)
    valid = (columns[None, :] < widths_of(block_crop)[:, None]).astype(F32).reshape(pn.px, 1)
    block_hot = jnp.repeat((block_crop[:, None] == ncp_ids[None, :]).astype(BF16), pn.S, axis=0)
    block_hot_t = jnp.repeat((ncp_ids[:, None] == block_crop[None, :]).astype(BF16), pn.S, axis=1)

    sel, sel_t, shifts = column_tables(pn)
    none = jnp.zeros((1, *w_point.shape), BF16)
    w = jnp.concatenate([w_atrous.transpose(1, 0, 2), w_point[None], w_pool[None], none], axis=0)
    proj = w_proj.reshape(pn.C, pn.proj // pn.C, pn.width)
    proj = jnp.pad(proj, ((0, 0), (0, pn.piece - pn.proj // pn.C), (0, 0)))
    if not pn.exchange:
        w = lax.all_gather(w, "row", axis=1, tiled=True)
        w = lax.dynamic_slice_in_dim(w, slice_of(pn, x * pn.C + col) * pn.cs, pn.cs, axis=1)
    flat = same.reshape(-1)
    p, xs, w_own, means, p4, own_cot, pieces = conv_forward(pn, feats, w, cot, proj, flat, sel, hot_t, inv_counts)
    full_proj = pieces[:, :, :pn.proj // pn.C].transpose(1, 0, 2, 3).reshape(5 * pn.width, pn.width)
    q, q4, d_proj, res, d_gains, d_biases = norms(
        pn, p, p4, gains, biases, valid, (1.0 / pixels)[None], full_proj, own_cot, block_hot, block_hot_t, sel_t
    )
    dw, dx, dproj_sum = conv_backward(
        pn, q, xs, w_own, d_proj, q4, means, hot_px, inv_counts, flat, lane_masks, shifts, sel_t
    )
    if pn.exchange:
        d_proj = dproj_sum
    else:
        whole = jnp.zeros((TAPS, channels, pn.width), BF16)
        whole = lax.dynamic_update_slice(whole, dw, (0, slice_of(pn, x * pn.C + col) * pn.cs, 0))
        whole = lax.psum(whole, "col")
        dw = lax.psum_scatter(whole, "row", scatter_dimension=1, tiled=True)
        d_proj = lax.psum(d_proj, "col")
        d_proj = lax.psum_scatter(d_proj.astype(F32), "row", scatter_dimension=0, tiled=True)
    result = res[:, :bc]
    dx = dx[:, :, :bc].transpose(1, 2, 0, 3).reshape(h, bc, channels)
    d_features = jnp.where(own_valid[:, :, None], dx, 0)
    d_point = dw[POINT].astype(F32)
    d_atrous = dw[:POINT].astype(F32).transpose(1, 0, 2)
    d_pool = dw[POOL].astype(F32)
    return (result, d_features, d_point, d_atrous, d_pool, d_proj, d_gains, d_biases)


def solution(mesh):
    return jax.shard_map(
        per_device,
        mesh=mesh,
        in_specs=(
            P("row", "col", None),
            P(),
            P(),
            P("row", None),
            P("row", None, None),
            P("row", None),
            P("row", None),
            P(),
            P(),
            P("row", "col", None),
        ),
        out_specs=(
            P("row", "col", None),
            P("row", "col", None),
            P("row", None),
            P("row", None, None),
            P("row", None),
            P("row", None),
            P(),
            P(),
        ),
        check_vma=False,
    )
```

```python
import functools

import jax
import jax.numpy as jnp
import numpy as np
from jax import lax
from jax.experimental import pallas as pl
from jax.experimental.pallas import tpu as pltpu
from jax.sharding import PartitionSpec as P

EPSILON = 1e-05
MARGIN = 18
DILATIONS = (6, 12, 18)
MEMBERS = 8
TAPS = 30
POINT, POOL, GROUPS = 27, 28, 10
MESH = pl.DeviceIdType.MESH
F32 = jnp.float32
BF16 = jnp.bfloat16

def up_to(value, multiple):
    return -(-value // multiple) * multiple


class Plan:
    def __init__(self, rows_axis, cols_axis, h, bc, channels, width, crops):
        self.R, self.C = rows_axis, cols_axis
        self.h, self.bc, self.channels, self.width = h, bc, channels, width
        self.G = MEMBERS // self.C
        self.slabs = self.R // self.G
        self.H = self.G * h
        self.cols = bc * self.C
        self.S = up_to(self.cols, 8)
        self.rpb = self.H // MEMBERS
        self.px = self.rpb * self.S
        self.own = MEMBERS * self.px
        self.hb = MARGIN // self.rpb
        self.nb = MEMBERS + 2 * self.hb
        self.ext = self.nb * self.px
        self.bp = up_to(bc, 16)
        self.cs = channels // MEMBERS
        self.crops = crops
        self.ncp = up_to(crops, 16)
        self.exchange = self.slabs == self.C and self.R == MEMBERS
        self.steps = tuple(d // self.rpb for d in DILATIONS)
        self.proj = 5 * width // self.R
        self.piece = up_to(self.proj // self.C, 16)


def home_of(pn, col):
    if pn.C != 4:
        return col
    y, c = col // 2, lax.rem(col, 2)
    return (1 - y) * 3 * c + y * (1 + c)


def slice_of(pn, k):
    return pn.G * home_of(pn, lax.rem(k, pn.C)) + k // pn.C


def remote(src, dst, send, recv, device):
    return pltpu.make_async_remote_copy(
        src_ref=src, dst_ref=dst, send_sem=send, recv_sem=recv, device_id=device, device_id_type=MESH
    )


def greet_all(pn, row, col):
    total = pn.R * pn.C
    barrier = pltpu.get_barrier_semaphore()
    me = row * pn.C + col

    def hello(k, carry):
        other = lax.rem(me + k, total)
        pl.semaphore_signal(
            barrier, inc=1, device_id=(other // pn.C, lax.rem(other, pn.C)), device_id_type=MESH
        )
        return carry

    lax.fori_loop(1, total, hello, 0)
    pl.semaphore_wait(barrier, total - 1)


def dot(a, b):
    return jnp.dot(a, b, preferred_element_type=F32)


def dot_nt(a, b):
    return lax.dot_general(a, b, (((1,), (1,)), ((), ())), preferred_element_type=F32)


def dot_tn(a, b):
    return lax.dot_general(a, b, (((0,), (0,)), ((), ())), preferred_element_type=F32)


def split_dot(dot_fn, a, b):
    high = a.astype(BF16)
    low = (a - high.astype(F32)).astype(BF16)
    return dot_fn(high, b) + dot_fn(low, b)


def conv_kernel(pn, feats, w_in, cot, proj, masks, sel, hot_t, inv_counts,
                p_out, x_out, w_out, m_out, p4_out, cot_out, proj_out,
                ring, xs, wbuf, acc, pbuf, cbuf, sbuf, rbuf, cx,
                f_s, f_r, h_s, h_r, c_s, c_r, j_s, j_r, t_s, t_r, w_s, w_r, w_l, e_s,
                r1_s, r1_r, r2_s, r2_r, o_s):
    row, col = lax.axis_index("row"), lax.axis_index("col")
    slab, x = row // pn.G, lax.rem(row, pn.G)
    me = x * pn.C + col
    core, quad = lax.rem(col, 2), me // 2
    h, H, bp, px, n = pn.h, pn.H, pn.bp, pn.px, pn.slabs
    many = 4

    def member(s, k):
        return (s * pn.G + k // pn.C, lax.rem(k, pn.C))

    greet_all(pn, row, col)

    own_cols = pl.ds(pl.multiple_of(col * bp, bp), bp)
    own_rows = pl.ds(MARGIN + h * x, h)
    sent = []
    for kk in range(1, MEMBERS):
        other = lax.rem(me + kk, MEMBERS)
        c = remote(feats.at[slice_of(pn, other)], ring.at[own_rows, own_cols], f_s.at[kk], f_r.at[kk], member(slab, other))
        c.start()
        sent.append(c)
    keep = pltpu.make_async_copy(feats.at[slice_of(pn, me)], ring.at[own_rows, own_cols], f_r.at[0])
    keep.start()

    home = home_of(pn, col)
    source, rising, falling = slab == home, (slab > home) & (slab < n - 1), (slab < home) & (slab > 0)
    help_up, help_down = (slab == n - 2) & (col == 1), (slab == 1) & (col == 0)
    half_rows = pn.cs // 2

    def order(k):
        return k - k // 7 + 3 * (k // 6 - k // 7)

    def taps(g):
        return pl.ds(3 * g, 3)

    def part_of(ref, g, half):
        return ref.at[taps(g), pl.ds(half * half_rows, half_rows)]

    def ship(g, half, up, src):
        to = slab + 1 if up else slab - 1
        return remote(part_of(src, g, half), part_of(wbuf, g, half), w_s.at[int(up), half, g], w_r.at[half, g],
                      (to * pn.G + x, col))

    def assist(g, up):
        to = slab + 1 if up else slab - 1
        return remote(part_of(w_in, g, 1), part_of(wbuf, g, 1), e_s.at[g], w_r.at[1, g], (to * pn.G + x, col + 2))

    def own_copy(g):
        return pltpu.make_async_copy(w_in.at[taps(g)], wbuf.at[taps(g)], w_l.at[g])

    def arrived(g):
        for half in (0, 1):
            at = part_of(wbuf, g, half)
            pltpu.make_async_copy(at, at, w_r.at[half, g]).wait()

    def pass_on(g):
        for role, up in ((rising, True), (falling, False)):
            @pl.when(role)
            def _(up=up):
                arrived(g)
                for half in (0, 1):
                    ship(g, half, up, wbuf).start()

    def w_wait(g):
        if pn.exchange:
            @pl.when(source)
            def _():
                own_copy(g).wait()

            @pl.when(jnp.logical_not(source | rising | falling))
            def _():
                arrived(g)
        else:
            own_copy(g).wait()

    def each_shipment(g, act):
        for half in (0, 1):
            @pl.when(source & ((slab < n - 2) if half else (slab < n - 1)))
            def _(half=half):
                act(ship(g, half, True, w_in))

            @pl.when(source & ((slab > 1) if half else (slab > 0)))
            def _(half=half):
                act(ship(g, half, False, w_in))

        @pl.when(help_up)
        def _():
            act(assist(g, True))

        @pl.when(help_down)
        def _():
            act(assist(g, False))

    if pn.exchange:
        def begin(g, carry):
            each_shipment(g, lambda c: c.start())

            @pl.when(source)
            def _():
                own_copy(g).start()

            return carry
    else:
        def begin(g, carry):
            own_copy(g).start()
            return carry

    early = 6
    lax.fori_loop(0, early, lambda k, carry: begin(order(k), carry), 0)

    cot_sent = []
    for cc in range(1, pn.C):
        cd = lax.rem(col + cc, pn.C)
        c = remote(cot.at[pl.ds(cd * pn.rpb, pn.rpb)], cx.at[:, own_cols], c_s.at[cc], c_r.at[cc], (row, cd))
        c.start()
        cot_sent.append(c)
    cot_keep = pltpu.make_async_copy(cot.at[pl.ds(col * pn.rpb, pn.rpb)], cx.at[:, own_cols], c_r.at[0])
    cot_keep.start()

    def proj_row(k):
        return remote(proj.at[col], proj_out.at[col, row], j_s.at[k], j_r.at[k], (lax.rem(row + k, pn.R), col))

    def proj_col(k):
        return remote(proj_out.at[col], proj_out.at[col], t_s.at[k], t_r.at[k], (row, lax.rem(col + k, pn.C)))

    def proj_begin(k, carry):
        proj_row(k).start()
        return carry

    def proj_wait(k, carry):
        proj_row(k).wait()
        return carry

    lax.fori_loop(1, pn.R, proj_begin, 0)
    proj_keep = pltpu.make_async_copy(proj.at[col], proj_out.at[col, row], j_r.at[0])
    proj_keep.start()

    @pl.when(slab == 0)
    def _():
        ring[pl.ds(0, MARGIN)] = jnp.zeros((MARGIN, pn.C * bp, pn.cs), BF16)

    @pl.when(slab == n - 1)
    def _():
        ring[pl.ds(MARGIN + H, MARGIN)] = jnp.zeros((MARGIN, pn.C * bp, pn.cs), BF16)

    def pass_many(first, end):
        def one(k, carry):
            pass_on(order(k))
            return carry

        if pn.exchange:
            lax.fori_loop(first, end, one, 0)

    pass_many(0, 3)
    for c in sent:
        c.wait()
    keep.wait()

    def margin_down():
        return remote(ring.at[pl.ds(MARGIN, MARGIN)], ring.at[pl.ds(MARGIN + H, MARGIN)], h_s.at[0], h_r.at[0],
                      member(slab - 1, me))

    def margin_up():
        return remote(ring.at[pl.ds(H, MARGIN)], ring.at[pl.ds(0, MARGIN)], h_s.at[1], h_r.at[1], member(slab + 1, me))

    @pl.when(slab > 0)
    def _():
        margin_down().start()

    @pl.when(slab < n - 1)
    def _():
        margin_up().start()

    lax.fori_loop(early, GROUPS, lambda k, carry: begin(order(k), carry), 0)

    def assemble(rp, carry):
        pair = ring[pl.ds(2 * rp, 2)].reshape(2 * pn.C * bp, pn.cs)
        moved = dot(sel[...], pair).astype(BF16)
        at = pl.multiple_of(rp * 2 * pn.S, 16)
        for v in range(7):
            xs[v, pl.ds(at, 2 * pn.S)] = moved[v * 2 * pn.S:(v + 1) * 2 * pn.S]
        return carry

    lax.fori_loop(MARGIN // 2, (MARGIN + H) // 2, assemble, 0, unroll=6)
    pass_many(3, 5)
    for c in cot_sent:
        c.wait()
    cot_keep.wait()
    for rp in range(pn.rpb // 2):
        pair = cx[2 * rp:2 * rp + 2].reshape(2 * pn.C * bp, pn.width)
        cot_out[pl.ds(rp * 2 * pn.S, 2 * pn.S)] = dot(sel[pl.ds(3 * 2 * pn.S, 2 * pn.S)], pair).astype(BF16)
    lax.fori_loop(1, pn.R, proj_wait, 0)
    proj_keep.wait()
    for k in range(1, pn.C):
        proj_col(k).start()
    pass_many(5, 6)

    @pl.when(slab > 0)
    def _():
        margin_down().wait_send()
        margin_up().wait_recv()

    @pl.when(slab < n - 1)
    def _():
        margin_up().wait_send()
        margin_down().wait_recv()

    lax.fori_loop(0, MARGIN // 2, assemble, 0, unroll=3)
    lax.fori_loop((MARGIN + H) // 2, pn.nb * pn.rpb // 2, assemble, 0, unroll=3)
    x_save = pltpu.make_async_copy(xs, x_out, o_s.at[0])
    x_save.start()

    def first_stage(slot):
        return remote(pbuf.at[slot, :, 1 - core], cbuf.at[slot], r1_s.at[slot], r1_r.at[slot], (row, col + 1 - 2 * core))

    def second_stage(slot, i):
        q = lax.rem(quad + i, MEMBERS // 2)
        return remote(sbuf.at[slot, i - 1], rbuf.at[slot, i - 1], r2_s.at[slot, i - 1], r2_r.at[slot, i - 1],
                      member(slab, 2 * q + core))

    def middle(slot):
        first_stage(slot).wait()
        for i in (1, 2, 3, 0):
            q = lax.rem(quad + i, MEMBERS // 2)
            s = pbuf[slot, q, core].astype(F32) + cbuf[slot, q].astype(F32)
            if i == 0:
                p_out[slot] = s
            else:
                sbuf[slot, i - 1] = s.astype(BF16)
                second_stage(slot, i).start()

    def last(slot):
        total = p_out[slot]
        for i in range(1, MEMBERS // 2):
            second_stage(slot, i).wait()
            total = total + rbuf[slot, i - 1].astype(F32)
        p_out[slot] = total

    def scatter(slot, rb, y):
        for r in range(many):
            pbuf[slot, (many * rb + r) // 2, r % 2] = y[r * px:(r + 1) * px].astype(BF16)

    def far(k):
        if k in (2, 4, 6, 8):
            pass_many(5 + k // 2, 6 + k // 2)
        w_wait(order(k))

    def point(rb, carry):
        at = pl.ds(pl.multiple_of((rb * many + pn.hb) * px, 16), many * px)
        scatter(0, rb, dot(xs[3, at], wbuf[POINT]))
        return carry

    for branch in (1, 2, 3):
        step = pn.steps[branch - 1]
        if branch == 3:
            far(6)
            lax.fori_loop(0, MEMBERS // many, point, 0)
            first_stage(0).start()
            middle(2)
        for i in (-1, 0, 1):
            g = 3 * (branch - 1) + i + 1
            mask_at = (2 * (branch - 1) + (i + 1) // 2) * H
            far(g + branch // 3)

            def block(rb, carry, step=step, i=i, g=g, mask_at=mask_at, branch=branch):
                at = pl.multiple_of(rb * many * px, 16)
                window = pl.ds(pl.multiple_of((rb * many + pn.hb + i * step) * px, 16), many * px)
                y = dot(xs[3 - branch, window], wbuf[3 * g])
                y = y + dot(xs[3, window], wbuf[3 * g + 1])
                y = y + dot(xs[3 + branch, window], wbuf[3 * g + 2])
                if i != 0:
                    y = jnp.concatenate(
                        [y[r * pn.S:(r + 1) * pn.S] * masks[mask_at + rb * many * pn.rpb + r]
                         for r in range(many * pn.rpb)], axis=0
                    )
                if i > -1:
                    y = y + acc[pl.ds(at, many * px)]
                if i < 1:
                    acc[pl.ds(at, many * px)] = y
                else:
                    scatter(branch, rb, y)
                return carry

            lax.fori_loop(0, MEMBERS // many, block, 0)
            if i == 0 and branch > 1:
                middle(branch - 1 if branch == 2 else 0)
        first_stage(branch).start()

    sums = dot(hot_t[...], xs[3, pl.ds(pn.hb * px, pn.own)])
    means = sums * inv_counts[...]
    m_out[...] = means
    p4_out[...] = split_dot(dot, means, wbuf[POOL])
    w_save = pltpu.make_async_copy(wbuf, w_out, o_s.at[1])
    w_save.start()
    middle(3)
    for slot in (1, 2, 0):
        last(slot)
    for k in range(1, pn.C):
        proj_col(k).wait()
    if pn.exchange:
        def settled(g, carry):
            each_shipment(g, lambda c: c.wait_send())
            for role, up in ((rising, True), (falling, False)):
                @pl.when(role)
                def _(up=up):
                    for half in (0, 1):
                        ship(g, half, up, wbuf).wait_send()
            return carry

        lax.fori_loop(0, GROUPS, settled, 0)
    last(3)
    x_save.wait()
    w_save.wait()


def conv_forward(pn, feats, w, cot, proj, masks, sel, hot_t, inv_counts):
    half = MEMBERS // 2
    dma = pltpu.SemaphoreType.DMA
    vmem = pl.BlockSpec(memory_space=pltpu.VMEM)
    hbm = pl.BlockSpec(memory_space=pl.ANY)
    shape = jax.ShapeDtypeStruct
    return pl.pallas_call(
        functools.partial(conv_kernel, pn),
        out_shape=(
            shape((4, pn.px, pn.width), F32),
            shape((7, pn.ext, pn.cs), BF16),
            shape((TAPS, pn.cs, pn.width), BF16),
            shape((pn.ncp, pn.cs), F32),
            shape((pn.ncp, pn.width), F32),
            shape((pn.px, pn.width), BF16),
            shape((pn.C, pn.R, pn.piece, pn.width), BF16),
        ),
        in_specs=[hbm, hbm, hbm, hbm, pl.BlockSpec(memory_space=pltpu.SMEM), vmem, vmem, vmem],
        out_specs=(vmem, hbm, hbm, vmem, vmem, vmem, vmem),
        scratch_shapes=[
            pltpu.VMEM((pn.nb * pn.rpb, pn.C * pn.bp, pn.cs), BF16),
            pltpu.VMEM((7, pn.ext, pn.cs), BF16),
            pltpu.VMEM((TAPS, pn.cs, pn.width), BF16),
            pltpu.VMEM((pn.own, pn.width), F32),
            pltpu.VMEM((4, half, 2, pn.px, pn.width), BF16),
            pltpu.VMEM((4, half, pn.px, pn.width), BF16),
            pltpu.VMEM((4, half - 1, pn.px, pn.width), BF16),
            pltpu.VMEM((4, half - 1, pn.px, pn.width), BF16),
            pltpu.VMEM((pn.rpb, pn.C * pn.bp, pn.width), BF16),
            dma((MEMBERS,)), dma((MEMBERS,)), dma((2,)), dma((2,)), dma((pn.C,)), dma((pn.C,)),
            dma((pn.R,)), dma((pn.R,)), dma((pn.C,)), dma((pn.C,)),
            dma((2, 2, GROUPS)), dma((2, GROUPS)), dma((GROUPS,)), dma((GROUPS,)),
            dma((4,)), dma((4,)), dma((4, 3)), dma((4, 3)), dma((2,)),
        ],
        compiler_params=pltpu.CompilerParams(collective_id=0, has_side_effects=True, vmem_limit_bytes=60 * 2**20),
        name="conv_forward",
    )(feats, w, cot, proj, masks, sel, hot_t, inv_counts)


def norm_kernel(pn, p, p4_in, gains, biases, valid, pixels, w_proj, cot, hot, hot_t, sel_t,
                q_out, q4_out, dproj_out, res_out, dg_out, db_out,
                norm, slope, hbuf, gact, dh4, rx,
                a1, b1, a2, b2, a3, b3, a4, b4, as_s, as_r, bs_s, bs_r, e_s, e_r):
    row, col = lax.axis_index("row"), lax.axis_index("col")
    slab, x = row // pn.G, lax.rem(row, pn.G)
    me = x * pn.C + col
    crops = float(pn.crops)
    v = valid[...]
    inv_px = pixels[0]
    width, bp = pn.width, pn.bp

    def member(s, k):
        return (s * pn.G + k // pn.C, lax.rem(k, pn.C))

    barrier = pltpu.get_barrier_semaphore()
    for kk in range(1, MEMBERS):
        pl.semaphore_signal(barrier, inc=1, device_id=member(slab, lax.rem(me + kk, MEMBERS)), device_id_type=MESH)

    def hello(k, carry):
        pl.semaphore_signal(barrier, inc=1, device_id=member(lax.rem(slab + k, pn.slabs), me), device_id_type=MESH)
        return carry

    lax.fori_loop(1, pn.slabs, hello, 0)

    def peer_a(n, abuf, kk):
        return remote(abuf.at[me], abuf.at[me], as_s.at[n, kk], as_r.at[n, kk], member(slab, lax.rem(me + kk, MEMBERS)))

    def peer_b(n, bbuf, k):
        return remote(bbuf.at[slab], bbuf.at[slab], bs_s.at[n, k], bs_r.at[n, k], member(lax.rem(slab + k, pn.slabs), me))

    def reduce_start(n, abuf):
        for kk in range(1, MEMBERS):
            peer_a(n, abuf, kk).start()

    def reduce_end(n, abuf, bbuf):
        for kk in range(1, MEMBERS):
            peer_a(n, abuf, kk).wait()
        total = abuf[0]
        for k in range(1, MEMBERS):
            total = total + abuf[k]
        bbuf[slab] = total
        for k in range(1, pn.slabs):
            peer_b(n, bbuf, k).start()
        for k in range(1, pn.slabs):
            peer_b(n, bbuf, k).wait()
        total = bbuf[0]
        for k in range(1, pn.slabs):
            total = total + bbuf[k]
        return total

    def column_sum(value):
        return jnp.sum(value, axis=0, keepdims=True)

    for b in range(4):
        pv = p[b] * v
        a1[me, pl.ds(b, 1)] = column_sum(pv)
        a1[me, pl.ds(4 + b, 1)] = column_sum(pv * p[b])
    a1[me, pl.ds(8, pn.ncp)] = p4_in[...]
    pl.semaphore_wait(barrier, MEMBERS - 1 + pn.slabs - 1)
    reduce_start(0, a1)
    total = reduce_end(0, a1, b1)
    inv = []
    for b in range(4):
        centre = total[b:b + 1] * inv_px
        scale = lax.rsqrt(total[4 + b:5 + b] * inv_px - centre * centre + EPSILON)
        inv.append(scale)
        n = (p[b] - centre) * scale
        u = gains[b:b + 1] * n + biases[b:b + 1]
        s = jax.nn.sigmoid(u)
        norm[b] = n
        slope[b] = s * (1.0 + u * (1.0 - s))
        hbuf[b] = (u * s).astype(BF16)
    p4 = total[8:8 + pn.ncp]
    centre4 = column_sum(p4) * (1.0 / crops)
    inv4 = lax.rsqrt(column_sum(p4 * p4) * (1.0 / crops) - centre4 * centre4 + EPSILON)
    n4 = (p4 - centre4) * inv4
    u4 = gains[4:5] * n4 + biases[4:5]
    s4 = jax.nn.sigmoid(u4)
    slope4 = s4 * (1.0 + u4 * (1.0 - s4))
    hbuf[4] = dot(hot[...], (u4 * s4).astype(BF16)).astype(BF16)

    p5 = dot(hbuf[0], w_proj[pl.ds(0, width)])
    for b in range(1, 5):
        p5 = p5 + dot(hbuf[b], w_proj[pl.ds(b * width, width)])
    pv = p5 * v
    a2[me, pl.ds(0, 1)] = column_sum(pv)
    a2[me, pl.ds(1, 1)] = column_sum(pv * p5)
    a2[me, pl.ds(2, 6)] = jnp.zeros((6, width), F32)
    reduce_start(1, a2)
    total = reduce_end(1, a2, b2)
    centre5 = total[0:1] * inv_px
    inv5 = lax.rsqrt(total[1:2] * inv_px - centre5 * centre5 + EPSILON)
    n5 = (p5 - centre5) * inv5
    u5 = gains[5:6] * n5 + biases[5:6]
    s5 = jax.nn.sigmoid(u5)
    g5 = cot[...].astype(F32) * v * (s5 * (1.0 + u5 * (1.0 - s5)))
    norm[4] = n5
    gact[4] = g5
    a3[me, pl.ds(0, 1)] = column_sum(g5)
    a3[me, pl.ds(1, 1)] = column_sum(g5 * n5)
    a3[me, pl.ds(2, 6)] = jnp.zeros((6, width), F32)
    reduce_start(2, a3)
    hbuf[5] = (v * u5 * s5).astype(BF16)
    for rp in range(pn.rpb // 2):
        pair = hbuf[5, pl.ds(rp * 2 * pn.S, 2 * pn.S)]
        rx[2 * rp:2 * rp + 2] = dot(sel_t[...], pair).astype(BF16).reshape(2, pn.C * bp, width)
    back = []
    for cc in range(1, pn.C):
        cd = lax.rem(col + cc, pn.C)
        c = remote(rx.at[:, pl.ds(pl.multiple_of(cd * bp, bp), bp)], res_out.at[pl.ds(col * pn.rpb, pn.rpb)],
                   e_s.at[cc], e_r.at[cc], (row, cd))
        c.start()
        back.append(c)
    c = pltpu.make_async_copy(rx.at[:, pl.ds(pl.multiple_of(col * bp, bp), bp)], res_out.at[pl.ds(col * pn.rpb, pn.rpb)],
                              e_r.at[0])
    c.start()
    back.append(c)
    total = reduce_end(2, a3, b3)
    db5, dg5 = total[0:1], total[1:2]
    q5 = (gains[5:6] * inv5 * (gact[4] - v * (db5 + norm[4] * dg5) * inv_px)).astype(BF16)
    hbuf[5] = q5

    for b in range(4):
        g = dot_nt(q5, w_proj[pl.ds(b * width, width)]) * slope[b]
        gact[b] = g
        a4[me, pl.ds(b, 1)] = column_sum(g)
        a4[me, pl.ds(4 + b, 1)] = column_sum(g * norm[b])
    dh4[...] = dot_nt(q5, w_proj[pl.ds(4 * width, width)])
    high = dh4[...].astype(BF16)
    low = (dh4[...] - high.astype(F32)).astype(BF16)
    a4[me, pl.ds(8, pn.ncp)] = dot(hot_t[...], high) + dot(hot_t[...], low)
    reduce_start(3, a4)
    for b in range(5):
        dproj_out[pl.ds(b * width, width)] = dot_tn(hbuf[b], hbuf[5]).astype(BF16)
    total = reduce_end(3, a4, b4)
    for b in range(4):
        db, dg = total[b:b + 1], total[4 + b:5 + b]
        db_out[pl.ds(b, 1)] = db
        dg_out[pl.ds(b, 1)] = dg
        q_out[b] = (gains[b:b + 1] * inv[b] * (gact[b] - v * (db + norm[b] * dg) * inv_px)).astype(BF16)
    g4 = total[8:8 + pn.ncp] * slope4
    db4, dg4 = column_sum(g4), column_sum(g4 * n4)
    db_out[pl.ds(4, 1)] = db4
    dg_out[pl.ds(4, 1)] = dg4
    db_out[pl.ds(5, 1)] = db5
    dg_out[pl.ds(5, 1)] = dg5
    q4_out[...] = (gains[4:5] * inv4 * (g4 - (db4 + n4 * dg4) * (1.0 / crops))).astype(BF16)
    for c in back:
        c.wait()


def norms(pn, p, p4, gains, biases, valid, pixels, w_proj, cot, hot, hot_t, sel_t):
    dma = pltpu.SemaphoreType.DMA
    vmem = pl.BlockSpec(memory_space=pltpu.VMEM)
    shape = jax.ShapeDtypeStruct
    big, small = 8 + pn.ncp, 8
    bufs = []
    for n in (big, small, small, big):
        bufs += [pltpu.VMEM((MEMBERS, n, pn.width), F32), pltpu.VMEM((pn.slabs, n, pn.width), F32)]
    return pl.pallas_call(
        functools.partial(norm_kernel, pn),
        out_shape=(
            shape((4, pn.px, pn.width), BF16),
            shape((pn.ncp, pn.width), BF16),
            shape((5 * pn.width, pn.width), BF16),
            shape((pn.h, pn.bp, pn.width), BF16),
            shape((6, pn.width), F32),
            shape((6, pn.width), F32),
        ),
        in_specs=[vmem] * 5 + [pl.BlockSpec(memory_space=pltpu.SMEM)] + [vmem] * 5,
        out_specs=(vmem,) * 6,
        scratch_shapes=[
            pltpu.VMEM((5, pn.px, pn.width), F32),
            pltpu.VMEM((4, pn.px, pn.width), F32),
            pltpu.VMEM((6, pn.px, pn.width), BF16),
            pltpu.VMEM((5, pn.px, pn.width), F32),
            pltpu.VMEM((pn.px, pn.width), F32),
            pltpu.VMEM((pn.rpb, pn.C * pn.bp, pn.width), BF16),
            *bufs,
            dma((4, MEMBERS)), dma((4, MEMBERS)), dma((4, pn.slabs)), dma((4, pn.slabs)), dma((pn.C,)), dma((pn.C,)),
        ],
        compiler_params=pltpu.CompilerParams(collective_id=1, has_side_effects=True, vmem_limit_bytes=48 * 2**20),
        name="norms",
    )(p, p4, gains, biases, valid, pixels, w_proj, cot, hot, hot_t, sel_t)


def back_kernel(pn, q_in, x_in, w_in, dproj_in, q4, means, hot_px, inv_counts, masks, lane_masks, shifts, sel_t,
                dw_out, dx_out, dproj_out,
                xs, wbuf, qraw, qs, qt, dxe, dwbuf, inn, hsend, hrecv, pack, dp1, dps, dp2, dpf,
                l_s, q_s, q_r, k_s, k_r, f_s, f_r, n_s, n_r, e_s, e_r, g_s, g_r, b_s, b_r, h_s, h_r, x_s, x_r,
                p1_s, p1_r, p2_s, p2_r, p3_s, p3_r):
    row, col = lax.axis_index("row"), lax.axis_index("col")
    slab, x = row // pn.G, lax.rem(row, pn.G)
    me = x * pn.C + col
    core, quad = lax.rem(col, 2), me // 2
    h, H, bp, px, S, n = pn.h, pn.H, pn.bp, pn.px, pn.S, pn.slabs
    half = MEMBERS // 2
    many = 4
    partner = (row, col + 1 - 2 * core)

    def member(s, k):
        return (s * pn.G + k // pn.C, lax.rem(k, pn.C))

    load_x = pltpu.make_async_copy(x_in, xs, l_s.at[0])
    load_w = pltpu.make_async_copy(w_in, wbuf, l_s.at[1])
    load_x.start()
    load_w.start()
    greet_all(pn, row, col)

    own_px = pl.ds(pl.multiple_of(me * px, 16), px)
    along_y, along_x = (row, lax.rem(col + 2, pn.C)), (slab * pn.G + lax.rem(x + 1, pn.G), col)
    from_y = x * pn.C + lax.rem(col + 2, pn.C)
    from_x = lax.rem(me + pn.C, MEMBERS)
    from_xy = lax.rem(from_y + pn.C, MEMBERS)

    def block_of(slot, k):
        return qraw.at[slot, pl.ds(pl.multiple_of(k * px, 16), px)]

    def to_y(slot):
        return remote(q_in.at[slot], qraw.at[slot, own_px], q_s.at[slot, 0], q_r.at[slot, 0], along_y)

    def to_x(slot):
        return remote(q_in.at[slot], qraw.at[slot, own_px], q_s.at[slot, 1], q_r.at[slot, 1], along_x)

    def on_to_x(slot):
        return remote(block_of(slot, from_y), block_of(slot, from_y), q_s.at[slot, 2], q_r.at[slot, 2], along_x)

    def to_partner(slot):
        return remote(q_in.at[slot], qraw.at[slot, own_px], k_s.at[slot], k_r.at[slot], partner)

    def passed(slot, i):
        at = block_of(slot, (from_y, from_x, from_xy)[i])
        return remote(at, at, f_s.at[slot, i], f_r.at[slot, i], partner)

    def kept(slot):
        return pltpu.make_async_copy(q_in.at[slot], qraw.at[slot, own_px], l_s.at[2 + slot])

    slots = (1, 2, 3, 0)
    for slot in slots:
        to_y(slot).start()
        to_partner(slot).start()
        kept(slot).start()
    to_x(slots[0]).start()

    block_rows = 5 * pn.width // MEMBERS
    home_slab = me // pn.G

    def dproj_slab(kk):
        other = lax.rem(me + kk, MEMBERS)
        return remote(dproj_in.at[pl.ds(pl.multiple_of(other * block_rows, 16), block_rows)], dp1.at[me],
                      p1_s.at[kk], p1_r.at[kk], member(slab, other))

    def dproj_own():
        return pltpu.make_async_copy(dproj_in.at[pl.ds(pl.multiple_of(me * block_rows, 16), block_rows)], dp1.at[me],
                                     p1_r.at[0])

    def dproj_home():
        return remote(dps, dp2.at[slab], p2_s.at[0], p2_r.at[slab], member(home_slab, me))

    def dproj_give(c):
        return remote(dpf, dproj_out, p3_s.at[c], p3_r.at[0], (slab * pn.G + lax.rem(me, pn.G), c))

    def clear(rb, carry):
        dxe[pl.ds(pl.multiple_of(rb * px, 16), px)] = jnp.zeros((px, pn.cs), F32)
        return carry

    lax.fori_loop(0, pn.nb, clear, 0)

    def receive_y(slot):
        to_y(slot).wait()
        on_to_x(slot).start()
        passed(slot, 0).start()
        if slot != slots[-1]:
            to_x(slots[slots.index(slot) + 1]).start()

    def receive_x(slot):
        to_x(slot).wait()
        passed(slot, 1).start()
        on_to_x(slot).wait()
        passed(slot, 2).start()

    def received(slot):
        to_partner(slot).wait()
        kept(slot).wait()
        for i in range(3):
            passed(slot, i).wait()

    home = home_of(pn, col)
    closing, rising, falling = slab == home, slab < home, slab > home
    first = (slab == 0) | (slab == n - 1)
    half_rows = pn.cs // 2
    detour_up, detour_down = (slab == 0) & (col == 2), (slab == n - 1) & (col == 3)
    relay_up, relay_down = (slab == 0) & (col == 0), (slab == n - 1) & (col == 1)

    def taps(g):
        return pl.ds(3 * g, 3)

    def part_of(ref, g, half):
        return ref.at[taps(g), pl.ds(half * half_rows, half_rows)]

    def link(g, half, up):
        side, to = (0, slab + 1) if up else (1, slab - 1)
        return remote(part_of(dwbuf, g, half), part_of(inn.at[side], g, half), n_s.at[half, g], n_r.at[side, half, g],
                      (to * pn.G + x, col))

    def detour(g, up):
        side = 0 if up else 1
        return remote(part_of(dwbuf, g, 1), part_of(inn.at[side], g, 1), n_s.at[1, g], e_r.at[g], (row, col - 2))

    def relay(g, up):
        side, to = (0, slab + 1) if up else (1, slab - 1)
        return remote(part_of(inn.at[side], g, 1), part_of(inn.at[side], g, 1), e_s.at[g], n_r.at[side, 1, g],
                      (to * pn.G + x, col))

    def early_links(g, act):
        for going, up, around in ((rising, True, detour_up), (falling, False, detour_down)):
            @pl.when(going & jnp.logical_not(around))
            def _(up=up):
                for half in (0, 1):
                    act(link(g, half, up))

            @pl.when(around)
            def _(up=up):
                act(detour(g, up))

    def late_links(g, act):
        for around, up in ((detour_up, True), (detour_down, False)):
            @pl.when(around)
            def _(up=up):
                act(link(g, 0, up))

    def arrived(g, side):
        for half in (0, 1):
            at = part_of(inn.at[side], g, half)
            pltpu.make_async_copy(at, at, n_r.at[side, half, g]).wait()

    def add(g, side):
        dwbuf[taps(g)] = (dwbuf[taps(g)].astype(F32) + inn[side, taps(g)].astype(F32)).astype(BF16)

    close_a, close_b = closing & jnp.logical_not(first), ((slab == 1) & (col == 0)) | ((slab == n - 2) & (col == 1))
    end_closing, end_getting = closing & first, first & (home_of(pn, lax.rem(col + 2, pn.C)) == slab)
    across = (row, lax.rem(col + 2, pn.C))

    def share_y(g, half, src):
        return remote(src, part_of(dw_out, g, half), g_s.at[0, half, g], g_r.at[half, g], across)

    def share_core(g, half, src):
        return remote(src, part_of(dw_out, g, half), g_s.at[1, half, g], g_r.at[half, g], partner)

    def share_on(g, half):
        return remote(part_of(dw_out, g, half), part_of(dw_out, g, half), g_s.at[0, half, g], g_r.at[half, g], partner)

    def share(g, half, src):
        share_y(g, half, src).start()
        share_core(g, half, src).start()
        pltpu.make_async_copy(src, part_of(dw_out, g, half), g_r.at[half, g]).start()

    def landed(g, half):
        at = part_of(dw_out, g, half)
        pltpu.make_async_copy(at, at, g_r.at[half, g]).wait()

    def partial(g, side):
        return remote(part_of(dwbuf, g, 1), part_of(inn.at[1 - side], g, 0), b_s.at[g], b_r.at[g], (row, col - 2))

    rows_of = (pl.ds(0, half_rows), pl.ds(half_rows, half_rows))

    def from_far(g):
        for here, side in ((slab == 1, 1), (slab == n - 2, 0)):
            @pl.when(close_a & here)
            def _(side=side):
                arrived(g, side)
                add(g, side)
                partial(g, side).start()

    def close_half(g):
        for here, side in ((slab == 1, 0), (slab == n - 2, 1)):
            @pl.when(close_a & here)
            def _(side=side):
                at = part_of(inn.at[side], g, 0)
                pltpu.make_async_copy(at, at, n_r.at[side, 0, g]).wait()
                dwbuf[taps(g), rows_of[0]] = (
                    dwbuf[taps(g), rows_of[0]].astype(F32) + inn[side, taps(g), rows_of[0]].astype(F32)
                ).astype(BF16)
                share(g, 0, part_of(dwbuf, g, 0))

            @pl.when(close_b & here)
            def _(side=side):
                at = part_of(inn.at[side], g, 1)
                pltpu.make_async_copy(at, at, n_r.at[side, 1, g]).wait()
                at = part_of(inn.at[side], g, 0)
                pltpu.make_async_copy(at, at, b_r.at[g]).wait()
                inn[side, taps(g), rows_of[1]] = (
                    inn[side, taps(g), rows_of[1]].astype(F32) + inn[side, taps(g), rows_of[0]].astype(F32)
                ).astype(BF16)
                share(g, 1, part_of(inn.at[side], g, 1))

    def relay_many(start, end):
        def one(g, carry):
            for role, up in ((relay_up, True), (relay_down, False)):
                @pl.when(role)
                def _(up=up):
                    at = part_of(inn.at[0 if up else 1], g, 1)
                    pltpu.make_async_copy(at, at, e_r.at[g]).wait()
                    relay(g, up).start()
            return carry

        if pn.exchange:
            lax.fori_loop(start, end, one, 0)

    def late(start, end):
        def one(g, carry):
            late_links(g, lambda c: c.start())
            return carry

        if pn.exchange:
            lax.fori_loop(start, end, one, 0)
        relay_many(start, end)

    def pass_on(g):
        for going, up in ((rising, True), (falling, False)):
            @pl.when(going & jnp.logical_not(first))
            def _(up=up):
                arrived(g, 0 if up else 1)
                add(g, 0 if up else 1)
                for half in (0, 1):
                    link(g, half, up).start()

    def close(g):
        for here, side in ((slab == 0, 1), (slab == n - 1, 0)):
            @pl.when(end_closing & here)
            def _(side=side):
                arrived(g, side)
                add(g, side)
                for half in (0, 1):
                    share(g, half, part_of(dwbuf, g, half))

    def serve(g):
        if not pn.exchange:
            return
        if g < GROUPS:
            pass_on(g)
        if g > 1:
            close(g - 2)
            from_far(g - 2)

    def last_round(g, carry):
        @pl.when(g < GROUPS)
        def _():
            close_half(g)

        @pl.when(g > 1)
        def _():
            before = jnp.maximum(g - 2, 0)
            for half, role in ((0, end_getting | close_b), (1, end_getting | close_a)):
                @pl.when(role)
                def _(half=half):
                    landed(before, half)
                    share_on(before, half).start()

        return carry

    def start_group(g):
        if not pn.exchange:
            return

        @pl.when(first)
        def _():
            early_links(g, lambda c: c.start())

    def weight_gradients(branch):
        qt[...] = qraw[branch].T
        for i in (-1, 0, 1):
            g = 3 * (branch - 1) + i + 1
            q_turned = qt[...]
            if i != 0:
                q_turned = q_turned * lane_masks[pl.ds(2 * (branch - 1) + (i + 1) // 2, 1)]
            window = pl.ds((pn.hb + i * pn.steps[branch - 1]) * px, pn.own)
            for j in (-1, 0, 1):
                dwbuf[3 * g + j + 1] = dot(q_turned, xs[3 + j * branch, window]).T.astype(BF16)
            if branch < 3:
                start_group(g)

    def feature_gradients(branch):
        def turn(rp, carry):
            at = pl.multiple_of(rp * 2 * S, 16)
            moved = dot(shifts[pl.ds((branch - 1) * 4 * S, 4 * S)], qraw[branch, pl.ds(at, 2 * S)]).astype(BF16)
            qs[branch - 1, 0, pl.ds(at, 2 * S)] = moved[:2 * S]
            qs[branch - 1, 1, pl.ds(at, 2 * S)] = moved[2 * S:]
            return carry

        lax.fori_loop(0, H // 2, turn, 0, unroll=6)
        for i in (-1, 0, 1):
            g = 3 * (branch - 1) + i + 1
            mask_at = (2 * (branch - 1) + (i + 1) // 2) * H

            def block(rb, carry, i=i, g=g, mask_at=mask_at):
                at = pl.ds(pl.multiple_of(rb * many * px, 16), many * px)
                y = dot_nt(qs[branch - 1, 0, at], wbuf[3 * g])
                y = y + dot_nt(qraw[branch, at], wbuf[3 * g + 1])
                y = y + dot_nt(qs[branch - 1, 1, at], wbuf[3 * g + 2])
                if i != 0:
                    y = jnp.concatenate(
                        [y[r * S:(r + 1) * S] * masks[mask_at + rb * many * pn.rpb + r] for r in range(many * pn.rpb)], axis=0
                    )
                to = pl.ds(pl.multiple_of((rb * many + pn.hb + i * pn.steps[branch - 1]) * px, 16), many * px)
                dxe[to] = dxe[to] + y
                return carry

            lax.fori_loop(0, MEMBERS // many, block, 0)

    receive_y(1)
    receive_y(2)
    load_x.wait()
    load_w.wait()
    receive_x(1)
    received(1)
    weight_gradients(1)
    receive_y(3)
    receive_x(2)
    feature_gradients(1)
    receive_y(0)
    received(2)
    weight_gradients(2)
    receive_x(3)
    serve(0)
    feature_gradients(2)
    received(3)
    receive_x(0)
    if pn.exchange:
        for kk in range(1, MEMBERS):
            dproj_slab(kk).start()
        dproj_own().start()
    serve(1)
    weight_gradients(3)
    serve(2)
    feature_gradients(3)

    hsend[0] = dxe[pl.ds(0, pn.hb * px)].astype(BF16)
    hsend[1] = dxe[pl.ds((pn.hb + MEMBERS) * px, pn.hb * px)].astype(BF16)

    @pl.when(slab > 0)
    def _():
        remote(hsend.at[0], hrecv.at[1], h_s.at[0], h_r.at[1], member(slab - 1, me)).start()

    @pl.when(slab < n - 1)
    def _():
        remote(hsend.at[1], hrecv.at[0], h_s.at[1], h_r.at[0], member(slab + 1, me)).start()

    for g in (6, 7, 8):
        start_group(g)
    late(0, GROUPS - 1)
    serve(3)

    if pn.exchange:
        for kk in range(1, MEMBERS):
            dproj_slab(kk).wait()
        dproj_own().wait()
        total = dp1[0].astype(F32)
        for m in range(1, MEMBERS):
            total = total + dp1[m].astype(F32)
        dps[...] = total.astype(BF16)

        @pl.when(slab != home_slab)
        def _():
            dproj_home().start()

        @pl.when(slab == home_slab)
        def _():
            pltpu.make_async_copy(dps, dp2.at[slab], p2_r.at[slab]).start()

    received(0)
    dwbuf[POOL] = dot_tn(means[...].astype(BF16), q4[...]).astype(BF16)
    dwbuf[POINT] = dot(qraw[0].T, xs[3, pl.ds(pn.hb * px, pn.own)]).T.astype(BF16)
    dwbuf[TAPS - 1] = jnp.zeros((pn.cs, pn.width), BF16)
    start_group(GROUPS - 1)
    late(GROUPS - 1, GROUPS)
    serve(4)
    pooled = dot_nt(q4[...], wbuf[POOL]) * inv_counts[...]
    pooled_high = pooled.astype(BF16)
    pooled_low = (pooled - pooled_high.astype(F32)).astype(BF16)

    def finish(rb, carry):
        at = pl.ds(pl.multiple_of(rb * many * px, 16), many * px)
        to = pl.ds(pl.multiple_of((rb * many + pn.hb) * px, 16), many * px)
        hot = hot_px[at]
        y = dot_nt(qraw[0, at], wbuf[POINT]) + dot(hot, pooled_high) + dot(hot, pooled_low)
        dxe[to] = dxe[to] + y
        return carry

    lax.fori_loop(0, MEMBERS // many, finish, 0)
    serve(5)

    @pl.when(slab > 0)
    def _():
        remote(hsend.at[0], hrecv.at[1], h_s.at[0], h_r.at[1], member(slab - 1, me)).wait_send()
        remote(hsend.at[1], hrecv.at[0], h_s.at[1], h_r.at[0], member(slab - 1, me)).wait_recv()

    @pl.when(slab < n - 1)
    def _():
        remote(hsend.at[1], hrecv.at[0], h_s.at[1], h_r.at[0], member(slab + 1, me)).wait_send()
        remote(hsend.at[0], hrecv.at[1], h_s.at[0], h_r.at[1], member(slab + 1, me)).wait_recv()

    @pl.when(slab == 0)
    def _():
        hrecv[0] = jnp.zeros((pn.hb * px, pn.cs), BF16)

    @pl.when(slab == n - 1)
    def _():
        hrecv[1] = jnp.zeros((pn.hb * px, pn.cs), BF16)

    for rb in range(pn.hb):
        low, high = (pn.hb + rb) * px, (MEMBERS + rb) * px
        dxe[pl.ds(low, px)] = dxe[pl.ds(low, px)] + hrecv[0, pl.ds(rb * px, px)].astype(F32)
        dxe[pl.ds(high, px)] = dxe[pl.ds(high, px)] + hrecv[1, pl.ds(rb * px, px)].astype(F32)

    def packing(rp, carry):
        pair = dxe[pl.ds(pl.multiple_of(pn.hb * px + rp * 2 * S, 16), 2 * S)].astype(BF16)
        pack[pl.ds(2 * rp, 2)] = dot(sel_t[...], pair).astype(BF16).reshape(2, pn.C * bp, pn.cs)
        return carry

    lax.fori_loop(0, H // 2, packing, 0, unroll=6)
    back = []
    for kk in range(1, MEMBERS):
        other = lax.rem(me + kk, MEMBERS)
        xo, co = other // pn.C, lax.rem(other, pn.C)
        c = remote(pack.at[pl.ds(xo * h, h), pl.ds(pl.multiple_of(co * bp, bp), bp)], dx_out.at[slice_of(pn, me)], x_s.at[kk], x_r.at[kk],
                   member(slab, other))
        c.start()
        back.append(c)
    c = pltpu.make_async_copy(pack.at[pl.ds(x * h, h), pl.ds(pl.multiple_of(col * bp, bp), bp)], dx_out.at[slice_of(pn, me)], x_r.at[0])
    c.start()
    back.append(c)

    if pn.exchange:
        done = 0
        for g, end in ((6, 1), (7, 3), (8, 4), (9, 6), (10, 7), (11, 8), (None, GROUPS + 2)):
            if g is not None:
                serve(g)
            lax.fori_loop(done, end, last_round, 0)
            done = end

        @pl.when(slab == home_slab)
        def _():
            for z in range(n):
                pltpu.make_async_copy(dp2.at[z], dp2.at[z], p2_r.at[z]).wait()
            total = dp2[0].astype(F32)
            for z in range(1, n):
                total = total + dp2[z].astype(F32)
            dpf[...] = total
            for c in range(pn.C):
                @pl.when((x == lax.rem(me, pn.G)) & (col == c))
                def _():
                    pltpu.make_async_copy(dpf, dproj_out, p3_r.at[0]).start()

                @pl.when(jnp.logical_not((x == lax.rem(me, pn.G)) & (col == c)))
                def _(c=c):
                    dproj_give(c).start()

        def settle(g, carry):
            early_links(g, lambda c: c.wait_send())
            late_links(g, lambda c: c.wait_send())
            for role, up in ((relay_up, True), (relay_down, False)):
                @pl.when(role)
                def _(up=up):
                    relay(g, up).wait_send()

            @pl.when(close_a)
            def _():
                partial(g, 0).wait_send()

            for half, gives, passes in ((0, end_closing | close_a, end_getting | close_b),
                                        (1, end_closing | close_b, end_getting | close_a)):
                @pl.when(gives)
                def _(half=half):
                    share_y(g, half, part_of(dwbuf, g, half)).wait_send()
                    share_core(g, half, part_of(dwbuf, g, half)).wait_send()

                @pl.when(passes)
                def _(half=half):
                    share_on(g, half).wait_send()

                @pl.when(jnp.logical_not(passes))
                def _(half=half):
                    landed(g, half)

            return carry

        lax.fori_loop(0, GROUPS, settle, 0)

        @pl.when(slab != home_slab)
        def _():
            dproj_home().wait_send()

        @pl.when(slab == home_slab)
        def _():
            for c in range(pn.C):
                @pl.when(jnp.logical_not((x == lax.rem(me, pn.G)) & (col == c)))
                def _(c=c):
                    dproj_give(c).wait_send()

        pltpu.make_async_copy(dproj_out, dproj_out, p3_r.at[0]).wait()
    else:
        c = pltpu.make_async_copy(dwbuf, dw_out, g_r.at[0, 0])
        c.start()
        c.wait()
        dproj_out[...] = jnp.zeros(dproj_out.shape, F32)
    for c in back:
        c.wait()


def conv_backward(pn, q, xs, w, dproj, q4, means, hot_px, inv_counts, masks, lane_masks, shifts, sel_t):
    dma = pltpu.SemaphoreType.DMA
    vmem = pl.BlockSpec(memory_space=pltpu.VMEM)
    hbm = pl.BlockSpec(memory_space=pl.ANY)
    shape = jax.ShapeDtypeStruct
    n = pn.slabs if pn.exchange else 1
    sums = TAPS if pn.exchange else 1
    block_rows = 5 * pn.width // MEMBERS
    return pl.pallas_call(
        functools.partial(back_kernel, pn),
        out_shape=(
            shape((TAPS, pn.cs, pn.width), BF16),
            shape((MEMBERS, pn.h, pn.bp, pn.cs), BF16),
            shape((block_rows, pn.width), F32),
        ),
        in_specs=[hbm] * 4 + [vmem] * 4 + [pl.BlockSpec(memory_space=pltpu.SMEM)] + [vmem] * 3,
        out_specs=(hbm, hbm, vmem),
        scratch_shapes=[
            pltpu.VMEM((7, pn.ext, pn.cs), BF16),
            pltpu.VMEM((TAPS, pn.cs, pn.width), BF16),
            pltpu.VMEM((4, pn.own, pn.width), BF16),
            pltpu.VMEM((3, 2, pn.own, pn.width), BF16),
            pltpu.VMEM((pn.width, pn.own), BF16),
            pltpu.VMEM((pn.ext, pn.cs), F32),
            pltpu.VMEM((TAPS, pn.cs, pn.width), BF16),
            pltpu.VMEM((2, sums, pn.cs, pn.width), BF16),
            pltpu.VMEM((2, pn.hb * pn.px, pn.cs), BF16),
            pltpu.VMEM((2, pn.hb * pn.px, pn.cs), BF16),
            pltpu.VMEM((pn.H, pn.C * pn.bp, pn.cs), BF16),
            pltpu.VMEM((MEMBERS, block_rows, pn.width), BF16),
            pltpu.VMEM((block_rows, pn.width), BF16),
            pltpu.VMEM((n, block_rows, pn.width), BF16),
            pltpu.VMEM((block_rows, pn.width), F32),
            dma((6,)), dma((4, 3)), dma((4, 3)), dma((4,)), dma((4,)), dma((4, 3)), dma((4, 3)),
            dma((2, GROUPS)), dma((2, 2, GROUPS)), dma((GROUPS,)), dma((GROUPS,)), dma((2, 2, GROUPS)), dma((2, GROUPS)),
            dma((GROUPS,)), dma((GROUPS,)),
            dma((2,)), dma((2,)), dma((MEMBERS,)), dma((MEMBERS,)),
            dma((MEMBERS,)), dma((MEMBERS,)), dma((1,)), dma((n,)), dma((pn.C,)), dma((1,)),
        ],
        compiler_params=pltpu.CompilerParams(collective_id=2, has_side_effects=True, vmem_limit_bytes=61900 * 1024),
        name="conv_backward",
    )(q, xs, w, dproj, q4, means, hot_px, inv_counts, masks, lane_masks, shifts, sel_t)


def column_tables(pn):
    S, bp, bc = pn.S, pn.bp, pn.bc
    sel = np.zeros((7, 2, S, 2, pn.C * bp), np.float32)
    shifts = np.zeros((3, 2, 2, S, 2, S), np.float32)
    for r in range(2):
        for c in range(pn.cols):
            for v in range(-3, 4):
                s = c + v * DILATIONS[0]
                if 0 <= s < pn.cols:
                    sel[v + 3, r, c, r, (s // bc) * bp + s % bc] = 1.0
            for b, d in enumerate(DILATIONS):
                for n, j in enumerate((-1, 1)):
                    s = c - j * d
                    if 0 <= s < pn.cols:
                        shifts[b, n, r, c, r, s] = 1.0
    sel = sel.reshape(7 * 2 * S, 2 * pn.C * bp)
    sel_t = sel[3 * 2 * S:4 * 2 * S].T
    return (jnp.asarray(sel, BF16), jnp.asarray(sel_t, BF16), jnp.asarray(shifts.reshape(12 * S, 2 * S), BF16))


def per_device(
    features, crop_rows, crop_cols, w_point, w_atrous, w_pool, w_proj, gains, biases, cotangent
):
    h, bc, channels = features.shape
    pn = Plan(lax.axis_size("row"), lax.axis_size("col"), h, bc, channels, gains.shape[1], crop_rows.shape[0])
    row, col = lax.axis_index("row"), lax.axis_index("col")
    slab, x = row // pn.G, row % pn.G
    crop_ids = jnp.arange(pn.crops, dtype=jnp.int32)
    ends = jnp.cumsum(crop_rows)
    counts = (crop_rows * crop_cols).astype(F32)
    pixels = jnp.sum(counts)

    def crop_of(rows):
        found = jnp.sum((rows[:, None] >= ends[None, :]).astype(jnp.int32), axis=1)
        return jnp.where(rows < 0, -1, found)

    def widths_of(crop):
        return jnp.sum(jnp.where(crop[:, None] == crop_ids[None, :], crop_cols[None, :], 0), axis=1)

    own_crop = crop_of(row * h + jnp.arange(h, dtype=jnp.int32))
    own_columns = col * bc + jnp.arange(bc, dtype=jnp.int32)
    own_valid = own_columns[None, :] < widths_of(own_crop)[:, None]
    masked = jnp.where(own_valid[:, :, None], features, 0)
    feats = masked.reshape(h, bc, MEMBERS, pn.cs).transpose(2, 0, 1, 3)
    feats = jnp.pad(feats, ((0, 0), (0, 0), (0, pn.bp - bc), (0, 0)))
    cot = jnp.pad(cotangent, ((0, 0), (0, pn.bp - bc), (0, 0)))

    slab_rows = slab * pn.H - MARGIN + jnp.arange(pn.H + 2 * MARGIN, dtype=jnp.int32)
    crops = crop_of(slab_rows)
    mid = crops[MARGIN:MARGIN + pn.H]
    same = jnp.stack(
        [crops[MARGIN + i * d:MARGIN + i * d + pn.H] == mid for d in DILATIONS for i in (-1, 1)]
    ).astype(F32)
    lane_masks = jnp.pad(jnp.repeat(same, pn.S, axis=1), ((0, 2), (0, 0))).astype(BF16)
    ncp_ids = jnp.arange(pn.ncp, dtype=jnp.int32)
    hot_rows = (mid[:, None] == ncp_ids[None, :]).astype(BF16)
    hot_px = jnp.repeat(hot_rows, pn.S, axis=0)
    hot_t = jnp.repeat(hot_rows.T, pn.S, axis=1)
    inv_counts = jnp.pad(1.0 / counts, (0, pn.ncp - pn.crops))[:, None]

    k = x * pn.C + col
    block_crop = lax.dynamic_slice_in_dim(mid, k * pn.rpb, pn.rpb)
    columns = jnp.arange(pn.S, dtype=jnp.int32)
    valid = (columns[None, :] < widths_of(block_crop)[:, None]).astype(F32).reshape(pn.px, 1)
    block_hot = jnp.repeat((block_crop[:, None] == ncp_ids[None, :]).astype(BF16), pn.S, axis=0)
    block_hot_t = jnp.repeat((ncp_ids[:, None] == block_crop[None, :]).astype(BF16), pn.S, axis=1)

    sel, sel_t, shifts = column_tables(pn)
    none = jnp.zeros((1, *w_point.shape), BF16)
    w = jnp.concatenate([w_atrous.transpose(1, 0, 2), w_point[None], w_pool[None], none], axis=0)
    proj = w_proj.reshape(pn.C, pn.proj // pn.C, pn.width)
    proj = jnp.pad(proj, ((0, 0), (0, pn.piece - pn.proj // pn.C), (0, 0)))
    if not pn.exchange:
        w = lax.all_gather(w, "row", axis=1, tiled=True)
        w = lax.dynamic_slice_in_dim(w, slice_of(pn, x * pn.C + col) * pn.cs, pn.cs, axis=1)
    flat = same.reshape(-1)
    p, xs, w_own, means, p4, own_cot, pieces = conv_forward(pn, feats, w, cot, proj, flat, sel, hot_t, inv_counts)
    full_proj = pieces[:, :, :pn.proj // pn.C].transpose(1, 0, 2, 3).reshape(5 * pn.width, pn.width)
    q, q4, d_proj, res, d_gains, d_biases = norms(
        pn, p, p4, gains, biases, valid, (1.0 / pixels)[None], full_proj, own_cot, block_hot, block_hot_t, sel_t
    )
    dw, dx, dproj_sum = conv_backward(
        pn, q, xs, w_own, d_proj, q4, means, hot_px, inv_counts, flat, lane_masks, shifts, sel_t
    )
    if pn.exchange:
        d_proj = dproj_sum
    else:
        whole = jnp.zeros((TAPS, channels, pn.width), BF16)
        whole = lax.dynamic_update_slice(whole, dw, (0, slice_of(pn, x * pn.C + col) * pn.cs, 0))
        whole = lax.psum(whole, "col")
        dw = lax.psum_scatter(whole, "row", scatter_dimension=1, tiled=True)
        d_proj = lax.psum(d_proj, "col")
        d_proj = lax.psum_scatter(d_proj.astype(F32), "row", scatter_dimension=0, tiled=True)
    result = res[:, :bc]
    dx = dx[:, :, :bc].transpose(1, 2, 0, 3).reshape(h, bc, channels)
    d_features = jnp.where(own_valid[:, :, None], dx, 0)
    d_point = dw[POINT].astype(F32)
    d_atrous = dw[:POINT].astype(F32).transpose(1, 0, 2)
    d_pool = dw[POOL].astype(F32)
    return (result, d_features, d_point, d_atrous, d_pool, d_proj, d_gains, d_biases)


def solution(mesh):
    return jax.shard_map(
        per_device,
        mesh=mesh,
        in_specs=(
            P("row", "col", None),
            P(),
            P(),
            P("row", None),
            P("row", None, None),
            P("row", None),
            P("row", None),
            P(),
            P(),
            P("row", "col", None),
        ),
        out_specs=(
            P("row", "col", None),
            P("row", "col", None),
            P("row", None),
            P("row", None, None),
            P("row", None),
            P("row", None),
            P(),
            P(),
        ),
        check_vma=False,
    )
```

```python
import functools

import jax
import jax.numpy as jnp
import numpy as np
from jax import lax
from jax.experimental import pallas as pl
from jax.experimental.pallas import tpu as pltpu
from jax.sharding import PartitionSpec as P

EPSILON = 1e-05
MARGIN = 18
DILATIONS = (6, 12, 18)
MEMBERS = 8
TAPS = 29
POINT, POOL, GROUPS = 27, 28, 10
MESH = pl.DeviceIdType.MESH
F32 = jnp.float32
BF16 = jnp.bfloat16

def up_to(value, multiple):
    return -(-value // multiple) * multiple


class Plan:
    def __init__(self, rows_axis, cols_axis, h, bc, channels, width, crops):
        self.R, self.C = rows_axis, cols_axis
        self.h, self.bc, self.channels, self.width = h, bc, channels, width
        self.G = MEMBERS // self.C
        self.slabs = self.R // self.G
        self.H = self.G * h
        self.cols = bc * self.C
        self.S = up_to(self.cols, 8)
        self.rpb = self.H // MEMBERS
        self.px = self.rpb * self.S
        self.own = MEMBERS * self.px
        self.hb = MARGIN // self.rpb
        self.nb = MEMBERS + 2 * self.hb
        self.ext = self.nb * self.px
        self.bp = up_to(bc, 16)
        self.cs = channels // MEMBERS
        self.crops = crops
        self.ncp = up_to(crops, 16)
        self.exchange = self.slabs == self.C and self.R == MEMBERS
        self.steps = tuple(d // self.rpb for d in DILATIONS)
        self.proj = 5 * width // self.R
        self.piece = up_to(self.proj // self.C, 16)


def home_of(pn, col):
    if pn.C != 4:
        return col
    y, c = col // 2, lax.rem(col, 2)
    return (1 - y) * 3 * c + y * (1 + c)


def slice_of(pn, k):
    return pn.G * home_of(pn, lax.rem(k, pn.C)) + k // pn.C


def remote(src, dst, send, recv, device):
    return pltpu.make_async_remote_copy(
        src_ref=src, dst_ref=dst, send_sem=send, recv_sem=recv, device_id=device, device_id_type=MESH
    )


def greet_all(pn, row, col):
    total = pn.R * pn.C
    barrier = pltpu.get_barrier_semaphore()
    me = row * pn.C + col

    def hello(k, carry):
        other = lax.rem(me + k, total)
        pl.semaphore_signal(
            barrier, inc=1, device_id=(other // pn.C, lax.rem(other, pn.C)), device_id_type=MESH
        )
        return carry

    lax.fori_loop(1, total, hello, 0)
    pl.semaphore_wait(barrier, total - 1)


def dot(a, b):
    return jnp.dot(a, b, preferred_element_type=F32)


def dot_nt(a, b):
    return lax.dot_general(a, b, (((1,), (1,)), ((), ())), preferred_element_type=F32)


def dot_tn(a, b):
    return lax.dot_general(a, b, (((0,), (0,)), ((), ())), preferred_element_type=F32)


def split_dot(dot_fn, a, b):
    high = a.astype(BF16)
    low = (a - high.astype(F32)).astype(BF16)
    return dot_fn(high, b) + dot_fn(low, b)


def conv_kernel(pn, feats, w_in, w_two, cot, proj, masks, sel, hot_t, inv_counts,
                p_out, x_out, w_out, m_out, p4_out, cot_out, proj_out,
                ring, xs, wbuf, acc, pbuf, cbuf, sbuf, rbuf, cx,
                f_s, f_r, h_s, h_r, c_s, c_r, j_s, j_r, t_s, t_r, w_s, w_r, w_l, e_s,
                r1_s, r1_r, r2_s, r2_r, o_s):
    row, col = lax.axis_index("row"), lax.axis_index("col")
    slab, x = row // pn.G, lax.rem(row, pn.G)
    me = x * pn.C + col
    core, quad = lax.rem(col, 2), me // 2
    h, H, bp, px, n = pn.h, pn.H, pn.bp, pn.px, pn.slabs
    many = 4

    def member(s, k):
        return (s * pn.G + k // pn.C, lax.rem(k, pn.C))

    greet_all(pn, row, col)

    own_cols = pl.ds(pl.multiple_of(col * bp, bp), bp)
    own_rows = pl.ds(MARGIN + h * x, h)
    sent = []
    for kk in range(1, MEMBERS):
        other = lax.rem(me + kk, MEMBERS)
        c = remote(feats.at[slice_of(pn, other)], ring.at[own_rows, own_cols], f_s.at[kk], f_r.at[kk], member(slab, other))
        c.start()
        sent.append(c)
    keep = pltpu.make_async_copy(feats.at[slice_of(pn, me)], ring.at[own_rows, own_cols], f_r.at[0])
    keep.start()

    home = home_of(pn, col)
    source, rising, falling = slab == home, (slab > home) & (slab < n - 1), (slab < home) & (slab > 0)
    help_up, help_down = (slab == n - 2) & (col == 1), (slab == 1) & (col == 0)
    half_rows = pn.cs // 2

    order = (0, 1, 2, 3, 4, 5, 9, 6, 7, 8)

    def taps(g):
        return pl.ds(POINT, 2) if isinstance(g, int) and g == GROUPS - 1 else pl.ds(3 * g, 3)

    def given(g, rows):
        if isinstance(g, int) and g == GROUPS - 1:
            return w_two.at[:, rows]
        return w_in.at[taps(g), rows]

    def half_of(half):
        return pl.ds(half * half_rows, half_rows)

    def part_of(ref, g, half):
        return ref.at[taps(g), half_of(half)]

    def ship(g, half, up, own):
        to = slab + 1 if up else slab - 1
        return remote(given(g, half_of(half)) if own else part_of(wbuf, g, half), part_of(wbuf, g, half), w_s.at[int(up), half, g], w_r.at[half, g],
                      (to * pn.G + x, col))

    def assist(g, up):
        to = slab + 1 if up else slab - 1
        return remote(given(g, half_of(1)), part_of(wbuf, g, 1), e_s.at[g], w_r.at[1, g], (to * pn.G + x, col + 2))

    def own_copy(g):
        return pltpu.make_async_copy(given(g, pl.ds(0, pn.cs)), wbuf.at[taps(g)], w_l.at[g])

    def arrived(g):
        for half in (0, 1):
            at = part_of(wbuf, g, half)
            pltpu.make_async_copy(at, at, w_r.at[half, g]).wait()

    def pass_on(g):
        for role, up in ((rising, True), (falling, False)):
            @pl.when(role)
            def _(up=up):
                arrived(g)
                for half in (0, 1):
                    ship(g, half, up, False).start()

    def w_wait(g):
        if pn.exchange:
            @pl.when(source)
            def _():
                own_copy(g).wait()

            @pl.when(jnp.logical_not(source | rising | falling))
            def _():
                arrived(g)
        else:
            own_copy(g).wait()

    def each_shipment(g, act):
        for half in (0, 1):
            @pl.when(source & ((slab < n - 2) if half else (slab < n - 1)))
            def _(half=half):
                act(ship(g, half, True, True))

            @pl.when(source & ((slab > 1) if half else (slab > 0)))
            def _(half=half):
                act(ship(g, half, False, True))

        @pl.when(help_up)
        def _():
            act(assist(g, True))

        @pl.when(help_down)
        def _():
            act(assist(g, False))

    if pn.exchange:
        def begin(g, carry):
            each_shipment(g, lambda c: c.start())

            @pl.when(source)
            def _():
                own_copy(g).start()

            return carry
    else:
        def begin(g, carry):
            own_copy(g).start()
            return carry

    early = 6
    lax.fori_loop(0, early, begin, 0)

    cot_sent = []
    for cc in range(1, pn.C):
        cd = lax.rem(col + cc, pn.C)
        c = remote(cot.at[pl.ds(cd * pn.rpb, pn.rpb)], cx.at[:, own_cols], c_s.at[cc], c_r.at[cc], (row, cd))
        c.start()
        cot_sent.append(c)
    cot_keep = pltpu.make_async_copy(cot.at[pl.ds(col * pn.rpb, pn.rpb)], cx.at[:, own_cols], c_r.at[0])
    cot_keep.start()

    def proj_row(k):
        return remote(proj.at[col], proj_out.at[col, row], j_s.at[k], j_r.at[k], (lax.rem(row + k, pn.R), col))

    def proj_col(k):
        return remote(proj_out.at[col], proj_out.at[col], t_s.at[k], t_r.at[k], (row, lax.rem(col + k, pn.C)))

    def proj_begin(k, carry):
        proj_row(k).start()
        return carry

    def proj_wait(k, carry):
        proj_row(k).wait()
        return carry

    lax.fori_loop(1, pn.R, proj_begin, 0)
    proj_keep = pltpu.make_async_copy(proj.at[col], proj_out.at[col, row], j_r.at[0])
    proj_keep.start()

    @pl.when(slab == 0)
    def _():
        ring[pl.ds(0, MARGIN)] = jnp.zeros((MARGIN, pn.C * bp, pn.cs), BF16)

    @pl.when(slab == n - 1)
    def _():
        ring[pl.ds(MARGIN + H, MARGIN)] = jnp.zeros((MARGIN, pn.C * bp, pn.cs), BF16)

    def pass_many(first, end):
        if pn.exchange:
            for k in range(first, end):
                pass_on(order[k])

    pass_many(0, 3)
    for c in sent:
        c.wait()
    keep.wait()

    def margin_down():
        return remote(ring.at[pl.ds(MARGIN, MARGIN)], ring.at[pl.ds(MARGIN + H, MARGIN)], h_s.at[0], h_r.at[0],
                      member(slab - 1, me))

    def margin_up():
        return remote(ring.at[pl.ds(H, MARGIN)], ring.at[pl.ds(0, MARGIN)], h_s.at[1], h_r.at[1], member(slab + 1, me))

    @pl.when(slab > 0)
    def _():
        margin_down().start()

    @pl.when(slab < n - 1)
    def _():
        margin_up().start()

    begin(GROUPS - 1, 0)
    lax.fori_loop(early, GROUPS - 1, begin, 0)

    def assemble(rp, carry):
        pair = ring[pl.ds(2 * rp, 2)].reshape(2 * pn.C * bp, pn.cs)
        moved = dot(sel[...], pair).astype(BF16)
        at = pl.multiple_of(rp * 2 * pn.S, 16)
        for v in range(7):
            xs[v, pl.ds(at, 2 * pn.S)] = moved[v * 2 * pn.S:(v + 1) * 2 * pn.S]
        return carry

    lax.fori_loop(MARGIN // 2, (MARGIN + H) // 2, assemble, 0, unroll=6)
    pass_many(3, 5)
    for c in cot_sent:
        c.wait()
    cot_keep.wait()
    for rp in range(pn.rpb // 2):
        pair = cx[2 * rp:2 * rp + 2].reshape(2 * pn.C * bp, pn.width)
        cot_out[pl.ds(rp * 2 * pn.S, 2 * pn.S)] = dot(sel[pl.ds(3 * 2 * pn.S, 2 * pn.S)], pair).astype(BF16)
    lax.fori_loop(1, pn.R, proj_wait, 0)
    proj_keep.wait()
    for k in range(1, pn.C):
        proj_col(k).start()
    pass_many(5, 6)

    @pl.when(slab > 0)
    def _():
        margin_down().wait_send()
        margin_up().wait_recv()

    @pl.when(slab < n - 1)
    def _():
        margin_up().wait_send()
        margin_down().wait_recv()

    lax.fori_loop(0, MARGIN // 2, assemble, 0, unroll=3)
    lax.fori_loop((MARGIN + H) // 2, pn.nb * pn.rpb // 2, assemble, 0, unroll=3)
    x_save = pltpu.make_async_copy(xs, x_out, o_s.at[0])
    x_save.start()

    def first_stage(slot):
        return remote(pbuf.at[slot, :, 1 - core], cbuf.at[slot], r1_s.at[slot], r1_r.at[slot], (row, col + 1 - 2 * core))

    def second_stage(slot, i):
        q = lax.rem(quad + i, MEMBERS // 2)
        return remote(sbuf.at[slot, i - 1], rbuf.at[slot, i - 1], r2_s.at[slot, i - 1], r2_r.at[slot, i - 1],
                      member(slab, 2 * q + core))

    def middle(slot):
        first_stage(slot).wait()
        for i in (1, 2, 3, 0):
            q = lax.rem(quad + i, MEMBERS // 2)
            s = pbuf[slot, q, core].astype(F32) + cbuf[slot, q].astype(F32)
            if i == 0:
                p_out[slot] = s
            else:
                sbuf[slot, i - 1] = s.astype(BF16)
                second_stage(slot, i).start()

    def last(slot):
        total = p_out[slot]
        for i in range(1, MEMBERS // 2):
            second_stage(slot, i).wait()
            total = total + rbuf[slot, i - 1].astype(F32)
        p_out[slot] = total

    def scatter(slot, rb, y):
        for r in range(many):
            pbuf[slot, (many * rb + r) // 2, r % 2] = y[r * px:(r + 1) * px].astype(BF16)

    def far(k):
        if k in (2, 4, 6, 8):
            pass_many(5 + k // 2, 6 + k // 2)
        w_wait(order[k])

    def point(rb, carry):
        at = pl.ds(pl.multiple_of((rb * many + pn.hb) * px, 16), many * px)
        scatter(0, rb, dot(xs[3, at], wbuf[POINT]))
        return carry

    for branch in (1, 2, 3):
        step = pn.steps[branch - 1]
        if branch == 3:
            far(6)
            lax.fori_loop(0, MEMBERS // many, point, 0)
            first_stage(0).start()
            middle(2)
        for i in (-1, 0, 1):
            g = 3 * (branch - 1) + i + 1
            mask_at = (2 * (branch - 1) + (i + 1) // 2) * H
            far(g + branch // 3)

            def block(rb, carry, step=step, i=i, g=g, mask_at=mask_at, branch=branch):
                at = pl.multiple_of(rb * many * px, 16)
                window = pl.ds(pl.multiple_of((rb * many + pn.hb + i * step) * px, 16), many * px)
                y = dot(xs[3 - branch, window], wbuf[3 * g])
                y = y + dot(xs[3, window], wbuf[3 * g + 1])
                y = y + dot(xs[3 + branch, window], wbuf[3 * g + 2])
                if i != 0:
                    y = jnp.concatenate(
                        [y[r * pn.S:(r + 1) * pn.S] * masks[mask_at + rb * many * pn.rpb + r]
                         for r in range(many * pn.rpb)], axis=0
                    )
                if i > -1:
                    y = y + acc[pl.ds(at, many * px)]
                if i < 1:
                    acc[pl.ds(at, many * px)] = y
                else:
                    scatter(branch, rb, y)
                return carry

            lax.fori_loop(0, MEMBERS // many, block, 0)
            if i == 0 and branch > 1:
                middle(branch - 1 if branch == 2 else 0)
        first_stage(branch).start()

    sums = dot(hot_t[...], xs[3, pl.ds(pn.hb * px, pn.own)])
    means = sums * inv_counts[...]
    m_out[...] = means
    p4_out[...] = split_dot(dot, means, wbuf[POOL])
    w_save = pltpu.make_async_copy(wbuf, w_out, o_s.at[1])
    w_save.start()
    middle(3)
    for slot in (1, 2, 0):
        last(slot)
    for k in range(1, pn.C):
        proj_col(k).wait()
    if pn.exchange:
        def settled(g, carry):
            each_shipment(g, lambda c: c.wait_send())
            for role, up in ((rising, True), (falling, False)):
                @pl.when(role)
                def _(up=up):
                    for half in (0, 1):
                        ship(g, half, up, False).wait_send()
            return carry

        lax.fori_loop(0, GROUPS - 1, settled, 0)
        settled(GROUPS - 1, 0)
    last(3)
    x_save.wait()
    w_save.wait()


def conv_forward(pn, feats, w, w_two, cot, proj, masks, sel, hot_t, inv_counts):
    half = MEMBERS // 2
    dma = pltpu.SemaphoreType.DMA
    vmem = pl.BlockSpec(memory_space=pltpu.VMEM)
    hbm = pl.BlockSpec(memory_space=pl.ANY)
    shape = jax.ShapeDtypeStruct
    return pl.pallas_call(
        functools.partial(conv_kernel, pn),
        out_shape=(
            shape((4, pn.px, pn.width), F32),
            shape((7, pn.ext, pn.cs), BF16),
            shape((TAPS, pn.cs, pn.width), BF16),
            shape((pn.ncp, pn.cs), F32),
            shape((pn.ncp, pn.width), F32),
            shape((pn.px, pn.width), BF16),
            shape((pn.C, pn.R, pn.piece, pn.width), BF16),
        ),
        in_specs=[hbm, hbm, hbm, hbm, hbm, pl.BlockSpec(memory_space=pltpu.SMEM), vmem, vmem, vmem],
        out_specs=(vmem, hbm, hbm, vmem, vmem, vmem, vmem),
        scratch_shapes=[
            pltpu.VMEM((pn.nb * pn.rpb, pn.C * pn.bp, pn.cs), BF16),
            pltpu.VMEM((7, pn.ext, pn.cs), BF16),
            pltpu.VMEM((TAPS, pn.cs, pn.width), BF16),
            pltpu.VMEM((pn.own, pn.width), F32),
            pltpu.VMEM((4, half, 2, pn.px, pn.width), BF16),
            pltpu.VMEM((4, half, pn.px, pn.width), BF16),
            pltpu.VMEM((4, half - 1, pn.px, pn.width), BF16),
            pltpu.VMEM((4, half - 1, pn.px, pn.width), BF16),
            pltpu.VMEM((pn.rpb, pn.C * pn.bp, pn.width), BF16),
            dma((MEMBERS,)), dma((MEMBERS,)), dma((2,)), dma((2,)), dma((pn.C,)), dma((pn.C,)),
            dma((pn.R,)), dma((pn.R,)), dma((pn.C,)), dma((pn.C,)),
            dma((2, 2, GROUPS)), dma((2, GROUPS)), dma((GROUPS,)), dma((GROUPS,)),
            dma((4,)), dma((4,)), dma((4, 3)), dma((4, 3)), dma((2,)),
        ],
        compiler_params=pltpu.CompilerParams(collective_id=0, has_side_effects=True, vmem_limit_bytes=60 * 2**20),
        name="conv_forward",
    )(feats, w, w_two, cot, proj, masks, sel, hot_t, inv_counts)


def norm_kernel(pn, p, p4_in, gains, biases, valid, pixels, w_proj, cot, hot, hot_t, sel_t,
                q_out, q4_out, dproj_out, res_out, dg_out, db_out,
                norm, slope, hbuf, gact, dh4, rx,
                a1, b1, a2, b2, a3, b3, a4, b4, as_s, as_r, bs_s, bs_r, e_s, e_r):
    row, col = lax.axis_index("row"), lax.axis_index("col")
    slab, x = row // pn.G, lax.rem(row, pn.G)
    me = x * pn.C + col
    crops = float(pn.crops)
    v = valid[...]
    inv_px = pixels[0]
    width, bp = pn.width, pn.bp

    def member(s, k):
        return (s * pn.G + k // pn.C, lax.rem(k, pn.C))

    barrier = pltpu.get_barrier_semaphore()
    for kk in range(1, MEMBERS):
        pl.semaphore_signal(barrier, inc=1, device_id=member(slab, lax.rem(me + kk, MEMBERS)), device_id_type=MESH)

    def hello(k, carry):
        pl.semaphore_signal(barrier, inc=1, device_id=member(lax.rem(slab + k, pn.slabs), me), device_id_type=MESH)
        return carry

    lax.fori_loop(1, pn.slabs, hello, 0)

    def peer_a(n, abuf, kk):
        return remote(abuf.at[me], abuf.at[me], as_s.at[n, kk], as_r.at[n, kk], member(slab, lax.rem(me + kk, MEMBERS)))

    def peer_b(n, bbuf, k):
        return remote(bbuf.at[slab], bbuf.at[slab], bs_s.at[n, k], bs_r.at[n, k], member(lax.rem(slab + k, pn.slabs), me))

    def reduce_start(n, abuf):
        for kk in range(1, MEMBERS):
            peer_a(n, abuf, kk).start()

    def reduce_end(n, abuf, bbuf):
        for kk in range(1, MEMBERS):
            peer_a(n, abuf, kk).wait()
        total = abuf[0]
        for k in range(1, MEMBERS):
            total = total + abuf[k]
        bbuf[slab] = total
        for k in range(1, pn.slabs):
            peer_b(n, bbuf, k).start()
        for k in range(1, pn.slabs):
            peer_b(n, bbuf, k).wait()
        total = bbuf[0]
        for k in range(1, pn.slabs):
            total = total + bbuf[k]
        return total

    def column_sum(value):
        return jnp.sum(value, axis=0, keepdims=True)

    for b in range(4):
        pv = p[b] * v
        a1[me, pl.ds(b, 1)] = column_sum(pv)
        a1[me, pl.ds(4 + b, 1)] = column_sum(pv * p[b])
    a1[me, pl.ds(8, pn.ncp)] = p4_in[...]
    pl.semaphore_wait(barrier, MEMBERS - 1 + pn.slabs - 1)
    reduce_start(0, a1)
    total = reduce_end(0, a1, b1)
    inv = []
    for b in range(4):
        centre = total[b:b + 1] * inv_px
        scale = lax.rsqrt(total[4 + b:5 + b] * inv_px - centre * centre + EPSILON)
        inv.append(scale)
        n = (p[b] - centre) * scale
        u = gains[b:b + 1] * n + biases[b:b + 1]
        s = jax.nn.sigmoid(u)
        norm[b] = n
        slope[b] = s * (1.0 + u * (1.0 - s))
        hbuf[b] = (u * s).astype(BF16)
    p4 = total[8:8 + pn.ncp]
    centre4 = column_sum(p4) * (1.0 / crops)
    inv4 = lax.rsqrt(column_sum(p4 * p4) * (1.0 / crops) - centre4 * centre4 + EPSILON)
    n4 = (p4 - centre4) * inv4
    u4 = gains[4:5] * n4 + biases[4:5]
    s4 = jax.nn.sigmoid(u4)
    slope4 = s4 * (1.0 + u4 * (1.0 - s4))
    hbuf[4] = dot(hot[...], (u4 * s4).astype(BF16)).astype(BF16)

    p5 = dot(hbuf[0], w_proj[pl.ds(0, width)])
    for b in range(1, 5):
        p5 = p5 + dot(hbuf[b], w_proj[pl.ds(b * width, width)])
    pv = p5 * v
    a2[me, pl.ds(0, 1)] = column_sum(pv)
    a2[me, pl.ds(1, 1)] = column_sum(pv * p5)
    a2[me, pl.ds(2, 6)] = jnp.zeros((6, width), F32)
    reduce_start(1, a2)
    total = reduce_end(1, a2, b2)
    centre5 = total[0:1] * inv_px
    inv5 = lax.rsqrt(total[1:2] * inv_px - centre5 * centre5 + EPSILON)
    n5 = (p5 - centre5) * inv5
    u5 = gains[5:6] * n5 + biases[5:6]
    s5 = jax.nn.sigmoid(u5)
    g5 = cot[...].astype(F32) * v * (s5 * (1.0 + u5 * (1.0 - s5)))
    norm[4] = n5
    gact[4] = g5
    a3[me, pl.ds(0, 1)] = column_sum(g5)
    a3[me, pl.ds(1, 1)] = column_sum(g5 * n5)
    a3[me, pl.ds(2, 6)] = jnp.zeros((6, width), F32)
    reduce_start(2, a3)
    hbuf[5] = (v * u5 * s5).astype(BF16)
    for rp in range(pn.rpb // 2):
        pair = hbuf[5, pl.ds(rp * 2 * pn.S, 2 * pn.S)]
        rx[2 * rp:2 * rp + 2] = dot(sel_t[...], pair).astype(BF16).reshape(2, pn.C * bp, width)
    back = []
    for cc in range(1, pn.C):
        cd = lax.rem(col + cc, pn.C)
        c = remote(rx.at[:, pl.ds(pl.multiple_of(cd * bp, bp), bp)], res_out.at[pl.ds(col * pn.rpb, pn.rpb)],
                   e_s.at[cc], e_r.at[cc], (row, cd))
        c.start()
        back.append(c)
    c = pltpu.make_async_copy(rx.at[:, pl.ds(pl.multiple_of(col * bp, bp), bp)], res_out.at[pl.ds(col * pn.rpb, pn.rpb)],
                              e_r.at[0])
    c.start()
    back.append(c)
    total = reduce_end(2, a3, b3)
    db5, dg5 = total[0:1], total[1:2]
    q5 = (gains[5:6] * inv5 * (gact[4] - v * (db5 + norm[4] * dg5) * inv_px)).astype(BF16)
    hbuf[5] = q5

    for b in range(4):
        g = dot_nt(q5, w_proj[pl.ds(b * width, width)]) * slope[b]
        gact[b] = g
        a4[me, pl.ds(b, 1)] = column_sum(g)
        a4[me, pl.ds(4 + b, 1)] = column_sum(g * norm[b])
    dh4[...] = dot_nt(q5, w_proj[pl.ds(4 * width, width)])
    high = dh4[...].astype(BF16)
    low = (dh4[...] - high.astype(F32)).astype(BF16)
    a4[me, pl.ds(8, pn.ncp)] = dot(hot_t[...], high) + dot(hot_t[...], low)
    reduce_start(3, a4)
    for b in range(5):
        dproj_out[pl.ds(b * width, width)] = dot_tn(hbuf[b], hbuf[5]).astype(BF16)
    total = reduce_end(3, a4, b4)
    for b in range(4):
        db, dg = total[b:b + 1], total[4 + b:5 + b]
        db_out[pl.ds(b, 1)] = db
        dg_out[pl.ds(b, 1)] = dg
        q_out[b] = (gains[b:b + 1] * inv[b] * (gact[b] - v * (db + norm[b] * dg) * inv_px)).astype(BF16)
    g4 = total[8:8 + pn.ncp] * slope4
    db4, dg4 = column_sum(g4), column_sum(g4 * n4)
    db_out[pl.ds(4, 1)] = db4
    dg_out[pl.ds(4, 1)] = dg4
    db_out[pl.ds(5, 1)] = db5
    dg_out[pl.ds(5, 1)] = dg5
    q4_out[...] = (gains[4:5] * inv4 * (g4 - (db4 + n4 * dg4) * (1.0 / crops))).astype(BF16)
    for c in back:
        c.wait()


def norms(pn, p, p4, gains, biases, valid, pixels, w_proj, cot, hot, hot_t, sel_t):
    dma = pltpu.SemaphoreType.DMA
    vmem = pl.BlockSpec(memory_space=pltpu.VMEM)
    shape = jax.ShapeDtypeStruct
    big, small = 8 + pn.ncp, 8
    bufs = []
    for n in (big, small, small, big):
        bufs += [pltpu.VMEM((MEMBERS, n, pn.width), F32), pltpu.VMEM((pn.slabs, n, pn.width), F32)]
    return pl.pallas_call(
        functools.partial(norm_kernel, pn),
        out_shape=(
            shape((4, pn.px, pn.width), BF16),
            shape((pn.ncp, pn.width), BF16),
            shape((5 * pn.width, pn.width), BF16),
            shape((pn.h, pn.bp, pn.width), BF16),
            shape((6, pn.width), F32),
            shape((6, pn.width), F32),
        ),
        in_specs=[vmem] * 5 + [pl.BlockSpec(memory_space=pltpu.SMEM)] + [vmem] * 5,
        out_specs=(vmem,) * 6,
        scratch_shapes=[
            pltpu.VMEM((5, pn.px, pn.width), F32),
            pltpu.VMEM((4, pn.px, pn.width), F32),
            pltpu.VMEM((6, pn.px, pn.width), BF16),
            pltpu.VMEM((5, pn.px, pn.width), F32),
            pltpu.VMEM((pn.px, pn.width), F32),
            pltpu.VMEM((pn.rpb, pn.C * pn.bp, pn.width), BF16),
            *bufs,
            dma((4, MEMBERS)), dma((4, MEMBERS)), dma((4, pn.slabs)), dma((4, pn.slabs)), dma((pn.C,)), dma((pn.C,)),
        ],
        compiler_params=pltpu.CompilerParams(collective_id=1, has_side_effects=True, vmem_limit_bytes=48 * 2**20),
        name="norms",
    )(p, p4, gains, biases, valid, pixels, w_proj, cot, hot, hot_t, sel_t)


def back_kernel(pn, q_in, x_in, w_in, dproj_in, q4, means, hot_rows, inv_counts, masks, lane_masks, shifts, sel_t,
                dw_out, dx_out, dproj_out,
                xs, wbuf, qraw, qs, qt, dxe, dwbuf, inn, hsend, hrecv, pack, pooled_rows, dp1, dps, dp2, dpf,
                l_s, q_s, q_r, k_s, k_r, f_s, f_r, n_s, n_r, e_s, e_r, g_s, g_r, b_s, b_r, h_s, h_r, x_s, x_r,
                p1_s, p1_r, p2_s, p2_r, p3_s, p3_r):
    row, col = lax.axis_index("row"), lax.axis_index("col")
    slab, x = row // pn.G, lax.rem(row, pn.G)
    me = x * pn.C + col
    core, quad = lax.rem(col, 2), me // 2
    h, H, bp, px, S, n = pn.h, pn.H, pn.bp, pn.px, pn.S, pn.slabs
    half = MEMBERS // 2
    many = 4
    partner = (row, col + 1 - 2 * core)

    def member(s, k):
        return (s * pn.G + k // pn.C, lax.rem(k, pn.C))

    load_x = pltpu.make_async_copy(x_in, xs, l_s.at[0])
    load_w = pltpu.make_async_copy(w_in, wbuf, l_s.at[1])
    load_x.start()
    load_w.start()
    greet_all(pn, row, col)

    own_px = pl.ds(pl.multiple_of(me * px, 16), px)
    along_y, along_x = (row, lax.rem(col + 2, pn.C)), (slab * pn.G + lax.rem(x + 1, pn.G), col)
    from_y = x * pn.C + lax.rem(col + 2, pn.C)
    from_x = lax.rem(me + pn.C, MEMBERS)
    from_xy = lax.rem(from_y + pn.C, MEMBERS)

    def block_of(slot, k):
        return qraw.at[slot, pl.ds(pl.multiple_of(k * px, 16), px)]

    def to_y(slot):
        return remote(q_in.at[slot], qraw.at[slot, own_px], q_s.at[slot, 0], q_r.at[slot, 0], along_y)

    def to_x(slot):
        return remote(q_in.at[slot], qraw.at[slot, own_px], q_s.at[slot, 1], q_r.at[slot, 1], along_x)

    def on_to_x(slot):
        return remote(block_of(slot, from_y), block_of(slot, from_y), q_s.at[slot, 2], q_r.at[slot, 2], along_x)

    def to_partner(slot):
        return remote(q_in.at[slot], qraw.at[slot, own_px], k_s.at[slot], k_r.at[slot], partner)

    def passed(slot, i):
        at = block_of(slot, (from_y, from_x, from_xy)[i])
        return remote(at, at, f_s.at[slot, i], f_r.at[slot, i], partner)

    def kept(slot):
        return pltpu.make_async_copy(q_in.at[slot], qraw.at[slot, own_px], l_s.at[2 + slot])

    slots = (1, 2, 3, 0)
    for slot in slots:
        to_y(slot).start()
        to_partner(slot).start()
        kept(slot).start()
    to_x(slots[0]).start()

    block_rows = 5 * pn.width // MEMBERS
    home_slab = me // pn.G

    def dproj_slab(kk):
        other = lax.rem(me + kk, MEMBERS)
        return remote(dproj_in.at[pl.ds(pl.multiple_of(other * block_rows, 16), block_rows)], dp1.at[me],
                      p1_s.at[kk], p1_r.at[kk], member(slab, other))

    def dproj_own():
        return pltpu.make_async_copy(dproj_in.at[pl.ds(pl.multiple_of(me * block_rows, 16), block_rows)], dp1.at[me],
                                     p1_r.at[0])

    def dproj_home():
        return remote(dps, dp2.at[slab], p2_s.at[0], p2_r.at[slab], member(home_slab, me))

    def dproj_give(c):
        return remote(dpf, dproj_out, p3_s.at[c], p3_r.at[0], (slab * pn.G + lax.rem(me, pn.G), c))

    def clear(rb, carry):
        dxe[pl.ds(pl.multiple_of(rb * px, 16), px)] = jnp.zeros((px, pn.cs), F32)
        return carry

    lax.fori_loop(0, pn.nb, clear, 0)

    def receive_y(slot):
        to_y(slot).wait()
        on_to_x(slot).start()
        passed(slot, 0).start()
        if slot != slots[-1]:
            to_x(slots[slots.index(slot) + 1]).start()

    def receive_x(slot):
        to_x(slot).wait()
        passed(slot, 1).start()
        on_to_x(slot).wait()
        passed(slot, 2).start()

    def received(slot):
        to_partner(slot).wait()
        kept(slot).wait()
        for i in range(3):
            passed(slot, i).wait()

    home = home_of(pn, col)
    closing, rising, falling = slab == home, slab < home, slab > home
    first = (slab == 0) | (slab == n - 1)
    half_rows = pn.cs // 2
    detour_up, detour_down = (slab == 0) & (col == 2), (slab == n - 1) & (col == 3)
    relay_up, relay_down = (slab == 0) & (col == 0), (slab == n - 1) & (col == 1)

    def taps(g):
        return pl.ds(3 * g, 3)

    def part_of(ref, g, half):
        return ref.at[taps(g), pl.ds(half * half_rows, half_rows)]

    def link(g, half, up):
        side, to = (0, slab + 1) if up else (1, slab - 1)
        return remote(part_of(dwbuf, g, half), part_of(inn.at[side], g, half), n_s.at[half, g], n_r.at[side, half, g],
                      (to * pn.G + x, col))

    def detour(g, up):
        side = 0 if up else 1
        return remote(part_of(dwbuf, g, 1), part_of(inn.at[side], g, 1), n_s.at[1, g], e_r.at[g], (row, col - 2))

    def relay(g, up):
        side, to = (0, slab + 1) if up else (1, slab - 1)
        return remote(part_of(inn.at[side], g, 1), part_of(inn.at[side], g, 1), e_s.at[g], n_r.at[side, 1, g],
                      (to * pn.G + x, col))

    def early_links(g, act):
        for going, up, around in ((rising, True, detour_up), (falling, False, detour_down)):
            @pl.when(going & jnp.logical_not(around))
            def _(up=up):
                for half in (0, 1):
                    act(link(g, half, up))

            @pl.when(around)
            def _(up=up):
                act(detour(g, up))

    def late_links(g, act):
        for around, up in ((detour_up, True), (detour_down, False)):
            @pl.when(around)
            def _(up=up):
                act(link(g, 0, up))

    def arrived(g, side):
        for half in (0, 1):
            at = part_of(inn.at[side], g, half)
            pltpu.make_async_copy(at, at, n_r.at[side, half, g]).wait()

    def add(g, side):
        dwbuf[taps(g)] = (dwbuf[taps(g)].astype(F32) + inn[side, taps(g)].astype(F32)).astype(BF16)

    close_a, close_b = closing & jnp.logical_not(first), ((slab == 1) & (col == 0)) | ((slab == n - 2) & (col == 1))
    end_closing, end_getting = closing & first, first & (home_of(pn, lax.rem(col + 2, pn.C)) == slab)
    across = (row, lax.rem(col + 2, pn.C))

    def share_y(g, half, src):
        return remote(src, part_of(dw_out, g, half), g_s.at[0, half, g], g_r.at[half, g], across)

    def share_core(g, half, src):
        return remote(src, part_of(dw_out, g, half), g_s.at[1, half, g], g_r.at[half, g], partner)

    def share_on(g, half):
        return remote(part_of(dw_out, g, half), part_of(dw_out, g, half), g_s.at[0, half, g], g_r.at[half, g], partner)

    def share(g, half, src):
        share_y(g, half, src).start()
        share_core(g, half, src).start()
        pltpu.make_async_copy(src, part_of(dw_out, g, half), g_r.at[half, g]).start()

    def landed(g, half):
        at = part_of(dw_out, g, half)
        pltpu.make_async_copy(at, at, g_r.at[half, g]).wait()

    def partial(g, side):
        return remote(part_of(dwbuf, g, 1), part_of(inn.at[1 - side], g, 0), b_s.at[g], b_r.at[g], (row, col - 2))

    rows_of = (pl.ds(0, half_rows), pl.ds(half_rows, half_rows))

    def from_far(g):
        for here, side in ((slab == 1, 1), (slab == n - 2, 0)):
            @pl.when(close_a & here)
            def _(side=side):
                arrived(g, side)
                add(g, side)
                partial(g, side).start()

    def close_half(g):
        for here, side in ((slab == 1, 0), (slab == n - 2, 1)):
            @pl.when(close_a & here)
            def _(side=side):
                at = part_of(inn.at[side], g, 0)
                pltpu.make_async_copy(at, at, n_r.at[side, 0, g]).wait()
                dwbuf[taps(g), rows_of[0]] = (
                    dwbuf[taps(g), rows_of[0]].astype(F32) + inn[side, taps(g), rows_of[0]].astype(F32)
                ).astype(BF16)
                share(g, 0, part_of(dwbuf, g, 0))

            @pl.when(close_b & here)
            def _(side=side):
                at = part_of(inn.at[side], g, 1)
                pltpu.make_async_copy(at, at, n_r.at[side, 1, g]).wait()
                at = part_of(inn.at[side], g, 0)
                pltpu.make_async_copy(at, at, b_r.at[g]).wait()
                inn[side, taps(g), rows_of[1]] = (
                    inn[side, taps(g), rows_of[1]].astype(F32) + inn[side, taps(g), rows_of[0]].astype(F32)
                ).astype(BF16)
                share(g, 1, part_of(inn.at[side], g, 1))

    def relay_many(start, end):
        def one(g, carry):
            for role, up in ((relay_up, True), (relay_down, False)):
                @pl.when(role)
                def _(up=up):
                    at = part_of(inn.at[0 if up else 1], g, 1)
                    pltpu.make_async_copy(at, at, e_r.at[g]).wait()
                    relay(g, up).start()
            return carry

        if pn.exchange:
            lax.fori_loop(start, end, one, 0)

    def late(start, end):
        def one(g, carry):
            late_links(g, lambda c: c.start())
            return carry

        if pn.exchange:
            lax.fori_loop(start, end, one, 0)
        relay_many(start, end)

    def pass_on(g):
        for going, up in ((rising, True), (falling, False)):
            @pl.when(going & jnp.logical_not(first))
            def _(up=up):
                arrived(g, 0 if up else 1)
                add(g, 0 if up else 1)
                for half in (0, 1):
                    link(g, half, up).start()

    def close(g):
        for here, side in ((slab == 0, 1), (slab == n - 1, 0)):
            @pl.when(end_closing & here)
            def _(side=side):
                arrived(g, side)
                add(g, side)
                for half in (0, 1):
                    share(g, half, part_of(dwbuf, g, half))

    def serve(g):
        if not pn.exchange:
            return
        if g < GROUPS:
            pass_on(g)
        if g > 1:
            close(g - 2)
            from_far(g - 2)

    def last_round(g, carry):
        @pl.when(g < GROUPS)
        def _():
            close_half(g)

        @pl.when(g > 1)
        def _():
            before = jnp.maximum(g - 2, 0)
            for half, role in ((0, end_getting | close_b), (1, end_getting | close_a)):
                @pl.when(role)
                def _(half=half):
                    landed(before, half)
                    share_on(before, half).start()

        return carry

    def start_group(g):
        if not pn.exchange:
            return

        @pl.when(first)
        def _():
            early_links(g, lambda c: c.start())

    def weight_gradients(branch):
        qt[...] = qraw[branch].T
        for i in (-1, 0, 1):
            g = 3 * (branch - 1) + i + 1
            q_turned = qt[...]
            if i != 0:
                q_turned = q_turned * lane_masks[pl.ds(2 * (branch - 1) + (i + 1) // 2, 1)]
            window = pl.ds((pn.hb + i * pn.steps[branch - 1]) * px, pn.own)
            for j in (-1, 0, 1):
                dwbuf[3 * g + j + 1] = dot(q_turned, xs[3 + j * branch, window]).T.astype(BF16)
            if branch < 3:
                start_group(g)

    def feature_gradients(branch):
        def turn(rp, carry):
            at = pl.multiple_of(rp * 2 * S, 16)
            moved = dot(shifts[pl.ds((branch - 1) * 4 * S, 4 * S)], qraw[branch, pl.ds(at, 2 * S)]).astype(BF16)
            qs[branch - 1, 0, pl.ds(at, 2 * S)] = moved[:2 * S]
            qs[branch - 1, 1, pl.ds(at, 2 * S)] = moved[2 * S:]
            return carry

        lax.fori_loop(0, H // 2, turn, 0, unroll=6)
        for i in (-1, 0, 1):
            g = 3 * (branch - 1) + i + 1
            mask_at = (2 * (branch - 1) + (i + 1) // 2) * H

            def block(rb, carry, i=i, g=g, mask_at=mask_at):
                at = pl.ds(pl.multiple_of(rb * many * px, 16), many * px)
                y = dot_nt(qs[branch - 1, 0, at], wbuf[3 * g])
                y = y + dot_nt(qraw[branch, at], wbuf[3 * g + 1])
                y = y + dot_nt(qs[branch - 1, 1, at], wbuf[3 * g + 2])
                if i != 0:
                    y = jnp.concatenate(
                        [y[r * S:(r + 1) * S] * masks[mask_at + rb * many * pn.rpb + r] for r in range(many * pn.rpb)], axis=0
                    )
                to = pl.ds(pl.multiple_of((rb * many + pn.hb + i * pn.steps[branch - 1]) * px, 16), many * px)
                dxe[to] = dxe[to] + y
                return carry

            lax.fori_loop(0, MEMBERS // many, block, 0)

    receive_y(1)
    receive_y(2)
    load_x.wait()
    load_w.wait()
    receive_x(1)
    received(1)
    weight_gradients(1)
    receive_y(3)
    receive_x(2)
    feature_gradients(1)
    receive_y(0)
    received(2)
    weight_gradients(2)
    receive_x(3)
    serve(0)
    feature_gradients(2)
    received(3)
    receive_x(0)
    if pn.exchange:
        for kk in range(1, MEMBERS):
            dproj_slab(kk).start()
        dproj_own().start()
    serve(1)
    weight_gradients(3)
    serve(2)
    feature_gradients(3)

    hsend[0] = dxe[pl.ds(0, pn.hb * px)].astype(BF16)
    hsend[1] = dxe[pl.ds((pn.hb + MEMBERS) * px, pn.hb * px)].astype(BF16)

    @pl.when(slab > 0)
    def _():
        remote(hsend.at[0], hrecv.at[1], h_s.at[0], h_r.at[1], member(slab - 1, me)).start()

    @pl.when(slab < n - 1)
    def _():
        remote(hsend.at[1], hrecv.at[0], h_s.at[1], h_r.at[0], member(slab + 1, me)).start()

    for g in (6, 7, 8):
        start_group(g)
    late(0, GROUPS - 1)
    serve(3)

    if pn.exchange:
        for kk in range(1, MEMBERS):
            dproj_slab(kk).wait()
        dproj_own().wait()
        total = dp1[0].astype(F32)
        for m in range(1, MEMBERS):
            total = total + dp1[m].astype(F32)
        dps[...] = total.astype(BF16)

        @pl.when(slab != home_slab)
        def _():
            dproj_home().start()

        @pl.when(slab == home_slab)
        def _():
            pltpu.make_async_copy(dps, dp2.at[slab], p2_r.at[slab]).start()

    received(0)
    dwbuf[POOL] = dot_tn(means[...].astype(BF16), q4[...]).astype(BF16)
    dwbuf[POINT] = dot(qraw[0].T, xs[3, pl.ds(pn.hb * px, pn.own)]).T.astype(BF16)
    dwbuf[3 * GROUPS - 1] = jnp.zeros((pn.cs, pn.width), BF16)
    start_group(GROUPS - 1)
    late(GROUPS - 1, GROUPS)
    serve(4)
    pooled = dot_nt(q4[...], wbuf[POOL]) * inv_counts[...]
    pooled_high = pooled.astype(BF16)
    pooled_low = (pooled - pooled_high.astype(F32)).astype(BF16)
    pooled_rows[...] = dot(hot_rows[...], pooled_high) + dot(hot_rows[...], pooled_low)

    def finish(rb, carry):
        at = pl.ds(pl.multiple_of(rb * many * px, 16), many * px)
        to = pl.ds(pl.multiple_of((rb * many + pn.hb) * px, 16), many * px)
        y = dot_nt(qraw[0, at], wbuf[POINT])
        y = jnp.concatenate(
            [y[r * S:(r + 1) * S] + pooled_rows[pl.ds(rb * many * pn.rpb + r, 1)] for r in range(many * pn.rpb)], axis=0
        )
        dxe[to] = dxe[to] + y
        return carry

    lax.fori_loop(0, MEMBERS // many, finish, 0)
    serve(5)

    @pl.when(slab > 0)
    def _():
        remote(hsend.at[0], hrecv.at[1], h_s.at[0], h_r.at[1], member(slab - 1, me)).wait_send()
        remote(hsend.at[1], hrecv.at[0], h_s.at[1], h_r.at[0], member(slab - 1, me)).wait_recv()

    @pl.when(slab < n - 1)
    def _():
        remote(hsend.at[1], hrecv.at[0], h_s.at[1], h_r.at[0], member(slab + 1, me)).wait_send()
        remote(hsend.at[0], hrecv.at[1], h_s.at[0], h_r.at[1], member(slab + 1, me)).wait_recv()

    @pl.when(slab == 0)
    def _():
        hrecv[0] = jnp.zeros((pn.hb * px, pn.cs), BF16)

    @pl.when(slab == n - 1)
    def _():
        hrecv[1] = jnp.zeros((pn.hb * px, pn.cs), BF16)

    for rb in range(pn.hb):
        low, high = (pn.hb + rb) * px, (MEMBERS + rb) * px
        dxe[pl.ds(low, px)] = dxe[pl.ds(low, px)] + hrecv[0, pl.ds(rb * px, px)].astype(F32)
        dxe[pl.ds(high, px)] = dxe[pl.ds(high, px)] + hrecv[1, pl.ds(rb * px, px)].astype(F32)

    column = lax.broadcasted_iota(jnp.int32, (S, pn.cs), 0).astype(F32)
    for b in range(H // 8):
        rows = []
        for r in range(8 * b, 8 * b + 8):
            values = dxe[pl.ds(pn.hb * px + r * S, S)]
            rows.append(jnp.where(column < masks[6 * H + r], values, 0.0))
        moved = dot(sel_t[...], jnp.concatenate(rows, axis=0).astype(BF16)).astype(BF16)
        pack[8 * b // h, :, pl.ds(8 * b % h, 8)] = moved.reshape(pn.cols, 8, pn.cs)
    own_lanes = pl.ds(pl.multiple_of(slice_of(pn, me) * pn.cs, 128), pn.cs)
    back = []
    for kk in range(1, MEMBERS):
        other = lax.rem(me + kk, MEMBERS)
        xo, co = other // pn.C, lax.rem(other, pn.C)
        c = remote(pack.at[xo, pl.ds(co * pn.bc, pn.bc)], dx_out.at[:, :, own_lanes], x_s.at[kk], x_r.at[kk],
                   member(slab, other))
        c.start()
        back.append(c)
    c = pltpu.make_async_copy(pack.at[x, pl.ds(col * pn.bc, pn.bc)], dx_out.at[:, :, own_lanes], x_r.at[0])
    c.start()
    back.append(c)

    def close_dproj():
        @pl.when(slab == home_slab)
        def _():
            for z in range(n):
                pltpu.make_async_copy(dp2.at[z], dp2.at[z], p2_r.at[z]).wait()
            total = dp2[0].astype(F32)
            for z in range(1, n):
                total = total + dp2[z].astype(F32)
            dpf[...] = total
            for c in range(pn.C):
                @pl.when((x == lax.rem(me, pn.G)) & (col == c))
                def _():
                    pltpu.make_async_copy(dpf, dproj_out, p3_r.at[0]).start()

                @pl.when(jnp.logical_not((x == lax.rem(me, pn.G)) & (col == c)))
                def _(c=c):
                    dproj_give(c).start()

    if pn.exchange:
        done = 0
        for g, end in ((6, 1), (7, 3), (8, 4), (9, 6), (10, 7), (11, 8), (None, GROUPS + 2)):
            if g is not None:
                serve(g)
            else:
                close_dproj()
            lax.fori_loop(done, end, last_round, 0)
            done = end

        def settle(g, carry):
            early_links(g, lambda c: c.wait_send())
            late_links(g, lambda c: c.wait_send())
            for role, up in ((relay_up, True), (relay_down, False)):
                @pl.when(role)
                def _(up=up):
                    relay(g, up).wait_send()

            @pl.when(close_a)
            def _():
                partial(g, 0).wait_send()

            for half, gives, passes in ((0, end_closing | close_a, end_getting | close_b),
                                        (1, end_closing | close_b, end_getting | close_a)):
                @pl.when(gives)
                def _(half=half):
                    share_y(g, half, part_of(dwbuf, g, half)).wait_send()
                    share_core(g, half, part_of(dwbuf, g, half)).wait_send()

                @pl.when(passes)
                def _(half=half):
                    share_on(g, half).wait_send()

                @pl.when(jnp.logical_not(passes))
                def _(half=half):
                    landed(g, half)

            return carry

        lax.fori_loop(0, GROUPS, settle, 0)

        @pl.when(slab != home_slab)
        def _():
            dproj_home().wait_send()

        @pl.when(slab == home_slab)
        def _():
            for c in range(pn.C):
                @pl.when(jnp.logical_not((x == lax.rem(me, pn.G)) & (col == c)))
                def _(c=c):
                    dproj_give(c).wait_send()

        pltpu.make_async_copy(dproj_out, dproj_out, p3_r.at[0]).wait()
    else:
        c = pltpu.make_async_copy(dwbuf, dw_out, g_r.at[0, 0])
        c.start()
        c.wait()
        dproj_out[...] = jnp.zeros(dproj_out.shape, F32)
    for c in back:
        c.wait()


def conv_backward(pn, q, xs, w, dproj, q4, means, hot_rows, inv_counts, masks, lane_masks, shifts, sel_t):
    dma = pltpu.SemaphoreType.DMA
    vmem = pl.BlockSpec(memory_space=pltpu.VMEM)
    hbm = pl.BlockSpec(memory_space=pl.ANY)
    shape = jax.ShapeDtypeStruct
    n = pn.slabs if pn.exchange else 1
    sums = 3 * GROUPS if pn.exchange else 1
    block_rows = 5 * pn.width // MEMBERS
    return pl.pallas_call(
        functools.partial(back_kernel, pn),
        out_shape=(
            shape((3 * GROUPS, pn.cs, pn.width), BF16),
            shape((pn.bc, pn.h, pn.channels), BF16),
            shape((block_rows, pn.width), F32),
        ),
        in_specs=[hbm] * 4 + [vmem] * 4 + [pl.BlockSpec(memory_space=pltpu.SMEM)] + [vmem] * 3,
        out_specs=(hbm, hbm, vmem),
        scratch_shapes=[
            pltpu.VMEM((7, pn.ext, pn.cs), BF16),
            pltpu.VMEM((TAPS, pn.cs, pn.width), BF16),
            pltpu.VMEM((4, pn.own, pn.width), BF16),
            pltpu.VMEM((3, 2, pn.own, pn.width), BF16),
            pltpu.VMEM((pn.width, pn.own), BF16),
            pltpu.VMEM((pn.ext, pn.cs), F32),
            pltpu.VMEM((3 * GROUPS, pn.cs, pn.width), BF16),
            pltpu.VMEM((2, sums, pn.cs, pn.width), BF16),
            pltpu.VMEM((2, pn.hb * pn.px, pn.cs), BF16),
            pltpu.VMEM((2, pn.hb * pn.px, pn.cs), BF16),
            pltpu.VMEM((pn.G, pn.cols, pn.h, pn.cs), BF16),
            pltpu.VMEM((pn.H, pn.cs), F32),
            pltpu.VMEM((MEMBERS, block_rows, pn.width), BF16),
            pltpu.VMEM((block_rows, pn.width), BF16),
            pltpu.VMEM((n, block_rows, pn.width), BF16),
            pltpu.VMEM((block_rows, pn.width), F32),
            dma((6,)), dma((4, 3)), dma((4, 3)), dma((4,)), dma((4,)), dma((4, 3)), dma((4, 3)),
            dma((2, GROUPS)), dma((2, 2, GROUPS)), dma((GROUPS,)), dma((GROUPS,)), dma((2, 2, GROUPS)), dma((2, GROUPS)),
            dma((GROUPS,)), dma((GROUPS,)),
            dma((2,)), dma((2,)), dma((MEMBERS,)), dma((MEMBERS,)),
            dma((MEMBERS,)), dma((MEMBERS,)), dma((1,)), dma((n,)), dma((pn.C,)), dma((1,)),
        ],
        compiler_params=pltpu.CompilerParams(collective_id=2, has_side_effects=True, vmem_limit_bytes=61900 * 1024),
        name="conv_backward",
    )(q, xs, w, dproj, q4, means, hot_rows, inv_counts, masks, lane_masks, shifts, sel_t)


def column_tables(pn):
    S, bp, bc = pn.S, pn.bp, pn.bc
    sel = np.zeros((7, 2, S, 2, pn.C * bp), np.float32)
    shifts = np.zeros((3, 2, 2, S, 2, S), np.float32)
    for r in range(2):
        for c in range(pn.cols):
            for v in range(-3, 4):
                s = c + v * DILATIONS[0]
                if 0 <= s < pn.cols:
                    sel[v + 3, r, c, r, (s // bc) * bp + s % bc] = 1.0
            for b, d in enumerate(DILATIONS):
                for n, j in enumerate((-1, 1)):
                    s = c - j * d
                    if 0 <= s < pn.cols:
                        shifts[b, n, r, c, r, s] = 1.0
    sel = sel.reshape(7 * 2 * S, 2 * pn.C * bp)
    sel_t = sel[3 * 2 * S:4 * 2 * S].T
    sel_c = np.zeros((pn.cols, 8, 8, S), np.float32)
    for c in range(pn.cols):
        for r in range(8):
            sel_c[c, r, r, c] = 1.0
    sel_c = sel_c.reshape(8 * pn.cols, 8 * S)
    return (jnp.asarray(sel, BF16), jnp.asarray(sel_t, BF16), jnp.asarray(sel_c, BF16), jnp.asarray(shifts.reshape(12 * S, 2 * S), BF16))


def per_device(
    features, crop_rows, crop_cols, w_point, w_atrous, w_pool, w_proj, gains, biases, cotangent
):
    h, bc, channels = features.shape
    pn = Plan(lax.axis_size("row"), lax.axis_size("col"), h, bc, channels, gains.shape[1], crop_rows.shape[0])
    row, col = lax.axis_index("row"), lax.axis_index("col")
    slab, x = row // pn.G, row % pn.G
    crop_ids = jnp.arange(pn.crops, dtype=jnp.int32)
    ends = jnp.cumsum(crop_rows)
    counts = (crop_rows * crop_cols).astype(F32)
    pixels = jnp.sum(counts)

    def crop_of(rows):
        found = jnp.sum((rows[:, None] >= ends[None, :]).astype(jnp.int32), axis=1)
        return jnp.where(rows < 0, -1, found)

    def widths_of(crop):
        return jnp.sum(jnp.where(crop[:, None] == crop_ids[None, :], crop_cols[None, :], 0), axis=1)

    own_crop = crop_of(row * h + jnp.arange(h, dtype=jnp.int32))
    own_columns = col * bc + jnp.arange(bc, dtype=jnp.int32)
    own_valid = own_columns[None, :] < widths_of(own_crop)[:, None]
    masked = jnp.where(own_valid[:, :, None], features, 0)
    feats = masked.reshape(h, bc, MEMBERS, pn.cs).transpose(2, 0, 1, 3)
    feats = jnp.pad(feats, ((0, 0), (0, 0), (0, pn.bp - bc), (0, 0)))
    cot = jnp.pad(cotangent, ((0, 0), (0, pn.bp - bc), (0, 0)))

    slab_rows = slab * pn.H - MARGIN + jnp.arange(pn.H + 2 * MARGIN, dtype=jnp.int32)
    crops = crop_of(slab_rows)
    mid = crops[MARGIN:MARGIN + pn.H]
    same = jnp.stack(
        [crops[MARGIN + i * d:MARGIN + i * d + pn.H] == mid for d in DILATIONS for i in (-1, 1)]
    ).astype(F32)
    lane_masks = jnp.pad(jnp.repeat(same, pn.S, axis=1), ((0, 2), (0, 0))).astype(BF16)
    ncp_ids = jnp.arange(pn.ncp, dtype=jnp.int32)
    hot_rows = (mid[:, None] == ncp_ids[None, :]).astype(BF16)
    hot_t = jnp.repeat(hot_rows.T, pn.S, axis=1)
    inv_counts = jnp.pad(1.0 / counts, (0, pn.ncp - pn.crops))[:, None]

    k = x * pn.C + col
    block_crop = lax.dynamic_slice_in_dim(mid, k * pn.rpb, pn.rpb)
    columns = jnp.arange(pn.S, dtype=jnp.int32)
    valid = (columns[None, :] < widths_of(block_crop)[:, None]).astype(F32).reshape(pn.px, 1)
    block_hot = jnp.repeat((block_crop[:, None] == ncp_ids[None, :]).astype(BF16), pn.S, axis=0)
    block_hot_t = jnp.repeat((ncp_ids[:, None] == block_crop[None, :]).astype(BF16), pn.S, axis=1)

    sel, sel_t, sel_c, shifts = column_tables(pn)
    w, w_two = w_atrous.transpose(1, 0, 2), jnp.stack([w_point, w_pool])
    proj = w_proj.reshape(pn.C, pn.proj // pn.C, pn.width)
    proj = jnp.pad(proj, ((0, 0), (0, pn.piece - pn.proj // pn.C), (0, 0)))
    if not pn.exchange:
        w = lax.all_gather(jnp.concatenate([w, w_two], axis=0), "row", axis=1, tiled=True)
        w = lax.dynamic_slice_in_dim(w, slice_of(pn, x * pn.C + col) * pn.cs, pn.cs, axis=1)
        w, w_two = w[:POINT], w[POINT:]
    flat = jnp.concatenate([same.reshape(-1), widths_of(mid).astype(F32)])
    p, xs, w_own, means, p4, own_cot, pieces = conv_forward(
        pn, feats, w, w_two, cot, proj, flat, sel, hot_t, inv_counts
    )
    full_proj = pieces[:, :, :pn.proj // pn.C].transpose(1, 0, 2, 3).reshape(5 * pn.width, pn.width)
    q, q4, d_proj, res, d_gains, d_biases = norms(
        pn, p, p4, gains, biases, valid, (1.0 / pixels)[None], full_proj, own_cot, block_hot, block_hot_t, sel_t
    )
    dw, dx, dproj_sum = conv_backward(
        pn, q, xs, w_own, d_proj, q4, means, hot_rows, inv_counts, flat, lane_masks, shifts, sel_c
    )
    if pn.exchange:
        d_proj = dproj_sum
    else:
        whole = jnp.zeros((3 * GROUPS, channels, pn.width), BF16)
        whole = lax.dynamic_update_slice(whole, dw, (0, slice_of(pn, x * pn.C + col) * pn.cs, 0))
        whole = lax.psum(whole, "col")
        dw = lax.psum_scatter(whole, "row", scatter_dimension=1, tiled=True)
        d_proj = lax.psum(d_proj, "col")
        d_proj = lax.psum_scatter(d_proj.astype(F32), "row", scatter_dimension=0, tiled=True)
    result = res[:, :bc]
    d_features = dx.transpose(1, 0, 2)
    d_point = dw[POINT].astype(F32)
    d_atrous = dw[:POINT].astype(F32).transpose(1, 0, 2)
    d_pool = dw[POOL].astype(F32)
    return (result, d_features, d_point, d_atrous, d_pool, d_proj, d_gains, d_biases)


def solution(mesh):
    return jax.shard_map(
        per_device,
        mesh=mesh,
        in_specs=(
            P("row", "col", None),
            P(),
            P(),
            P("row", None),
            P("row", None, None),
            P("row", None),
            P("row", None),
            P(),
            P(),
            P("row", "col", None),
        ),
        out_specs=(
            P("row", "col", None),
            P("row", "col", None),
            P("row", None),
            P("row", None, None),
            P("row", None),
            P("row", None),
            P(),
            P(),
        ),
        check_vma=False,
    )
```

```python
import functools

import jax
import jax.numpy as jnp
import numpy as np
from jax import lax
from jax.experimental import pallas as pl
from jax.experimental.pallas import tpu as pltpu
from jax.sharding import PartitionSpec as P

EPSILON = 1e-05
MARGIN = 18
DILATIONS = (6, 12, 18)
MEMBERS = 8
TAPS = 29
POINT, POOL, GROUPS = 27, 28, 10
YIELD = 8
MESH = pl.DeviceIdType.MESH
F32 = jnp.float32
BF16 = jnp.bfloat16

def up_to(value, multiple):
    return -(-value // multiple) * multiple


class Plan:
    def __init__(self, rows_axis, cols_axis, h, bc, channels, width, crops):
        self.R, self.C = rows_axis, cols_axis
        self.h, self.bc, self.channels, self.width = h, bc, channels, width
        self.G = MEMBERS // self.C
        self.slabs = self.R // self.G
        self.H = self.G * h
        self.cols = bc * self.C
        self.S = up_to(self.cols, 8)
        self.rpb = self.H // MEMBERS
        self.px = self.rpb * self.S
        self.own = MEMBERS * self.px
        self.hb = MARGIN // self.rpb
        self.nb = MEMBERS + 2 * self.hb
        self.ext = self.nb * self.px
        self.bp = up_to(bc, 16)
        self.cs = channels // MEMBERS
        self.crops = crops
        self.ncp = up_to(crops, 16)
        self.exchange = self.slabs == self.C and self.R == MEMBERS
        self.steps = tuple(d // self.rpb for d in DILATIONS)
        self.proj = 5 * width // self.R
        self.piece = up_to(self.proj // self.C, 16)


def home_of(pn, col):
    if pn.C != 4:
        return col
    y, c = col // 2, lax.rem(col, 2)
    return (1 - y) * 3 * c + y * (1 + c)


def slice_of(pn, k):
    return pn.G * home_of(pn, lax.rem(k, pn.C)) + k // pn.C


def remote(src, dst, send, recv, device):
    return pltpu.make_async_remote_copy(
        src_ref=src, dst_ref=dst, send_sem=send, recv_sem=recv, device_id=device, device_id_type=MESH
    )


def greet_all(pn, row, col):
    total = pn.R * pn.C
    barrier = pltpu.get_barrier_semaphore()
    me = row * pn.C + col

    def hello(k, carry):
        other = lax.rem(me + k, total)
        pl.semaphore_signal(
            barrier, inc=1, device_id=(other // pn.C, lax.rem(other, pn.C)), device_id_type=MESH
        )
        return carry

    lax.fori_loop(1, total, hello, 0)
    pl.semaphore_wait(barrier, total - 1)


def dot(a, b):
    return jnp.dot(a, b, preferred_element_type=F32)


def dot_nt(a, b):
    return lax.dot_general(a, b, (((1,), (1,)), ((), ())), preferred_element_type=F32)


def dot_tn(a, b):
    return lax.dot_general(a, b, (((0,), (0,)), ((), ())), preferred_element_type=F32)


def split_dot(dot_fn, a, b):
    high = a.astype(BF16)
    low = (a - high.astype(F32)).astype(BF16)
    return dot_fn(high, b) + dot_fn(low, b)


def conv_kernel(pn, feats, w_in, w_two, cot, proj, masks, sel, hot_t, inv_counts,
                p_out, x_out, w_out, m_out, p4_out, cot_out, proj_out,
                ring, xs, wbuf, acc, pbuf, cbuf, sbuf, rbuf, cx,
                f_s, f_r, h_s, h_r, c_s, c_r, j_s, j_r, t_s, t_r, w_s, w_r, w_l, e_s,
                r1_s, r1_r, r2_s, r2_r, o_s):
    row, col = lax.axis_index("row"), lax.axis_index("col")
    slab, x = row // pn.G, lax.rem(row, pn.G)
    me = x * pn.C + col
    core, quad = lax.rem(col, 2), me // 2
    h, H, bp, px, n = pn.h, pn.H, pn.bp, pn.px, pn.slabs
    many = 4

    def member(s, k):
        return (s * pn.G + k // pn.C, lax.rem(k, pn.C))

    greet_all(pn, row, col)

    own_cols = pl.ds(pl.multiple_of(col * bp, bp), bp)
    own_rows = pl.ds(MARGIN + h * x, h)
    sent = []
    for kk in range(1, MEMBERS):
        other = lax.rem(me + kk, MEMBERS)
        c = remote(feats.at[slice_of(pn, other)], ring.at[own_rows, own_cols], f_s.at[kk], f_r.at[kk], member(slab, other))
        c.start()
        sent.append(c)
    keep = pltpu.make_async_copy(feats.at[slice_of(pn, me)], ring.at[own_rows, own_cols], f_r.at[0])
    keep.start()

    home = home_of(pn, col)
    source, rising, falling = slab == home, (slab > home) & (slab < n - 1), (slab < home) & (slab > 0)
    help_up, help_down = (slab == n - 2) & (col == 1), (slab == 1) & (col == 0)
    half_rows = pn.cs // 2

    order = (0, 1, 2, 3, 4, 5, 9, 6, 7, 8)

    def taps(g):
        return pl.ds(POINT, 2) if isinstance(g, int) and g == GROUPS - 1 else pl.ds(3 * g, 3)

    def given(g, rows):
        if isinstance(g, int) and g == GROUPS - 1:
            return w_two.at[:, rows]
        return w_in.at[taps(g), rows]

    def half_of(half):
        return pl.ds(half * half_rows, half_rows)

    def part_of(ref, g, half):
        return ref.at[taps(g), half_of(half)]

    def ship(g, half, up, own):
        to = slab + 1 if up else slab - 1
        return remote(given(g, half_of(half)) if own else part_of(wbuf, g, half), part_of(wbuf, g, half), w_s.at[int(up), half, g], w_r.at[half, g],
                      (to * pn.G + x, col))

    def assist(g, up):
        to = slab + 1 if up else slab - 1
        return remote(given(g, half_of(1)), part_of(wbuf, g, 1), e_s.at[g], w_r.at[1, g], (to * pn.G + x, col + 2))

    def own_copy(g):
        return pltpu.make_async_copy(given(g, pl.ds(0, pn.cs)), wbuf.at[taps(g)], w_l.at[g])

    def arrived(g):
        for half in (0, 1):
            at = part_of(wbuf, g, half)
            pltpu.make_async_copy(at, at, w_r.at[half, g]).wait()

    def pass_on(g):
        for role, up in ((rising, True), (falling, False)):
            @pl.when(role)
            def _(up=up):
                arrived(g)
                for half in (0, 1):
                    ship(g, half, up, False).start()

    def w_wait(g):
        if pn.exchange:
            @pl.when(source)
            def _():
                own_copy(g).wait()

            @pl.when(jnp.logical_not(source | rising | falling))
            def _():
                arrived(g)
        else:
            own_copy(g).wait()

    def each_shipment(g, act):
        for half in (0, 1):
            @pl.when(source & ((slab < n - 2) if half else (slab < n - 1)))
            def _(half=half):
                act(ship(g, half, True, True))

            @pl.when(source & ((slab > 1) if half else (slab > 0)))
            def _(half=half):
                act(ship(g, half, False, True))

        @pl.when(help_up)
        def _():
            act(assist(g, True))

        @pl.when(help_down)
        def _():
            act(assist(g, False))

    if pn.exchange:
        def begin(g, carry):
            each_shipment(g, lambda c: c.start())

            @pl.when(source)
            def _():
                own_copy(g).start()

            return carry
    else:
        def begin(g, carry):
            own_copy(g).start()
            return carry

    early = 6
    lax.fori_loop(0, early, begin, 0)

    cot_sent = []
    for cc in range(1, pn.C):
        cd = lax.rem(col + cc, pn.C)
        c = remote(cot.at[pl.ds(cd * pn.rpb, pn.rpb)], cx.at[:, own_cols], c_s.at[cc], c_r.at[cc], (row, cd))
        c.start()
        cot_sent.append(c)
    cot_keep = pltpu.make_async_copy(cot.at[pl.ds(col * pn.rpb, pn.rpb)], cx.at[:, own_cols], c_r.at[0])
    cot_keep.start()

    def proj_row(k):
        return remote(proj.at[col], proj_out.at[col, row], j_s.at[k], j_r.at[k], (lax.rem(row + k, pn.R), col))

    def proj_col(k):
        return remote(proj_out.at[col], proj_out.at[col], t_s.at[k], t_r.at[k], (row, lax.rem(col + k, pn.C)))

    def proj_begin(k, carry):
        proj_row(k).start()
        return carry

    def proj_wait(k, carry):
        proj_row(k).wait()
        return carry

    lax.fori_loop(1, pn.R, proj_begin, 0)
    proj_keep = pltpu.make_async_copy(proj.at[col], proj_out.at[col, row], j_r.at[0])
    proj_keep.start()

    @pl.when(slab == 0)
    def _():
        ring[pl.ds(0, MARGIN)] = jnp.zeros((MARGIN, pn.C * bp, pn.cs), BF16)

    @pl.when(slab == n - 1)
    def _():
        ring[pl.ds(MARGIN + H, MARGIN)] = jnp.zeros((MARGIN, pn.C * bp, pn.cs), BF16)

    def pass_many(first, end):
        if pn.exchange:
            for k in range(first, end):
                pass_on(order[k])

    pass_many(0, 3)
    for c in sent:
        c.wait()
    keep.wait()

    def margin_down():
        return remote(ring.at[pl.ds(MARGIN, MARGIN)], ring.at[pl.ds(MARGIN + H, MARGIN)], h_s.at[0], h_r.at[0],
                      member(slab - 1, me))

    def margin_up():
        return remote(ring.at[pl.ds(H, MARGIN)], ring.at[pl.ds(0, MARGIN)], h_s.at[1], h_r.at[1], member(slab + 1, me))

    @pl.when(slab > 0)
    def _():
        margin_down().start()

    @pl.when(slab < n - 1)
    def _():
        margin_up().start()

    begin(GROUPS - 1, 0)
    lax.fori_loop(early, GROUPS - 1, begin, 0)

    column = lax.broadcasted_iota(jnp.int32, (pn.S, pn.cs), 0).astype(F32)

    def assemble(rp, carry):
        pair = ring[pl.ds(2 * rp, 2)].reshape(2 * pn.C * bp, pn.cs)
        moved = dot(sel[...], pair)
        at = pl.multiple_of(rp * 2 * pn.S, 16)
        wide = [masks[6 * H + 2 * rp + r] for r in range(2)]
        for v in range(7):
            rows = [
                jnp.where(column + float(DILATIONS[0] * (v - 3)) < wide[r], moved[(2 * v + r) * pn.S:(2 * v + r + 1) * pn.S], 0.0)
                for r in range(2)
            ]
            xs[v, pl.ds(at, 2 * pn.S)] = jnp.concatenate(rows, axis=0).astype(BF16)
        return carry

    lax.fori_loop(MARGIN // 2, (MARGIN + H) // 2, assemble, 0, unroll=6)
    pass_many(3, 5)
    for c in cot_sent:
        c.wait()
    cot_keep.wait()
    for rp in range(pn.rpb // 2):
        pair = cx[2 * rp:2 * rp + 2].reshape(2 * pn.C * bp, pn.width)
        cot_out[pl.ds(rp * 2 * pn.S, 2 * pn.S)] = dot(sel[pl.ds(3 * 2 * pn.S, 2 * pn.S)], pair).astype(BF16)
    lax.fori_loop(1, pn.R, proj_wait, 0)
    proj_keep.wait()
    for k in range(1, pn.C):
        proj_col(k).start()
    pass_many(5, 6)

    @pl.when(slab > 0)
    def _():
        margin_down().wait_send()
        margin_up().wait_recv()

    @pl.when(slab < n - 1)
    def _():
        margin_up().wait_send()
        margin_down().wait_recv()

    lax.fori_loop(0, MARGIN // 2, assemble, 0, unroll=3)
    lax.fori_loop((MARGIN + H) // 2, pn.nb * pn.rpb // 2, assemble, 0, unroll=3)
    x_save = pltpu.make_async_copy(xs, x_out, o_s.at[0])
    x_save.start()

    def first_stage(slot):
        return remote(pbuf.at[slot, :, 1 - core], cbuf.at[slot], r1_s.at[slot], r1_r.at[slot], (row, col + 1 - 2 * core))

    def second_stage(slot, i):
        q = lax.rem(quad + i, MEMBERS // 2)
        return remote(sbuf.at[slot, i - 1], rbuf.at[slot, i - 1], r2_s.at[slot, i - 1], r2_r.at[slot, i - 1],
                      member(slab, 2 * q + core))

    def middle(slot):
        first_stage(slot).wait()
        for i in (1, 2, 3, 0):
            q = lax.rem(quad + i, MEMBERS // 2)
            s = pbuf[slot, q, core].astype(F32) + cbuf[slot, q].astype(F32)
            if i == 0:
                p_out[slot] = s
            else:
                sbuf[slot, i - 1] = s.astype(BF16)
                second_stage(slot, i).start()

    def last(slot):
        total = p_out[slot]
        for i in range(1, MEMBERS // 2):
            second_stage(slot, i).wait()
            total = total + rbuf[slot, i - 1].astype(F32)
        p_out[slot] = total

    def scatter(slot, rb, y):
        for r in range(many):
            pbuf[slot, (many * rb + r) // 2, r % 2] = y[r * px:(r + 1) * px].astype(BF16)

    def far(k):
        if k in (2, 4, 6, 8):
            pass_many(5 + k // 2, 6 + k // 2)
        w_wait(order[k])

    def point(rb, carry):
        at = pl.ds(pl.multiple_of((rb * many + pn.hb) * px, 16), many * px)
        scatter(0, rb, dot(xs[3, at], wbuf[POINT]))
        return carry

    for branch in (1, 2, 3):
        step = pn.steps[branch - 1]
        if branch == 3:
            far(6)
            lax.fori_loop(0, MEMBERS // many, point, 0)
            first_stage(0).start()
            middle(2)
        for i in (-1, 0, 1):
            g = 3 * (branch - 1) + i + 1
            mask_at = (2 * (branch - 1) + (i + 1) // 2) * H
            far(g + branch // 3)

            def block(rb, carry, step=step, i=i, g=g, mask_at=mask_at, branch=branch):
                at = pl.multiple_of(rb * many * px, 16)
                window = pl.ds(pl.multiple_of((rb * many + pn.hb + i * step) * px, 16), many * px)
                y = dot(xs[3 - branch, window], wbuf[3 * g])
                y = y + dot(xs[3, window], wbuf[3 * g + 1])
                y = y + dot(xs[3 + branch, window], wbuf[3 * g + 2])
                if i != 0:
                    y = jnp.concatenate(
                        [y[r * pn.S:(r + 1) * pn.S] * masks[mask_at + rb * many * pn.rpb + r]
                         for r in range(many * pn.rpb)], axis=0
                    )
                if i > -1:
                    y = y + acc[pl.ds(at, many * px)]
                if i < 1:
                    acc[pl.ds(at, many * px)] = y
                else:
                    scatter(branch, rb, y)
                return carry

            lax.fori_loop(0, MEMBERS // many, block, 0)
            if i == 0 and branch > 1:
                middle(branch - 1 if branch == 2 else 0)
        first_stage(branch).start()

    sums = dot(hot_t[...], xs[3, pl.ds(pn.hb * px, pn.own)])
    means = sums * inv_counts[...]
    m_out[...] = means
    p4_out[...] = split_dot(dot, means, wbuf[POOL])
    w_save = pltpu.make_async_copy(wbuf, w_out, o_s.at[1])
    w_save.start()
    middle(3)
    for slot in (1, 2, 0):
        last(slot)
    for k in range(1, pn.C):
        proj_col(k).wait()
    if pn.exchange:
        def settled(g, carry):
            each_shipment(g, lambda c: c.wait_send())
            for role, up in ((rising, True), (falling, False)):
                @pl.when(role)
                def _(up=up):
                    for half in (0, 1):
                        ship(g, half, up, False).wait_send()
            return carry

        lax.fori_loop(0, GROUPS - 1, settled, 0)
        settled(GROUPS - 1, 0)
    last(3)
    x_save.wait()
    w_save.wait()


def conv_forward(pn, feats, w, w_two, cot, proj, masks, sel, hot_t, inv_counts):
    half = MEMBERS // 2
    dma = pltpu.SemaphoreType.DMA
    vmem = pl.BlockSpec(memory_space=pltpu.VMEM)
    hbm = pl.BlockSpec(memory_space=pl.ANY)
    shape = jax.ShapeDtypeStruct
    return pl.pallas_call(
        functools.partial(conv_kernel, pn),
        out_shape=(
            shape((4, pn.px, pn.width), F32),
            shape((7, pn.ext, pn.cs), BF16),
            shape((TAPS, pn.cs, pn.width), BF16),
            shape((pn.ncp, pn.cs), F32),
            shape((pn.ncp, pn.width), F32),
            shape((pn.px, pn.width), BF16),
            shape((pn.C, pn.R, pn.piece, pn.width), BF16),
        ),
        in_specs=[hbm, hbm, hbm, hbm, hbm, pl.BlockSpec(memory_space=pltpu.SMEM), vmem, vmem, vmem],
        out_specs=(vmem, hbm, hbm, vmem, vmem, vmem, vmem),
        scratch_shapes=[
            pltpu.VMEM((pn.nb * pn.rpb, pn.C * pn.bp, pn.cs), BF16),
            pltpu.VMEM((7, pn.ext, pn.cs), BF16),
            pltpu.VMEM((TAPS, pn.cs, pn.width), BF16),
            pltpu.VMEM((pn.own, pn.width), F32),
            pltpu.VMEM((4, half, 2, pn.px, pn.width), BF16),
            pltpu.VMEM((4, half, pn.px, pn.width), BF16),
            pltpu.VMEM((4, half - 1, pn.px, pn.width), BF16),
            pltpu.VMEM((4, half - 1, pn.px, pn.width), BF16),
            pltpu.VMEM((pn.rpb, pn.C * pn.bp, pn.width), BF16),
            dma((MEMBERS,)), dma((MEMBERS,)), dma((2,)), dma((2,)), dma((pn.C,)), dma((pn.C,)),
            dma((pn.R,)), dma((pn.R,)), dma((pn.C,)), dma((pn.C,)),
            dma((2, 2, GROUPS)), dma((2, GROUPS)), dma((GROUPS,)), dma((GROUPS,)),
            dma((4,)), dma((4,)), dma((4, 3)), dma((4, 3)), dma((2,)),
        ],
        compiler_params=pltpu.CompilerParams(collective_id=0, has_side_effects=True, vmem_limit_bytes=60 * 2**20),
        name="conv_forward",
    )(feats, w, w_two, cot, proj, masks, sel, hot_t, inv_counts)


def norm_kernel(pn, p, p4_in, gains, biases, valid, pixels, w_proj, cot, hot, hot_t, sel_t,
                q_out, q4_out, dproj_out, res_out, dg_out, db_out,
                norm, slope, hbuf, gact, dh4, rx,
                a1, b1, a2, b2, a3, b3, a4, b4, as_s, as_r, bs_s, bs_r, e_s, e_r):
    row, col = lax.axis_index("row"), lax.axis_index("col")
    slab, x = row // pn.G, lax.rem(row, pn.G)
    me = x * pn.C + col
    crops = float(pn.crops)
    v = valid[...]
    inv_px = pixels[0]
    width, bp = pn.width, pn.bp

    def member(s, k):
        return (s * pn.G + k // pn.C, lax.rem(k, pn.C))

    barrier = pltpu.get_barrier_semaphore()
    for kk in range(1, MEMBERS):
        pl.semaphore_signal(barrier, inc=1, device_id=member(slab, lax.rem(me + kk, MEMBERS)), device_id_type=MESH)

    def hello(k, carry):
        pl.semaphore_signal(barrier, inc=1, device_id=member(lax.rem(slab + k, pn.slabs), me), device_id_type=MESH)
        return carry

    lax.fori_loop(1, pn.slabs, hello, 0)

    def peer_a(n, abuf, kk):
        return remote(abuf.at[me], abuf.at[me], as_s.at[n, kk], as_r.at[n, kk], member(slab, lax.rem(me + kk, MEMBERS)))

    def peer_b(n, bbuf, k):
        return remote(bbuf.at[slab], bbuf.at[slab], bs_s.at[n, k], bs_r.at[n, k], member(lax.rem(slab + k, pn.slabs), me))

    def reduce_start(n, abuf):
        for kk in range(1, MEMBERS):
            peer_a(n, abuf, kk).start()

    def reduce_end(n, abuf, bbuf):
        for kk in range(1, MEMBERS):
            peer_a(n, abuf, kk).wait()
        total = abuf[0]
        for k in range(1, MEMBERS):
            total = total + abuf[k]
        bbuf[slab] = total
        for k in range(1, pn.slabs):
            peer_b(n, bbuf, k).start()
        for k in range(1, pn.slabs):
            peer_b(n, bbuf, k).wait()
        total = bbuf[0]
        for k in range(1, pn.slabs):
            total = total + bbuf[k]
        return total

    def column_sum(value):
        return jnp.sum(value, axis=0, keepdims=True)

    for b in range(4):
        pv = p[b] * v
        a1[me, pl.ds(b, 1)] = column_sum(pv)
        a1[me, pl.ds(4 + b, 1)] = column_sum(pv * p[b])
    a1[me, pl.ds(8, pn.ncp)] = p4_in[...]
    pl.semaphore_wait(barrier, MEMBERS - 1 + pn.slabs - 1)
    reduce_start(0, a1)
    total = reduce_end(0, a1, b1)
    inv = []
    for b in range(4):
        centre = total[b:b + 1] * inv_px
        scale = lax.rsqrt(total[4 + b:5 + b] * inv_px - centre * centre + EPSILON)
        inv.append(scale)
        n = (p[b] - centre) * scale
        u = gains[b:b + 1] * n + biases[b:b + 1]
        s = jax.nn.sigmoid(u)
        norm[b] = n
        slope[b] = s * (1.0 + u * (1.0 - s))
        hbuf[b] = (u * s).astype(BF16)
    p4 = total[8:8 + pn.ncp]
    centre4 = column_sum(p4) * (1.0 / crops)
    inv4 = lax.rsqrt(column_sum(p4 * p4) * (1.0 / crops) - centre4 * centre4 + EPSILON)
    n4 = (p4 - centre4) * inv4
    u4 = gains[4:5] * n4 + biases[4:5]
    s4 = jax.nn.sigmoid(u4)
    slope4 = s4 * (1.0 + u4 * (1.0 - s4))
    hbuf[4] = dot(hot[...], (u4 * s4).astype(BF16)).astype(BF16)

    p5 = dot(hbuf[0], w_proj[pl.ds(0, width)])
    for b in range(1, 5):
        p5 = p5 + dot(hbuf[b], w_proj[pl.ds(b * width, width)])
    pv = p5 * v
    a2[me, pl.ds(0, 1)] = column_sum(pv)
    a2[me, pl.ds(1, 1)] = column_sum(pv * p5)
    a2[me, pl.ds(2, 6)] = jnp.zeros((6, width), F32)
    reduce_start(1, a2)
    total = reduce_end(1, a2, b2)
    centre5 = total[0:1] * inv_px
    inv5 = lax.rsqrt(total[1:2] * inv_px - centre5 * centre5 + EPSILON)
    n5 = (p5 - centre5) * inv5
    u5 = gains[5:6] * n5 + biases[5:6]
    s5 = jax.nn.sigmoid(u5)
    g5 = cot[...].astype(F32) * v * (s5 * (1.0 + u5 * (1.0 - s5)))
    norm[4] = n5
    gact[4] = g5
    a3[me, pl.ds(0, 1)] = column_sum(g5)
    a3[me, pl.ds(1, 1)] = column_sum(g5 * n5)
    a3[me, pl.ds(2, 6)] = jnp.zeros((6, width), F32)
    reduce_start(2, a3)
    hbuf[5] = (v * u5 * s5).astype(BF16)
    for rp in range(pn.rpb // 2):
        pair = hbuf[5, pl.ds(rp * 2 * pn.S, 2 * pn.S)]
        rx[2 * rp:2 * rp + 2] = dot(sel_t[...], pair).astype(BF16).reshape(2, pn.C * bp, width)
    back = []
    for cc in range(1, pn.C):
        cd = lax.rem(col + cc, pn.C)
        c = remote(rx.at[:, pl.ds(pl.multiple_of(cd * bp, bp), bp)], res_out.at[pl.ds(col * pn.rpb, pn.rpb)],
                   e_s.at[cc], e_r.at[cc], (row, cd))
        c.start()
        back.append(c)
    c = pltpu.make_async_copy(rx.at[:, pl.ds(pl.multiple_of(col * bp, bp), bp)], res_out.at[pl.ds(col * pn.rpb, pn.rpb)],
                              e_r.at[0])
    c.start()
    back.append(c)
    total = reduce_end(2, a3, b3)
    db5, dg5 = total[0:1], total[1:2]
    q5 = (gains[5:6] * inv5 * (gact[4] - v * (db5 + norm[4] * dg5) * inv_px)).astype(BF16)
    hbuf[5] = q5

    for b in range(4):
        g = dot_nt(q5, w_proj[pl.ds(b * width, width)]) * slope[b]
        gact[b] = g
        a4[me, pl.ds(b, 1)] = column_sum(g)
        a4[me, pl.ds(4 + b, 1)] = column_sum(g * norm[b])
    dh4[...] = dot_nt(q5, w_proj[pl.ds(4 * width, width)])
    high = dh4[...].astype(BF16)
    low = (dh4[...] - high.astype(F32)).astype(BF16)
    a4[me, pl.ds(8, pn.ncp)] = dot(hot_t[...], high) + dot(hot_t[...], low)
    reduce_start(3, a4)
    for b in range(5):
        dproj_out[pl.ds(b * width, width)] = dot_tn(hbuf[b], hbuf[5]).astype(BF16)
    total = reduce_end(3, a4, b4)
    for b in range(4):
        db, dg = total[b:b + 1], total[4 + b:5 + b]
        db_out[pl.ds(b, 1)] = db
        dg_out[pl.ds(b, 1)] = dg
        q_out[b] = (gains[b:b + 1] * inv[b] * (gact[b] - v * (db + norm[b] * dg) * inv_px)).astype(BF16)
    g4 = total[8:8 + pn.ncp] * slope4
    db4, dg4 = column_sum(g4), column_sum(g4 * n4)
    db_out[pl.ds(4, 1)] = db4
    dg_out[pl.ds(4, 1)] = dg4
    db_out[pl.ds(5, 1)] = db5
    dg_out[pl.ds(5, 1)] = dg5
    q4_out[...] = (gains[4:5] * inv4 * (g4 - (db4 + n4 * dg4) * (1.0 / crops))).astype(BF16)
    for c in back:
        c.wait()


def norms(pn, p, p4, gains, biases, valid, pixels, w_proj, cot, hot, hot_t, sel_t):
    dma = pltpu.SemaphoreType.DMA
    vmem = pl.BlockSpec(memory_space=pltpu.VMEM)
    shape = jax.ShapeDtypeStruct
    big, small = 8 + pn.ncp, 8
    bufs = []
    for n in (big, small, small, big):
        bufs += [pltpu.VMEM((MEMBERS, n, pn.width), F32), pltpu.VMEM((pn.slabs, n, pn.width), F32)]
    return pl.pallas_call(
        functools.partial(norm_kernel, pn),
        out_shape=(
            shape((4, pn.px, pn.width), BF16),
            shape((pn.ncp, pn.width), BF16),
            shape((5 * pn.width, pn.width), BF16),
            shape((pn.h, pn.bp, pn.width), BF16),
            shape((6, pn.width), F32),
            shape((6, pn.width), F32),
        ),
        in_specs=[vmem] * 5 + [pl.BlockSpec(memory_space=pltpu.SMEM)] + [vmem] * 5,
        out_specs=(vmem,) * 6,
        scratch_shapes=[
            pltpu.VMEM((5, pn.px, pn.width), F32),
            pltpu.VMEM((4, pn.px, pn.width), F32),
            pltpu.VMEM((6, pn.px, pn.width), BF16),
            pltpu.VMEM((5, pn.px, pn.width), F32),
            pltpu.VMEM((pn.px, pn.width), F32),
            pltpu.VMEM((pn.rpb, pn.C * pn.bp, pn.width), BF16),
            *bufs,
            dma((4, MEMBERS)), dma((4, MEMBERS)), dma((4, pn.slabs)), dma((4, pn.slabs)), dma((pn.C,)), dma((pn.C,)),
        ],
        compiler_params=pltpu.CompilerParams(collective_id=1, has_side_effects=True, vmem_limit_bytes=48 * 2**20),
        name="norms",
    )(p, p4, gains, biases, valid, pixels, w_proj, cot, hot, hot_t, sel_t)


def back_kernel(pn, q_in, x_in, w_in, dproj_in, q4, means, hot_rows, inv_counts, masks, lane_masks, shifts, sel_t,
                dw_out, dx_out, dproj_out,
                xs, wbuf, qraw, qs, qt, dxe, dwbuf, inn, hsend, hrecv, pack, pooled_rows, dp1, dps, dp2, dpf,
                l_s, q_s, q_r, k_s, k_r, f_s, f_r, n_s, n_r, e_s, e_r, g_s, g_r, b_s, b_r, turn_sem, h_s, h_r, x_s, x_r,
                p1_s, p1_r, p2_s, p2_r, p3_s, p3_r):
    row, col = lax.axis_index("row"), lax.axis_index("col")
    slab, x = row // pn.G, lax.rem(row, pn.G)
    me = x * pn.C + col
    core, quad = lax.rem(col, 2), me // 2
    h, H, bp, px, S, n = pn.h, pn.H, pn.bp, pn.px, pn.S, pn.slabs
    half = MEMBERS // 2
    many = 4
    partner = (row, col + 1 - 2 * core)

    def member(s, k):
        return (s * pn.G + k // pn.C, lax.rem(k, pn.C))

    load_x = pltpu.make_async_copy(x_in, xs, l_s.at[0])
    load_w = pltpu.make_async_copy(w_in, wbuf, l_s.at[1])
    load_x.start()
    load_w.start()
    greet_all(pn, row, col)

    slots = (1, 2, 3, 0)
    own_px = pl.ds(pl.multiple_of(me * px, 16), px)
    along_y, along_x = (row, lax.rem(col + 2, pn.C)), (slab * pn.G + lax.rem(x + 1, pn.G), col)
    from_y = x * pn.C + lax.rem(col + 2, pn.C)
    from_x = lax.rem(me + pn.C, MEMBERS)
    from_xy = lax.rem(from_y + pn.C, MEMBERS)

    def block_of(slot, k):
        return qraw.at[slot, pl.ds(pl.multiple_of(k * px, 16), px)]

    def to_y(slot):
        return remote(q_in.at[slot], qraw.at[slot, own_px], q_s.at[slot, 0], q_r.at[slot, 0], along_y)

    def to_x(slot):
        return remote(q_in.at[slot], qraw.at[slot, own_px], q_s.at[slot, 1], q_r.at[slot, 1], along_x)

    def on_to_x(slot):
        if slot == slots[0]:
            return remote(q_in.at[slot], qraw.at[slot, own_px], q_s.at[slot, 2], q_r.at[slot, 2], member(slab, from_xy))
        return remote(block_of(slot, from_y), block_of(slot, from_y), q_s.at[slot, 2], q_r.at[slot, 2], along_x)

    def to_partner(slot):
        return remote(q_in.at[slot], qraw.at[slot, own_px], k_s.at[slot], k_r.at[slot], partner)

    def passed(slot, i):
        at = block_of(slot, (from_y, from_x, from_xy)[i])
        return remote(at, at, f_s.at[slot, i], f_r.at[slot, i], partner)

    def kept(slot):
        return pltpu.make_async_copy(q_in.at[slot], qraw.at[slot, own_px], l_s.at[2 + slot])

    to_x(slots[0]).start()
    on_to_x(slots[0]).start()
    for slot in slots:
        to_y(slot).start()
        to_partner(slot).start()
        kept(slot).start()

    block_rows = 5 * pn.width // MEMBERS
    home_slab = me // pn.G

    def dproj_slab(kk):
        other = lax.rem(me + kk, MEMBERS)
        return remote(dproj_in.at[pl.ds(pl.multiple_of(other * block_rows, 16), block_rows)], dp1.at[me],
                      p1_s.at[kk], p1_r.at[kk], member(slab, other))

    def dproj_own():
        return pltpu.make_async_copy(dproj_in.at[pl.ds(pl.multiple_of(me * block_rows, 16), block_rows)], dp1.at[me],
                                     p1_r.at[0])

    def dproj_home():
        return remote(dps, dp2.at[slab], p2_s.at[0], p2_r.at[slab], member(home_slab, me))

    def dproj_give(c):
        return remote(dpf, dproj_out, p3_s.at[c], p3_r.at[0], (slab * pn.G + lax.rem(me, pn.G), c))

    def clear(rb, carry):
        dxe[pl.ds(pl.multiple_of(rb * px, 16), px)] = jnp.zeros((px, pn.cs), F32)
        return carry

    lax.fori_loop(0, pn.nb, clear, 0)

    def receive_y(slot):
        to_y(slot).wait()
        if slot != slots[0]:
            on_to_x(slot).start()
        passed(slot, 0).start()
        if slot != slots[-1]:
            to_x(slots[slots.index(slot) + 1]).start()

    def receive_x(slot):
        to_x(slot).wait()
        passed(slot, 1).start()
        on_to_x(slot).wait()
        passed(slot, 2).start()

    def received(slot):
        to_partner(slot).wait()
        kept(slot).wait()
        for i in range(3):
            passed(slot, i).wait()

    home = home_of(pn, col)
    closing, rising, falling = slab == home, slab < home, slab > home
    first = (slab == 0) | (slab == n - 1)
    half_rows = pn.cs // 2
    detour_up, detour_down = (slab == 0) & (col == 2), (slab == n - 1) & (col == 3)
    yielding = first & jnp.logical_not(closing | detour_up | detour_down)
    relay_up, relay_down = (slab == 0) & (col == 0), (slab == n - 1) & (col == 1)

    def taps(g):
        return pl.ds(POINT, 2) if isinstance(g, int) and g == GROUPS - 1 else pl.ds(3 * g, 3)

    def part_of(ref, g, half):
        return ref.at[taps(g), pl.ds(half * half_rows, half_rows)]

    def link(g, half, up):
        side, to = (0, slab + 1) if up else (1, slab - 1)
        return remote(part_of(dwbuf, g, half), part_of(inn.at[side], g, half), n_s.at[half, g], n_r.at[side, half, g],
                      (to * pn.G + x, col))

    def detour(g, up):
        side = 0 if up else 1
        return remote(part_of(dwbuf, g, 1), part_of(inn.at[side], g, 1), n_s.at[1, g], e_r.at[g], (row, col - 2))

    def relay(g, up):
        side, to = (0, slab + 1) if up else (1, slab - 1)
        return remote(part_of(inn.at[side], g, 1), part_of(inn.at[side], g, 1), e_s.at[g], n_r.at[side, 1, g],
                      (to * pn.G + x, col))

    def early_links(g, act):
        for going, up, around in ((rising, True, detour_up), (falling, False, detour_down)):
            @pl.when(going & jnp.logical_not(around))
            def _(up=up):
                for half in (0, 1):
                    act(link(g, half, up))

            @pl.when(around)
            def _(up=up):
                act(detour(g, up))

    def late_links(g, act):
        for around, up in ((detour_up, True), (detour_down, False)):
            @pl.when(around)
            def _(up=up):
                act(link(g, 0, up))

    def arrived(g, side):
        for half in (0, 1):
            at = part_of(inn.at[side], g, half)
            pltpu.make_async_copy(at, at, n_r.at[side, half, g]).wait()

    def add(g, side):
        dwbuf[taps(g)] = (dwbuf[taps(g)].astype(F32) + inn[side, taps(g)].astype(F32)).astype(BF16)

    close_a, close_b = closing & jnp.logical_not(first), ((slab == 1) & (col == 0)) | ((slab == n - 2) & (col == 1))
    end_closing, end_getting = closing & first, first & (home_of(pn, lax.rem(col + 2, pn.C)) == slab)
    across = (row, lax.rem(col + 2, pn.C))

    def share_y(g, half, src):
        return remote(src, part_of(dw_out, g, half), g_s.at[0, half, g], g_r.at[half, g], across)

    def share_core(g, half, src):
        return remote(src, part_of(dw_out, g, half), g_s.at[1, half, g], g_r.at[half, g], partner)

    def share_on(g, half):
        return remote(part_of(dw_out, g, half), part_of(dw_out, g, half), g_s.at[0, half, g], g_r.at[half, g], partner)

    def share(g, half, src):
        share_y(g, half, src).start()
        share_core(g, half, src).start()
        pltpu.make_async_copy(src, part_of(dw_out, g, half), g_r.at[half, g]).start()

    def landed(g, half):
        at = part_of(dw_out, g, half)
        pltpu.make_async_copy(at, at, g_r.at[half, g]).wait()

    def partial(g, side):
        return remote(part_of(dwbuf, g, 1), part_of(inn.at[1 - side], g, 0), b_s.at[g], b_r.at[g], (row, col - 2))

    rows_of = (pl.ds(0, half_rows), pl.ds(half_rows, half_rows))

    def from_far(g):
        for here, side in ((slab == 1, 1), (slab == n - 2, 0)):
            @pl.when(close_a & here)
            def _(side=side):
                arrived(g, side)
                add(g, side)
                partial(g, side).start()

    def close_half(g):
        for here, side in ((slab == 1, 0), (slab == n - 2, 1)):
            @pl.when(close_a & here)
            def _(side=side):
                at = part_of(inn.at[side], g, 0)
                pltpu.make_async_copy(at, at, n_r.at[side, 0, g]).wait()
                dwbuf[taps(g), rows_of[0]] = (
                    dwbuf[taps(g), rows_of[0]].astype(F32) + inn[side, taps(g), rows_of[0]].astype(F32)
                ).astype(BF16)
                share(g, 0, part_of(dwbuf, g, 0))

            @pl.when(close_b & here)
            def _(side=side):
                at = part_of(inn.at[side], g, 1)
                pltpu.make_async_copy(at, at, n_r.at[side, 1, g]).wait()
                at = part_of(inn.at[side], g, 0)
                pltpu.make_async_copy(at, at, b_r.at[g]).wait()
                inn[side, taps(g), rows_of[1]] = (
                    inn[side, taps(g), rows_of[1]].astype(F32) + inn[side, taps(g), rows_of[0]].astype(F32)
                ).astype(BF16)
                share(g, 1, part_of(inn.at[side], g, 1))

    def give_way():
        @pl.when(yielding)
        def _():
            for g in range(YIELD):
                early_links(g, lambda c: c.wait_send())
            pl.semaphore_signal(turn_sem, inc=1, device_id=partner, device_id_type=MESH)

        @pl.when(detour_up | detour_down)
        def _():
            pl.semaphore_wait(turn_sem, 1)

        for g in range(GROUPS):
            late_links(g, lambda c: c.start())

    def relay_all():
        for role, up in ((relay_up, True), (relay_down, False)):
            @pl.when(role)
            def _(up=up):
                pl.semaphore_wait(turn_sem, 1)
                for g in range(GROUPS):
                    at = part_of(inn.at[0 if up else 1], g, 1)
                    pltpu.make_async_copy(at, at, e_r.at[g]).wait()
                    relay(g, up).start()

    def pass_on(g):
        for going, up in ((rising, True), (falling, False)):
            @pl.when(going & jnp.logical_not(first))
            def _(up=up):
                arrived(g, 0 if up else 1)
                add(g, 0 if up else 1)
                for half in (0, 1):
                    link(g, half, up).start()

    def close(g):
        for here, side in ((slab == 0, 1), (slab == n - 1, 0)):
            @pl.when(end_closing & here)
            def _(side=side):
                arrived(g, side)
                add(g, side)
                for half in (0, 1):
                    share(g, half, part_of(dwbuf, g, half))

    def serve(g):
        if not pn.exchange:
            return
        if g < GROUPS:
            pass_on(g)
        if g > 1:
            close(g - 2)
            from_far(g - 2)

    def last_round(g):
        if g < GROUPS:
            close_half(g)
        if g > 1:
            for half, role in ((0, end_getting | close_b), (1, end_getting | close_a)):
                @pl.when(role)
                def _(half=half):
                    landed(g - 2, half)
                    share_on(g - 2, half).start()

    def start_group(g):
        if not pn.exchange:
            return

        @pl.when(first)
        def _():
            early_links(g, lambda c: c.start())

    def weight_gradients(branch):
        qt[...] = qraw[branch].T
        for i in (-1, 0, 1):
            g = 3 * (branch - 1) + i + 1
            q_turned = qt[...]
            if i != 0:
                q_turned = q_turned * lane_masks[pl.ds(2 * (branch - 1) + (i + 1) // 2, 1)]
            window = pl.ds((pn.hb + i * pn.steps[branch - 1]) * px, pn.own)
            for j in (-1, 0, 1):
                dwbuf[3 * g + j + 1] = dot(q_turned, xs[3 + j * branch, window]).T.astype(BF16)
            if branch < 3:
                start_group(g)

    def feature_gradients(branch):
        def turn(rp, carry):
            at = pl.multiple_of(rp * 2 * S, 16)
            moved = dot(shifts[pl.ds((branch - 1) * 4 * S, 4 * S)], qraw[branch, pl.ds(at, 2 * S)]).astype(BF16)
            qs[branch - 1, 0, pl.ds(at, 2 * S)] = moved[:2 * S]
            qs[branch - 1, 1, pl.ds(at, 2 * S)] = moved[2 * S:]
            return carry

        lax.fori_loop(0, H // 2, turn, 0, unroll=6)
        for i in (-1, 0, 1):
            g = 3 * (branch - 1) + i + 1
            mask_at = (2 * (branch - 1) + (i + 1) // 2) * H

            def block(rb, carry, i=i, g=g, mask_at=mask_at):
                at = pl.ds(pl.multiple_of(rb * many * px, 16), many * px)
                y = dot_nt(qs[branch - 1, 0, at], wbuf[3 * g])
                y = y + dot_nt(qraw[branch, at], wbuf[3 * g + 1])
                y = y + dot_nt(qs[branch - 1, 1, at], wbuf[3 * g + 2])
                if i != 0:
                    y = jnp.concatenate(
                        [y[r * S:(r + 1) * S] * masks[mask_at + rb * many * pn.rpb + r] for r in range(many * pn.rpb)], axis=0
                    )
                to = pl.ds(pl.multiple_of((rb * many + pn.hb + i * pn.steps[branch - 1]) * px, 16), many * px)
                dxe[to] = dxe[to] + y
                return carry

            lax.fori_loop(0, MEMBERS // many, block, 0)

    receive_y(1)
    receive_y(2)
    load_x.wait()
    load_w.wait()
    receive_x(1)
    received(1)
    weight_gradients(1)
    receive_y(3)
    receive_x(2)
    feature_gradients(1)
    receive_y(0)
    received(2)
    weight_gradients(2)
    receive_x(3)
    serve(0)
    feature_gradients(2)
    received(3)
    receive_x(0)
    if pn.exchange:
        for kk in range(1, MEMBERS):
            dproj_slab(kk).start()
        dproj_own().start()
    serve(1)
    weight_gradients(3)
    serve(2)
    feature_gradients(3)

    hsend[0] = dxe[pl.ds(0, pn.hb * px)].astype(BF16)
    hsend[1] = dxe[pl.ds((pn.hb + MEMBERS) * px, pn.hb * px)].astype(BF16)

    @pl.when(slab > 0)
    def _():
        remote(hsend.at[0], hrecv.at[1], h_s.at[0], h_r.at[1], member(slab - 1, me)).start()

    @pl.when(slab < n - 1)
    def _():
        remote(hsend.at[1], hrecv.at[0], h_s.at[1], h_r.at[0], member(slab + 1, me)).start()

    for g in (6, 7, 8):
        start_group(g)
    serve(3)

    if pn.exchange:
        for kk in range(1, MEMBERS):
            dproj_slab(kk).wait()
        dproj_own().wait()
        total = dp1[0].astype(F32)
        for m in range(1, MEMBERS):
            total = total + dp1[m].astype(F32)
        dps[...] = total.astype(BF16)

        @pl.when(slab != home_slab)
        def _():
            dproj_home().start()

        @pl.when(slab == home_slab)
        def _():
            pltpu.make_async_copy(dps, dp2.at[slab], p2_r.at[slab]).start()

    received(0)
    dwbuf[POOL] = dot_tn(means[...].astype(BF16), q4[...]).astype(BF16)
    dwbuf[POINT] = dot(qraw[0].T, xs[3, pl.ds(pn.hb * px, pn.own)]).T.astype(BF16)
    start_group(GROUPS - 1)
    serve(4)
    pooled = dot_nt(q4[...], wbuf[POOL]) * inv_counts[...]
    pooled_high = pooled.astype(BF16)
    pooled_low = (pooled - pooled_high.astype(F32)).astype(BF16)
    pooled_rows[...] = dot(hot_rows[...], pooled_high) + dot(hot_rows[...], pooled_low)

    def finish(rb, carry):
        at = pl.ds(pl.multiple_of(rb * many * px, 16), many * px)
        to = pl.ds(pl.multiple_of((rb * many + pn.hb) * px, 16), many * px)
        y = dot_nt(qraw[0, at], wbuf[POINT])
        y = jnp.concatenate(
            [y[r * S:(r + 1) * S] + pooled_rows[pl.ds(rb * many * pn.rpb + r, 1)] for r in range(many * pn.rpb)], axis=0
        )
        dxe[to] = dxe[to] + y
        return carry

    lax.fori_loop(0, MEMBERS // many, finish, 0)
    if pn.exchange:
        relay_all()
    serve(5)

    @pl.when(slab > 0)
    def _():
        remote(hsend.at[0], hrecv.at[1], h_s.at[0], h_r.at[1], member(slab - 1, me)).wait_send()
        remote(hsend.at[1], hrecv.at[0], h_s.at[1], h_r.at[0], member(slab - 1, me)).wait_recv()

    @pl.when(slab < n - 1)
    def _():
        remote(hsend.at[1], hrecv.at[0], h_s.at[1], h_r.at[0], member(slab + 1, me)).wait_send()
        remote(hsend.at[0], hrecv.at[1], h_s.at[0], h_r.at[1], member(slab + 1, me)).wait_recv()

    @pl.when(slab == 0)
    def _():
        hrecv[0] = jnp.zeros((pn.hb * px, pn.cs), BF16)

    @pl.when(slab == n - 1)
    def _():
        hrecv[1] = jnp.zeros((pn.hb * px, pn.cs), BF16)

    for rb in range(pn.hb):
        low, high = (pn.hb + rb) * px, (MEMBERS + rb) * px
        dxe[pl.ds(low, px)] = dxe[pl.ds(low, px)] + hrecv[0, pl.ds(rb * px, px)].astype(F32)
        dxe[pl.ds(high, px)] = dxe[pl.ds(high, px)] + hrecv[1, pl.ds(rb * px, px)].astype(F32)

    column = lax.broadcasted_iota(jnp.int32, (S, pn.cs), 0).astype(F32)
    for b in range(H // 8):
        rows = []
        for r in range(8 * b, 8 * b + 8):
            values = dxe[pl.ds(pn.hb * px + r * S, S)]
            rows.append(jnp.where(column < masks[6 * H + MARGIN + r], values, 0.0))
        moved = dot(sel_t[...], jnp.concatenate(rows, axis=0).astype(BF16)).astype(BF16)
        pack[8 * b // h, :, pl.ds(8 * b % h, 8)] = moved.reshape(pn.cols, 8, pn.cs)
    own_lanes = pl.ds(pl.multiple_of(slice_of(pn, me) * pn.cs, 128), pn.cs)
    back = []
    for kk in range(1, MEMBERS):
        other = lax.rem(me + kk, MEMBERS)
        xo, co = other // pn.C, lax.rem(other, pn.C)
        c = remote(pack.at[xo, pl.ds(co * pn.bc, pn.bc)], dx_out.at[:, :, own_lanes], x_s.at[kk], x_r.at[kk],
                   member(slab, other))
        c.start()
        back.append(c)
    c = pltpu.make_async_copy(pack.at[x, pl.ds(col * pn.bc, pn.bc)], dx_out.at[:, :, own_lanes], x_r.at[0])
    c.start()
    back.append(c)

    def close_dproj():
        @pl.when(slab == home_slab)
        def _():
            for z in range(n):
                pltpu.make_async_copy(dp2.at[z], dp2.at[z], p2_r.at[z]).wait()
            total = dp2[0].astype(F32)
            for z in range(1, n):
                total = total + dp2[z].astype(F32)
            dpf[...] = total
            for c in range(pn.C):
                @pl.when((x == lax.rem(me, pn.G)) & (col == c))
                def _():
                    pltpu.make_async_copy(dpf, dproj_out, p3_r.at[0]).start()

                @pl.when(jnp.logical_not((x == lax.rem(me, pn.G)) & (col == c)))
                def _(c=c):
                    dproj_give(c).start()

    if pn.exchange:
        serve(6)
        serve(7)
        give_way()
        for g in range(8, GROUPS + 2):
            serve(g)
        close_dproj()
        for g in range(GROUPS + 2):
            last_round(g)

        def settle(g, carry):
            @pl.when(jnp.logical_not(yielding & (g < YIELD)))
            def _():
                early_links(g, lambda c: c.wait_send())

            late_links(g, lambda c: c.wait_send())
            for role, up in ((relay_up, True), (relay_down, False)):
                @pl.when(role)
                def _(up=up):
                    relay(g, up).wait_send()

            @pl.when(close_a)
            def _():
                partial(g, 0).wait_send()

            for half, gives, passes in ((0, end_closing | close_a, end_getting | close_b),
                                        (1, end_closing | close_b, end_getting | close_a)):
                @pl.when(gives)
                def _(half=half):
                    share_y(g, half, part_of(dwbuf, g, half)).wait_send()
                    share_core(g, half, part_of(dwbuf, g, half)).wait_send()

                @pl.when(passes)
                def _(half=half):
                    share_on(g, half).wait_send()

                @pl.when(jnp.logical_not(passes))
                def _(half=half):
                    landed(g, half)

            return carry

        lax.fori_loop(0, GROUPS - 1, settle, 0)
        settle(GROUPS - 1, 0)

        @pl.when(slab != home_slab)
        def _():
            dproj_home().wait_send()

        @pl.when(slab == home_slab)
        def _():
            for c in range(pn.C):
                @pl.when(jnp.logical_not((x == lax.rem(me, pn.G)) & (col == c)))
                def _(c=c):
                    dproj_give(c).wait_send()

        pltpu.make_async_copy(dproj_out, dproj_out, p3_r.at[0]).wait()
    else:
        c = pltpu.make_async_copy(dwbuf, dw_out, g_r.at[0, 0])
        c.start()
        c.wait()
        dproj_out[...] = jnp.zeros(dproj_out.shape, F32)
    for c in back:
        c.wait()


def conv_backward(pn, q, xs, w, dproj, q4, means, hot_rows, inv_counts, masks, lane_masks, shifts, sel_t):
    dma = pltpu.SemaphoreType.DMA
    vmem = pl.BlockSpec(memory_space=pltpu.VMEM)
    hbm = pl.BlockSpec(memory_space=pl.ANY)
    shape = jax.ShapeDtypeStruct
    n = pn.slabs if pn.exchange else 1
    sums = TAPS if pn.exchange else 1
    block_rows = 5 * pn.width // MEMBERS
    return pl.pallas_call(
        functools.partial(back_kernel, pn),
        out_shape=(
            shape((TAPS, pn.cs, pn.width), BF16),
            shape((pn.bc, pn.h, pn.channels), BF16),
            shape((block_rows, pn.width), F32),
        ),
        in_specs=[hbm] * 4 + [vmem] * 4 + [pl.BlockSpec(memory_space=pltpu.SMEM)] + [vmem] * 3,
        out_specs=(hbm, hbm, vmem),
        scratch_shapes=[
            pltpu.VMEM((7, pn.ext, pn.cs), BF16),
            pltpu.VMEM((TAPS, pn.cs, pn.width), BF16),
            pltpu.VMEM((4, pn.own, pn.width), BF16),
            pltpu.VMEM((3, 2, pn.own, pn.width), BF16),
            pltpu.VMEM((pn.width, pn.own), BF16),
            pltpu.VMEM((pn.ext, pn.cs), F32),
            pltpu.VMEM((TAPS, pn.cs, pn.width), BF16),
            pltpu.VMEM((2, sums, pn.cs, pn.width), BF16),
            pltpu.VMEM((2, pn.hb * pn.px, pn.cs), BF16),
            pltpu.VMEM((2, pn.hb * pn.px, pn.cs), BF16),
            pltpu.VMEM((pn.G, pn.cols, pn.h, pn.cs), BF16),
            pltpu.VMEM((pn.H, pn.cs), F32),
            pltpu.VMEM((MEMBERS, block_rows, pn.width), BF16),
            pltpu.VMEM((block_rows, pn.width), BF16),
            pltpu.VMEM((n, block_rows, pn.width), BF16),
            pltpu.VMEM((block_rows, pn.width), F32),
            dma((6,)), dma((4, 3)), dma((4, 3)), dma((4,)), dma((4,)), dma((4, 3)), dma((4, 3)),
            dma((2, GROUPS)), dma((2, 2, GROUPS)), dma((GROUPS,)), dma((GROUPS,)), dma((2, 2, GROUPS)), dma((2, GROUPS)),
            dma((GROUPS,)), dma((GROUPS,)), pltpu.SemaphoreType.REGULAR,
            dma((2,)), dma((2,)), dma((MEMBERS,)), dma((MEMBERS,)),
            dma((MEMBERS,)), dma((MEMBERS,)), dma((1,)), dma((n,)), dma((pn.C,)), dma((1,)),
        ],
        compiler_params=pltpu.CompilerParams(collective_id=2, has_side_effects=True, vmem_limit_bytes=61900 * 1024),
        name="conv_backward",
    )(q, xs, w, dproj, q4, means, hot_rows, inv_counts, masks, lane_masks, shifts, sel_t)


def column_tables(pn):
    S, bp, bc = pn.S, pn.bp, pn.bc
    sel = np.zeros((7, 2, S, 2, pn.C * bp), np.float32)
    shifts = np.zeros((3, 2, 2, S, 2, S), np.float32)
    for r in range(2):
        for c in range(pn.cols):
            for v in range(-3, 4):
                s = c + v * DILATIONS[0]
                if 0 <= s < pn.cols:
                    sel[v + 3, r, c, r, (s // bc) * bp + s % bc] = 1.0
            for b, d in enumerate(DILATIONS):
                for n, j in enumerate((-1, 1)):
                    s = c - j * d
                    if 0 <= s < pn.cols:
                        shifts[b, n, r, c, r, s] = 1.0
    sel = sel.reshape(7 * 2 * S, 2 * pn.C * bp)
    sel_t = sel[3 * 2 * S:4 * 2 * S].T
    sel_c = np.zeros((pn.cols, 8, 8, S), np.float32)
    for c in range(pn.cols):
        for r in range(8):
            sel_c[c, r, r, c] = 1.0
    sel_c = sel_c.reshape(8 * pn.cols, 8 * S)
    return (jnp.asarray(sel, BF16), jnp.asarray(sel_t, BF16), jnp.asarray(sel_c, BF16), jnp.asarray(shifts.reshape(12 * S, 2 * S), BF16))


def per_device(
    features, crop_rows, crop_cols, w_point, w_atrous, w_pool, w_proj, gains, biases, cotangent
):
    h, bc, channels = features.shape
    pn = Plan(lax.axis_size("row"), lax.axis_size("col"), h, bc, channels, gains.shape[1], crop_rows.shape[0])
    row, col = lax.axis_index("row"), lax.axis_index("col")
    slab, x = row // pn.G, row % pn.G
    crop_ids = jnp.arange(pn.crops, dtype=jnp.int32)
    ends = jnp.cumsum(crop_rows)
    counts = (crop_rows * crop_cols).astype(F32)
    pixels = jnp.sum(counts)

    def crop_of(rows):
        found = jnp.sum((rows[:, None] >= ends[None, :]).astype(jnp.int32), axis=1)
        return jnp.where(rows < 0, -1, found)

    def widths_of(crop):
        return jnp.sum(jnp.where(crop[:, None] == crop_ids[None, :], crop_cols[None, :], 0), axis=1)

    feats = features.reshape(h, bc, MEMBERS, pn.cs).transpose(2, 0, 1, 3)
    feats = jnp.pad(feats, ((0, 0), (0, 0), (0, pn.bp - bc), (0, 0)))
    cot = jnp.pad(cotangent, ((0, 0), (0, pn.bp - bc), (0, 0)))

    slab_rows = slab * pn.H - MARGIN + jnp.arange(pn.H + 2 * MARGIN, dtype=jnp.int32)
    crops = crop_of(slab_rows)
    mid = crops[MARGIN:MARGIN + pn.H]
    same = jnp.stack(
        [crops[MARGIN + i * d:MARGIN + i * d + pn.H] == mid for d in DILATIONS for i in (-1, 1)]
    ).astype(F32)
    lane_masks = jnp.pad(jnp.repeat(same, pn.S, axis=1), ((0, 2), (0, 0))).astype(BF16)
    ncp_ids = jnp.arange(pn.ncp, dtype=jnp.int32)
    hot_rows = (mid[:, None] == ncp_ids[None, :]).astype(BF16)
    hot_t = jnp.repeat(hot_rows.T, pn.S, axis=1)
    inv_counts = jnp.pad(1.0 / counts, (0, pn.ncp - pn.crops))[:, None]

    k = x * pn.C + col
    block_crop = lax.dynamic_slice_in_dim(mid, k * pn.rpb, pn.rpb)
    columns = jnp.arange(pn.S, dtype=jnp.int32)
    valid = (columns[None, :] < widths_of(block_crop)[:, None]).astype(F32).reshape(pn.px, 1)
    block_hot = jnp.repeat((block_crop[:, None] == ncp_ids[None, :]).astype(BF16), pn.S, axis=0)
    block_hot_t = jnp.repeat((ncp_ids[:, None] == block_crop[None, :]).astype(BF16), pn.S, axis=1)

    sel, sel_t, sel_c, shifts = column_tables(pn)
    w, w_two = w_atrous.transpose(1, 0, 2), jnp.stack([w_point, w_pool])
    proj = w_proj.reshape(pn.C, pn.proj // pn.C, pn.width)
    proj = jnp.pad(proj, ((0, 0), (0, pn.piece - pn.proj // pn.C), (0, 0)))
    if not pn.exchange:
        w = lax.all_gather(jnp.concatenate([w, w_two], axis=0), "row", axis=1, tiled=True)
        w = lax.dynamic_slice_in_dim(w, slice_of(pn, x * pn.C + col) * pn.cs, pn.cs, axis=1)
        w, w_two = w[:POINT], w[POINT:]
    flat = jnp.concatenate([same.reshape(-1), widths_of(crops).astype(F32)])
    p, xs, w_own, means, p4, own_cot, pieces = conv_forward(
        pn, feats, w, w_two, cot, proj, flat, sel, hot_t, inv_counts
    )
    full_proj = pieces[:, :, :pn.proj // pn.C].transpose(1, 0, 2, 3).reshape(5 * pn.width, pn.width)
    q, q4, d_proj, res, d_gains, d_biases = norms(
        pn, p, p4, gains, biases, valid, (1.0 / pixels)[None], full_proj, own_cot, block_hot, block_hot_t, sel_t
    )
    dw, dx, dproj_sum = conv_backward(
        pn, q, xs, w_own, d_proj, q4, means, hot_rows, inv_counts, flat, lane_masks, shifts, sel_c
    )
    if pn.exchange:
        d_proj = dproj_sum
    else:
        whole = jnp.zeros((TAPS, channels, pn.width), BF16)
        whole = lax.dynamic_update_slice(whole, dw, (0, slice_of(pn, x * pn.C + col) * pn.cs, 0))
        whole = lax.psum(whole, "col")
        dw = lax.psum_scatter(whole, "row", scatter_dimension=1, tiled=True)
        d_proj = lax.psum(d_proj, "col")
        d_proj = lax.psum_scatter(d_proj.astype(F32), "row", scatter_dimension=0, tiled=True)
    result = res[:, :bc]
    d_features = dx.transpose(1, 0, 2)
    d_point = dw[POINT].astype(F32)
    d_atrous = dw[:POINT].astype(F32).transpose(1, 0, 2)
    d_pool = dw[POOL].astype(F32)
    return (result, d_features, d_point, d_atrous, d_pool, d_proj, d_gains, d_biases)


def solution(mesh):
    return jax.shard_map(
        per_device,
        mesh=mesh,
        in_specs=(
            P("row", "col", None),
            P(),
            P(),
            P("row", None),
            P("row", None, None),
            P("row", None),
            P("row", None),
            P(),
            P(),
            P("row", "col", None),
        ),
        out_specs=(
            P("row", "col", None),
            P("row", "col", None),
            P("row", None),
            P("row", None, None),
            P("row", None),
            P("row", None),
            P(),
            P(),
        ),
        check_vma=False,
    )
```

```python
import functools

import jax
import jax.numpy as jnp
import numpy as np
from jax import lax
from jax.experimental import pallas as pl
from jax.experimental.pallas import tpu as pltpu
from jax.sharding import PartitionSpec as P

EPSILON = 1e-05
MARGIN = 18
DILATIONS = (6, 12, 18)
MEMBERS = 8
TAPS = 29
POINT, POOL, GROUPS = 27, 28, 10
YIELD = 8
MESH = pl.DeviceIdType.MESH
F32 = jnp.float32
BF16 = jnp.bfloat16

def up_to(value, multiple):
    return -(-value // multiple) * multiple


class Plan:
    def __init__(self, rows_axis, cols_axis, h, bc, channels, width, crops):
        self.R, self.C = rows_axis, cols_axis
        self.h, self.bc, self.channels, self.width = h, bc, channels, width
        self.G = MEMBERS // self.C
        self.slabs = self.R // self.G
        self.H = self.G * h
        self.cols = bc * self.C
        self.S = up_to(self.cols, 8)
        self.rpb = self.H // MEMBERS
        self.px = self.rpb * self.S
        self.own = MEMBERS * self.px
        self.hb = MARGIN // self.rpb
        self.nb = MEMBERS + 2 * self.hb
        self.ext = self.nb * self.px
        self.bp = up_to(bc, 16)
        self.cs = channels // MEMBERS
        self.crops = crops
        self.ncp = up_to(crops, 16)
        self.exchange = self.slabs == self.C and self.R == MEMBERS
        self.steps = tuple(d // self.rpb for d in DILATIONS)
        self.proj = 5 * width // self.R
        self.piece = up_to(self.proj // self.C, 16)


def home_of(pn, col):
    if pn.C != 4:
        return col
    y, c = col // 2, lax.rem(col, 2)
    return (1 - y) * 3 * c + y * (1 + c)


def slice_of(pn, k):
    return pn.G * home_of(pn, lax.rem(k, pn.C)) + k // pn.C


def remote(src, dst, send, recv, device):
    return pltpu.make_async_remote_copy(
        src_ref=src, dst_ref=dst, send_sem=send, recv_sem=recv, device_id=device, device_id_type=MESH
    )


def greet_all(pn, row, col):
    total = pn.R * pn.C
    barrier = pltpu.get_barrier_semaphore()
    me = row * pn.C + col

    def hello(k, carry):
        other = lax.rem(me + k, total)
        pl.semaphore_signal(
            barrier, inc=1, device_id=(other // pn.C, lax.rem(other, pn.C)), device_id_type=MESH
        )
        return carry

    lax.fori_loop(1, total, hello, 0)
    pl.semaphore_wait(barrier, total - 1)


def dot(a, b):
    return jnp.dot(a, b, preferred_element_type=F32)


def dot_nt(a, b):
    return lax.dot_general(a, b, (((1,), (1,)), ((), ())), preferred_element_type=F32)


def dot_tn(a, b):
    return lax.dot_general(a, b, (((0,), (0,)), ((), ())), preferred_element_type=F32)


def split_dot(dot_fn, a, b):
    high = a.astype(BF16)
    low = (a - high.astype(F32)).astype(BF16)
    return dot_fn(high, b) + dot_fn(low, b)


def conv_kernel(pn, feats, w_in, w_two, cot, proj, masks, sel, hot_t, inv_counts,
                p_out, x_out, w_out, m_out, p4_out, cot_out, proj_out,
                ring, xs, wbuf, acc, pbuf, cbuf, sbuf, rbuf, cx,
                f_s, f_r, h_s, h_r, c_s, c_r, j_s, j_r, t_s, t_r, w_s, w_r, w_l, e_s,
                r1_s, r1_r, r2_s, r2_r, o_s):
    row, col = lax.axis_index("row"), lax.axis_index("col")
    slab, x = row // pn.G, lax.rem(row, pn.G)
    me = x * pn.C + col
    core, quad = lax.rem(col, 2), me // 2
    h, H, bp, px, n = pn.h, pn.H, pn.bp, pn.px, pn.slabs
    many = 4

    def member(s, k):
        return (s * pn.G + k // pn.C, lax.rem(k, pn.C))

    greet_all(pn, row, col)

    own_cols = pl.ds(pl.multiple_of(col * bp, bp), bp)
    own_rows = pl.ds(MARGIN + h * x, h)
    sent = []
    for kk in range(1, MEMBERS):
        other = lax.rem(me + kk, MEMBERS)
        c = remote(feats.at[slice_of(pn, other)], ring.at[own_rows, own_cols], f_s.at[kk], f_r.at[kk], member(slab, other))
        c.start()
        sent.append(c)
    keep = pltpu.make_async_copy(feats.at[slice_of(pn, me)], ring.at[own_rows, own_cols], f_r.at[0])
    keep.start()

    home = home_of(pn, col)
    source, rising, falling = slab == home, (slab > home) & (slab < n - 1), (slab < home) & (slab > 0)
    help_up, help_down = (slab == n - 2) & (col == 1), (slab == 1) & (col == 0)
    half_rows = pn.cs // 2

    order = (0, 1, 2, 3, 4, 5, 9, 6, 7, 8)

    def taps(g):
        return pl.ds(POINT, 2) if isinstance(g, int) and g == GROUPS - 1 else pl.ds(3 * g, 3)

    def given(g, rows):
        if isinstance(g, int) and g == GROUPS - 1:
            return w_two.at[:, rows]
        return w_in.at[taps(g), rows]

    def half_of(half):
        return pl.ds(half * half_rows, half_rows)

    def part_of(ref, g, half):
        return ref.at[taps(g), half_of(half)]

    def ship(g, half, up, own):
        to = slab + 1 if up else slab - 1
        return remote(given(g, half_of(half)) if own else part_of(wbuf, g, half), part_of(wbuf, g, half), w_s.at[int(up), half, g], w_r.at[half, g],
                      (to * pn.G + x, col))

    def assist(g, up):
        to = slab + 1 if up else slab - 1
        return remote(given(g, half_of(1)), part_of(wbuf, g, 1), e_s.at[g], w_r.at[1, g], (to * pn.G + x, col + 2))

    def own_copy(g):
        return pltpu.make_async_copy(given(g, pl.ds(0, pn.cs)), wbuf.at[taps(g)], w_l.at[g])

    def arrived(g):
        for half in (0, 1):
            at = part_of(wbuf, g, half)
            pltpu.make_async_copy(at, at, w_r.at[half, g]).wait()

    def pass_on(g):
        for role, up in ((rising, True), (falling, False)):
            @pl.when(role)
            def _(up=up):
                arrived(g)
                for half in (0, 1):
                    ship(g, half, up, False).start()

    def w_wait(g):
        if pn.exchange:
            @pl.when(source)
            def _():
                own_copy(g).wait()

            @pl.when(jnp.logical_not(source | rising | falling))
            def _():
                arrived(g)
        else:
            own_copy(g).wait()

    def each_shipment(g, act):
        for half in (0, 1):
            @pl.when(source & ((slab < n - 2) if half else (slab < n - 1)))
            def _(half=half):
                act(ship(g, half, True, True))

            @pl.when(source & ((slab > 1) if half else (slab > 0)))
            def _(half=half):
                act(ship(g, half, False, True))

        @pl.when(help_up)
        def _():
            act(assist(g, True))

        @pl.when(help_down)
        def _():
            act(assist(g, False))

    if pn.exchange:
        def begin(g, carry):
            each_shipment(g, lambda c: c.start())

            @pl.when(source)
            def _():
                own_copy(g).start()

            return carry
    else:
        def begin(g, carry):
            own_copy(g).start()
            return carry

    early = 6
    lax.fori_loop(0, early, begin, 0)

    cot_sent = []
    for cc in range(1, pn.C):
        cd = lax.rem(col + cc, pn.C)
        c = remote(cot.at[pl.ds(cd * pn.rpb, pn.rpb)], cx.at[:, own_cols], c_s.at[cc], c_r.at[cc], (row, cd))
        c.start()
        cot_sent.append(c)
    cot_keep = pltpu.make_async_copy(cot.at[pl.ds(col * pn.rpb, pn.rpb)], cx.at[:, own_cols], c_r.at[0])
    cot_keep.start()

    def proj_row(k):
        return remote(proj.at[col], proj_out.at[col, row], j_s.at[k], j_r.at[k], (lax.rem(row + k, pn.R), col))

    def proj_col(k):
        return remote(proj_out.at[col], proj_out.at[col], t_s.at[k], t_r.at[k], (row, lax.rem(col + k, pn.C)))

    def proj_begin(k, carry):
        proj_row(k).start()
        return carry

    def proj_wait(k, carry):
        proj_row(k).wait()
        return carry

    lax.fori_loop(1, pn.R, proj_begin, 0)
    proj_keep = pltpu.make_async_copy(proj.at[col], proj_out.at[col, row], j_r.at[0])
    proj_keep.start()

    @pl.when(slab == 0)
    def _():
        ring[pl.ds(0, MARGIN)] = jnp.zeros((MARGIN, pn.C * bp, pn.cs), BF16)

    @pl.when(slab == n - 1)
    def _():
        ring[pl.ds(MARGIN + H, MARGIN)] = jnp.zeros((MARGIN, pn.C * bp, pn.cs), BF16)

    def pass_many(first, end):
        if pn.exchange:
            for k in range(first, end):
                pass_on(order[k])

    pass_many(0, 3)
    for c in sent:
        c.wait()
    keep.wait()

    def margin_down():
        return remote(ring.at[pl.ds(MARGIN, MARGIN)], ring.at[pl.ds(MARGIN + H, MARGIN)], h_s.at[0], h_r.at[0],
                      member(slab - 1, me))

    def margin_up():
        return remote(ring.at[pl.ds(H, MARGIN)], ring.at[pl.ds(0, MARGIN)], h_s.at[1], h_r.at[1], member(slab + 1, me))

    @pl.when(slab > 0)
    def _():
        margin_down().start()

    @pl.when(slab < n - 1)
    def _():
        margin_up().start()

    begin(GROUPS - 1, 0)
    lax.fori_loop(early, GROUPS - 1, begin, 0)

    column = lax.broadcasted_iota(jnp.int32, (pn.S, pn.cs), 0).astype(F32)

    def assemble(rp, carry):
        pair = ring[pl.ds(2 * rp, 2)].reshape(2 * pn.C * bp, pn.cs)
        moved = dot(sel[...], pair)
        at = pl.multiple_of(rp * 2 * pn.S, 16)
        wide = [masks[6 * H + 2 * rp + r] for r in range(2)]
        for v in range(7):
            rows = [
                jnp.where(column + float(DILATIONS[0] * (v - 3)) < wide[r], moved[(2 * v + r) * pn.S:(2 * v + r + 1) * pn.S], 0.0)
                for r in range(2)
            ]
            xs[v, pl.ds(at, 2 * pn.S)] = jnp.concatenate(rows, axis=0).astype(BF16)
        return carry

    lax.fori_loop(MARGIN // 2, (MARGIN + H) // 2, assemble, 0, unroll=6)
    pass_many(3, 5)
    for c in cot_sent:
        c.wait()
    cot_keep.wait()
    for rp in range(pn.rpb // 2):
        pair = cx[2 * rp:2 * rp + 2].reshape(2 * pn.C * bp, pn.width)
        cot_out[pl.ds(rp * 2 * pn.S, 2 * pn.S)] = dot(sel[pl.ds(3 * 2 * pn.S, 2 * pn.S)], pair).astype(BF16)
    lax.fori_loop(1, pn.R, proj_wait, 0)
    proj_keep.wait()
    for k in range(1, pn.C):
        proj_col(k).start()
    pass_many(5, 6)

    @pl.when(slab > 0)
    def _():
        margin_down().wait_send()
        margin_up().wait_recv()

    @pl.when(slab < n - 1)
    def _():
        margin_up().wait_send()
        margin_down().wait_recv()

    lax.fori_loop(0, MARGIN // 2, assemble, 0, unroll=3)
    lax.fori_loop((MARGIN + H) // 2, pn.nb * pn.rpb // 2, assemble, 0, unroll=3)
    x_save = pltpu.make_async_copy(xs, x_out, o_s.at[0])
    x_save.start()

    def first_stage(slot):
        return remote(pbuf.at[slot, :, 1 - core], cbuf.at[slot], r1_s.at[slot], r1_r.at[slot], (row, col + 1 - 2 * core))

    def second_stage(slot, i):
        q = lax.rem(quad + i, MEMBERS // 2)
        return remote(sbuf.at[slot, i - 1], rbuf.at[slot, i - 1], r2_s.at[slot, i - 1], r2_r.at[slot, i - 1],
                      member(slab, 2 * q + core))

    def middle(slot):
        first_stage(slot).wait()
        for i in (1, 2, 3, 0):
            q = lax.rem(quad + i, MEMBERS // 2)
            s = pbuf[slot, q, core].astype(F32) + cbuf[slot, q].astype(F32)
            if i == 0:
                p_out[slot] = s
            else:
                sbuf[slot, i - 1] = s.astype(BF16)
                second_stage(slot, i).start()

    def last(slot):
        total = p_out[slot]
        for i in range(1, MEMBERS // 2):
            second_stage(slot, i).wait()
            total = total + rbuf[slot, i - 1].astype(F32)
        p_out[slot] = total

    def scatter(slot, rb, y):
        for r in range(many):
            pbuf[slot, (many * rb + r) // 2, r % 2] = y[r * px:(r + 1) * px].astype(BF16)

    def far(k):
        if k in (2, 4, 6, 8):
            pass_many(5 + k // 2, 6 + k // 2)
        w_wait(order[k])

    def point(rb, carry):
        at = pl.ds(pl.multiple_of((rb * many + pn.hb) * px, 16), many * px)
        scatter(0, rb, dot(xs[3, at], wbuf[POINT]))
        return carry

    for branch in (1, 2, 3):
        step = pn.steps[branch - 1]
        if branch == 3:
            far(6)
            lax.fori_loop(0, MEMBERS // many, point, 0)
            first_stage(0).start()
            middle(2)
        for i in (-1, 0, 1):
            g = 3 * (branch - 1) + i + 1
            mask_at = (2 * (branch - 1) + (i + 1) // 2) * H
            far(g + branch // 3)

            def block(rb, carry, step=step, i=i, g=g, mask_at=mask_at, branch=branch):
                at = pl.multiple_of(rb * many * px, 16)
                window = pl.ds(pl.multiple_of((rb * many + pn.hb + i * step) * px, 16), many * px)
                y = dot(xs[3 - branch, window], wbuf[3 * g])
                y = y + dot(xs[3, window], wbuf[3 * g + 1])
                y = y + dot(xs[3 + branch, window], wbuf[3 * g + 2])
                if i != 0:
                    y = jnp.concatenate(
                        [y[r * pn.S:(r + 1) * pn.S] * masks[mask_at + rb * many * pn.rpb + r]
                         for r in range(many * pn.rpb)], axis=0
                    )
                if i > -1:
                    y = y + acc[pl.ds(at, many * px)]
                if i < 1:
                    acc[pl.ds(at, many * px)] = y
                else:
                    scatter(branch, rb, y)
                return carry

            lax.fori_loop(0, MEMBERS // many, block, 0)
            if i == 0 and branch > 1:
                middle(branch - 1 if branch == 2 else 0)
        first_stage(branch).start()

    sums = dot(hot_t[...], xs[3, pl.ds(pn.hb * px, pn.own)])
    means = sums * inv_counts[...]
    m_out[...] = means
    p4_out[...] = split_dot(dot, means, wbuf[POOL])
    w_save = pltpu.make_async_copy(wbuf, w_out, o_s.at[1])
    w_save.start()
    middle(3)
    for slot in (1, 2, 0):
        last(slot)
    for k in range(1, pn.C):
        proj_col(k).wait()
    if pn.exchange:
        def settled(g, carry):
            each_shipment(g, lambda c: c.wait_send())
            for role, up in ((rising, True), (falling, False)):
                @pl.when(role)
                def _(up=up):
                    for half in (0, 1):
                        ship(g, half, up, False).wait_send()
            return carry

        lax.fori_loop(0, GROUPS - 1, settled, 0)
        settled(GROUPS - 1, 0)
    last(3)
    x_save.wait()
    w_save.wait()


def conv_forward(pn, feats, w, w_two, cot, proj, masks, sel, hot_t, inv_counts):
    half = MEMBERS // 2
    dma = pltpu.SemaphoreType.DMA
    vmem = pl.BlockSpec(memory_space=pltpu.VMEM)
    hbm = pl.BlockSpec(memory_space=pl.ANY)
    shape = jax.ShapeDtypeStruct
    return pl.pallas_call(
        functools.partial(conv_kernel, pn),
        out_shape=(
            shape((4, pn.px, pn.width), F32),
            shape((7, pn.ext, pn.cs), BF16),
            shape((TAPS, pn.cs, pn.width), BF16),
            shape((pn.ncp, pn.cs), F32),
            shape((pn.ncp, pn.width), F32),
            shape((pn.px, pn.width), BF16),
            shape((pn.C, pn.R, pn.piece, pn.width), BF16),
        ),
        in_specs=[hbm, hbm, hbm, hbm, hbm, pl.BlockSpec(memory_space=pltpu.SMEM), vmem, vmem, vmem],
        out_specs=(vmem, hbm, hbm, vmem, vmem, vmem, vmem),
        scratch_shapes=[
            pltpu.VMEM((pn.nb * pn.rpb, pn.C * pn.bp, pn.cs), BF16),
            pltpu.VMEM((7, pn.ext, pn.cs), BF16),
            pltpu.VMEM((TAPS, pn.cs, pn.width), BF16),
            pltpu.VMEM((pn.own, pn.width), F32),
            pltpu.VMEM((4, half, 2, pn.px, pn.width), BF16),
            pltpu.VMEM((4, half, pn.px, pn.width), BF16),
            pltpu.VMEM((4, half - 1, pn.px, pn.width), BF16),
            pltpu.VMEM((4, half - 1, pn.px, pn.width), BF16),
            pltpu.VMEM((pn.rpb, pn.C * pn.bp, pn.width), BF16),
            dma((MEMBERS,)), dma((MEMBERS,)), dma((2,)), dma((2,)), dma((pn.C,)), dma((pn.C,)),
            dma((pn.R,)), dma((pn.R,)), dma((pn.C,)), dma((pn.C,)),
            dma((2, 2, GROUPS)), dma((2, GROUPS)), dma((GROUPS,)), dma((GROUPS,)),
            dma((4,)), dma((4,)), dma((4, 3)), dma((4, 3)), dma((2,)),
        ],
        compiler_params=pltpu.CompilerParams(collective_id=0, has_side_effects=True, vmem_limit_bytes=60 * 2**20),
        name="conv_forward",
    )(feats, w, w_two, cot, proj, masks, sel, hot_t, inv_counts)


def norm_kernel(pn, p, p4_in, gains, biases, valid, pixels, w_proj, cot, hot, hot_t, sel_t,
                q_out, q4_out, dproj_out, res_out, dg_out, db_out,
                norm, slope, hbuf, gact, dh4, rx,
                a1, b1, a2, b2, a3, b3, a4, b4, as_s, as_r, bs_s, bs_r, e_s, e_r):
    row, col = lax.axis_index("row"), lax.axis_index("col")
    slab, x = row // pn.G, lax.rem(row, pn.G)
    me = x * pn.C + col
    crops = float(pn.crops)
    v = valid[...]
    inv_px = pixels[0]
    width, bp = pn.width, pn.bp

    def member(s, k):
        return (s * pn.G + k // pn.C, lax.rem(k, pn.C))

    barrier = pltpu.get_barrier_semaphore()
    for kk in range(1, MEMBERS):
        pl.semaphore_signal(barrier, inc=1, device_id=member(slab, lax.rem(me + kk, MEMBERS)), device_id_type=MESH)

    def hello(k, carry):
        pl.semaphore_signal(barrier, inc=1, device_id=member(lax.rem(slab + k, pn.slabs), me), device_id_type=MESH)
        return carry

    lax.fori_loop(1, pn.slabs, hello, 0)

    def peer_a(n, abuf, kk):
        return remote(abuf.at[me], abuf.at[me], as_s.at[n, kk], as_r.at[n, kk], member(slab, lax.rem(me + kk, MEMBERS)))

    def peer_b(n, bbuf, k):
        return remote(bbuf.at[slab], bbuf.at[slab], bs_s.at[n, k], bs_r.at[n, k], member(lax.rem(slab + k, pn.slabs), me))

    def reduce_start(n, abuf):
        for kk in range(1, MEMBERS):
            peer_a(n, abuf, kk).start()

    def reduce_end(n, abuf, bbuf):
        for kk in range(1, MEMBERS):
            peer_a(n, abuf, kk).wait()
        total = abuf[0]
        for k in range(1, MEMBERS):
            total = total + abuf[k]
        bbuf[slab] = total
        for k in range(1, pn.slabs):
            peer_b(n, bbuf, k).start()
        for k in range(1, pn.slabs):
            peer_b(n, bbuf, k).wait()
        total = bbuf[0]
        for k in range(1, pn.slabs):
            total = total + bbuf[k]
        return total

    def column_sum(value):
        return jnp.sum(value, axis=0, keepdims=True)

    for b in range(4):
        pv = p[b] * v
        a1[me, pl.ds(b, 1)] = column_sum(pv)
        a1[me, pl.ds(4 + b, 1)] = column_sum(pv * p[b])
    a1[me, pl.ds(8, pn.ncp)] = p4_in[...]
    pl.semaphore_wait(barrier, MEMBERS - 1 + pn.slabs - 1)
    reduce_start(0, a1)
    total = reduce_end(0, a1, b1)
    inv = []
    for b in range(4):
        centre = total[b:b + 1] * inv_px
        scale = lax.rsqrt(total[4 + b:5 + b] * inv_px - centre * centre + EPSILON)
        inv.append(scale)
        n = (p[b] - centre) * scale
        u = gains[b:b + 1] * n + biases[b:b + 1]
        s = jax.nn.sigmoid(u)
        norm[b] = n
        slope[b] = s * (1.0 + u * (1.0 - s))
        hbuf[b] = (u * s).astype(BF16)
    p4 = total[8:8 + pn.ncp]
    centre4 = column_sum(p4) * (1.0 / crops)
    inv4 = lax.rsqrt(column_sum(p4 * p4) * (1.0 / crops) - centre4 * centre4 + EPSILON)
    n4 = (p4 - centre4) * inv4
    u4 = gains[4:5] * n4 + biases[4:5]
    s4 = jax.nn.sigmoid(u4)
    slope4 = s4 * (1.0 + u4 * (1.0 - s4))
    hbuf[4] = dot(hot[...], (u4 * s4).astype(BF16)).astype(BF16)

    p5 = dot(hbuf[0], w_proj[pl.ds(0, width)])
    for b in range(1, 5):
        p5 = p5 + dot(hbuf[b], w_proj[pl.ds(b * width, width)])
    pv = p5 * v
    a2[me, pl.ds(0, 1)] = column_sum(pv)
    a2[me, pl.ds(1, 1)] = column_sum(pv * p5)
    a2[me, pl.ds(2, 6)] = jnp.zeros((6, width), F32)
    reduce_start(1, a2)
    total = reduce_end(1, a2, b2)
    centre5 = total[0:1] * inv_px
    inv5 = lax.rsqrt(total[1:2] * inv_px - centre5 * centre5 + EPSILON)
    n5 = (p5 - centre5) * inv5
    u5 = gains[5:6] * n5 + biases[5:6]
    s5 = jax.nn.sigmoid(u5)
    g5 = cot[...].astype(F32) * v * (s5 * (1.0 + u5 * (1.0 - s5)))
    norm[4] = n5
    gact[4] = g5
    a3[me, pl.ds(0, 1)] = column_sum(g5)
    a3[me, pl.ds(1, 1)] = column_sum(g5 * n5)
    a3[me, pl.ds(2, 6)] = jnp.zeros((6, width), F32)
    reduce_start(2, a3)
    hbuf[5] = (v * u5 * s5).astype(BF16)
    for rp in range(pn.rpb // 2):
        pair = hbuf[5, pl.ds(rp * 2 * pn.S, 2 * pn.S)]
        rx[2 * rp:2 * rp + 2] = dot(sel_t[...], pair).astype(BF16).reshape(2, pn.C * bp, width)
    back = []
    for cc in range(1, pn.C):
        cd = lax.rem(col + cc, pn.C)
        c = remote(rx.at[:, pl.ds(pl.multiple_of(cd * bp, bp), bp)], res_out.at[pl.ds(col * pn.rpb, pn.rpb)],
                   e_s.at[cc], e_r.at[cc], (row, cd))
        c.start()
        back.append(c)
    c = pltpu.make_async_copy(rx.at[:, pl.ds(pl.multiple_of(col * bp, bp), bp)], res_out.at[pl.ds(col * pn.rpb, pn.rpb)],
                              e_r.at[0])
    c.start()
    back.append(c)
    total = reduce_end(2, a3, b3)
    db5, dg5 = total[0:1], total[1:2]
    q5 = (gains[5:6] * inv5 * (gact[4] - v * (db5 + norm[4] * dg5) * inv_px)).astype(BF16)
    hbuf[5] = q5

    for b in range(4):
        g = dot_nt(q5, w_proj[pl.ds(b * width, width)]) * slope[b]
        gact[b] = g
        a4[me, pl.ds(b, 1)] = column_sum(g)
        a4[me, pl.ds(4 + b, 1)] = column_sum(g * norm[b])
    dh4[...] = dot_nt(q5, w_proj[pl.ds(4 * width, width)])
    high = dh4[...].astype(BF16)
    low = (dh4[...] - high.astype(F32)).astype(BF16)
    a4[me, pl.ds(8, pn.ncp)] = dot(hot_t[...], high) + dot(hot_t[...], low)
    reduce_start(3, a4)
    for b in range(5):
        dproj_out[pl.ds(b * width, width)] = dot_tn(hbuf[b], hbuf[5]).astype(BF16)
    total = reduce_end(3, a4, b4)
    for b in range(4):
        db, dg = total[b:b + 1], total[4 + b:5 + b]
        db_out[pl.ds(b, 1)] = db
        dg_out[pl.ds(b, 1)] = dg
        q_out[b] = (gains[b:b + 1] * inv[b] * (gact[b] - v * (db + norm[b] * dg) * inv_px)).astype(BF16)
    g4 = total[8:8 + pn.ncp] * slope4
    db4, dg4 = column_sum(g4), column_sum(g4 * n4)
    db_out[pl.ds(4, 1)] = db4
    dg_out[pl.ds(4, 1)] = dg4
    db_out[pl.ds(5, 1)] = db5
    dg_out[pl.ds(5, 1)] = dg5
    q4_out[...] = (gains[4:5] * inv4 * (g4 - (db4 + n4 * dg4) * (1.0 / crops))).astype(BF16)
    for c in back:
        c.wait()


def norms(pn, p, p4, gains, biases, valid, pixels, w_proj, cot, hot, hot_t, sel_t):
    dma = pltpu.SemaphoreType.DMA
    vmem = pl.BlockSpec(memory_space=pltpu.VMEM)
    shape = jax.ShapeDtypeStruct
    big, small = 8 + pn.ncp, 8
    bufs = []
    for n in (big, small, small, big):
        bufs += [pltpu.VMEM((MEMBERS, n, pn.width), F32), pltpu.VMEM((pn.slabs, n, pn.width), F32)]
    return pl.pallas_call(
        functools.partial(norm_kernel, pn),
        out_shape=(
            shape((4, pn.px, pn.width), BF16),
            shape((pn.ncp, pn.width), BF16),
            shape((5 * pn.width, pn.width), BF16),
            shape((pn.h, pn.bp, pn.width), BF16),
            shape((6, pn.width), F32),
            shape((6, pn.width), F32),
        ),
        in_specs=[vmem] * 5 + [pl.BlockSpec(memory_space=pltpu.SMEM)] + [vmem] * 5,
        out_specs=(vmem,) * 6,
        scratch_shapes=[
            pltpu.VMEM((5, pn.px, pn.width), F32),
            pltpu.VMEM((4, pn.px, pn.width), F32),
            pltpu.VMEM((6, pn.px, pn.width), BF16),
            pltpu.VMEM((5, pn.px, pn.width), F32),
            pltpu.VMEM((pn.px, pn.width), F32),
            pltpu.VMEM((pn.rpb, pn.C * pn.bp, pn.width), BF16),
            *bufs,
            dma((4, MEMBERS)), dma((4, MEMBERS)), dma((4, pn.slabs)), dma((4, pn.slabs)), dma((pn.C,)), dma((pn.C,)),
        ],
        compiler_params=pltpu.CompilerParams(collective_id=1, has_side_effects=True, vmem_limit_bytes=48 * 2**20),
        name="norms",
    )(p, p4, gains, biases, valid, pixels, w_proj, cot, hot, hot_t, sel_t)


def back_kernel(pn, q_in, x_in, w_in, dproj_in, q4, means, hot_rows, inv_counts, masks, lane_masks, shifts, sel_t,
                dw_out, dx_out, dproj_out,
                xs, wbuf, qraw, qs, qt, dxe, dwbuf, inn, hsend, hrecv, pack, pooled_rows, dp1, dps, dp2, dpf,
                l_s, q_s, q_r, k_s, k_r, f_s, f_r, n_s, n_r, e_s, e_r, g_s, g_r, b_s, b_r, turn_sem, h_s, h_r, x_s, x_r,
                p1_s, p1_r, p2_s, p2_r, p3_s, p3_r):
    row, col = lax.axis_index("row"), lax.axis_index("col")
    slab, x = row // pn.G, lax.rem(row, pn.G)
    me = x * pn.C + col
    core, quad = lax.rem(col, 2), me // 2
    h, H, bp, px, S, n = pn.h, pn.H, pn.bp, pn.px, pn.S, pn.slabs
    half = MEMBERS // 2
    many = 4
    partner = (row, col + 1 - 2 * core)

    def member(s, k):
        return (s * pn.G + k // pn.C, lax.rem(k, pn.C))

    load_x = pltpu.make_async_copy(x_in, xs, l_s.at[0])
    load_w = pltpu.make_async_copy(w_in, wbuf, l_s.at[1])
    load_x.start()
    load_w.start()
    greet_all(pn, row, col)

    slots = (1, 2, 3, 0)
    own_px = pl.ds(pl.multiple_of(me * px, 16), px)
    along_y, along_x = (row, lax.rem(col + 2, pn.C)), (slab * pn.G + lax.rem(x + 1, pn.G), col)
    from_y = x * pn.C + lax.rem(col + 2, pn.C)
    from_x = lax.rem(me + pn.C, MEMBERS)
    from_xy = lax.rem(from_y + pn.C, MEMBERS)

    def block_of(slot, k):
        return qraw.at[slot, pl.ds(pl.multiple_of(k * px, 16), px)]

    def to_y(slot):
        return remote(q_in.at[slot], qraw.at[slot, own_px], q_s.at[slot, 0], q_r.at[slot, 0], along_y)

    def to_x(slot):
        return remote(q_in.at[slot], qraw.at[slot, own_px], q_s.at[slot, 1], q_r.at[slot, 1], along_x)

    def on_to_x(slot):
        if slot == slots[0]:
            return remote(q_in.at[slot], qraw.at[slot, own_px], q_s.at[slot, 2], q_r.at[slot, 2], member(slab, from_xy))
        return remote(block_of(slot, from_y), block_of(slot, from_y), q_s.at[slot, 2], q_r.at[slot, 2], along_x)

    def to_partner(slot):
        return remote(q_in.at[slot], qraw.at[slot, own_px], k_s.at[slot], k_r.at[slot], partner)

    def passed(slot, i):
        at = block_of(slot, (from_y, from_x, from_xy)[i])
        return remote(at, at, f_s.at[slot, i], f_r.at[slot, i], partner)

    def kept(slot):
        return pltpu.make_async_copy(q_in.at[slot], qraw.at[slot, own_px], l_s.at[2 + slot])

    to_x(slots[0]).start()
    on_to_x(slots[0]).start()
    for slot in slots:
        to_y(slot).start()
        to_partner(slot).start()
        kept(slot).start()

    block_rows = 5 * pn.width // MEMBERS
    home_slab = me // pn.G

    def dproj_slab(kk):
        other = lax.rem(me + kk, MEMBERS)
        return remote(dproj_in.at[pl.ds(pl.multiple_of(other * block_rows, 16), block_rows)], dp1.at[me],
                      p1_s.at[kk], p1_r.at[kk], member(slab, other))

    def dproj_own():
        return pltpu.make_async_copy(dproj_in.at[pl.ds(pl.multiple_of(me * block_rows, 16), block_rows)], dp1.at[me],
                                     p1_r.at[0])

    def dproj_home():
        return remote(dps, dp2.at[slab], p2_s.at[0], p2_r.at[slab], member(home_slab, me))

    def dproj_give(c):
        return remote(dpf, dproj_out, p3_s.at[c], p3_r.at[0], (slab * pn.G + lax.rem(me, pn.G), c))

    def clear(rb, carry):
        dxe[pl.ds(pl.multiple_of(rb * px, 16), px)] = jnp.zeros((px, pn.cs), F32)
        return carry

    lax.fori_loop(0, pn.nb, clear, 0)

    def receive_y(slot):
        to_y(slot).wait()
        if slot != slots[0]:
            on_to_x(slot).start()
        passed(slot, 0).start()
        if slot != slots[-1]:
            to_x(slots[slots.index(slot) + 1]).start()

    def receive_x(slot):
        to_x(slot).wait()
        passed(slot, 1).start()
        on_to_x(slot).wait()
        passed(slot, 2).start()

    def received(slot):
        to_partner(slot).wait()
        kept(slot).wait()
        for i in range(3):
            passed(slot, i).wait()

    home = home_of(pn, col)
    closing, rising, falling = slab == home, slab < home, slab > home
    first = (slab == 0) | (slab == n - 1)
    half_rows = pn.cs // 2
    detour_up, detour_down = (slab == 0) & (col == 2), (slab == n - 1) & (col == 3)
    yielding = first & jnp.logical_not(closing | detour_up | detour_down)
    relay_up, relay_down = (slab == 0) & (col == 0), (slab == n - 1) & (col == 1)

    def taps(g):
        return pl.ds(POINT, 2) if isinstance(g, int) and g == GROUPS - 1 else pl.ds(3 * g, 3)

    def part_of(ref, g, half):
        return ref.at[taps(g), pl.ds(half * half_rows, half_rows)]

    def link(g, half, up):
        side, to = (0, slab + 1) if up else (1, slab - 1)
        return remote(part_of(dwbuf, g, half), part_of(inn.at[side], g, half), n_s.at[half, g], n_r.at[side, half, g],
                      (to * pn.G + x, col))

    def detour(g, up):
        side = 0 if up else 1
        return remote(part_of(dwbuf, g, 1), part_of(inn.at[side], g, 1), n_s.at[1, g], e_r.at[g], (row, col - 2))

    def relay(g, up):
        side, to = (0, slab + 1) if up else (1, slab - 1)
        return remote(part_of(inn.at[side], g, 1), part_of(inn.at[side], g, 1), e_s.at[g], n_r.at[side, 1, g],
                      (to * pn.G + x, col))

    def early_links(g, act):
        for going, up, around in ((rising, True, detour_up), (falling, False, detour_down)):
            @pl.when(going & jnp.logical_not(around))
            def _(up=up):
                for half in (0, 1):
                    act(link(g, half, up))

            @pl.when(around)
            def _(up=up):
                act(detour(g, up))

    def late_links(g, act):
        for around, up in ((detour_up, True), (detour_down, False)):
            @pl.when(around)
            def _(up=up):
                act(link(g, 0, up))

    def arrived(g, side):
        for half in (0, 1):
            at = part_of(inn.at[side], g, half)
            pltpu.make_async_copy(at, at, n_r.at[side, half, g]).wait()

    def add(g, side):
        dwbuf[taps(g)] = (dwbuf[taps(g)].astype(F32) + inn[side, taps(g)].astype(F32)).astype(BF16)

    close_a, close_b = closing & jnp.logical_not(first), ((slab == 1) & (col == 0)) | ((slab == n - 2) & (col == 1))
    end_closing, end_getting = closing & first, first & (home_of(pn, lax.rem(col + 2, pn.C)) == slab)
    across = (row, lax.rem(col + 2, pn.C))

    def share_y(g, half, src):
        return remote(src, part_of(dw_out, g, half), g_s.at[0, half, g], g_r.at[half, g], across)

    def share_core(g, half, src):
        return remote(src, part_of(dw_out, g, half), g_s.at[1, half, g], g_r.at[half, g], partner)

    def share_on(g, half):
        return remote(part_of(dw_out, g, half), part_of(dw_out, g, half), g_s.at[0, half, g], g_r.at[half, g], partner)

    def share(g, half, src):
        share_y(g, half, src).start()
        share_core(g, half, src).start()
        pltpu.make_async_copy(src, part_of(dw_out, g, half), g_r.at[half, g]).start()

    def landed(g, half):
        at = part_of(dw_out, g, half)
        pltpu.make_async_copy(at, at, g_r.at[half, g]).wait()

    def partial(g, side):
        return remote(part_of(dwbuf, g, 1), part_of(inn.at[1 - side], g, 0), b_s.at[g], b_r.at[g], (row, col - 2))

    rows_of = (pl.ds(0, half_rows), pl.ds(half_rows, half_rows))

    def from_far(g):
        for here, side in ((slab == 1, 1), (slab == n - 2, 0)):
            @pl.when(close_a & here)
            def _(side=side):
                arrived(g, side)
                add(g, side)
                partial(g, side).start()

    def close_half(g):
        for here, side in ((slab == 1, 0), (slab == n - 2, 1)):
            @pl.when(close_a & here)
            def _(side=side):
                at = part_of(inn.at[side], g, 0)
                pltpu.make_async_copy(at, at, n_r.at[side, 0, g]).wait()
                dwbuf[taps(g), rows_of[0]] = (
                    dwbuf[taps(g), rows_of[0]].astype(F32) + inn[side, taps(g), rows_of[0]].astype(F32)
                ).astype(BF16)
                share(g, 0, part_of(dwbuf, g, 0))

            @pl.when(close_b & here)
            def _(side=side):
                at = part_of(inn.at[side], g, 1)
                pltpu.make_async_copy(at, at, n_r.at[side, 1, g]).wait()
                at = part_of(inn.at[side], g, 0)
                pltpu.make_async_copy(at, at, b_r.at[g]).wait()
                inn[side, taps(g), rows_of[1]] = (
                    inn[side, taps(g), rows_of[1]].astype(F32) + inn[side, taps(g), rows_of[0]].astype(F32)
                ).astype(BF16)
                share(g, 1, part_of(inn.at[side], g, 1))

    def give_way():
        @pl.when(yielding)
        def _():
            for g in range(YIELD):
                early_links(g, lambda c: c.wait_send())
            pl.semaphore_signal(turn_sem, inc=1, device_id=partner, device_id_type=MESH)

        @pl.when(detour_up | detour_down)
        def _():
            pl.semaphore_wait(turn_sem, 1)

        for g in range(GROUPS):
            late_links(g, lambda c: c.start())

    def relay_all():
        for role, up in ((relay_up, True), (relay_down, False)):
            @pl.when(role)
            def _(up=up):
                pl.semaphore_wait(turn_sem, 1)
                for g in range(GROUPS):
                    at = part_of(inn.at[0 if up else 1], g, 1)
                    pltpu.make_async_copy(at, at, e_r.at[g]).wait()
                    relay(g, up).start()

    def pass_on(g, hop):
        for going, up in ((rising, True), (falling, False)):
            at_hop = (slab == 1) if up == (hop == 1) else (slab != 1)

            @pl.when(going & jnp.logical_not(first) & at_hop)
            def _(up=up):
                arrived(g, 0 if up else 1)
                add(g, 0 if up else 1)
                for half in (0, 1):
                    link(g, half, up).start()

    def close(g):
        for here, side in ((slab == 0, 1), (slab == n - 1, 0)):
            @pl.when(end_closing & here)
            def _(side=side):
                arrived(g, side)
                add(g, side)
                for half in (0, 1):
                    share(g, half, part_of(dwbuf, g, half))

    def serve(g):
        if not pn.exchange:
            return
        if g < GROUPS:
            pass_on(g, 1)
        if 0 < g <= GROUPS:
            pass_on(g - 1, 2)
        if g > 1:
            close(g - 2)
            from_far(g - 2)

    def last_round(g):
        if g < GROUPS:
            close_half(g)
        if g > 1:
            for half, role in ((0, end_getting | close_b), (1, end_getting | close_a)):
                @pl.when(role)
                def _(half=half):
                    landed(g - 2, half)
                    share_on(g - 2, half).start()

    def start_group(g):
        if not pn.exchange:
            return

        @pl.when(first)
        def _():
            early_links(g, lambda c: c.start())

    def weight_gradients(branch):
        qt[...] = qraw[branch].T
        for i in (-1, 0, 1):
            g = 3 * (branch - 1) + i + 1
            q_turned = qt[...]
            if i != 0:
                q_turned = q_turned * lane_masks[pl.ds(2 * (branch - 1) + (i + 1) // 2, 1)]
            window = pl.ds((pn.hb + i * pn.steps[branch - 1]) * px, pn.own)
            for j in (-1, 0, 1):
                dwbuf[3 * g + j + 1] = dot(q_turned, xs[3 + j * branch, window]).T.astype(BF16)
            if branch < 3:
                start_group(g)

    def feature_gradients(branch):
        def turn(rp, carry):
            at = pl.multiple_of(rp * 2 * S, 16)
            moved = dot(shifts[pl.ds((branch - 1) * 4 * S, 4 * S)], qraw[branch, pl.ds(at, 2 * S)]).astype(BF16)
            qs[branch - 1, 0, pl.ds(at, 2 * S)] = moved[:2 * S]
            qs[branch - 1, 1, pl.ds(at, 2 * S)] = moved[2 * S:]
            return carry

        lax.fori_loop(0, H // 2, turn, 0, unroll=6)
        for i in (-1, 0, 1):
            g = 3 * (branch - 1) + i + 1
            mask_at = (2 * (branch - 1) + (i + 1) // 2) * H

            def block(rb, carry, i=i, g=g, mask_at=mask_at):
                at = pl.ds(pl.multiple_of(rb * many * px, 16), many * px)
                y = dot_nt(qs[branch - 1, 0, at], wbuf[3 * g])
                y = y + dot_nt(qraw[branch, at], wbuf[3 * g + 1])
                y = y + dot_nt(qs[branch - 1, 1, at], wbuf[3 * g + 2])
                if i != 0:
                    y = jnp.concatenate(
                        [y[r * S:(r + 1) * S] * masks[mask_at + rb * many * pn.rpb + r] for r in range(many * pn.rpb)], axis=0
                    )
                to = pl.ds(pl.multiple_of((rb * many + pn.hb + i * pn.steps[branch - 1]) * px, 16), many * px)
                dxe[to] = dxe[to] + y
                return carry

            lax.fori_loop(0, MEMBERS // many, block, 0)

    receive_y(1)
    receive_y(2)
    load_x.wait()
    load_w.wait()
    receive_x(1)
    received(1)
    weight_gradients(1)
    receive_y(3)
    receive_x(2)
    feature_gradients(1)
    receive_y(0)
    received(2)
    weight_gradients(2)
    receive_x(3)
    serve(0)
    feature_gradients(2)
    received(3)
    receive_x(0)
    if pn.exchange:
        for kk in range(1, MEMBERS):
            dproj_slab(kk).start()
        dproj_own().start()
    serve(1)
    weight_gradients(3)
    serve(2)
    feature_gradients(3)

    hsend[0] = dxe[pl.ds(0, pn.hb * px)].astype(BF16)
    hsend[1] = dxe[pl.ds((pn.hb + MEMBERS) * px, pn.hb * px)].astype(BF16)

    @pl.when(slab > 0)
    def _():
        remote(hsend.at[0], hrecv.at[1], h_s.at[0], h_r.at[1], member(slab - 1, me)).start()

    @pl.when(slab < n - 1)
    def _():
        remote(hsend.at[1], hrecv.at[0], h_s.at[1], h_r.at[0], member(slab + 1, me)).start()

    for g in (6, 7, 8):
        start_group(g)
    serve(3)

    if pn.exchange:
        for kk in range(1, MEMBERS):
            dproj_slab(kk).wait()
        dproj_own().wait()
        total = dp1[0].astype(F32)
        for m in range(1, MEMBERS):
            total = total + dp1[m].astype(F32)
        dps[...] = total.astype(BF16)

        @pl.when(slab != home_slab)
        def _():
            dproj_home().start()

        @pl.when(slab == home_slab)
        def _():
            pltpu.make_async_copy(dps, dp2.at[slab], p2_r.at[slab]).start()

    received(0)
    dwbuf[POOL] = dot_tn(means[...].astype(BF16), q4[...]).astype(BF16)
    dwbuf[POINT] = dot(qraw[0].T, xs[3, pl.ds(pn.hb * px, pn.own)]).T.astype(BF16)
    start_group(GROUPS - 1)
    serve(4)
    pooled = dot_nt(q4[...], wbuf[POOL]) * inv_counts[...]
    pooled_high = pooled.astype(BF16)
    pooled_low = (pooled - pooled_high.astype(F32)).astype(BF16)
    pooled_rows[...] = dot(hot_rows[...], pooled_high) + dot(hot_rows[...], pooled_low)

    def finish(rb, carry):
        at = pl.ds(pl.multiple_of(rb * many * px, 16), many * px)
        to = pl.ds(pl.multiple_of((rb * many + pn.hb) * px, 16), many * px)
        y = dot_nt(qraw[0, at], wbuf[POINT])
        y = jnp.concatenate(
            [y[r * S:(r + 1) * S] + pooled_rows[pl.ds(rb * many * pn.rpb + r, 1)] for r in range(many * pn.rpb)], axis=0
        )
        dxe[to] = dxe[to] + y
        return carry

    lax.fori_loop(0, MEMBERS // many, finish, 0)
    if pn.exchange:
        relay_all()
    serve(5)

    @pl.when(slab > 0)
    def _():
        remote(hsend.at[0], hrecv.at[1], h_s.at[0], h_r.at[1], member(slab - 1, me)).wait_send()
        remote(hsend.at[1], hrecv.at[0], h_s.at[1], h_r.at[0], member(slab - 1, me)).wait_recv()

    @pl.when(slab < n - 1)
    def _():
        remote(hsend.at[1], hrecv.at[0], h_s.at[1], h_r.at[0], member(slab + 1, me)).wait_send()
        remote(hsend.at[0], hrecv.at[1], h_s.at[0], h_r.at[1], member(slab + 1, me)).wait_recv()

    @pl.when(slab == 0)
    def _():
        hrecv[0] = jnp.zeros((pn.hb * px, pn.cs), BF16)

    @pl.when(slab == n - 1)
    def _():
        hrecv[1] = jnp.zeros((pn.hb * px, pn.cs), BF16)

    for rb in range(pn.hb):
        low, high = (pn.hb + rb) * px, (MEMBERS + rb) * px
        dxe[pl.ds(low, px)] = dxe[pl.ds(low, px)] + hrecv[0, pl.ds(rb * px, px)].astype(F32)
        dxe[pl.ds(high, px)] = dxe[pl.ds(high, px)] + hrecv[1, pl.ds(rb * px, px)].astype(F32)

    column = lax.broadcasted_iota(jnp.int32, (S, pn.cs), 0).astype(F32)
    for b in range(H // 8):
        rows = []
        for r in range(8 * b, 8 * b + 8):
            values = dxe[pl.ds(pn.hb * px + r * S, S)]
            rows.append(jnp.where(column < masks[6 * H + MARGIN + r], values, 0.0))
        moved = dot(sel_t[...], jnp.concatenate(rows, axis=0).astype(BF16)).astype(BF16)
        pack[8 * b // h, :, pl.ds(8 * b % h, 8)] = moved.reshape(pn.cols, 8, pn.cs)
    own_lanes = pl.ds(pl.multiple_of(slice_of(pn, me) * pn.cs, 128), pn.cs)
    back = []
    for kk in range(1, MEMBERS):
        other = lax.rem(me + kk, MEMBERS)
        xo, co = other // pn.C, lax.rem(other, pn.C)
        c = remote(pack.at[xo, pl.ds(co * pn.bc, pn.bc)], dx_out.at[:, :, own_lanes], x_s.at[kk], x_r.at[kk],
                   member(slab, other))
        c.start()
        back.append(c)
    c = pltpu.make_async_copy(pack.at[x, pl.ds(col * pn.bc, pn.bc)], dx_out.at[:, :, own_lanes], x_r.at[0])
    c.start()
    back.append(c)

    def close_dproj():
        @pl.when(slab == home_slab)
        def _():
            for z in range(n):
                pltpu.make_async_copy(dp2.at[z], dp2.at[z], p2_r.at[z]).wait()
            total = dp2[0].astype(F32)
            for z in range(1, n):
                total = total + dp2[z].astype(F32)
            dpf[...] = total
            for c in range(pn.C):
                @pl.when((x == lax.rem(me, pn.G)) & (col == c))
                def _():
                    pltpu.make_async_copy(dpf, dproj_out, p3_r.at[0]).start()

                @pl.when(jnp.logical_not((x == lax.rem(me, pn.G)) & (col == c)))
                def _(c=c):
                    dproj_give(c).start()

    if pn.exchange:
        serve(6)
        serve(7)
        give_way()
        for g in range(8, GROUPS + 2):
            serve(g)
        close_dproj()
        for g in range(GROUPS + 2):
            last_round(g)

        def settle(g, carry):
            @pl.when(jnp.logical_not(yielding & (g < YIELD)))
            def _():
                early_links(g, lambda c: c.wait_send())

            late_links(g, lambda c: c.wait_send())
            for role, up in ((relay_up, True), (relay_down, False)):
                @pl.when(role)
                def _(up=up):
                    relay(g, up).wait_send()

            @pl.when(close_a)
            def _():
                partial(g, 0).wait_send()

            for half, gives, passes in ((0, end_closing | close_a, end_getting | close_b),
                                        (1, end_closing | close_b, end_getting | close_a)):
                @pl.when(gives)
                def _(half=half):
                    share_y(g, half, part_of(dwbuf, g, half)).wait_send()
                    share_core(g, half, part_of(dwbuf, g, half)).wait_send()

                @pl.when(passes)
                def _(half=half):
                    share_on(g, half).wait_send()

                @pl.when(jnp.logical_not(passes))
                def _(half=half):
                    landed(g, half)

            return carry

        lax.fori_loop(0, GROUPS - 1, settle, 0)
        settle(GROUPS - 1, 0)

        @pl.when(slab != home_slab)
        def _():
            dproj_home().wait_send()

        @pl.when(slab == home_slab)
        def _():
            for c in range(pn.C):
                @pl.when(jnp.logical_not((x == lax.rem(me, pn.G)) & (col == c)))
                def _(c=c):
                    dproj_give(c).wait_send()

        pltpu.make_async_copy(dproj_out, dproj_out, p3_r.at[0]).wait()
    else:
        c = pltpu.make_async_copy(dwbuf, dw_out, g_r.at[0, 0])
        c.start()
        c.wait()
        dproj_out[...] = jnp.zeros(dproj_out.shape, F32)
    for c in back:
        c.wait()


def conv_backward(pn, q, xs, w, dproj, q4, means, hot_rows, inv_counts, masks, lane_masks, shifts, sel_t):
    dma = pltpu.SemaphoreType.DMA
    vmem = pl.BlockSpec(memory_space=pltpu.VMEM)
    hbm = pl.BlockSpec(memory_space=pl.ANY)
    shape = jax.ShapeDtypeStruct
    n = pn.slabs if pn.exchange else 1
    sums = TAPS if pn.exchange else 1
    block_rows = 5 * pn.width // MEMBERS
    return pl.pallas_call(
        functools.partial(back_kernel, pn),
        out_shape=(
            shape((TAPS, pn.cs, pn.width), BF16),
            shape((pn.bc, pn.h, pn.channels), BF16),
            shape((block_rows, pn.width), F32),
        ),
        in_specs=[hbm] * 4 + [vmem] * 4 + [pl.BlockSpec(memory_space=pltpu.SMEM)] + [vmem] * 3,
        out_specs=(hbm, hbm, vmem),
        scratch_shapes=[
            pltpu.VMEM((7, pn.ext, pn.cs), BF16),
            pltpu.VMEM((TAPS, pn.cs, pn.width), BF16),
            pltpu.VMEM((4, pn.own, pn.width), BF16),
            pltpu.VMEM((3, 2, pn.own, pn.width), BF16),
            pltpu.VMEM((pn.width, pn.own), BF16),
            pltpu.VMEM((pn.ext, pn.cs), F32),
            pltpu.VMEM((TAPS, pn.cs, pn.width), BF16),
            pltpu.VMEM((2, sums, pn.cs, pn.width), BF16),
            pltpu.VMEM((2, pn.hb * pn.px, pn.cs), BF16),
            pltpu.VMEM((2, pn.hb * pn.px, pn.cs), BF16),
            pltpu.VMEM((pn.G, pn.cols, pn.h, pn.cs), BF16),
            pltpu.VMEM((pn.H, pn.cs), F32),
            pltpu.VMEM((MEMBERS, block_rows, pn.width), BF16),
            pltpu.VMEM((block_rows, pn.width), BF16),
            pltpu.VMEM((n, block_rows, pn.width), BF16),
            pltpu.VMEM((block_rows, pn.width), F32),
            dma((6,)), dma((4, 3)), dma((4, 3)), dma((4,)), dma((4,)), dma((4, 3)), dma((4, 3)),
            dma((2, GROUPS)), dma((2, 2, GROUPS)), dma((GROUPS,)), dma((GROUPS,)), dma((2, 2, GROUPS)), dma((2, GROUPS)),
            dma((GROUPS,)), dma((GROUPS,)), pltpu.SemaphoreType.REGULAR,
            dma((2,)), dma((2,)), dma((MEMBERS,)), dma((MEMBERS,)),
            dma((MEMBERS,)), dma((MEMBERS,)), dma((1,)), dma((n,)), dma((pn.C,)), dma((1,)),
        ],
        compiler_params=pltpu.CompilerParams(collective_id=2, has_side_effects=True, vmem_limit_bytes=61900 * 1024),
        name="conv_backward",
    )(q, xs, w, dproj, q4, means, hot_rows, inv_counts, masks, lane_masks, shifts, sel_t)


def column_tables(pn):
    S, bp, bc = pn.S, pn.bp, pn.bc
    sel = np.zeros((7, 2, S, 2, pn.C * bp), np.float32)
    shifts = np.zeros((3, 2, 2, S, 2, S), np.float32)
    for r in range(2):
        for c in range(pn.cols):
            for v in range(-3, 4):
                s = c + v * DILATIONS[0]
                if 0 <= s < pn.cols:
                    sel[v + 3, r, c, r, (s // bc) * bp + s % bc] = 1.0
            for b, d in enumerate(DILATIONS):
                for n, j in enumerate((-1, 1)):
                    s = c - j * d
                    if 0 <= s < pn.cols:
                        shifts[b, n, r, c, r, s] = 1.0
    sel = sel.reshape(7 * 2 * S, 2 * pn.C * bp)
    sel_t = sel[3 * 2 * S:4 * 2 * S].T
    sel_c = np.zeros((pn.cols, 8, 8, S), np.float32)
    for c in range(pn.cols):
        for r in range(8):
            sel_c[c, r, r, c] = 1.0
    sel_c = sel_c.reshape(8 * pn.cols, 8 * S)
    return (jnp.asarray(sel, BF16), jnp.asarray(sel_t, BF16), jnp.asarray(sel_c, BF16), jnp.asarray(shifts.reshape(12 * S, 2 * S), BF16))


def per_device(
    features, crop_rows, crop_cols, w_point, w_atrous, w_pool, w_proj, gains, biases, cotangent
):
    h, bc, channels = features.shape
    pn = Plan(lax.axis_size("row"), lax.axis_size("col"), h, bc, channels, gains.shape[1], crop_rows.shape[0])
    row, col = lax.axis_index("row"), lax.axis_index("col")
    slab, x = row // pn.G, row % pn.G
    crop_ids = jnp.arange(pn.crops, dtype=jnp.int32)
    ends = jnp.cumsum(crop_rows)
    counts = (crop_rows * crop_cols).astype(F32)
    pixels = jnp.sum(counts)

    def crop_of(rows):
        found = jnp.sum((rows[:, None] >= ends[None, :]).astype(jnp.int32), axis=1)
        return jnp.where(rows < 0, -1, found)

    def widths_of(crop):
        return jnp.sum(jnp.where(crop[:, None] == crop_ids[None, :], crop_cols[None, :], 0), axis=1)

    feats = features.reshape(h, bc, MEMBERS, pn.cs).transpose(2, 0, 1, 3)
    feats = jnp.pad(feats, ((0, 0), (0, 0), (0, pn.bp - bc), (0, 0)))
    cot = jnp.pad(cotangent, ((0, 0), (0, pn.bp - bc), (0, 0)))

    slab_rows = slab * pn.H - MARGIN + jnp.arange(pn.H + 2 * MARGIN, dtype=jnp.int32)
    crops = crop_of(slab_rows)
    mid = crops[MARGIN:MARGIN + pn.H]
    same = jnp.stack(
        [crops[MARGIN + i * d:MARGIN + i * d + pn.H] == mid for d in DILATIONS for i in (-1, 1)]
    ).astype(F32)
    lane_masks = jnp.pad(jnp.repeat(same, pn.S, axis=1), ((0, 2), (0, 0))).astype(BF16)
    ncp_ids = jnp.arange(pn.ncp, dtype=jnp.int32)
    hot_rows = (mid[:, None] == ncp_ids[None, :]).astype(BF16)
    hot_t = jnp.repeat(hot_rows.T, pn.S, axis=1)
    inv_counts = jnp.pad(1.0 / counts, (0, pn.ncp - pn.crops))[:, None]

    k = x * pn.C + col
    block_crop = lax.dynamic_slice_in_dim(mid, k * pn.rpb, pn.rpb)
    columns = jnp.arange(pn.S, dtype=jnp.int32)
    valid = (columns[None, :] < widths_of(block_crop)[:, None]).astype(F32).reshape(pn.px, 1)
    block_hot = jnp.repeat((block_crop[:, None] == ncp_ids[None, :]).astype(BF16), pn.S, axis=0)
    block_hot_t = jnp.repeat((ncp_ids[:, None] == block_crop[None, :]).astype(BF16), pn.S, axis=1)

    sel, sel_t, sel_c, shifts = column_tables(pn)
    w, w_two = w_atrous.transpose(1, 0, 2), jnp.stack([w_point, w_pool])
    proj = w_proj.reshape(pn.C, pn.proj // pn.C, pn.width)
    proj = jnp.pad(proj, ((0, 0), (0, pn.piece - pn.proj // pn.C), (0, 0)))
    if not pn.exchange:
        w = lax.all_gather(jnp.concatenate([w, w_two], axis=0), "row", axis=1, tiled=True)
        w = lax.dynamic_slice_in_dim(w, slice_of(pn, x * pn.C + col) * pn.cs, pn.cs, axis=1)
        w, w_two = w[:POINT], w[POINT:]
    flat = jnp.concatenate([same.reshape(-1), widths_of(crops).astype(F32)])
    p, xs, w_own, means, p4, own_cot, pieces = conv_forward(
        pn, feats, w, w_two, cot, proj, flat, sel, hot_t, inv_counts
    )
    full_proj = pieces[:, :, :pn.proj // pn.C].transpose(1, 0, 2, 3).reshape(5 * pn.width, pn.width)
    q, q4, d_proj, res, d_gains, d_biases = norms(
        pn, p, p4, gains, biases, valid, (1.0 / pixels)[None], full_proj, own_cot, block_hot, block_hot_t, sel_t
    )
    dw, dx, dproj_sum = conv_backward(
        pn, q, xs, w_own, d_proj, q4, means, hot_rows, inv_counts, flat, lane_masks, shifts, sel_c
    )
    if pn.exchange:
        d_proj = dproj_sum
    else:
        whole = jnp.zeros((TAPS, channels, pn.width), BF16)
        whole = lax.dynamic_update_slice(whole, dw, (0, slice_of(pn, x * pn.C + col) * pn.cs, 0))
        whole = lax.psum(whole, "col")
        dw = lax.psum_scatter(whole, "row", scatter_dimension=1, tiled=True)
        d_proj = lax.psum(d_proj, "col")
        d_proj = lax.psum_scatter(d_proj.astype(F32), "row", scatter_dimension=0, tiled=True)
    result = res[:, :bc]
    d_features = dx.transpose(1, 0, 2)
    d_point = dw[POINT].astype(F32)
    d_atrous = dw[:POINT].astype(F32).transpose(1, 0, 2)
    d_pool = dw[POOL].astype(F32)
    return (result, d_features, d_point, d_atrous, d_pool, d_proj, d_gains, d_biases)


def solution(mesh):
    return jax.shard_map(
        per_device,
        mesh=mesh,
        in_specs=(
            P("row", "col", None),
            P(),
            P(),
            P("row", None),
            P("row", None, None),
            P("row", None),
            P("row", None),
            P(),
            P(),
            P("row", "col", None),
        ),
        out_specs=(
            P("row", "col", None),
            P("row", "col", None),
            P("row", None),
            P("row", None, None),
            P("row", None),
            P("row", None),
            P(),
            P(),
        ),
        check_vma=False,
    )
```

```python
import functools

import jax
import jax.numpy as jnp
import numpy as np
from jax import lax
from jax.experimental import pallas as pl
from jax.experimental.pallas import tpu as pltpu
from jax.sharding import PartitionSpec as P

EPSILON = 1e-05
MARGIN = 18
DILATIONS = (6, 12, 18)
MEMBERS = 8
TAPS = 29
POINT, POOL, GROUPS = 27, 28, 10
YIELD = 5
MESH = pl.DeviceIdType.MESH
F32 = jnp.float32
BF16 = jnp.bfloat16

def up_to(value, multiple):
    return -(-value // multiple) * multiple


class Plan:
    def __init__(self, rows_axis, cols_axis, h, bc, channels, width, crops):
        self.R, self.C = rows_axis, cols_axis
        self.h, self.bc, self.channels, self.width = h, bc, channels, width
        self.G = MEMBERS // self.C
        self.slabs = self.R // self.G
        self.H = self.G * h
        self.cols = bc * self.C
        self.S = up_to(self.cols, 8)
        self.rpb = self.H // MEMBERS
        self.px = self.rpb * self.S
        self.own = MEMBERS * self.px
        self.hb = MARGIN // self.rpb
        self.nb = MEMBERS + 2 * self.hb
        self.ext = self.nb * self.px
        self.bp = up_to(bc, 16)
        self.cs = channels // MEMBERS
        self.crops = crops
        self.ncp = up_to(crops, 16)
        self.exchange = self.slabs == self.C and self.R == MEMBERS
        self.steps = tuple(d // self.rpb for d in DILATIONS)
        self.proj = 5 * width // self.R
        self.piece = up_to(self.proj // self.C, 16)


def home_of(pn, col):
    if pn.C != 4:
        return col
    y, c = col // 2, lax.rem(col, 2)
    return (1 - y) * 3 * c + y * (1 + c)


def slice_of(pn, k):
    return pn.G * home_of(pn, lax.rem(k, pn.C)) + k // pn.C


def remote(src, dst, send, recv, device):
    return pltpu.make_async_remote_copy(
        src_ref=src, dst_ref=dst, send_sem=send, recv_sem=recv, device_id=device, device_id_type=MESH
    )


def greet_all(pn, row, col):
    total = pn.R * pn.C
    barrier = pltpu.get_barrier_semaphore()
    me = row * pn.C + col

    def hello(k, carry):
        other = lax.rem(me + k, total)
        pl.semaphore_signal(
            barrier, inc=1, device_id=(other // pn.C, lax.rem(other, pn.C)), device_id_type=MESH
        )
        return carry

    lax.fori_loop(1, total, hello, 0)
    pl.semaphore_wait(barrier, total - 1)


def dot(a, b):
    return jnp.dot(a, b, preferred_element_type=F32)


def dot_nt(a, b):
    return lax.dot_general(a, b, (((1,), (1,)), ((), ())), preferred_element_type=F32)


def dot_tn(a, b):
    return lax.dot_general(a, b, (((0,), (0,)), ((), ())), preferred_element_type=F32)


def split_dot(dot_fn, a, b):
    high = a.astype(BF16)
    low = (a - high.astype(F32)).astype(BF16)
    return dot_fn(high, b) + dot_fn(low, b)


def conv_kernel(pn, feats, w_in, w_two, cot, proj, masks, sel, hot_t, inv_counts,
                p_out, x_out, w_out, m_out, p4_out, cot_out, proj_out,
                ring, xs, wbuf, acc, pbuf, cbuf, sbuf, rbuf, cx,
                f_s, f_r, h_s, h_r, c_s, c_r, j_s, j_r, t_s, t_r, w_s, w_r, w_l, e_s,
                r1_s, r1_r, r2_s, r2_r, o_s):
    row, col = lax.axis_index("row"), lax.axis_index("col")
    slab, x = row // pn.G, lax.rem(row, pn.G)
    me = x * pn.C + col
    core, quad = lax.rem(col, 2), me // 2
    h, H, bp, px, n = pn.h, pn.H, pn.bp, pn.px, pn.slabs
    many = 4

    def member(s, k):
        return (s * pn.G + k // pn.C, lax.rem(k, pn.C))

    greet_all(pn, row, col)

    own_cols = pl.ds(pl.multiple_of(col * bp, bp), bp)
    own_rows = pl.ds(MARGIN + h * x, h)
    sent = []
    for kk in range(1, MEMBERS):
        other = lax.rem(me + kk, MEMBERS)
        c = remote(feats.at[slice_of(pn, other)], ring.at[own_rows, own_cols], f_s.at[kk], f_r.at[kk], member(slab, other))
        c.start()
        sent.append(c)
    keep = pltpu.make_async_copy(feats.at[slice_of(pn, me)], ring.at[own_rows, own_cols], f_r.at[0])
    keep.start()

    home = home_of(pn, col)
    source, rising, falling = slab == home, (slab > home) & (slab < n - 1), (slab < home) & (slab > 0)
    help_up, help_down = (slab == n - 2) & (col == 1), (slab == 1) & (col == 0)
    half_rows = pn.cs // 2

    order = (0, 1, 2, 3, 4, 5, 9, 6, 7, 8)

    def taps(g):
        return pl.ds(POINT, 2) if isinstance(g, int) and g == GROUPS - 1 else pl.ds(3 * g, 3)

    def given(g, rows):
        if isinstance(g, int) and g == GROUPS - 1:
            return w_two.at[:, rows]
        return w_in.at[taps(g), rows]

    def half_of(half):
        return pl.ds(half * half_rows, half_rows)

    def part_of(ref, g, half):
        return ref.at[taps(g), half_of(half)]

    def ship(g, half, up, own):
        to = slab + 1 if up else slab - 1
        return remote(given(g, half_of(half)) if own else part_of(wbuf, g, half), part_of(wbuf, g, half), w_s.at[int(up), half, g], w_r.at[half, g],
                      (to * pn.G + x, col))

    def assist(g, up):
        to = slab + 1 if up else slab - 1
        return remote(given(g, half_of(1)), part_of(wbuf, g, 1), e_s.at[g], w_r.at[1, g], (to * pn.G + x, col + 2))

    def own_copy(g):
        return pltpu.make_async_copy(given(g, pl.ds(0, pn.cs)), wbuf.at[taps(g)], w_l.at[g])

    def arrived(g):
        for half in (0, 1):
            at = part_of(wbuf, g, half)
            pltpu.make_async_copy(at, at, w_r.at[half, g]).wait()

    def pass_on(g):
        for role, up in ((rising, True), (falling, False)):
            @pl.when(role)
            def _(up=up):
                arrived(g)
                for half in (0, 1):
                    ship(g, half, up, False).start()

    def w_wait(g):
        if pn.exchange:
            @pl.when(source)
            def _():
                own_copy(g).wait()

            @pl.when(jnp.logical_not(source | rising | falling))
            def _():
                arrived(g)
        else:
            own_copy(g).wait()

    def each_shipment(g, act):
        for half in (0, 1):
            @pl.when(source & ((slab < n - 2) if half else (slab < n - 1)))
            def _(half=half):
                act(ship(g, half, True, True))

            @pl.when(source & ((slab > 1) if half else (slab > 0)))
            def _(half=half):
                act(ship(g, half, False, True))

        @pl.when(help_up)
        def _():
            act(assist(g, True))

        @pl.when(help_down)
        def _():
            act(assist(g, False))

    if pn.exchange:
        def begin(g, carry):
            each_shipment(g, lambda c: c.start())

            @pl.when(source)
            def _():
                own_copy(g).start()

            return carry
    else:
        def begin(g, carry):
            own_copy(g).start()
            return carry

    early = 6
    lax.fori_loop(0, early, begin, 0)

    cot_sent = []
    for cc in range(1, pn.C):
        cd = lax.rem(col + cc, pn.C)
        c = remote(cot.at[pl.ds(cd * pn.rpb, pn.rpb)], cx.at[:, own_cols], c_s.at[cc], c_r.at[cc], (row, cd))
        c.start()
        cot_sent.append(c)
    cot_keep = pltpu.make_async_copy(cot.at[pl.ds(col * pn.rpb, pn.rpb)], cx.at[:, own_cols], c_r.at[0])
    cot_keep.start()

    def proj_row(k):
        return remote(proj.at[col], proj_out.at[col, row], j_s.at[k], j_r.at[k], (lax.rem(row + k, pn.R), col))

    def proj_col(k):
        return remote(proj_out.at[col], proj_out.at[col], t_s.at[k], t_r.at[k], (row, lax.rem(col + k, pn.C)))

    def proj_begin(k, carry):
        proj_row(k).start()
        return carry

    def proj_wait(k, carry):
        proj_row(k).wait()
        return carry

    lax.fori_loop(1, pn.R, proj_begin, 0)
    proj_keep = pltpu.make_async_copy(proj.at[col], proj_out.at[col, row], j_r.at[0])
    proj_keep.start()

    @pl.when(slab == 0)
    def _():
        ring[pl.ds(0, MARGIN)] = jnp.zeros((MARGIN, pn.C * bp, pn.cs), BF16)

    @pl.when(slab == n - 1)
    def _():
        ring[pl.ds(MARGIN + H, MARGIN)] = jnp.zeros((MARGIN, pn.C * bp, pn.cs), BF16)

    def pass_many(first, end):
        if pn.exchange:
            for k in range(first, end):
                pass_on(order[k])

    pass_many(0, 3)
    for c in sent:
        c.wait()
    keep.wait()

    def margin_down():
        return remote(ring.at[pl.ds(MARGIN, MARGIN)], ring.at[pl.ds(MARGIN + H, MARGIN)], h_s.at[0], h_r.at[0],
                      member(slab - 1, me))

    def margin_up():
        return remote(ring.at[pl.ds(H, MARGIN)], ring.at[pl.ds(0, MARGIN)], h_s.at[1], h_r.at[1], member(slab + 1, me))

    @pl.when(slab > 0)
    def _():
        margin_down().start()

    @pl.when(slab < n - 1)
    def _():
        margin_up().start()

    begin(GROUPS - 1, 0)
    lax.fori_loop(early, GROUPS - 1, begin, 0)

    column = lax.broadcasted_iota(jnp.int32, (pn.S, pn.cs), 0).astype(F32)

    def assemble(rp, carry):
        pair = ring[pl.ds(2 * rp, 2)].reshape(2 * pn.C * bp, pn.cs)
        moved = dot(sel[...], pair)
        at = pl.multiple_of(rp * 2 * pn.S, 16)
        wide = [masks[6 * H + 2 * rp + r] for r in range(2)]
        for v in range(7):
            rows = [
                jnp.where(column + float(DILATIONS[0] * (v - 3)) < wide[r], moved[(2 * v + r) * pn.S:(2 * v + r + 1) * pn.S], 0.0)
                for r in range(2)
            ]
            xs[v, pl.ds(at, 2 * pn.S)] = jnp.concatenate(rows, axis=0).astype(BF16)
        return carry

    lax.fori_loop(MARGIN // 2, (MARGIN + H) // 2, assemble, 0, unroll=6)
    pass_many(3, 5)
    for c in cot_sent:
        c.wait()
    cot_keep.wait()
    for rp in range(pn.rpb // 2):
        pair = cx[2 * rp:2 * rp + 2].reshape(2 * pn.C * bp, pn.width)
        cot_out[pl.ds(rp * 2 * pn.S, 2 * pn.S)] = dot(sel[pl.ds(3 * 2 * pn.S, 2 * pn.S)], pair).astype(BF16)
    lax.fori_loop(1, pn.R, proj_wait, 0)
    proj_keep.wait()
    for k in range(1, pn.C):
        proj_col(k).start()
    pass_many(5, 6)

    @pl.when(slab > 0)
    def _():
        margin_down().wait_send()
        margin_up().wait_recv()

    @pl.when(slab < n - 1)
    def _():
        margin_up().wait_send()
        margin_down().wait_recv()

    lax.fori_loop(0, MARGIN // 2, assemble, 0, unroll=3)
    lax.fori_loop((MARGIN + H) // 2, pn.nb * pn.rpb // 2, assemble, 0, unroll=3)
    x_save = pltpu.make_async_copy(xs, x_out, o_s.at[0])
    x_save.start()

    def first_stage(slot):
        return remote(pbuf.at[slot, :, 1 - core], cbuf.at[slot], r1_s.at[slot], r1_r.at[slot], (row, col + 1 - 2 * core))

    def second_stage(slot, i):
        q = lax.rem(quad + i, MEMBERS // 2)
        return remote(sbuf.at[slot, i - 1], rbuf.at[slot, i - 1], r2_s.at[slot, i - 1], r2_r.at[slot, i - 1],
                      member(slab, 2 * q + core))

    def middle(slot):
        first_stage(slot).wait()
        for i in (1, 2, 3, 0):
            q = lax.rem(quad + i, MEMBERS // 2)
            s = pbuf[slot, q, core].astype(F32) + cbuf[slot, q].astype(F32)
            if i == 0:
                p_out[slot] = s
            else:
                sbuf[slot, i - 1] = s.astype(BF16)
                second_stage(slot, i).start()

    def last(slot):
        total = p_out[slot]
        for i in range(1, MEMBERS // 2):
            second_stage(slot, i).wait()
            total = total + rbuf[slot, i - 1].astype(F32)
        p_out[slot] = total

    def scatter(slot, rb, y):
        for r in range(many):
            pbuf[slot, (many * rb + r) // 2, r % 2] = y[r * px:(r + 1) * px].astype(BF16)

    def far(k):
        if k in (2, 4, 6, 8):
            pass_many(5 + k // 2, 6 + k // 2)
        w_wait(order[k])

    def point(rb, carry):
        at = pl.ds(pl.multiple_of((rb * many + pn.hb) * px, 16), many * px)
        scatter(0, rb, dot(xs[3, at], wbuf[POINT]))
        return carry

    for branch in (1, 2, 3):
        step = pn.steps[branch - 1]
        if branch == 3:
            far(6)
            lax.fori_loop(0, MEMBERS // many, point, 0)
            first_stage(0).start()
            middle(2)
        for i in (-1, 0, 1):
            g = 3 * (branch - 1) + i + 1
            mask_at = (2 * (branch - 1) + (i + 1) // 2) * H
            far(g + branch // 3)

            def block(rb, carry, step=step, i=i, g=g, mask_at=mask_at, branch=branch):
                at = pl.multiple_of(rb * many * px, 16)
                window = pl.ds(pl.multiple_of((rb * many + pn.hb + i * step) * px, 16), many * px)
                y = dot(xs[3 - branch, window], wbuf[3 * g])
                y = y + dot(xs[3, window], wbuf[3 * g + 1])
                y = y + dot(xs[3 + branch, window], wbuf[3 * g + 2])
                if i != 0:
                    y = jnp.concatenate(
                        [y[r * pn.S:(r + 1) * pn.S] * masks[mask_at + rb * many * pn.rpb + r]
                         for r in range(many * pn.rpb)], axis=0
                    )
                if i > -1:
                    y = y + acc[pl.ds(at, many * px)]
                if i < 1:
                    acc[pl.ds(at, many * px)] = y
                else:
                    scatter(branch, rb, y)
                return carry

            lax.fori_loop(0, MEMBERS // many, block, 0)
            if i == 0 and branch > 1:
                middle(branch - 1 if branch == 2 else 0)
        first_stage(branch).start()

    sums = dot(hot_t[...], xs[3, pl.ds(pn.hb * px, pn.own)])
    means = sums * inv_counts[...]
    m_out[...] = means
    p4_out[...] = split_dot(dot, means, wbuf[POOL])
    w_save = pltpu.make_async_copy(wbuf, w_out, o_s.at[1])
    w_save.start()
    middle(3)
    for slot in (1, 2, 0):
        last(slot)
    for k in range(1, pn.C):
        proj_col(k).wait()
    if pn.exchange:
        def settled(g, carry):
            each_shipment(g, lambda c: c.wait_send())
            for role, up in ((rising, True), (falling, False)):
                @pl.when(role)
                def _(up=up):
                    for half in (0, 1):
                        ship(g, half, up, False).wait_send()
            return carry

        lax.fori_loop(0, GROUPS - 1, settled, 0)
        settled(GROUPS - 1, 0)
    last(3)
    x_save.wait()
    w_save.wait()


def conv_forward(pn, feats, w, w_two, cot, proj, masks, sel, hot_t, inv_counts):
    half = MEMBERS // 2
    dma = pltpu.SemaphoreType.DMA
    vmem = pl.BlockSpec(memory_space=pltpu.VMEM)
    hbm = pl.BlockSpec(memory_space=pl.ANY)
    shape = jax.ShapeDtypeStruct
    return pl.pallas_call(
        functools.partial(conv_kernel, pn),
        out_shape=(
            shape((4, pn.px, pn.width), F32),
            shape((7, pn.ext, pn.cs), BF16),
            shape((TAPS, pn.cs, pn.width), BF16),
            shape((pn.ncp, pn.cs), F32),
            shape((pn.ncp, pn.width), F32),
            shape((pn.px, pn.width), BF16),
            shape((pn.C, pn.R, pn.piece, pn.width), BF16),
        ),
        in_specs=[hbm, hbm, hbm, hbm, hbm, pl.BlockSpec(memory_space=pltpu.SMEM), vmem, vmem, vmem],
        out_specs=(vmem, hbm, hbm, vmem, vmem, vmem, vmem),
        scratch_shapes=[
            pltpu.VMEM((pn.nb * pn.rpb, pn.C * pn.bp, pn.cs), BF16),
            pltpu.VMEM((7, pn.ext, pn.cs), BF16),
            pltpu.VMEM((TAPS, pn.cs, pn.width), BF16),
            pltpu.VMEM((pn.own, pn.width), F32),
            pltpu.VMEM((4, half, 2, pn.px, pn.width), BF16),
            pltpu.VMEM((4, half, pn.px, pn.width), BF16),
            pltpu.VMEM((4, half - 1, pn.px, pn.width), BF16),
            pltpu.VMEM((4, half - 1, pn.px, pn.width), BF16),
            pltpu.VMEM((pn.rpb, pn.C * pn.bp, pn.width), BF16),
            dma((MEMBERS,)), dma((MEMBERS,)), dma((2,)), dma((2,)), dma((pn.C,)), dma((pn.C,)),
            dma((pn.R,)), dma((pn.R,)), dma((pn.C,)), dma((pn.C,)),
            dma((2, 2, GROUPS)), dma((2, GROUPS)), dma((GROUPS,)), dma((GROUPS,)),
            dma((4,)), dma((4,)), dma((4, 3)), dma((4, 3)), dma((2,)),
        ],
        compiler_params=pltpu.CompilerParams(collective_id=0, has_side_effects=True, vmem_limit_bytes=60 * 2**20),
        name="conv_forward",
    )(feats, w, w_two, cot, proj, masks, sel, hot_t, inv_counts)


def norm_kernel(pn, p, p4_in, gains, biases, valid, pixels, w_proj, cot, hot, hot_t, sel_t,
                q_out, q4_out, dproj_out, res_out, dg_out, db_out,
                norm, slope, hbuf, gact, dh4, rx,
                a1, b1, a2, b2, a3, b3, a4, b4, as_s, as_r, bs_s, bs_r, e_s, e_r):
    row, col = lax.axis_index("row"), lax.axis_index("col")
    slab, x = row // pn.G, lax.rem(row, pn.G)
    me = x * pn.C + col
    crops = float(pn.crops)
    v = valid[...]
    inv_px = pixels[0]
    width, bp = pn.width, pn.bp

    def member(s, k):
        return (s * pn.G + k // pn.C, lax.rem(k, pn.C))

    barrier = pltpu.get_barrier_semaphore()
    for kk in range(1, MEMBERS):
        pl.semaphore_signal(barrier, inc=1, device_id=member(slab, lax.rem(me + kk, MEMBERS)), device_id_type=MESH)

    def hello(k, carry):
        pl.semaphore_signal(barrier, inc=1, device_id=member(lax.rem(slab + k, pn.slabs), me), device_id_type=MESH)
        return carry

    lax.fori_loop(1, pn.slabs, hello, 0)

    def peer_a(n, abuf, kk):
        return remote(abuf.at[me], abuf.at[me], as_s.at[n, kk], as_r.at[n, kk], member(slab, lax.rem(me + kk, MEMBERS)))

    def peer_b(n, bbuf, k):
        return remote(bbuf.at[slab], bbuf.at[slab], bs_s.at[n, k], bs_r.at[n, k], member(lax.rem(slab + k, pn.slabs), me))

    def reduce_start(n, abuf):
        for kk in range(1, MEMBERS):
            peer_a(n, abuf, kk).start()

    def reduce_end(n, abuf, bbuf):
        for kk in range(1, MEMBERS):
            peer_a(n, abuf, kk).wait()
        total = abuf[0]
        for k in range(1, MEMBERS):
            total = total + abuf[k]
        bbuf[slab] = total
        for k in range(1, pn.slabs):
            peer_b(n, bbuf, k).start()
        for k in range(1, pn.slabs):
            peer_b(n, bbuf, k).wait()
        total = bbuf[0]
        for k in range(1, pn.slabs):
            total = total + bbuf[k]
        return total

    def column_sum(value):
        return jnp.sum(value, axis=0, keepdims=True)

    for b in range(4):
        pv = p[b] * v
        a1[me, pl.ds(b, 1)] = column_sum(pv)
        a1[me, pl.ds(4 + b, 1)] = column_sum(pv * p[b])
    a1[me, pl.ds(8, pn.ncp)] = p4_in[...]
    pl.semaphore_wait(barrier, MEMBERS - 1 + pn.slabs - 1)
    reduce_start(0, a1)
    total = reduce_end(0, a1, b1)
    inv = []
    for b in range(4):
        centre = total[b:b + 1] * inv_px
        scale = lax.rsqrt(total[4 + b:5 + b] * inv_px - centre * centre + EPSILON)
        inv.append(scale)
        n = (p[b] - centre) * scale
        u = gains[b:b + 1] * n + biases[b:b + 1]
        s = jax.nn.sigmoid(u)
        norm[b] = n
        slope[b] = s * (1.0 + u * (1.0 - s))
        hbuf[b] = (u * s).astype(BF16)
    p4 = total[8:8 + pn.ncp]
    centre4 = column_sum(p4) * (1.0 / crops)
    inv4 = lax.rsqrt(column_sum(p4 * p4) * (1.0 / crops) - centre4 * centre4 + EPSILON)
    n4 = (p4 - centre4) * inv4
    u4 = gains[4:5] * n4 + biases[4:5]
    s4 = jax.nn.sigmoid(u4)
    slope4 = s4 * (1.0 + u4 * (1.0 - s4))
    hbuf[4] = dot(hot[...], (u4 * s4).astype(BF16)).astype(BF16)

    p5 = dot(hbuf[0], w_proj[pl.ds(0, width)])
    for b in range(1, 5):
        p5 = p5 + dot(hbuf[b], w_proj[pl.ds(b * width, width)])
    pv = p5 * v
    a2[me, pl.ds(0, 1)] = column_sum(pv)
    a2[me, pl.ds(1, 1)] = column_sum(pv * p5)
    a2[me, pl.ds(2, 6)] = jnp.zeros((6, width), F32)
    reduce_start(1, a2)
    total = reduce_end(1, a2, b2)
    centre5 = total[0:1] * inv_px
    inv5 = lax.rsqrt(total[1:2] * inv_px - centre5 * centre5 + EPSILON)
    n5 = (p5 - centre5) * inv5
    u5 = gains[5:6] * n5 + biases[5:6]
    s5 = jax.nn.sigmoid(u5)
    g5 = cot[...].astype(F32) * v * (s5 * (1.0 + u5 * (1.0 - s5)))
    norm[4] = n5
    gact[4] = g5
    a3[me, pl.ds(0, 1)] = column_sum(g5)
    a3[me, pl.ds(1, 1)] = column_sum(g5 * n5)
    a3[me, pl.ds(2, 6)] = jnp.zeros((6, width), F32)
    reduce_start(2, a3)
    hbuf[5] = (v * u5 * s5).astype(BF16)
    for rp in range(pn.rpb // 2):
        pair = hbuf[5, pl.ds(rp * 2 * pn.S, 2 * pn.S)]
        rx[2 * rp:2 * rp + 2] = dot(sel_t[...], pair).astype(BF16).reshape(2, pn.C * bp, width)
    back = []
    for cc in range(1, pn.C):
        cd = lax.rem(col + cc, pn.C)
        c = remote(rx.at[:, pl.ds(pl.multiple_of(cd * bp, bp), bp)], res_out.at[pl.ds(col * pn.rpb, pn.rpb)],
                   e_s.at[cc], e_r.at[cc], (row, cd))
        c.start()
        back.append(c)
    c = pltpu.make_async_copy(rx.at[:, pl.ds(pl.multiple_of(col * bp, bp), bp)], res_out.at[pl.ds(col * pn.rpb, pn.rpb)],
                              e_r.at[0])
    c.start()
    back.append(c)
    total = reduce_end(2, a3, b3)
    db5, dg5 = total[0:1], total[1:2]
    q5 = (gains[5:6] * inv5 * (gact[4] - v * (db5 + norm[4] * dg5) * inv_px)).astype(BF16)
    hbuf[5] = q5

    for b in range(4):
        g = dot_nt(q5, w_proj[pl.ds(b * width, width)]) * slope[b]
        gact[b] = g
        a4[me, pl.ds(b, 1)] = column_sum(g)
        a4[me, pl.ds(4 + b, 1)] = column_sum(g * norm[b])
    dh4[...] = dot_nt(q5, w_proj[pl.ds(4 * width, width)])
    high = dh4[...].astype(BF16)
    low = (dh4[...] - high.astype(F32)).astype(BF16)
    a4[me, pl.ds(8, pn.ncp)] = dot(hot_t[...], high) + dot(hot_t[...], low)
    reduce_start(3, a4)
    for b in range(5):
        dproj_out[pl.ds(b * width, width)] = dot_tn(hbuf[b], hbuf[5]).astype(BF16)
    total = reduce_end(3, a4, b4)
    for b in range(4):
        db, dg = total[b:b + 1], total[4 + b:5 + b]
        db_out[pl.ds(b, 1)] = db
        dg_out[pl.ds(b, 1)] = dg
        q_out[b] = (gains[b:b + 1] * inv[b] * (gact[b] - v * (db + norm[b] * dg) * inv_px)).astype(BF16)
    g4 = total[8:8 + pn.ncp] * slope4
    db4, dg4 = column_sum(g4), column_sum(g4 * n4)
    db_out[pl.ds(4, 1)] = db4
    dg_out[pl.ds(4, 1)] = dg4
    db_out[pl.ds(5, 1)] = db5
    dg_out[pl.ds(5, 1)] = dg5
    q4_out[...] = (gains[4:5] * inv4 * (g4 - (db4 + n4 * dg4) * (1.0 / crops))).astype(BF16)
    for c in back:
        c.wait()


def norms(pn, p, p4, gains, biases, valid, pixels, w_proj, cot, hot, hot_t, sel_t):
    dma = pltpu.SemaphoreType.DMA
    vmem = pl.BlockSpec(memory_space=pltpu.VMEM)
    shape = jax.ShapeDtypeStruct
    big, small = 8 + pn.ncp, 8
    bufs = []
    for n in (big, small, small, big):
        bufs += [pltpu.VMEM((MEMBERS, n, pn.width), F32), pltpu.VMEM((pn.slabs, n, pn.width), F32)]
    return pl.pallas_call(
        functools.partial(norm_kernel, pn),
        out_shape=(
            shape((4, pn.px, pn.width), BF16),
            shape((pn.ncp, pn.width), BF16),
            shape((5 * pn.width, pn.width), BF16),
            shape((pn.h, pn.bp, pn.width), BF16),
            shape((6, pn.width), F32),
            shape((6, pn.width), F32),
        ),
        in_specs=[vmem] * 5 + [pl.BlockSpec(memory_space=pltpu.SMEM)] + [vmem] * 5,
        out_specs=(vmem,) * 6,
        scratch_shapes=[
            pltpu.VMEM((5, pn.px, pn.width), F32),
            pltpu.VMEM((4, pn.px, pn.width), F32),
            pltpu.VMEM((6, pn.px, pn.width), BF16),
            pltpu.VMEM((5, pn.px, pn.width), F32),
            pltpu.VMEM((pn.px, pn.width), F32),
            pltpu.VMEM((pn.rpb, pn.C * pn.bp, pn.width), BF16),
            *bufs,
            dma((4, MEMBERS)), dma((4, MEMBERS)), dma((4, pn.slabs)), dma((4, pn.slabs)), dma((pn.C,)), dma((pn.C,)),
        ],
        compiler_params=pltpu.CompilerParams(collective_id=1, has_side_effects=True, vmem_limit_bytes=48 * 2**20),
        name="norms",
    )(p, p4, gains, biases, valid, pixels, w_proj, cot, hot, hot_t, sel_t)


def back_kernel(pn, q_in, x_in, w_in, dproj_in, q4, means, hot_rows, inv_counts, masks, lane_masks, shifts, sel_t,
                dw_out, dx_out, dproj_out,
                xs, wbuf, qraw, qs, qt, dxe, dwbuf, inn, hsend, hrecv, pack, pooled_rows, dp1, dps, dp2, dpf,
                l_s, q_s, q_r, k_s, k_r, f_s, f_r, n_s, n_r, e_s, e_r, g_s, g_r, b_s, b_r, turn_sem, h_s, h_r, x_s, x_r,
                p1_s, p1_r, p2_s, p2_r, p3_s, p3_r):
    row, col = lax.axis_index("row"), lax.axis_index("col")
    slab, x = row // pn.G, lax.rem(row, pn.G)
    me = x * pn.C + col
    core, quad = lax.rem(col, 2), me // 2
    h, H, bp, px, S, n = pn.h, pn.H, pn.bp, pn.px, pn.S, pn.slabs
    half = MEMBERS // 2
    many = 4
    partner = (row, col + 1 - 2 * core)

    def member(s, k):
        return (s * pn.G + k // pn.C, lax.rem(k, pn.C))

    load_x = pltpu.make_async_copy(x_in, xs, l_s.at[0])
    load_w = pltpu.make_async_copy(w_in, wbuf, l_s.at[1])
    load_x.start()
    load_w.start()
    greet_all(pn, row, col)

    slots = (1, 2, 3, 0)
    own_px = pl.ds(pl.multiple_of(me * px, 16), px)
    along_y, along_x = (row, lax.rem(col + 2, pn.C)), (slab * pn.G + lax.rem(x + 1, pn.G), col)
    from_y = x * pn.C + lax.rem(col + 2, pn.C)
    from_x = lax.rem(me + pn.C, MEMBERS)
    from_xy = lax.rem(from_y + pn.C, MEMBERS)

    def block_of(slot, k):
        return qraw.at[slot, pl.ds(pl.multiple_of(k * px, 16), px)]

    def to_y(slot):
        return remote(q_in.at[slot], qraw.at[slot, own_px], q_s.at[slot, 0], q_r.at[slot, 0], along_y)

    def to_x(slot):
        return remote(q_in.at[slot], qraw.at[slot, own_px], q_s.at[slot, 1], q_r.at[slot, 1], along_x)

    def on_to_x(slot):
        if slot == slots[0]:
            return remote(q_in.at[slot], qraw.at[slot, own_px], q_s.at[slot, 2], q_r.at[slot, 2], member(slab, from_xy))
        return remote(block_of(slot, from_y), block_of(slot, from_y), q_s.at[slot, 2], q_r.at[slot, 2], along_x)

    def to_partner(slot):
        return remote(q_in.at[slot], qraw.at[slot, own_px], k_s.at[slot], k_r.at[slot], partner)

    def passed(slot, i):
        at = block_of(slot, (from_y, from_x, from_xy)[i])
        return remote(at, at, f_s.at[slot, i], f_r.at[slot, i], partner)

    def kept(slot):
        return pltpu.make_async_copy(q_in.at[slot], qraw.at[slot, own_px], l_s.at[2 + slot])

    to_x(slots[0]).start()
    on_to_x(slots[0]).start()
    for slot in slots:
        to_y(slot).start()
        to_partner(slot).start()
        kept(slot).start()

    block_rows = 5 * pn.width // MEMBERS
    home_slab = me // pn.G

    def dproj_slab(kk):
        other = lax.rem(me + kk, MEMBERS)
        return remote(dproj_in.at[pl.ds(pl.multiple_of(other * block_rows, 16), block_rows)], dp1.at[me],
                      p1_s.at[kk], p1_r.at[kk], member(slab, other))

    def dproj_own():
        return pltpu.make_async_copy(dproj_in.at[pl.ds(pl.multiple_of(me * block_rows, 16), block_rows)], dp1.at[me],
                                     p1_r.at[0])

    def dproj_home():
        return remote(dps, dp2.at[slab], p2_s.at[0], p2_r.at[slab], member(home_slab, me))

    def dproj_give(c):
        return remote(dpf, dproj_out, p3_s.at[c], p3_r.at[0], (slab * pn.G + lax.rem(me, pn.G), c))

    def clear(rb, carry):
        dxe[pl.ds(pl.multiple_of(rb * px, 16), px)] = jnp.zeros((px, pn.cs), F32)
        return carry

    lax.fori_loop(0, pn.nb, clear, 0)

    def receive_y(slot):
        to_y(slot).wait()
        if slot != slots[0]:
            on_to_x(slot).start()
        passed(slot, 0).start()
        if slot != slots[-1]:
            to_x(slots[slots.index(slot) + 1]).start()

    def receive_x(slot):
        to_x(slot).wait()
        passed(slot, 1).start()
        on_to_x(slot).wait()
        passed(slot, 2).start()

    def received(slot):
        to_partner(slot).wait()
        kept(slot).wait()
        for i in range(3):
            passed(slot, i).wait()

    home = home_of(pn, col)
    closing, rising, falling = slab == home, slab < home, slab > home
    first = (slab == 0) | (slab == n - 1)
    half_rows = pn.cs // 2
    detour_up, detour_down = (slab == 0) & (col == 2), (slab == n - 1) & (col == 3)
    yielding = first & jnp.logical_not(closing | detour_up | detour_down)
    relay_up, relay_down = (slab == 0) & (col == 0), (slab == n - 1) & (col == 1)

    def taps(g):
        return pl.ds(POINT, 2) if isinstance(g, int) and g == GROUPS - 1 else pl.ds(3 * g, 3)

    def part_of(ref, g, half):
        return ref.at[taps(g), pl.ds(half * half_rows, half_rows)]

    def link(g, half, up):
        side, to = (0, slab + 1) if up else (1, slab - 1)
        return remote(part_of(dwbuf, g, half), part_of(inn.at[side], g, half), n_s.at[half, g], n_r.at[side, half, g],
                      (to * pn.G + x, col))

    def detour(g, up):
        side = 0 if up else 1
        return remote(part_of(dwbuf, g, 1), part_of(inn.at[side], g, 1), n_s.at[1, g], e_r.at[g], (row, col - 2))

    def relay(g, up):
        side, to = (0, slab + 1) if up else (1, slab - 1)
        return remote(part_of(inn.at[side], g, 1), part_of(inn.at[side], g, 1), e_s.at[g], n_r.at[side, 1, g],
                      (to * pn.G + x, col))

    def early_links(g, act):
        for going, up, around in ((rising, True, detour_up), (falling, False, detour_down)):
            @pl.when(going & jnp.logical_not(around))
            def _(up=up):
                for half in (0, 1):
                    act(link(g, half, up))

            @pl.when(around)
            def _(up=up):
                act(detour(g, up))

    def late_links(g, act):
        for around, up in ((detour_up, True), (detour_down, False)):
            @pl.when(around)
            def _(up=up):
                act(link(g, 0, up))

    def arrived(g, side):
        for half in (0, 1):
            at = part_of(inn.at[side], g, half)
            pltpu.make_async_copy(at, at, n_r.at[side, half, g]).wait()

    def add(g, side):
        dwbuf[taps(g)] = (dwbuf[taps(g)].astype(F32) + inn[side, taps(g)].astype(F32)).astype(BF16)

    close_a, close_b = closing & jnp.logical_not(first), ((slab == 1) & (col == 0)) | ((slab == n - 2) & (col == 1))
    end_closing, end_getting = closing & first, first & (home_of(pn, lax.rem(col + 2, pn.C)) == slab)
    across = (row, lax.rem(col + 2, pn.C))

    def share_y(g, half, src):
        return remote(src, part_of(dw_out, g, half), g_s.at[0, half, g], g_r.at[half, g], across)

    def share_core(g, half, src):
        return remote(src, part_of(dw_out, g, half), g_s.at[1, half, g], g_r.at[half, g], partner)

    def share_on(g, half):
        return remote(part_of(dw_out, g, half), part_of(dw_out, g, half), g_s.at[0, half, g], g_r.at[half, g], partner)

    def share(g, half, src):
        share_y(g, half, src).start()
        share_core(g, half, src).start()
        pltpu.make_async_copy(src, part_of(dw_out, g, half), g_r.at[half, g]).start()

    def landed(g, half):
        at = part_of(dw_out, g, half)
        pltpu.make_async_copy(at, at, g_r.at[half, g]).wait()

    def partial(g, side):
        return remote(part_of(dwbuf, g, 1), part_of(inn.at[1 - side], g, 0), b_s.at[g], b_r.at[g], (row, col - 2))

    rows_of = (pl.ds(0, half_rows), pl.ds(half_rows, half_rows))

    def from_far(g):
        for here, side in ((slab == 1, 1), (slab == n - 2, 0)):
            @pl.when(close_a & here)
            def _(side=side):
                arrived(g, side)
                add(g, side)
                partial(g, side).start()

    def close_half(g):
        for here, side in ((slab == 1, 0), (slab == n - 2, 1)):
            @pl.when(close_a & here)
            def _(side=side):
                at = part_of(inn.at[side], g, 0)
                pltpu.make_async_copy(at, at, n_r.at[side, 0, g]).wait()
                dwbuf[taps(g), rows_of[0]] = (
                    dwbuf[taps(g), rows_of[0]].astype(F32) + inn[side, taps(g), rows_of[0]].astype(F32)
                ).astype(BF16)
                share(g, 0, part_of(dwbuf, g, 0))

            @pl.when(close_b & here)
            def _(side=side):
                at = part_of(inn.at[side], g, 1)
                pltpu.make_async_copy(at, at, n_r.at[side, 1, g]).wait()
                at = part_of(inn.at[side], g, 0)
                pltpu.make_async_copy(at, at, b_r.at[g]).wait()
                inn[side, taps(g), rows_of[1]] = (
                    inn[side, taps(g), rows_of[1]].astype(F32) + inn[side, taps(g), rows_of[0]].astype(F32)
                ).astype(BF16)
                share(g, 1, part_of(inn.at[side], g, 1))

    def give_way():
        @pl.when(yielding)
        def _():
            for g in range(YIELD):
                early_links(g, lambda c: c.wait_send())
            pl.semaphore_signal(turn_sem, inc=1, device_id=partner, device_id_type=MESH)

        @pl.when(detour_up | detour_down)
        def _():
            pl.semaphore_wait(turn_sem, 1)

        for g in range(GROUPS):
            late_links(g, lambda c: c.start())

    def relay_all():
        for role, up in ((relay_up, True), (relay_down, False)):
            @pl.when(role)
            def _(up=up):
                pl.semaphore_wait(turn_sem, 1)
                for g in range(GROUPS):
                    at = part_of(inn.at[0 if up else 1], g, 1)
                    pltpu.make_async_copy(at, at, e_r.at[g]).wait()
                    relay(g, up).start()

    def pass_on(g):
        for going, up in ((rising, True), (falling, False)):
            @pl.when(going & jnp.logical_not(first))
            def _(up=up):
                arrived(g, 0 if up else 1)
                add(g, 0 if up else 1)
                for half in (0, 1):
                    link(g, half, up).start()

    def close(g):
        for here, side in ((slab == 0, 1), (slab == n - 1, 0)):
            @pl.when(end_closing & here)
            def _(side=side):
                arrived(g, side)
                add(g, side)
                for half in (0, 1):
                    share(g, half, part_of(dwbuf, g, half))

    def serve(g):
        if not pn.exchange:
            return
        if g < GROUPS:
            pass_on(g)
        if g > 1:
            close(g - 2)
            from_far(g - 2)

    def last_round(g):
        if g < GROUPS:
            close_half(g)
        if g > 1:
            for half, role in ((0, end_getting | close_b), (1, end_getting | close_a)):
                @pl.when(role)
                def _(half=half):
                    landed(g - 2, half)
                    share_on(g - 2, half).start()

    def start_group(g):
        if not pn.exchange:
            return

        @pl.when(first)
        def _():
            early_links(g, lambda c: c.start())

    def weight_gradients(branch):
        qt[...] = qraw[branch].T
        for i in (-1, 0, 1):
            g = 3 * (branch - 1) + i + 1
            q_turned = qt[...]
            if i != 0:
                q_turned = q_turned * lane_masks[pl.ds(2 * (branch - 1) + (i + 1) // 2, 1)]
            window = pl.ds((pn.hb + i * pn.steps[branch - 1]) * px, pn.own)
            for j in (-1, 0, 1):
                dwbuf[3 * g + j + 1] = dot(q_turned, xs[3 + j * branch, window]).T.astype(BF16)
            if branch < 3:
                start_group(g)

    def feature_gradients(branch):
        def turn(rp, carry):
            at = pl.multiple_of(rp * 2 * S, 16)
            moved = dot(shifts[pl.ds((branch - 1) * 4 * S, 4 * S)], qraw[branch, pl.ds(at, 2 * S)]).astype(BF16)
            qs[branch - 1, 0, pl.ds(at, 2 * S)] = moved[:2 * S]
            qs[branch - 1, 1, pl.ds(at, 2 * S)] = moved[2 * S:]
            return carry

        lax.fori_loop(0, H // 2, turn, 0, unroll=6)
        for i in (-1, 0, 1):
            g = 3 * (branch - 1) + i + 1
            mask_at = (2 * (branch - 1) + (i + 1) // 2) * H

            def block(rb, carry, i=i, g=g, mask_at=mask_at):
                at = pl.ds(pl.multiple_of(rb * many * px, 16), many * px)
                y = dot_nt(qs[branch - 1, 0, at], wbuf[3 * g])
                y = y + dot_nt(qraw[branch, at], wbuf[3 * g + 1])
                y = y + dot_nt(qs[branch - 1, 1, at], wbuf[3 * g + 2])
                if i != 0:
                    y = jnp.concatenate(
                        [y[r * S:(r + 1) * S] * masks[mask_at + rb * many * pn.rpb + r] for r in range(many * pn.rpb)], axis=0
                    )
                to = pl.ds(pl.multiple_of((rb * many + pn.hb + i * pn.steps[branch - 1]) * px, 16), many * px)
                dxe[to] = dxe[to] + y
                return carry

            lax.fori_loop(0, MEMBERS // many, block, 0)

    receive_y(1)
    receive_y(2)
    load_x.wait()
    load_w.wait()
    receive_x(1)
    received(1)
    weight_gradients(1)
    receive_y(3)
    receive_x(2)
    feature_gradients(1)
    receive_y(0)
    received(2)
    weight_gradients(2)
    receive_x(3)
    serve(0)
    feature_gradients(2)
    received(3)
    receive_x(0)
    if pn.exchange:
        for kk in range(1, MEMBERS):
            dproj_slab(kk).start()
        dproj_own().start()
    serve(1)
    weight_gradients(3)
    serve(2)
    feature_gradients(3)

    hsend[0] = dxe[pl.ds(0, pn.hb * px)].astype(BF16)
    hsend[1] = dxe[pl.ds((pn.hb + MEMBERS) * px, pn.hb * px)].astype(BF16)

    @pl.when(slab > 0)
    def _():
        remote(hsend.at[0], hrecv.at[1], h_s.at[0], h_r.at[1], member(slab - 1, me)).start()

    @pl.when(slab < n - 1)
    def _():
        remote(hsend.at[1], hrecv.at[0], h_s.at[1], h_r.at[0], member(slab + 1, me)).start()

    for g in (6, 7, 8):
        start_group(g)
    serve(3)

    if pn.exchange:
        for kk in range(1, MEMBERS):
            dproj_slab(kk).wait()
        dproj_own().wait()
        total = dp1[0].astype(F32)
        for m in range(1, MEMBERS):
            total = total + dp1[m].astype(F32)
        dps[...] = total.astype(BF16)

        @pl.when(slab != home_slab)
        def _():
            dproj_home().start()

        @pl.when(slab == home_slab)
        def _():
            pltpu.make_async_copy(dps, dp2.at[slab], p2_r.at[slab]).start()

    received(0)
    dwbuf[POOL] = dot_tn(means[...].astype(BF16), q4[...]).astype(BF16)
    dwbuf[POINT] = dot(qraw[0].T, xs[3, pl.ds(pn.hb * px, pn.own)]).T.astype(BF16)
    start_group(GROUPS - 1)
    serve(4)
    pooled = dot_nt(q4[...], wbuf[POOL]) * inv_counts[...]
    pooled_high = pooled.astype(BF16)
    pooled_low = (pooled - pooled_high.astype(F32)).astype(BF16)
    pooled_rows[...] = dot(hot_rows[...], pooled_high) + dot(hot_rows[...], pooled_low)

    def finish(rb, carry):
        at = pl.ds(pl.multiple_of(rb * many * px, 16), many * px)
        to = pl.ds(pl.multiple_of((rb * many + pn.hb) * px, 16), many * px)
        y = dot_nt(qraw[0, at], wbuf[POINT])
        y = jnp.concatenate(
            [y[r * S:(r + 1) * S] + pooled_rows[pl.ds(rb * many * pn.rpb + r, 1)] for r in range(many * pn.rpb)], axis=0
        )
        dxe[to] = dxe[to] + y
        return carry

    lax.fori_loop(0, MEMBERS // many, finish, 0)
    if pn.exchange:
        relay_all()
    serve(5)

    @pl.when(slab > 0)
    def _():
        remote(hsend.at[0], hrecv.at[1], h_s.at[0], h_r.at[1], member(slab - 1, me)).wait_send()
        remote(hsend.at[1], hrecv.at[0], h_s.at[1], h_r.at[0], member(slab - 1, me)).wait_recv()

    @pl.when(slab < n - 1)
    def _():
        remote(hsend.at[1], hrecv.at[0], h_s.at[1], h_r.at[0], member(slab + 1, me)).wait_send()
        remote(hsend.at[0], hrecv.at[1], h_s.at[0], h_r.at[1], member(slab + 1, me)).wait_recv()

    @pl.when(slab == 0)
    def _():
        hrecv[0] = jnp.zeros((pn.hb * px, pn.cs), BF16)

    @pl.when(slab == n - 1)
    def _():
        hrecv[1] = jnp.zeros((pn.hb * px, pn.cs), BF16)

    for rb in range(pn.hb):
        low, high = (pn.hb + rb) * px, (MEMBERS + rb) * px
        dxe[pl.ds(low, px)] = dxe[pl.ds(low, px)] + hrecv[0, pl.ds(rb * px, px)].astype(F32)
        dxe[pl.ds(high, px)] = dxe[pl.ds(high, px)] + hrecv[1, pl.ds(rb * px, px)].astype(F32)

    column = lax.broadcasted_iota(jnp.int32, (S, pn.cs), 0).astype(F32)
    for b in range(H // 8):
        rows = []
        for r in range(8 * b, 8 * b + 8):
            values = dxe[pl.ds(pn.hb * px + r * S, S)]
            rows.append(jnp.where(column < masks[6 * H + MARGIN + r], values, 0.0))
        moved = dot(sel_t[...], jnp.concatenate(rows, axis=0).astype(BF16)).astype(BF16)
        pack[8 * b // h, :, pl.ds(8 * b % h, 8)] = moved.reshape(pn.cols, 8, pn.cs)
    own_lanes = pl.ds(pl.multiple_of(slice_of(pn, me) * pn.cs, 128), pn.cs)
    back = []
    for kk in range(1, MEMBERS):
        other = lax.rem(me + kk, MEMBERS)
        xo, co = other // pn.C, lax.rem(other, pn.C)
        c = remote(pack.at[xo, pl.ds(co * pn.bc, pn.bc)], dx_out.at[:, :, own_lanes], x_s.at[kk], x_r.at[kk],
                   member(slab, other))
        c.start()
        back.append(c)
    c = pltpu.make_async_copy(pack.at[x, pl.ds(col * pn.bc, pn.bc)], dx_out.at[:, :, own_lanes], x_r.at[0])
    c.start()
    back.append(c)

    def close_dproj():
        @pl.when(slab == home_slab)
        def _():
            for z in range(n):
                pltpu.make_async_copy(dp2.at[z], dp2.at[z], p2_r.at[z]).wait()
            total = dp2[0].astype(F32)
            for z in range(1, n):
                total = total + dp2[z].astype(F32)
            dpf[...] = total
            for c in range(pn.C):
                @pl.when((x == lax.rem(me, pn.G)) & (col == c))
                def _():
                    pltpu.make_async_copy(dpf, dproj_out, p3_r.at[0]).start()

                @pl.when(jnp.logical_not((x == lax.rem(me, pn.G)) & (col == c)))
                def _(c=c):
                    dproj_give(c).start()

    if pn.exchange:
        serve(6)
        serve(7)
        give_way()
        for g in range(8, GROUPS + 2):
            serve(g)
        close_dproj()
        for g in range(GROUPS + 2):
            last_round(g)

        def settle(g, carry):
            @pl.when(jnp.logical_not(yielding & (g < YIELD)))
            def _():
                early_links(g, lambda c: c.wait_send())

            late_links(g, lambda c: c.wait_send())
            for role, up in ((relay_up, True), (relay_down, False)):
                @pl.when(role)
                def _(up=up):
                    relay(g, up).wait_send()

            @pl.when(close_a)
            def _():
                partial(g, 0).wait_send()

            for half, gives, passes in ((0, end_closing | close_a, end_getting | close_b),
                                        (1, end_closing | close_b, end_getting | close_a)):
                @pl.when(gives)
                def _(half=half):
                    share_y(g, half, part_of(dwbuf, g, half)).wait_send()
                    share_core(g, half, part_of(dwbuf, g, half)).wait_send()

                @pl.when(passes)
                def _(half=half):
                    share_on(g, half).wait_send()

                @pl.when(jnp.logical_not(passes))
                def _(half=half):
                    landed(g, half)

            return carry

        lax.fori_loop(0, GROUPS - 1, settle, 0)
        settle(GROUPS - 1, 0)

        @pl.when(slab != home_slab)
        def _():
            dproj_home().wait_send()

        @pl.when(slab == home_slab)
        def _():
            for c in range(pn.C):
                @pl.when(jnp.logical_not((x == lax.rem(me, pn.G)) & (col == c)))
                def _(c=c):
                    dproj_give(c).wait_send()

        pltpu.make_async_copy(dproj_out, dproj_out, p3_r.at[0]).wait()
    else:
        c = pltpu.make_async_copy(dwbuf, dw_out, g_r.at[0, 0])
        c.start()
        c.wait()
        dproj_out[...] = jnp.zeros(dproj_out.shape, F32)
    for c in back:
        c.wait()


def conv_backward(pn, q, xs, w, dproj, q4, means, hot_rows, inv_counts, masks, lane_masks, shifts, sel_t):
    dma = pltpu.SemaphoreType.DMA
    vmem = pl.BlockSpec(memory_space=pltpu.VMEM)
    hbm = pl.BlockSpec(memory_space=pl.ANY)
    shape = jax.ShapeDtypeStruct
    n = pn.slabs if pn.exchange else 1
    sums = TAPS if pn.exchange else 1
    block_rows = 5 * pn.width // MEMBERS
    return pl.pallas_call(
        functools.partial(back_kernel, pn),
        out_shape=(
            shape((TAPS, pn.cs, pn.width), BF16),
            shape((pn.bc, pn.h, pn.channels), BF16),
            shape((block_rows, pn.width), F32),
        ),
        in_specs=[hbm] * 4 + [vmem] * 4 + [pl.BlockSpec(memory_space=pltpu.SMEM)] + [vmem] * 3,
        out_specs=(hbm, hbm, vmem),
        scratch_shapes=[
            pltpu.VMEM((7, pn.ext, pn.cs), BF16),
            pltpu.VMEM((TAPS, pn.cs, pn.width), BF16),
            pltpu.VMEM((4, pn.own, pn.width), BF16),
            pltpu.VMEM((3, 2, pn.own, pn.width), BF16),
            pltpu.VMEM((pn.width, pn.own), BF16),
            pltpu.VMEM((pn.ext, pn.cs), F32),
            pltpu.VMEM((TAPS, pn.cs, pn.width), BF16),
            pltpu.VMEM((2, sums, pn.cs, pn.width), BF16),
            pltpu.VMEM((2, pn.hb * pn.px, pn.cs), BF16),
            pltpu.VMEM((2, pn.hb * pn.px, pn.cs), BF16),
            pltpu.VMEM((pn.G, pn.cols, pn.h, pn.cs), BF16),
            pltpu.VMEM((pn.H, pn.cs), F32),
            pltpu.VMEM((MEMBERS, block_rows, pn.width), BF16),
            pltpu.VMEM((block_rows, pn.width), BF16),
            pltpu.VMEM((n, block_rows, pn.width), BF16),
            pltpu.VMEM((block_rows, pn.width), F32),
            dma((6,)), dma((4, 3)), dma((4, 3)), dma((4,)), dma((4,)), dma((4, 3)), dma((4, 3)),
            dma((2, GROUPS)), dma((2, 2, GROUPS)), dma((GROUPS,)), dma((GROUPS,)), dma((2, 2, GROUPS)), dma((2, GROUPS)),
            dma((GROUPS,)), dma((GROUPS,)), pltpu.SemaphoreType.REGULAR,
            dma((2,)), dma((2,)), dma((MEMBERS,)), dma((MEMBERS,)),
            dma((MEMBERS,)), dma((MEMBERS,)), dma((1,)), dma((n,)), dma((pn.C,)), dma((1,)),
        ],
        compiler_params=pltpu.CompilerParams(collective_id=2, has_side_effects=True, vmem_limit_bytes=61900 * 1024),
        name="conv_backward",
    )(q, xs, w, dproj, q4, means, hot_rows, inv_counts, masks, lane_masks, shifts, sel_t)


def column_tables(pn):
    S, bp, bc = pn.S, pn.bp, pn.bc
    sel = np.zeros((7, 2, S, 2, pn.C * bp), np.float32)
    shifts = np.zeros((3, 2, 2, S, 2, S), np.float32)
    for r in range(2):
        for c in range(pn.cols):
            for v in range(-3, 4):
                s = c + v * DILATIONS[0]
                if 0 <= s < pn.cols:
                    sel[v + 3, r, c, r, (s // bc) * bp + s % bc] = 1.0
            for b, d in enumerate(DILATIONS):
                for n, j in enumerate((-1, 1)):
                    s = c - j * d
                    if 0 <= s < pn.cols:
                        shifts[b, n, r, c, r, s] = 1.0
    sel = sel.reshape(7 * 2 * S, 2 * pn.C * bp)
    sel_t = sel[3 * 2 * S:4 * 2 * S].T
    sel_c = np.zeros((pn.cols, 8, 8, S), np.float32)
    for c in range(pn.cols):
        for r in range(8):
            sel_c[c, r, r, c] = 1.0
    sel_c = sel_c.reshape(8 * pn.cols, 8 * S)
    return (jnp.asarray(sel, BF16), jnp.asarray(sel_t, BF16), jnp.asarray(sel_c, BF16), jnp.asarray(shifts.reshape(12 * S, 2 * S), BF16))


def per_device(
    features, crop_rows, crop_cols, w_point, w_atrous, w_pool, w_proj, gains, biases, cotangent
):
    h, bc, channels = features.shape
    pn = Plan(lax.axis_size("row"), lax.axis_size("col"), h, bc, channels, gains.shape[1], crop_rows.shape[0])
    row, col = lax.axis_index("row"), lax.axis_index("col")
    slab, x = row // pn.G, row % pn.G
    crop_ids = jnp.arange(pn.crops, dtype=jnp.int32)
    ends = jnp.cumsum(crop_rows)
    counts = (crop_rows * crop_cols).astype(F32)
    pixels = jnp.sum(counts)

    def crop_of(rows):
        found = jnp.sum((rows[:, None] >= ends[None, :]).astype(jnp.int32), axis=1)
        return jnp.where(rows < 0, -1, found)

    def widths_of(crop):
        return jnp.sum(jnp.where(crop[:, None] == crop_ids[None, :], crop_cols[None, :], 0), axis=1)

    feats = features.reshape(h, bc, MEMBERS, pn.cs).transpose(2, 0, 1, 3)
    feats = jnp.pad(feats, ((0, 0), (0, 0), (0, pn.bp - bc), (0, 0)))
    cot = jnp.pad(cotangent, ((0, 0), (0, pn.bp - bc), (0, 0)))

    slab_rows = slab * pn.H - MARGIN + jnp.arange(pn.H + 2 * MARGIN, dtype=jnp.int32)
    crops = crop_of(slab_rows)
    mid = crops[MARGIN:MARGIN + pn.H]
    same = jnp.stack(
        [crops[MARGIN + i * d:MARGIN + i * d + pn.H] == mid for d in DILATIONS for i in (-1, 1)]
    ).astype(F32)
    lane_masks = jnp.pad(jnp.repeat(same, pn.S, axis=1), ((0, 2), (0, 0))).astype(BF16)
    ncp_ids = jnp.arange(pn.ncp, dtype=jnp.int32)
    hot_rows = (mid[:, None] == ncp_ids[None, :]).astype(BF16)
    hot_t = jnp.repeat(hot_rows.T, pn.S, axis=1)
    inv_counts = jnp.pad(1.0 / counts, (0, pn.ncp - pn.crops))[:, None]

    k = x * pn.C + col
    block_crop = lax.dynamic_slice_in_dim(mid, k * pn.rpb, pn.rpb)
    columns = jnp.arange(pn.S, dtype=jnp.int32)
    valid = (columns[None, :] < widths_of(block_crop)[:, None]).astype(F32).reshape(pn.px, 1)
    block_hot = jnp.repeat((block_crop[:, None] == ncp_ids[None, :]).astype(BF16), pn.S, axis=0)
    block_hot_t = jnp.repeat((ncp_ids[:, None] == block_crop[None, :]).astype(BF16), pn.S, axis=1)

    sel, sel_t, sel_c, shifts = column_tables(pn)
    w, w_two = w_atrous.transpose(1, 0, 2), jnp.stack([w_point, w_pool])
    proj = w_proj.reshape(pn.C, pn.proj // pn.C, pn.width)
    proj = jnp.pad(proj, ((0, 0), (0, pn.piece - pn.proj // pn.C), (0, 0)))
    if not pn.exchange:
        w = lax.all_gather(jnp.concatenate([w, w_two], axis=0), "row", axis=1, tiled=True)
        w = lax.dynamic_slice_in_dim(w, slice_of(pn, x * pn.C + col) * pn.cs, pn.cs, axis=1)
        w, w_two = w[:POINT], w[POINT:]
    flat = jnp.concatenate([same.reshape(-1), widths_of(crops).astype(F32)])
    p, xs, w_own, means, p4, own_cot, pieces = conv_forward(
        pn, feats, w, w_two, cot, proj, flat, sel, hot_t, inv_counts
    )
    full_proj = pieces[:, :, :pn.proj // pn.C].transpose(1, 0, 2, 3).reshape(5 * pn.width, pn.width)
    q, q4, d_proj, res, d_gains, d_biases = norms(
        pn, p, p4, gains, biases, valid, (1.0 / pixels)[None], full_proj, own_cot, block_hot, block_hot_t, sel_t
    )
    dw, dx, dproj_sum = conv_backward(
        pn, q, xs, w_own, d_proj, q4, means, hot_rows, inv_counts, flat, lane_masks, shifts, sel_c
    )
    if pn.exchange:
        d_proj = dproj_sum
    else:
        whole = jnp.zeros((TAPS, channels, pn.width), BF16)
        whole = lax.dynamic_update_slice(whole, dw, (0, slice_of(pn, x * pn.C + col) * pn.cs, 0))
        whole = lax.psum(whole, "col")
        dw = lax.psum_scatter(whole, "row", scatter_dimension=1, tiled=True)
        d_proj = lax.psum(d_proj, "col")
        d_proj = lax.psum_scatter(d_proj.astype(F32), "row", scatter_dimension=0, tiled=True)
    result = res[:, :bc]
    d_features = dx.transpose(1, 0, 2)
    d_point = dw[POINT].astype(F32)
    d_atrous = dw[:POINT].astype(F32).transpose(1, 0, 2)
    d_pool = dw[POOL].astype(F32)
    return (result, d_features, d_point, d_atrous, d_pool, d_proj, d_gains, d_biases)


def solution(mesh):
    return jax.shard_map(
        per_device,
        mesh=mesh,
        in_specs=(
            P("row", "col", None),
            P(),
            P(),
            P("row", None),
            P("row", None, None),
            P("row", None),
            P("row", None),
            P(),
            P(),
            P("row", "col", None),
        ),
        out_specs=(
            P("row", "col", None),
            P("row", "col", None),
            P("row", None),
            P("row", None, None),
            P("row", None),
            P("row", None),
            P(),
            P(),
        ),
        check_vma=False,
    )
```
